32 devices in a mesh: groups: 2 (over y), row: 4 (over z), col: 4 (over x, core).
Axes of the slice: x: 2, y: 2, z: 4, core: 2. Of those that a mesh axis runs over, the one named last changes fastest.
Arguments:
- alignment_embedding: bfloat16 [16, 512, 64], P(None, ('groups', 'row', 'col')), parts along dimension 1, may hold values from -6 to 6
- alignment_cell_exists: int32 [16, 512], P(None, ('groups', 'row', 'col')), parts along dimension 1, may hold values 0 or 1
- alignment_lines_exist: int32 [32], P('groups'), parts along dimension 0, may hold values 0 or 1
- sitewise_factors: bfloat16 [64, 64], replicated, may hold values from -0.75 to 0.75
- pairing_matrix: bfloat16 [1024, 128], replicated, may hold values from -0.1875 to 0.1875
- offset_vector: float32 [128], replicated, may hold values from -3 to 3
- upstream_adjoint: bfloat16 [512, 256, 128], P(('groups', 'row'), 'col'), parts along dimension 0, may hold values from -6 to 6
Outputs:
- coupling_update: bfloat16 [512, 256, 128], P(('groups', 'row'), 'col'), parts along dimension 0
- alignment_embedding_adjoint: float32 [16, 512, 64], P(None, ('groups', 'row', 'col')), parts along dimension 1
- sitewise_factors_adjoint: float32 [128, 64], P('groups'), parts along dimension 0
- pairing_matrix_adjoint: float32 [2048, 128], P('groups'), parts along dimension 0
- offset_vector_slope: float32 [256], P('groups'), parts along dimension 0
The draws below stay inside these ranges and needn't reach their ends.
There are 2 independent parts, one for each index of `groups`. The reference program is written for one: setup_inputs(seed, part) draws one part's arguments, and reference() takes and returns one part's arrays. A program takes and returns all parts, laid end to end along the dimension named above; an argument that names none is the same for every part. Nothing has to cross between parts.
All inputs are finite; a program needn't handle non-finite values. No bound on the sum of `alignment_cell_exists` on one device may be relied on, other than what follows from the above.
Results may differ from the reference program's by a relative error of at most 0.0095.
Values may be sent and summed in bfloat16 or wider, within the bound.
No kernel may reach another device: no remote copies, remote signals or barrier semaphores. Data moves between devices by JAX's collectives and lax.ppermute only.
A program may use at most 64 MiB of HBM per device.

```python
import jax
import jax.numpy as jnp
from jax import lax

ALIGN_FEATURES = 64
PROJ_DEPTH = 32
PAIR_FEATURES = 128
ALIGN_DEPTH = 16
BLK = 64
WINDOW_LENGTH = 256


def touch_ends(array, rng, least, high):
    shape = array.shape
    index_at = [jax.random.randint(jax.random.fold_in(rng, axis), (), 0, shape[axis]) for axis in range(len(shape))]
    array = array.at[tuple(index_at)].set(least)
    longest = shape.index(max(shape))
    index_at[longest] = (index_at[longest] + 1) % shape[longest]
    return array.at[tuple(index_at)].set(high)


def levels(stream_key, extent, split, low, top_value):
    level = 1.0
    for axis_at, parts in split:
        draws = jax.random.uniform(jax.random.fold_in(jax.random.fold_in(stream_key, 6), axis_at), (parts,), jnp.float32, low / len(split), top_value / len(split))
        level = level * jnp.repeat(jnp.exp(draws), extent[axis_at] // parts).reshape((-1,) + (1,) * (len(extent) - 1 - axis_at))
    return level


def bell_draw(key, extent, deviation, limit, pieces=(), kind=jnp.bfloat16):
    loudness = levels(key, extent, pieces, -0.22, 0.18) if pieces else 1.0
    entries = jax.random.normal(key, extent, jnp.float32) * deviation * loudness
    return jnp.minimum(jnp.maximum(entries, -limit), limit).astype(kind)


def setup_inputs(seed: int = 0, part: int = 0) -> dict:
    splits = jax.random.split(jax.random.key(seed), 8)
    own_keys = jax.random.split(jax.random.fold_in(splits[7], part), 8)
    alignment_embedding = bell_draw(own_keys[0], (ALIGN_DEPTH, WINDOW_LENGTH, ALIGN_FEATURES), 1.0, 6.0, ((1, 16),))
    alignment_cell_exists = touch_ends((jax.random.randint(own_keys[1], (ALIGN_DEPTH, WINDOW_LENGTH), 0, 4) < 3).astype(jnp.int32), jax.random.fold_in(own_keys[1], 1), 0, 1)
    alignment_lines_exist = touch_ends((jax.random.randint(own_keys[2], (ALIGN_DEPTH,), 0, 8) < 7).astype(jnp.int32), jax.random.fold_in(own_keys[2], 1), 0, 1)
    sitewise_factors = bell_draw(splits[3], (ALIGN_FEATURES, 2 * PROJ_DEPTH), ALIGN_FEATURES ** -0.5, 0.75)
    pairing_matrix = bell_draw(splits[4], (PROJ_DEPTH * PROJ_DEPTH, PAIR_FEATURES), (PROJ_DEPTH * PROJ_DEPTH) ** -0.5, 0.1875)
    offset_vector = bell_draw(splits[5], (PAIR_FEATURES,), 0.5, 3.0, (), jnp.float32)
    upstream_adjoint = bell_draw(own_keys[6], (WINDOW_LENGTH, WINDOW_LENGTH, PAIR_FEATURES), 1.0, 6.0, ((0, 4), (1, 4)))
    return {"alignment_embedding": alignment_embedding, "alignment_cell_exists": alignment_cell_exists, "alignment_lines_exist": alignment_lines_exist, "sitewise_factors": sitewise_factors, "pairing_matrix": pairing_matrix, "offset_vector": offset_vector, "upstream_adjoint": upstream_adjoint}


def layer_norm(forward_results):
    center = forward_results - lax.optimization_barrier(jnp.mean(forward_results, axis=-1, keepdims=True))
    spread = lax.optimization_barrier(jnp.mean(center * center, axis=-1, keepdims=True))
    return center * lax.rsqrt(spread + 1e-05)

def reference(alignment_embedding, alignment_cell_exists, alignment_lines_exist, sitewise_factors, pairing_matrix, offset_vector, upstream_adjoint):
    highest = lax.Precision.HIGHEST
    forward_results = alignment_embedding.astype(jnp.float32)
    normed = layer_norm(forward_results).astype(jnp.bfloat16)
    weight = (alignment_cell_exists * alignment_lines_exist[:, None]).astype(jnp.float32)
    proj = jnp.einsum('stk,kn->stn', normed.astype(jnp.float32), sitewise_factors.astype(jnp.float32))
    proj = (proj * weight[:, :, None]).astype(jnp.bfloat16)
    tokens_first = jnp.transpose(proj, (1, 0, 2))
    left_all = tokens_first[:, :, :PROJ_DEPTH]
    right_all = tokens_first[:, :, PROJ_DEPTH:]
    weight_t = weight.T
    count = jnp.dot(weight_t, weight_t.T, precision=highest)
    right_f = right_all.astype(jnp.float32)

    def one_block(carry, index):
        d_right, d_wout = carry
        start = (index * BLK).astype(jnp.int32)
        left_rows = lax.dynamic_slice_in_dim(left_all, start, BLK, 0).astype(jnp.float32)
        count_rows = lax.dynamic_slice_in_dim(count, start, BLK, 0)
        cot_rows = lax.dynamic_slice_in_dim(upstream_adjoint, start, BLK, 0).reshape(BLK * WINDOW_LENGTH, PAIR_FEATURES)
        outer = jnp.einsum('isc,jse->ijce', left_rows, right_f).reshape(BLK, WINDOW_LENGTH, PROJ_DEPTH * PROJ_DEPTH)
        outer = (outer / (count_rows + 0.001)[:, :, None]).astype(jnp.bfloat16)
        flat = outer.reshape(BLK * WINDOW_LENGTH, PROJ_DEPTH * PROJ_DEPTH)
        pair_rows = (jnp.dot(flat, pairing_matrix, preferred_element_type=jnp.float32) + offset_vector).astype(jnp.bfloat16)
        d_wout = d_wout + jnp.dot(flat.T, cot_rows, preferred_element_type=jnp.float32)
        d_outer = jnp.dot(cot_rows, pairing_matrix.T, preferred_element_type=jnp.float32).reshape(BLK, WINDOW_LENGTH, PROJ_DEPTH * PROJ_DEPTH)
        d_outer = (d_outer / (count_rows + 0.001)[:, :, None]).astype(jnp.bfloat16)
        d_outer = d_outer.reshape(BLK, WINDOW_LENGTH, PROJ_DEPTH, PROJ_DEPTH).astype(jnp.float32)
        adjoint_leftside = jnp.einsum('ijce,jse->isc', d_outer, right_f)
        d_right = d_right + jnp.einsum('ijce,isc->jse', d_outer, left_rows)
        return ((d_right, d_wout), (pair_rows.reshape(BLK, WINDOW_LENGTH, PAIR_FEATURES), adjoint_leftside))
    initial_accumulator = (jnp.zeros((WINDOW_LENGTH, ALIGN_DEPTH, PROJ_DEPTH), jnp.float32), jnp.zeros((PROJ_DEPTH * PROJ_DEPTH, PAIR_FEATURES), jnp.float32))
    (d_right, pairing_matrix_adjoint), (pair_blocks, adjoint_leftside_pieces) = lax.scan(one_block, initial_accumulator, jnp.arange(WINDOW_LENGTH // BLK, dtype=jnp.int32))
    coupling_update = pair_blocks.reshape(WINDOW_LENGTH, WINDOW_LENGTH, PAIR_FEATURES)
    adjoint_leftside = adjoint_leftside_pieces.reshape(WINDOW_LENGTH, ALIGN_DEPTH, PROJ_DEPTH)
    offset_vector_slope = lax.optimization_barrier(jnp.sum(upstream_adjoint.astype(jnp.float32), axis=(0, 1)))
    d_proj = jnp.transpose(jnp.concatenate([adjoint_leftside, d_right], axis=-1), (1, 0, 2)) * weight[:, :, None]
    sitewise_factors_adjoint = jnp.einsum('stk,stn->kn', normed.astype(jnp.float32), d_proj, precision=highest)
    standardized_adjoint = jnp.einsum('stn,kn->stk', d_proj, sitewise_factors.astype(jnp.float32), precision=highest)
    unused, reverse_pass_rule = jax.vjp(layer_norm, forward_results)
    alignment_embedding_adjoint = reverse_pass_rule(standardized_adjoint)[0]
    return (coupling_update, alignment_embedding_adjoint, sitewise_factors_adjoint, pairing_matrix_adjoint, offset_vector_slope)
```

```python
import functools

import jax
import jax.numpy as jnp
from jax import lax
from jax.experimental import pallas as pl
from jax.experimental.pallas import tpu as pltpu
from jax.sharding import PartitionSpec as P

F32 = jnp.float32
BF16 = jnp.bfloat16
LANES = 128
VMEM_LIMIT = 40 * 1024 * 1024
NT = (((1,), (1,)), ((), ()))


def dot(left, right):
    return jnp.dot(left, right, preferred_element_type=F32)


def dot_nt(left, right):
    return lax.dot_general(left, right, NT, preferred_element_type=F32)


def iota(shape, axis):
    return lax.broadcasted_iota(jnp.int32, shape, axis)


def one_hot(mask):
    return jnp.where(mask, 1.0, 0.0).astype(BF16)


def full(shape):
    return pl.BlockSpec(shape, lambda *g: (0,) * len(shape))


def cost(flops, nbytes):
    return pl.CostEstimate(flops=int(flops), bytes_accessed=int(nbytes), transcendentals=0)


def call(kernel, grid, in_specs, out_specs, out_shape, scratch=(), estimate=None):
    return pl.pallas_call(
        kernel,
        grid=grid,
        in_specs=in_specs,
        out_specs=out_specs,
        out_shape=out_shape,
        scratch_shapes=list(scratch),
        compiler_params=pltpu.CompilerParams(vmem_limit_bytes=VMEM_LIMIT),
        cost_estimate=estimate,
    )


def stats(x):
    center = x - jnp.mean(x, axis=-1, keepdims=True)
    scale = lax.rsqrt(jnp.mean(center * center, axis=-1, keepdims=True) + 1e-05)
    return center * scale, scale


def prep_kernel(depth, own, x_ref, cell_ref, line_ref, by_token_ref, by_row_ref):
    rows = depth * own
    normed, _ = stats(x_ref[...].astype(F32))
    features = normed.shape[1]
    cell = cell_ref[...].astype(F32).astype(BF16)
    pick = one_hot(iota((rows, depth), 0) // own == iota((rows, depth), 1))
    line = line_ref[...].astype(F32)
    line_column = jnp.sum(pick.astype(F32) * line, axis=1, keepdims=True)
    cells = dot(pick, cell)
    here = iota((rows, own), 0) % own == iota((rows, own), 1)
    weight = jnp.sum(jnp.where(here, cells, 0.0), axis=1, keepdims=True) * line_column
    masked = normed.astype(BF16).astype(F32) * weight
    wide = jnp.concatenate([masked, jnp.zeros((rows, LANES - features), F32)], axis=1)
    lane = iota((rows, LANES), 1)
    at = lane == features + iota((rows, LANES), 0) // own
    wide = (wide + jnp.where(at, weight, 0.0)).astype(BF16)
    by_row_ref[...] = wide
    p, q = iota((rows, rows), 0), iota((rows, rows), 1)
    swap = one_hot(q == (p % depth) * own + p // depth)
    by_token_ref[...] = dot(swap, wide).astype(BF16)


def scaled_pair(up_ref, inv, at):
    parts = [up_ref[i].astype(F32) * inv[:, i : i + 1] for i in (at, at + 1)]
    return jnp.concatenate(parts, axis=1).astype(BF16)


def fill_v(up_ref, inv, bt, v_ref, depth):
    chunk, _, pair = up_ref.shape
    width = v_ref.shape[0]
    for at in range(0, chunk, 2):
        v = dot(bt, scaled_pair(up_ref, inv, at)).astype(BF16)
        for k in range(2):
            part = v[:, k * pair : (k + 1) * pair].reshape(width, depth, pair)
            v_ref[:, (at + k) * depth : (at + k + 1) * depth, :] = part


def fill_t(a_chunk, wc_ref, t_ref, depth):
    chunk, rows, pair = t_ref.shape
    width = rows // depth
    for e in range(0, width, 2):
        t = dot(a_chunk, wc_ref[:, e * pair : (e + 2) * pair]).astype(BF16)
        for k in range(2):
            part = t[:, k * pair : (k + 1) * pair].reshape(chunk, depth, pair)
            t_ref[:, (e + k) * depth : (e + k + 1) * depth, :] = part


def two(ref, at):
    return jnp.concatenate([ref[at], ref[at + 1]], axis=1)


def weight_kernel(depth, n, pieces, *refs):
    a_refs, b_refs = refs[:pieces], refs[pieces : 2 * pieces]
    up_ref, w_ref, wt_ref, perm_ref = refs[2 * pieces : 2 * pieces + 4]
    outs = refs[2 * pieces + 4 :]
    mi_ref, mj_ref, a_ref, b_ref, bt_ref, inv_ref, bias_ref = outs[:7]
    send_refs = outs[7 : 7 + n]
    at_ref, v_ref, acc_ref = outs[7 + n :]
    g, last = pl.program_id(0), pl.num_programs(0) - 1
    chunk, block, pair = up_ref.shape
    features = w_ref.shape[0]
    width = w_ref.shape[1] // 2
    r, c = lax.axis_index("row"), lax.axis_index("col")

    @pl.when(g == 0)
    def _():
        if pieces == 1:
            mi_ref[...] = a_refs[0][...]
            mj_ref[...] = b_refs[0][...]
        else:
            own = block // pieces
            for k in range(pieces):
                src = lax.rem(c - k + n, n)
                rows = pl.ds(pl.multiple_of(src * own * depth, own * depth), own * depth)
                mi_ref[rows, :] = a_refs[k][...]
                src = lax.rem(r - k + n, n)
                rows = pl.ds(pl.multiple_of(src * own, own), own)
                for s in range(depth):
                    mj_ref[s, rows, :] = b_refs[k][s * own : (s + 1) * own, :]
        pad = jnp.zeros((LANES - features, 2 * width), BF16)
        w = jnp.concatenate([w_ref[...], pad], axis=0)
        pad = jnp.zeros((2 * width, LANES - features), BF16)
        wt = jnp.concatenate([wt_ref[...], pad], axis=1)
        mi = mi_ref[...]
        a_ref[...] = dot(mi, w[:, :width]).astype(BF16)
        at_ref[...] = dot_nt(wt[:width, :], mi).astype(BF16)
        b = jnp.zeros((block, width * depth), F32)
        seen = jnp.zeros((block, LANES), F32)
        for s in range(depth):
            mj = mj_ref[s]
            seen = seen + mj.astype(F32)
            part = dot(mj, w[:, width:]).astype(BF16)
            b = b + dot(part, perm_ref[s * width : (s + 1) * width, :])
        b_ref[...] = b.astype(BF16)
        bt_ref[...] = b.T.astype(BF16)
        keep = iota((block, LANES), 1) >= features
        seen_j = jnp.where(keep, seen, 0.0).astype(BF16)
        rows = block * depth
        gather = one_hot(iota((block, rows), 0) == iota((block, rows), 1) // depth)
        seen_i = dot(gather, mi).astype(BF16)
        for k in range(block // chunk):
            count = dot_nt(seen_j, seen_i[k * chunk : (k + 1) * chunk, :])
            inv_ref[k] = 1.0 / (count + 0.001)
        acc_ref[...] = jnp.zeros_like(acc_ref)
        bias_ref[...] = jnp.zeros_like(bias_ref)

    bias_ref[0:1, :] += jnp.sum(
        jnp.sum(up_ref[...].astype(F32), axis=0), axis=0, keepdims=True
    )
    fill_v(up_ref, inv_ref[g], bt_ref[...], v_ref, depth)
    span = chunk * depth
    a_t = at_ref[:, pl.ds(pl.multiple_of(g * span, span), span)]
    for e in range(0, width, 2):
        part = dot(a_t, two(v_ref, e))
        for k in range(2):
            acc_ref[(e + k) * width : (e + k + 1) * width, :] += part[:, k * pair : (k + 1) * pair]

    @pl.when(g == last)
    def _():
        rows = acc_ref.shape[0] // n
        for k in range(n):
            at = pl.multiple_of(lax.rem(c + k, n) * rows, rows)
            send_refs[k][...] = acc_ref[pl.ds(at, rows), :].astype(BF16)


def token_kernel(depth, n, split, *refs):
    up_ref, inv_ref, a_ref, bt_ref, wc_ref, mi_ref, mj_ref, perm_ref, bias_ref = refs[:9]
    outs = refs[9:]
    small_ref = outs[0]
    count = n if split else 1
    da_refs, db_refs = outs[1 : 1 + count], outs[1 + count : 1 + 2 * count]
    v_ref, t_ref, da_ref, db_ref = outs[1 + 2 * count :]
    g, last = pl.program_id(0), pl.num_programs(0) - 1
    chunk, block, pair = up_ref.shape
    width = wc_ref.shape[0]
    span = chunk * depth
    r, c = lax.axis_index("row"), lax.axis_index("col")
    inv = inv_ref[g]

    @pl.when(g == 0)
    def _():
        db_ref[...] = jnp.zeros_like(db_ref)

    fill_v(up_ref, inv, bt_ref[...], v_ref, depth)
    d_a = jnp.zeros((width, span), F32)
    for e in range(0, width, 2):
        d_a = d_a + dot_nt(wc_ref[:, e * pair : (e + 2) * pair], two(v_ref, e))
    da_ref[:, pl.ds(pl.multiple_of(g * span, span), span)] = d_a.astype(BF16)
    a_chunk = a_ref[pl.ds(pl.multiple_of(g * span, span), span), :]
    fill_t(a_chunk, wc_ref, t_ref, depth)
    d_b = db_ref[...]
    for at in range(0, chunk, 2):
        d_b = d_b + dot_nt(scaled_pair(up_ref, inv, at), two(t_ref, at))
    db_ref[...] = d_b

    @pl.when(g == last)
    def _():
        d_b = db_ref[...].astype(BF16)
        turned = dot_nt(perm_ref[...], d_b).astype(BF16)
        left = dot(da_ref[...], mi_ref[...])
        right = jnp.zeros((width, LANES), F32)
        for s in range(depth):
            right = right + dot(turned[s * width : (s + 1) * width, :], mj_ref[s])
        small_ref[0:width, :] = left
        small_ref[width : 2 * width, :] = right
        small_ref[2 * width :, :] = jnp.zeros_like(small_ref[2 * width :, :])
        small_ref[2 * width : 2 * width + 1, :] = bias_ref[0:1, :]
        if split:
            own = block // n
            for k in range(n):
                lanes = own * depth
                at = pl.multiple_of(lax.rem(c + k, n) * lanes, lanes)
                da_refs[k][...] = da_ref[:, pl.ds(at, lanes)]
                at = pl.multiple_of(lax.rem(r + k, n) * own, own)
                db_refs[k][...] = db_ref[pl.ds(at, own), :].astype(BF16)
        else:
            da_refs[0][...] = da_ref[...]
            db_refs[0][...] = d_b


def update_kernel(depth, inv_ref, a_ref, b_ref, wc_ref, offset_ref, out_ref, t_ref):
    g = pl.program_id(0)
    chunk, block, pair = out_ref.shape
    span = chunk * depth
    inv = inv_ref[g]
    fill_t(a_ref[pl.ds(pl.multiple_of(g * span, span), span), :], wc_ref, t_ref, depth)
    b = b_ref[...]
    offset = offset_ref[...]
    for at in range(0, chunk, 2):
        part = dot(b, two(t_ref, at))
        for k in range(2):
            value = part[:, k * pair : (k + 1) * pair] * inv[:, at + k : at + k + 1] + offset
            out_ref[at + k] = value.astype(BF16)


def sum_kernel(axis, n, *refs):
    ins, outs = refs[:n], refs[n:]
    me = lax.axis_index(axis)
    for k in range(n):
        at = lax.rem(me + k, n)
        total = ins[0][at].astype(F32)
        for ref in ins[1:]:
            total = total + ref[at].astype(F32)
        outs[k][...] = total.astype(BF16)


def owner_kernel(depth, own, n, *refs):
    da_refs, db_refs = refs[:n], refs[n : 2 * n]
    x_ref, message_ref, wt_ref, perm_ref, out_ref = refs[2 * n :]
    rows = depth * own
    width = wt_ref.shape[0] // 2
    features = x_ref.shape[1]
    p, q = iota((rows, rows), 0), iota((rows, rows), 1)
    swap = one_hot(q == (p % own) * depth + p // own)
    d_a = jnp.zeros((rows, width), F32)
    d_b = jnp.zeros((own, width * depth), F32)
    for k in range(n):
        d_a = d_a + dot_nt(swap, da_refs[k][...])
        d_b = d_b + dot_nt(db_refs[k][...], perm_ref[...])
    d_b = jnp.concatenate([d_b[:, s * width : (s + 1) * width] for s in range(depth)], axis=0)
    highest = lax.Precision.HIGHEST
    wt = wt_ref[...].astype(F32)
    d_normed = jnp.dot(d_a, wt[:width, :], precision=highest, preferred_element_type=F32)
    d_normed = d_normed + jnp.dot(d_b, wt[width:, :], precision=highest, preferred_element_type=F32)
    message = message_ref[...].astype(F32)
    mask = iota((rows, LANES), 1) >= features
    d_normed = d_normed * jnp.sum(jnp.where(mask, message, 0.0), axis=1, keepdims=True)
    normed, scale = stats(x_ref[...].astype(F32))
    mean = jnp.mean(d_normed, axis=-1, keepdims=True)
    along = jnp.mean(d_normed * normed, axis=-1, keepdims=True)
    out_ref[...] = scale * (d_normed - mean - normed * along)


def place_kernel(n, *refs):
    ins, out_ref, full_ref = refs[:n], refs[n], refs[n + 1]
    r, c = lax.axis_index("row"), lax.axis_index("col")
    width = out_ref.shape[0]
    each = width // (n * n)
    for k in range(n):
        col = lax.rem(c - k + n, n)
        for m in range(n):
            row = lax.rem(r - m + n, n)
            value = ins[k][m].astype(F32).reshape(each, width, LANES)
            full_ref[pl.ds((col * n + row) * each, each)] = value
    for e in range(width):
        out_ref[:, e, :] = full_ref[e]


def per_device(
    n,
    alignment_embedding,
    alignment_cell_exists,
    alignment_lines_exist,
    sitewise_factors,
    pairing_matrix,
    offset_vector,
    upstream_adjoint,
):
    depth, own, features = alignment_embedding.shape
    width = sitewise_factors.shape[1] // 2
    block, pair = upstream_adjoint.shape[0], upstream_adjoint.shape[2]
    rows, chunk = depth * own, 16
    steps = block // chunk
    split = own % 16 == 0
    axes = ("row", "col")
    sds = jax.ShapeDtypeStruct

    def along_col(x, k):
        return lax.ppermute(x, "col", [(i, (i + k) % n) for i in range(n)])

    def along_row(x, k):
        return lax.ppermute(x, "row", [(i, (i + k) % n) for i in range(n)])

    def to_column(x, k):
        pairs = [(i * n + j, (j + k) % n * n + i) for i in range(n) for j in range(n)]
        return lax.ppermute(x, axes, pairs)

    def to_owner(x, k):
        pairs = [(i * n + j, j * n + (i + k) % n) for i in range(n) for j in range(n)]
        return lax.ppermute(x, axes, pairs)

    r, c = lax.axis_index("row"), lax.axis_index("col")

    def cut(x, axis, at):
        size = x.shape[axis] // n
        return lax.dynamic_slice_in_dim(x, at % n * size, size, axis)

    x = alignment_embedding.reshape(rows, features)
    by_token, by_row = call(
        functools.partial(prep_kernel, depth, own),
        (),
        [full(x.shape), full(alignment_cell_exists.shape), full((1, depth))],
        [full((rows, LANES))] * 2,
        [sds((rows, LANES), BF16)] * 2,
    )(x, alignment_cell_exists, alignment_lines_exist.reshape(1, depth))
    a_pieces = [by_token] + [along_col(by_token, k) for k in range(1, n)]
    b_pieces = [to_column(by_row, k) for k in range(n)]
    if not split:
        order = (c - jnp.arange(n)) % n
        held = jnp.zeros((n, rows, LANES), BF16).at[order].set(jnp.stack(a_pieces))
        a_pieces = [held.reshape(block * depth, LANES)]
        order = (r - jnp.arange(n)) % n
        held = jnp.zeros((n, depth, own, LANES), BF16)
        held = held.at[order].set(jnp.stack(b_pieces).reshape(n, depth, own, LANES))
        b_pieces = [held.transpose(1, 0, 2, 3).reshape(depth, block, LANES)]
    pieces = len(a_pieces)

    wide = width * depth
    source = jnp.arange(wide)
    perm = (jnp.arange(wide)[None, :] == (source % width * depth + source // width)[:, None]).astype(BF16)
    factors_t = sitewise_factors.T
    pairing_wide = pairing_matrix.reshape(width, width * pair)
    up_spec = pl.BlockSpec((chunk, block, pair), lambda g: (g, 0, 0))
    tokens = block * depth
    out_shapes = [
        sds((tokens, LANES), BF16),
        sds((depth, block, LANES), BF16),
        sds((tokens, width), BF16),
        sds((block, wide), BF16),
        sds((wide, block), BF16),
        sds((steps, block, chunk), F32),
        sds((8, pair), F32),
    ] + [sds((width * width // n, pair), BF16)] * n
    outs = call(
        functools.partial(weight_kernel, depth, n, pieces),
        (steps,),
        [full(p.shape) for p in a_pieces]
        + [full(p.shape) for p in b_pieces]
        + [up_spec, full(sitewise_factors.shape), full(factors_t.shape), full(perm.shape)],
        [full(o.shape) for o in out_shapes],
        out_shapes,
        [
            pltpu.VMEM((width, tokens), BF16),
            pltpu.VMEM((width, chunk * depth, pair), BF16),
            pltpu.VMEM((width * width, pair), F32),
        ],
        cost(5e9, 8e6),
    )(*a_pieces, *b_pieces, upstream_adjoint, sitewise_factors, factors_t, perm)
    mi, mj, a, b, b_t, inv, bias = outs[:7]
    sends = list(outs[7:])

    shard = width * width // (n * n)
    parts = [sends[0]] + [along_col(sends[k], k) for k in range(1, n)]
    parts = [part.reshape(n, shard, pair) for part in parts]

    count = n if split else 1
    piece = block // count
    out_shapes = (
        [sds((2 * width + 16, LANES), F32)]
        + [sds((width, piece * depth), BF16)] * count
        + [sds((piece, wide), BF16)] * count
    )
    outs = call(
        functools.partial(token_kernel, depth, n, split),
        (steps,),
        [up_spec]
        + [full(v.shape) for v in (inv, a, b_t, pairing_wide, mi, mj, perm, bias)],
        [full(o.shape) for o in out_shapes],
        out_shapes,
        [
            pltpu.VMEM((width, chunk * depth, pair), BF16),
            pltpu.VMEM((chunk, wide, pair), BF16),
            pltpu.VMEM((width, tokens), BF16),
            pltpu.VMEM((block, wide), F32),
        ],
        cost(8e9, 8e6),
    )(upstream_adjoint, inv, a, b_t, pairing_wide, mi, mj, perm, bias)
    small = outs[0]
    d_a, d_b = list(outs[1 : 1 + count]), list(outs[1 + count :])
    if not split:
        d_a = [cut(d_a[0], 1, c + k) for k in range(n)]
        d_b = [cut(d_b[0], 0, r + k) for k in range(n)]
    d_a = [d_a[0]] + [along_col(d_a[k], k) for k in range(1, n)]
    d_b = [to_owner(d_b[k], k) for k in range(n)]
    small = small + sum(along_col(small, k) for k in range(1, n))
    small = small + sum(along_row(small, k) for k in range(1, n))

    shards = call(
        functools.partial(sum_kernel, "row", n),
        (),
        [full(part.shape) for part in parts],
        [full((shard, pair))] * n,
        [sds((shard, pair), BF16)] * n,
    )(*parts)
    mine = [shards[0].astype(F32)] + [along_row(shards[k], k).astype(F32) for k in range(1, n)]
    mine = sum(mine).astype(BF16)
    gathered = jnp.stack([mine] + [along_row(mine, k) for k in range(1, n)])
    gathered = [gathered] + [along_col(gathered, k) for k in range(1, n)]

    coupling_update = call(
        functools.partial(update_kernel, depth),
        (steps,),
        [full(v.shape) for v in (inv, a, b, pairing_wide)] + [full((1, pair))],
        up_spec,
        sds((block, block, pair), BF16),
        [pltpu.VMEM((chunk, wide, pair), BF16)],
        cost(5e9, 8e6),
    )(inv, a, b, pairing_wide, offset_vector.reshape(1, pair))

    embedding_adjoint = call(
        functools.partial(owner_kernel, depth, own, n),
        (),
        [full(v.shape) for v in d_a + d_b]
        + [full(v.shape) for v in (x, by_row, factors_t, perm)],
        full((rows, features)),
        sds((rows, features), F32),
    )(*d_a, *d_b, x, by_row, factors_t, perm)

    if width % (n * n) == 0:
        placed = call(
            functools.partial(place_kernel, n),
            (),
            [full(part.shape) for part in gathered],
            full((width, width, pair)),
            sds((width, width, pair), F32),
            [pltpu.VMEM((width, width, pair), F32)],
        )(*gathered)
    else:
        held = jnp.stack(gathered)
        held = held[(c - jnp.arange(n)) % n][:, (r - jnp.arange(n)) % n]
        placed = held.astype(F32).reshape(width, width, pair).transpose(1, 0, 2)
    factors = jnp.concatenate([small[:width], small[width : 2 * width]], axis=0)
    return (
        coupling_update,
        embedding_adjoint.reshape(depth, own, features),
        factors[:, :features].T,
        placed.reshape(width * width, pair),
        small[2 * width],
    )


def solution(mesh):
    n = mesh.shape["col"]
    placed = (
        P(None, ("groups", "row", "col"), None),
        P(None, ("groups", "row", "col")),
        P("groups"),
        P(),
        P(),
        P(),
        P(("groups", "row"), "col", None),
    )
    return jax.shard_map(
        functools.partial(per_device, n),
        mesh=mesh,
        in_specs=placed,
        out_specs=(
            P(("groups", "row"), "col", None),
            P(None, ("groups", "row", "col"), None),
            P("groups", None),
            P("groups", None),
            P("groups"),
        ),
        check_vma=False,
    )
```

```python
import functools

import jax
import jax.numpy as jnp
from jax import lax
from jax.experimental import pallas as pl
from jax.experimental.pallas import tpu as pltpu
from jax.sharding import PartitionSpec as P

F32 = jnp.float32
BF16 = jnp.bfloat16
LANES = 128
VMEM_LIMIT = 40 * 1024 * 1024
NT = (((1,), (1,)), ((), ()))


def dot(left, right):
    return jnp.dot(left, right, preferred_element_type=F32)


def dot_nt(left, right):
    return lax.dot_general(left, right, NT, preferred_element_type=F32)


def iota(shape, axis):
    return lax.broadcasted_iota(jnp.int32, shape, axis)


def one_hot(mask):
    return jnp.where(mask, 1.0, 0.0).astype(BF16)


def full(shape):
    return pl.BlockSpec(shape, lambda *g: (0,) * len(shape))


def cost(flops, nbytes):
    return pl.CostEstimate(flops=int(flops), bytes_accessed=int(nbytes), transcendentals=0)


def call(kernel, grid, in_specs, out_specs, out_shape, scratch=(), estimate=None):
    return pl.pallas_call(
        kernel,
        grid=grid,
        in_specs=in_specs,
        out_specs=out_specs,
        out_shape=out_shape,
        scratch_shapes=list(scratch),
        compiler_params=pltpu.CompilerParams(vmem_limit_bytes=VMEM_LIMIT),
        cost_estimate=estimate,
    )


def stats(x):
    center = x - jnp.mean(x, axis=-1, keepdims=True)
    scale = lax.rsqrt(jnp.mean(center * center, axis=-1, keepdims=True) + 1e-05)
    return center * scale, scale


def prep_kernel(depth, own, x_ref, cell_ref, line_ref, by_token_ref, by_row_ref):
    rows = depth * own
    normed, _ = stats(x_ref[...].astype(F32))
    features = normed.shape[1]
    cell = cell_ref[...].astype(F32).astype(BF16)
    pick = one_hot(iota((rows, depth), 0) // own == iota((rows, depth), 1))
    line = line_ref[...].astype(F32)
    line_column = jnp.sum(pick.astype(F32) * line, axis=1, keepdims=True)
    cells = dot(pick, cell)
    here = iota((rows, own), 0) % own == iota((rows, own), 1)
    weight = jnp.sum(jnp.where(here, cells, 0.0), axis=1, keepdims=True) * line_column
    masked = normed.astype(BF16).astype(F32) * weight
    wide = jnp.concatenate([masked, jnp.zeros((rows, LANES - features), F32)], axis=1)
    lane = iota((rows, LANES), 1)
    at = lane == features + iota((rows, LANES), 0) // own
    wide = (wide + jnp.where(at, weight, 0.0)).astype(BF16)
    by_row_ref[...] = wide
    p, q = iota((rows, rows), 0), iota((rows, rows), 1)
    swap = one_hot(q == (p % depth) * own + p // depth)
    by_token_ref[...] = dot(swap, wide).astype(BF16)


def scaled_pair(up_ref, inv, at):
    parts = [up_ref[i].astype(F32) * inv[:, i : i + 1] for i in (at, at + 1)]
    return jnp.concatenate(parts, axis=1).astype(BF16)


def fill_v(up_ref, inv, bt, v_ref, depth):
    chunk, _, pair = up_ref.shape
    width = v_ref.shape[0]
    for at in range(0, chunk, 2):
        v = dot(bt, scaled_pair(up_ref, inv, at)).astype(BF16)
        for k in range(2):
            part = v[:, k * pair : (k + 1) * pair].reshape(width, depth, pair)
            v_ref[:, (at + k) * depth : (at + k + 1) * depth, :] = part


def fill_t(a_chunk, wc_ref, t_ref, depth):
    chunk, rows, pair = t_ref.shape
    width = rows // depth
    for e in range(0, width, 2):
        t = dot(a_chunk, wc_ref[:, e * pair : (e + 2) * pair]).astype(BF16)
        for k in range(2):
            part = t[:, k * pair : (k + 1) * pair].reshape(chunk, depth, pair)
            t_ref[:, (e + k) * depth : (e + k + 1) * depth, :] = part


def two(ref, at):
    return jnp.concatenate([ref[at], ref[at + 1]], axis=1)


def weight_kernel(depth, n, pieces, *refs):
    a_refs, b_refs = refs[:pieces], refs[pieces : 2 * pieces]
    up_ref, w_ref, wt_ref, perm_ref, wc_ref = refs[2 * pieces : 2 * pieces + 5]
    outs = refs[2 * pieces + 5 :]
    mi_ref, mj_ref, a_ref, b_ref, inv_ref, bias_ref, dw_ref, da_ref = outs[:8]
    bt_ref, at_ref, v_ref, acc_ref = outs[8:]
    g, last = pl.program_id(0), pl.num_programs(0) - 1
    chunk, block, pair = up_ref.shape
    features = w_ref.shape[0]
    width = w_ref.shape[1] // 2
    r, c = lax.axis_index("row"), lax.axis_index("col")

    @pl.when(g == 0)
    def _():
        if pieces == 1:
            mi_ref[...] = a_refs[0][...]
            mj_ref[...] = b_refs[0][...]
        else:
            own = block // pieces
            for k in range(pieces):
                src = lax.rem(c - k + n, n)
                rows = pl.ds(pl.multiple_of(src * own * depth, own * depth), own * depth)
                mi_ref[rows, :] = a_refs[k][...]
                src = lax.rem(r - k + n, n)
                rows = pl.ds(pl.multiple_of(src * own, own), own)
                for s in range(depth):
                    mj_ref[s, rows, :] = b_refs[k][s * own : (s + 1) * own, :]
        pad = jnp.zeros((LANES - features, 2 * width), BF16)
        w = jnp.concatenate([w_ref[...], pad], axis=0)
        pad = jnp.zeros((2 * width, LANES - features), BF16)
        wt = jnp.concatenate([wt_ref[...], pad], axis=1)
        mi = mi_ref[...]
        a_ref[...] = dot(mi, w[:, :width]).astype(BF16)
        at_ref[...] = dot_nt(wt[:width, :], mi).astype(BF16)
        b = jnp.zeros((block, width * depth), F32)
        seen = jnp.zeros((block, LANES), F32)
        for s in range(depth):
            mj = mj_ref[s]
            seen = seen + mj.astype(F32)
            part = dot(mj, w[:, width:]).astype(BF16)
            b = b + dot(part, perm_ref[s * width : (s + 1) * width, :])
        b_ref[...] = b.astype(BF16)
        bt_ref[...] = b.T.astype(BF16)
        keep = iota((block, LANES), 1) >= features
        seen_j = jnp.where(keep, seen, 0.0).astype(BF16)
        rows = block * depth
        gather = one_hot(iota((block, rows), 0) == iota((block, rows), 1) // depth)
        seen_i = dot(gather, mi).astype(BF16)
        for k in range(block // chunk):
            count = dot_nt(seen_j, seen_i[k * chunk : (k + 1) * chunk, :])
            inv_ref[k] = 1.0 / (count + 0.001)
        acc_ref[...] = jnp.zeros_like(acc_ref)
        bias_ref[...] = jnp.zeros_like(bias_ref)

    bias_ref[0:1, :] += jnp.sum(
        jnp.sum(up_ref[...].astype(F32), axis=0), axis=0, keepdims=True
    )
    fill_v(up_ref, inv_ref[g], bt_ref[...], v_ref, depth)
    span = chunk * depth
    a_t = at_ref[:, pl.ds(pl.multiple_of(g * span, span), span)]
    d_a = jnp.zeros((width, span), F32)
    for e in range(0, width, 2):
        v = two(v_ref, e)
        part = dot(a_t, v)
        for k in range(2):
            acc_ref[(e + k) * width : (e + k + 1) * width, :] += part[:, k * pair : (k + 1) * pair]
        d_a = d_a + dot_nt(wc_ref[:, e * pair : (e + 2) * pair], v)
    da_ref[:, pl.ds(pl.multiple_of(g * span, span), span)] = d_a.astype(BF16)

    @pl.when(g == last)
    def _():
        dw_ref[...] = acc_ref[...].astype(BF16)


def token_kernel(depth, *refs):
    up_ref, inv_ref, a_ref, wc_ref, mi_ref, mj_ref, perm_ref, bias_ref, da_ref = refs[:9]
    small_ref, out_ref, t_ref, db_ref = refs[9:]
    g, last = pl.program_id(0), pl.num_programs(0) - 1
    chunk = up_ref.shape[0]
    width = wc_ref.shape[0]
    span = chunk * depth
    inv = inv_ref[g]

    @pl.when(g == 0)
    def _():
        db_ref[...] = jnp.zeros_like(db_ref)

    a_chunk = a_ref[pl.ds(pl.multiple_of(g * span, span), span), :]
    fill_t(a_chunk, wc_ref, t_ref, depth)
    d_b = db_ref[...]
    for at in range(0, chunk, 2):
        d_b = d_b + dot_nt(scaled_pair(up_ref, inv, at), two(t_ref, at))
    db_ref[...] = d_b

    @pl.when(g == last)
    def _():
        d_b = db_ref[...].astype(BF16)
        out_ref[...] = d_b
        turned = dot_nt(perm_ref[...], d_b).astype(BF16)
        right = jnp.zeros((width, LANES), F32)
        for s in range(depth):
            right = right + dot(turned[s * width : (s + 1) * width, :], mj_ref[s])
        small_ref[0:width, :] = dot(da_ref[...], mi_ref[...]).astype(BF16)
        small_ref[width : 2 * width, :] = right.astype(BF16)
        tail = jnp.broadcast_to(bias_ref[0:1, :], (16, LANES))
        small_ref[2 * width :, :] = tail.astype(BF16)


def update_kernel(depth, inv_ref, a_ref, b_ref, wc_ref, offset_ref, out_ref, t_ref):
    g = pl.program_id(0)
    chunk, block, pair = out_ref.shape
    span = chunk * depth
    inv = inv_ref[g]
    fill_t(a_ref[pl.ds(pl.multiple_of(g * span, span), span), :], wc_ref, t_ref, depth)
    b = b_ref[...]
    offset = offset_ref[...]
    for at in range(0, chunk, 2):
        part = dot(b, two(t_ref, at))
        for k in range(2):
            value = part[:, k * pair : (k + 1) * pair] * inv[:, at + k : at + k + 1] + offset
            out_ref[at + k] = value.astype(BF16)


def owner_kernel(depth, own, *refs):
    da_refs, db_refs = refs[:2], refs[2:4]
    x_ref, message_ref, wt_ref, perm_ref, out_ref = refs[4:]
    rows = depth * own
    width = wt_ref.shape[0] // 2
    features = x_ref.shape[1]
    p, q = iota((rows, rows), 0), iota((rows, rows), 1)
    swap = one_hot(q == (p % own) * depth + p // own)
    d_a = jnp.zeros((rows, width), F32)
    d_b = jnp.zeros((own, width * depth), F32)
    for k in range(2):
        d_a = d_a + dot_nt(swap, da_refs[k][...])
        d_b = d_b + dot_nt(db_refs[k][...], perm_ref[...])
    d_b = jnp.concatenate([d_b[:, s * width : (s + 1) * width] for s in range(depth)], axis=0)
    highest = lax.Precision.HIGHEST
    wt = wt_ref[...].astype(F32)
    d_normed = jnp.dot(d_a, wt[:width, :], precision=highest, preferred_element_type=F32)
    d_normed = d_normed + jnp.dot(d_b, wt[width:, :], precision=highest, preferred_element_type=F32)
    message = message_ref[...].astype(F32)
    mask = iota((rows, LANES), 1) >= features
    d_normed = d_normed * jnp.sum(jnp.where(mask, message, 0.0), axis=1, keepdims=True)
    normed, scale = stats(x_ref[...].astype(F32))
    mean = jnp.mean(d_normed, axis=-1, keepdims=True)
    along = jnp.mean(d_normed * normed, axis=-1, keepdims=True)
    out_ref[...] = scale * (d_normed - mean - normed * along)


def place_kernel(in_ref, out_ref):
    for e in range(in_ref.shape[0]):
        out_ref[:, e, :] = in_ref[e].astype(F32)


def lay_out(x):
    rows, lanes = x.shape
    if lanes % LANES:
        return x.reshape(-1, LANES)
    return x.reshape(rows, lanes // LANES, LANES).transpose(1, 0, 2).reshape(-1, LANES)


def lay_back(x, rows, lanes):
    if lanes % LANES:
        return x.reshape(rows, lanes)
    return x.reshape(lanes // LANES, rows, LANES).transpose(1, 0, 2).reshape(rows, lanes)


def bit_of(axis, bit):
    return (lax.axis_index(axis) >> bit) & 1


def swap_parts(parts, axis, bit, n):
    parts = [part.reshape(-1, LANES) for part in parts]
    message = jnp.concatenate(parts, axis=0) if len(parts) > 1 else parts[0]
    message = lax.ppermute(message, axis, [(i, i ^ (1 << bit)) for i in range(n)])
    got, at = [], 0
    for part in parts:
        got.append(message[at : at + part.shape[0]])
        at += part.shape[0]
    return got


def halves(x, axis, bit):
    x = x.reshape((x.shape[0] // 2, 2) + x.shape[1:])
    here = bit_of(axis, bit)
    keep = lax.dynamic_index_in_dim(x, here, 1, keepdims=False)
    return keep, lax.dynamic_index_in_dim(x, 1 - here, 1, keepdims=False)


def in_order(mine, other, axis, bit, at):
    first = bit_of(axis, bit) == 0
    low = jnp.where(first, mine, other)
    return jnp.stack([low, jnp.where(first, other, mine)], axis=at)


def add(mine, other):
    other = other.reshape(mine.shape)
    return lax.optimization_barrier((mine.astype(F32) + other.astype(F32)).astype(BF16))


def per_device(
    n,
    alignment_embedding,
    alignment_cell_exists,
    alignment_lines_exist,
    sitewise_factors,
    pairing_matrix,
    offset_vector,
    upstream_adjoint,
):
    depth, own, features = alignment_embedding.shape
    width = sitewise_factors.shape[1] // 2
    block, pair = upstream_adjoint.shape[0], upstream_adjoint.shape[2]
    rows, chunk = depth * own, 16
    steps = block // chunk
    split = own % 16 == 0
    axes = ("row", "col")
    sds = jax.ShapeDtypeStruct

    def along_col(x, k):
        return lax.ppermute(x, "col", [(i, (i + k) % n) for i in range(n)])

    def along_row(x, k):
        return lax.ppermute(x, "row", [(i, (i + k) % n) for i in range(n)])

    def to_column(x, k):
        pairs = [(i * n + j, (j + k) % n * n + i) for i in range(n) for j in range(n)]
        return lax.ppermute(x, axes, pairs)

    r, c = lax.axis_index("row"), lax.axis_index("col")
    x = alignment_embedding.reshape(rows, features)
    by_token, by_row = call(
        functools.partial(prep_kernel, depth, own),
        (),
        [full(x.shape), full(alignment_cell_exists.shape), full((1, depth))],
        [full((rows, LANES))] * 2,
        [sds((rows, LANES), BF16)] * 2,
    )(x, alignment_cell_exists, alignment_lines_exist.reshape(1, depth))
    a_pieces = [by_token] + [along_col(by_token, k) for k in range(1, n)]
    b_pieces = [to_column(by_row, k) for k in range(n)]
    if not split:
        order = (c - jnp.arange(n)) % n
        held = jnp.zeros((n, rows, LANES), BF16).at[order].set(jnp.stack(a_pieces))
        a_pieces = [held.reshape(block * depth, LANES)]
        order = (r - jnp.arange(n)) % n
        held = jnp.zeros((n, depth, own, LANES), BF16)
        held = held.at[order].set(jnp.stack(b_pieces).reshape(n, depth, own, LANES))
        b_pieces = [held.transpose(1, 0, 2, 3).reshape(depth, block, LANES)]
    pieces = len(a_pieces)

    wide = width * depth
    source = jnp.arange(wide)
    perm = (jnp.arange(wide)[None, :] == (source % width * depth + source // width)[:, None]).astype(BF16)
    factors_t = sitewise_factors.T
    pairing_wide = pairing_matrix.reshape(width, width * pair)
    up_spec = pl.BlockSpec((chunk, block, pair), lambda g: (g, 0, 0))
    tokens = block * depth
    out_shapes = [
        sds((tokens, LANES), BF16),
        sds((depth, block, LANES), BF16),
        sds((tokens, width), BF16),
        sds((block, wide), BF16),
        sds((steps, block, chunk), F32),
        sds((8, pair), F32),
        sds((width * width, pair), BF16),
        sds((width, tokens), BF16),
    ]
    outs = call(
        functools.partial(weight_kernel, depth, n, pieces),
        (steps,),
        [full(p.shape) for p in a_pieces]
        + [full(p.shape) for p in b_pieces]
        + [up_spec]
        + [full(v.shape) for v in (sitewise_factors, factors_t, perm, pairing_wide)],
        [full(o.shape) for o in out_shapes],
        out_shapes,
        [
            pltpu.VMEM((wide, block), BF16),
            pltpu.VMEM((width, tokens), BF16),
            pltpu.VMEM((width, chunk * depth, pair), BF16),
            pltpu.VMEM((width * width, pair), F32),
        ],
        cost(5e9, 8e6),
    )(*a_pieces, *b_pieces, upstream_adjoint, sitewise_factors, factors_t, perm, pairing_wide)
    mi, mj, a, b, inv, bias, d_pairing, d_a = outs

    bits = n.bit_length() - 1
    d_pairing = d_pairing.reshape(n, -1, LANES)
    d_a = jnp.stack([lay_out(d_a[:, k * rows : (k + 1) * rows]) for k in range(n)])
    da_parts = [d_a]
    for bit in range(bits):
        keep, go = halves(d_pairing, "col", bit)
        if bit:
            d_a = add(*da_parts)
        da_keep, da_go = halves(d_a, "col", bit)
        got, da_got = swap_parts([go, da_go], "col", bit, n)
        d_pairing = add(keep, got)
        da_parts = [da_keep, da_got.reshape(da_keep.shape)]

    out_shapes = [sds((2 * width + 16, LANES), BF16), sds((block, wide), BF16)]
    small, d_b = call(
        functools.partial(token_kernel, depth),
        (steps,),
        [up_spec]
        + [full(v.shape) for v in (inv, a, pairing_wide, mi, mj, perm, bias)]
        + [full((width, tokens))],
        [full(o.shape) for o in out_shapes],
        out_shapes,
        [pltpu.VMEM((chunk, wide, pair), BF16), pltpu.VMEM((block, wide), F32)],
        cost(5e9, 8e6),
    )(upstream_adjoint, inv, a, pairing_wide, mi, mj, perm, bias, outs[7])

    d_b = jnp.stack([lay_out(d_b[k * own : (k + 1) * own]) for k in range(n)])[:, None]
    for bit in range(bits):
        keep, go = halves(d_b, "col", bit)
        got, small_got = swap_parts([go, small], "col", bit, n)
        small = add(small, small_got)
        d_b = in_order(keep, got.reshape(keep.shape), "col", bit, 1)
        d_b = d_b.reshape((keep.shape[0], -1) + keep.shape[2:])
    db_parts = [d_b[0]]
    for bit in range(bits):
        if bit:
            db_parts = [add(*db_parts)]
        db_keep, db_go = halves(db_parts[0], "row", bit)
        got, db_got, small_got = swap_parts([d_pairing, db_go, small], "row", bit, n)
        d_pairing = add(d_pairing, got)
        small = add(small, small_got)
        db_parts = [db_keep, db_got.reshape(db_keep.shape)]
    d_pairing = d_pairing.reshape(1, -1, LANES)
    for bit in reversed(range(bits)):
        (got,) = swap_parts([d_pairing], "col", bit, n)
        d_pairing = in_order(d_pairing, got.reshape(d_pairing.shape), "col", bit, 1)
        d_pairing = d_pairing.reshape((-1,) + d_pairing.shape[2:])
    d_a = [lay_back(part[0], width, rows) for part in da_parts]
    d_b = [lay_back(part[0], own, wide) for part in db_parts]

    coupling_update = call(
        functools.partial(update_kernel, depth),
        (steps,),
        [full(v.shape) for v in (inv, a, b, pairing_wide)] + [full((1, pair))],
        up_spec,
        sds((block, block, pair), BF16),
        [pltpu.VMEM((chunk, wide, pair), BF16)],
        cost(5e9, 8e6),
    )(inv, a, b, pairing_wide, offset_vector.reshape(1, pair))

    embedding_adjoint = call(
        functools.partial(owner_kernel, depth, own),
        (),
        [full(v.shape) for v in d_a + d_b]
        + [full(v.shape) for v in (x, by_row, factors_t, perm)],
        full((rows, features)),
        sds((rows, features), F32),
    )(*d_a, *d_b, x, by_row, factors_t, perm)

    d_pairing = d_pairing.reshape(width, width, pair)
    placed = call(
        place_kernel,
        (),
        [full(d_pairing.shape)],
        full((width, width, pair)),
        sds((width, width, pair), F32),
    )(d_pairing)
    small = small.astype(F32)
    factors = jnp.concatenate([small[:width], small[width : 2 * width]], axis=0)
    return (
        coupling_update,
        embedding_adjoint.reshape(depth, own, features),
        factors[:, :features].T,
        placed.reshape(width * width, pair),
        small[2 * width],
    )


def solution(mesh):
    n = mesh.shape["col"]
    placed = (
        P(None, ("groups", "row", "col"), None),
        P(None, ("groups", "row", "col")),
        P("groups"),
        P(),
        P(),
        P(),
        P(("groups", "row"), "col", None),
    )
    return jax.shard_map(
        functools.partial(per_device, n),
        mesh=mesh,
        in_specs=placed,
        out_specs=(
            P(("groups", "row"), "col", None),
            P(None, ("groups", "row", "col"), None),
            P("groups", None),
            P("groups", None),
            P("groups"),
        ),
        check_vma=False,
    )
```

```python
import functools

import jax
import jax.numpy as jnp
from jax import lax
from jax.experimental import pallas as pl
from jax.experimental.pallas import tpu as pltpu
from jax.sharding import PartitionSpec as P

F32 = jnp.float32
BF16 = jnp.bfloat16
LANES = 128
VMEM_LIMIT = 40 * 1024 * 1024
NT = (((1,), (1,)), ((), ()))


def dot(left, right):
    return jnp.dot(left, right, preferred_element_type=F32)


def dot_nt(left, right):
    return lax.dot_general(left, right, NT, preferred_element_type=F32)


def iota(shape, axis):
    return lax.broadcasted_iota(jnp.int32, shape, axis)


def one_hot(mask):
    return jnp.where(mask, 1.0, 0.0).astype(BF16)


def full(shape):
    return pl.BlockSpec(shape, lambda *g: (0,) * len(shape))


def cost(flops, nbytes):
    return pl.CostEstimate(flops=int(flops), bytes_accessed=int(nbytes), transcendentals=0)


def call(kernel, grid, in_specs, out_specs, out_shape, scratch=(), estimate=None):
    return pl.pallas_call(
        kernel,
        grid=grid,
        in_specs=in_specs,
        out_specs=out_specs,
        out_shape=out_shape,
        scratch_shapes=list(scratch),
        compiler_params=pltpu.CompilerParams(vmem_limit_bytes=VMEM_LIMIT),
        cost_estimate=estimate,
    )


def stats(x):
    center = x - jnp.mean(x, axis=-1, keepdims=True)
    scale = lax.rsqrt(jnp.mean(center * center, axis=-1, keepdims=True) + 1e-05)
    return center * scale, scale


def prep_kernel(depth, own, *refs):
    by_token_ref, by_row_ref, w_ref, wt_ref, x_ref, offset_ref = refs[5:11]
    cell_ref, line_ref, factors_ref, sem = refs[11:]
    rows = depth * own
    targets = (x_ref, cell_ref, line_ref, factors_ref, offset_ref)
    copies = [
        pltpu.make_async_copy(src, dst, sem.at[k])
        for k, (src, dst) in enumerate(zip(refs[:5], targets))
    ]
    for copy in copies:
        copy.start()
    p, q = iota((rows, rows), 0), iota((rows, rows), 1)
    swap = one_hot(q == (p % depth) * own + p // depth)
    pick = one_hot(iota((rows, depth), 0) // own == iota((rows, depth), 1))
    here = iota((rows, own), 0) % own == iota((rows, own), 1)
    for copy in copies:
        copy.wait()
    normed, _ = stats(x_ref[...].astype(F32))
    features = normed.shape[1]
    cell = cell_ref[...].astype(F32).astype(BF16)
    line = line_ref[...].astype(F32)
    line_column = jnp.sum(pick.astype(F32) * line, axis=1, keepdims=True)
    cells = dot(pick, cell)
    weight = jnp.sum(jnp.where(here, cells, 0.0), axis=1, keepdims=True) * line_column
    masked = normed.astype(BF16).astype(F32) * weight
    wide = jnp.concatenate([masked, jnp.zeros((rows, LANES - features), F32)], axis=1)
    lane = iota((rows, LANES), 1)
    at = lane == features + iota((rows, LANES), 0) // own
    wide = (wide + jnp.where(at, weight, 0.0)).astype(BF16)
    by_row_ref[...] = wide
    by_token_ref[...] = dot(swap, wide).astype(BF16)
    factors = factors_ref[...]
    width = factors.shape[1]
    w_ref[...] = jnp.concatenate([factors, jnp.zeros((LANES - features, width), BF16)], axis=0)
    same = one_hot(iota((width, width), 0) == iota((width, width), 1))
    turned = lax.dot_general(same, factors, (((1,), (1,)), ((), ())), preferred_element_type=F32)
    pad = jnp.zeros((width, LANES - features), F32)
    wt_ref[...] = jnp.concatenate([turned, pad], axis=1).astype(BF16)


def scaled_pair(up_ref, inv, at):
    parts = [up_ref[i].astype(F32) * inv[:, i : i + 1] for i in (at, at + 1)]
    return jnp.concatenate(parts, axis=1).astype(BF16)


def fill_v(up_ref, inv, bt, v_ref, depth):
    chunk, _, pair = up_ref.shape
    width = v_ref.shape[0]
    for at in range(0, chunk, 2):
        v = dot(bt, scaled_pair(up_ref, inv, at)).astype(BF16)
        for k in range(2):
            part = v[:, k * pair : (k + 1) * pair].reshape(width, depth, pair)
            v_ref[:, (at + k) * depth : (at + k + 1) * depth, :] = part


def fill_t(a_chunk, wc_ref, t_ref, depth):
    chunk, rows, pair = t_ref.shape
    width = rows // depth
    for e in range(0, width, 2):
        t = dot(a_chunk, wc_ref[:, e * pair : (e + 2) * pair]).astype(BF16)
        for k in range(2):
            part = t[:, k * pair : (k + 1) * pair].reshape(chunk, depth, pair)
            t_ref[:, (e + k) * depth : (e + k + 1) * depth, :] = part


def two(ref, at):
    return jnp.concatenate([ref[at], ref[at + 1]], axis=1)


def weight_kernel(depth, features, n, pieces, *refs):
    a_refs, b_refs = refs[:pieces], refs[pieces : 2 * pieces]
    up_ref, w_ref, wt_ref, perm_ref, wc_ref = refs[2 * pieces : 2 * pieces + 5]
    outs = refs[2 * pieces + 5 :]
    mi_ref, mj_ref, a_ref, b_ref, inv_ref, bias_ref, dw_ref, da_ref = outs[:8]
    bt_ref, at_ref, v_ref, acc_ref = outs[8:]
    g, last = pl.program_id(0), pl.num_programs(0) - 1
    chunk, block, pair = up_ref.shape
    width = w_ref.shape[1] // 2
    r, c = lax.axis_index("row"), lax.axis_index("col")

    @pl.when(g == 0)
    def _():
        if pieces == 1:
            mi_ref[...] = a_refs[0][...]
            mj_ref[...] = b_refs[0][...]
        else:
            own = block // pieces
            for k in range(pieces):
                src = lax.rem(c - k + n, n)
                rows = pl.ds(pl.multiple_of(src * own * depth, own * depth), own * depth)
                mi_ref[rows, :] = a_refs[k][...]
                src = lax.rem(r - k + n, n)
                rows = pl.ds(pl.multiple_of(src * own, own), own)
                for s in range(depth):
                    mj_ref[s, rows, :] = b_refs[k][s * own : (s + 1) * own, :]
        w, wt = w_ref[...], wt_ref[...]
        mi = mi_ref[...]
        a_ref[...] = dot(mi, w[:, :width]).astype(BF16)
        at_ref[...] = dot_nt(wt[:width, :], mi).astype(BF16)
        b = jnp.zeros((block, width * depth), F32)
        seen = jnp.zeros((block, LANES), F32)
        for s in range(depth):
            mj = mj_ref[s]
            seen = seen + mj.astype(F32)
            part = dot(mj, w[:, width:]).astype(BF16)
            b = b + dot(part, perm_ref[s * width : (s + 1) * width, :])
        b_ref[...] = b.astype(BF16)
        bt_ref[...] = b.T.astype(BF16)
        keep = iota((block, LANES), 1) >= features
        seen_j = jnp.where(keep, seen, 0.0).astype(BF16)
        rows = block * depth
        gather = one_hot(iota((block, rows), 0) == iota((block, rows), 1) // depth)
        seen_i = dot(gather, mi).astype(BF16)
        for k in range(block // chunk):
            count = dot_nt(seen_j, seen_i[k * chunk : (k + 1) * chunk, :])
            inv_ref[k] = 1.0 / (count + 0.001)
        acc_ref[...] = jnp.zeros_like(acc_ref)
        bias_ref[...] = jnp.zeros_like(bias_ref)

    bias_ref[0:1, :] += jnp.sum(
        jnp.sum(up_ref[...].astype(F32), axis=0), axis=0, keepdims=True
    )
    fill_v(up_ref, inv_ref[g], bt_ref[...], v_ref, depth)
    span = chunk * depth
    a_t = at_ref[:, pl.ds(pl.multiple_of(g * span, span), span)]
    d_a = jnp.zeros((width, span), F32)
    for e in range(0, width, 2):
        v = two(v_ref, e)
        part = dot(a_t, v)
        for k in range(2):
            acc_ref[(e + k) * width : (e + k + 1) * width, :] += part[:, k * pair : (k + 1) * pair]
        d_a = d_a + dot_nt(wc_ref[:, e * pair : (e + 2) * pair], v)
    da_ref[:, pl.ds(pl.multiple_of(g * span, span), span)] = d_a.astype(BF16)

    @pl.when(g == last)
    def _():
        dw_ref[...] = acc_ref[...].astype(BF16)


def token_kernel(depth, features, *refs):
    up_ref, inv_ref, a_ref, wc_ref, mi_ref, mj_ref, perm_ref, bias_ref, da_ref = refs[:9]
    small_ref, out_ref, t_ref, db_ref = refs[9:]
    g, last = pl.program_id(0), pl.num_programs(0) - 1
    chunk = up_ref.shape[0]
    width = wc_ref.shape[0]
    span = chunk * depth
    inv = inv_ref[g]

    @pl.when(g == 0)
    def _():
        db_ref[...] = jnp.zeros_like(db_ref)

    a_chunk = a_ref[pl.ds(pl.multiple_of(g * span, span), span), :]
    fill_t(a_chunk, wc_ref, t_ref, depth)
    d_b = db_ref[...]
    for at in range(0, chunk, 2):
        d_b = d_b + dot_nt(scaled_pair(up_ref, inv, at), two(t_ref, at))
    db_ref[...] = d_b

    @pl.when(g == last)
    def _():
        d_b = db_ref[...].astype(BF16)
        out_ref[...] = d_b
        turned = dot_nt(perm_ref[...], d_b).astype(BF16)
        right = jnp.zeros((width, LANES), F32)
        for s in range(depth):
            right = right + dot(turned[s * width : (s + 1) * width, :], mj_ref[s])
        left = dot(da_ref[...], mi_ref[...])
        small = jnp.concatenate([left[:, :features], right[:, :features]], axis=1)
        small_ref[0:width, :] = small.astype(BF16)
        small_ref[width:, :] = jnp.broadcast_to(bias_ref[0:1, :], (16, LANES)).astype(BF16)


def update_kernel(depth, inv_ref, a_ref, b_ref, wc_ref, offset_ref, out_ref, t_ref):
    g = pl.program_id(0)
    chunk, block, pair = out_ref.shape
    span = chunk * depth
    inv = inv_ref[g]
    fill_t(a_ref[pl.ds(pl.multiple_of(g * span, span), span), :], wc_ref, t_ref, depth)
    b = b_ref[...]
    offset = offset_ref[...]
    for at in range(0, chunk, 2):
        part = dot(b, two(t_ref, at))
        for k in range(2):
            value = part[:, k * pair : (k + 1) * pair] * inv[:, at + k : at + k + 1] + offset
            out_ref[at + k] = value.astype(BF16)


def owner_kernel(depth, own, features, *refs):
    da_refs, db_ref, small_refs = refs[:2], refs[2], refs[3:5]
    x_ref, message_ref, wt_ref, perm_ref, out_ref, factors_ref, bias_ref = refs[5:]
    rows = depth * own
    width = wt_ref.shape[0] // 2
    p, q = iota((rows, rows), 0), iota((rows, rows), 1)
    swap = one_hot(q == (p % own) * depth + p // own)
    d_a = dot_nt(swap, da_refs[0][...]) + dot_nt(swap, da_refs[1][...])
    d_b = dot_nt(db_ref[...], perm_ref[...])
    d_b = jnp.concatenate([d_b[:, s * width : (s + 1) * width] for s in range(depth)], axis=0)
    highest = lax.Precision.HIGHEST
    wt = wt_ref[...].astype(F32)
    d_normed = jnp.dot(d_a, wt[:width, :], precision=highest, preferred_element_type=F32)
    d_normed = d_normed + jnp.dot(d_b, wt[width:, :], precision=highest, preferred_element_type=F32)
    message = message_ref[...].astype(F32)
    mask = iota((rows, LANES), 1) >= features
    weight = jnp.sum(jnp.where(mask, message, 0.0), axis=1, keepdims=True)
    d_normed = d_normed[:, :features] * weight
    normed, scale = stats(x_ref[...].astype(F32))
    mean = jnp.mean(d_normed, axis=-1, keepdims=True)
    along = jnp.mean(d_normed * normed, axis=-1, keepdims=True)
    out_ref[...] = scale * (d_normed - mean - normed * along)
    small = small_refs[0][...].astype(F32) + small_refs[1][...].astype(F32)
    turned = small[:width].T
    factors_ref[...] = jnp.concatenate([turned[:features], turned[features:]], axis=1)
    bias_ref[...] = small[width : width + 1]


def place_kernel(in_ref, out_ref):
    for e in range(in_ref.shape[0]):
        out_ref[:, e, :] = in_ref[e].astype(F32)


def lay_out(x):
    rows, lanes = x.shape
    if lanes % LANES:
        return x.reshape(-1, LANES)
    return x.reshape(rows, lanes // LANES, LANES).transpose(1, 0, 2).reshape(-1, LANES)


def lay_back(x, rows, lanes):
    if lanes % LANES:
        return x.reshape(rows, lanes)
    return x.reshape(lanes // LANES, rows, LANES).transpose(1, 0, 2).reshape(rows, lanes)


def bit_of(axis, bit):
    return (lax.axis_index(axis) >> bit) & 1


def swap_parts(parts, axis, bit, n):
    parts = [part.reshape(-1, LANES) for part in parts]
    message = jnp.concatenate(parts, axis=0) if len(parts) > 1 else parts[0]
    message = lax.ppermute(message, axis, [(i, i ^ (1 << bit)) for i in range(n)])
    got, at = [], 0
    for part in parts:
        got.append(message[at : at + part.shape[0]])
        at += part.shape[0]
    return got


def halves(x, axis, bit, at):
    here = bit_of(axis, bit)
    keep = lax.dynamic_index_in_dim(x, here, at, keepdims=False)
    return keep, lax.dynamic_index_in_dim(x, 1 - here, at, keepdims=False)


def split_high(x):
    return x.reshape((2, x.shape[0] // 2) + x.shape[1:])


def in_order(mine, other, axis, bit, at):
    first = bit_of(axis, bit) == 0
    low = jnp.where(first, mine, other)
    return jnp.stack([low, jnp.where(first, other, mine)], axis=at)


def add(mine, other):
    other = other.reshape(mine.shape)
    return lax.optimization_barrier((mine.astype(F32) + other.astype(F32)).astype(BF16))


def per_device(
    n,
    alignment_embedding,
    alignment_cell_exists,
    alignment_lines_exist,
    sitewise_factors,
    pairing_matrix,
    offset_vector,
    upstream_adjoint,
):
    depth, own, features = alignment_embedding.shape
    width = sitewise_factors.shape[1] // 2
    block, pair = upstream_adjoint.shape[0], upstream_adjoint.shape[2]
    rows, chunk = depth * own, 16
    steps = block // chunk
    split = own % 16 == 0
    axes = ("row", "col")
    sds = jax.ShapeDtypeStruct

    def along_col(x, k):
        return lax.ppermute(x, "col", [(i, (i + k) % n) for i in range(n)])

    def along_row(x, k):
        return lax.ppermute(x, "row", [(i, (i + k) % n) for i in range(n)])

    def to_column(x, k):
        pairs = [(i * n + j, (j + k) % n * n + i) for i in range(n) for j in range(n)]
        return lax.ppermute(x, axes, pairs)

    r, c = lax.axis_index("row"), lax.axis_index("col")
    x = alignment_embedding.reshape(rows, features)
    line = alignment_lines_exist.reshape(1, depth)
    offset = offset_vector.reshape(1, pair)
    args = (x, alignment_cell_exists, line, sitewise_factors, offset)
    out_shapes = [
        sds((rows, LANES), BF16),
        sds((rows, LANES), BF16),
        sds((LANES, 2 * width), BF16),
        sds((2 * width, LANES), BF16),
        sds(x.shape, x.dtype),
        sds(offset.shape, F32),
    ]
    by_token, by_row, factors, factors_t, x, offset = call(
        functools.partial(prep_kernel, depth, own),
        (),
        [pl.BlockSpec(memory_space=pl.ANY)] * len(args),
        [full(o.shape) for o in out_shapes],
        out_shapes,
        [pltpu.VMEM(v.shape, v.dtype) for v in args[1:4]] + [pltpu.SemaphoreType.DMA((5,))],
    )(*args)
    a_pieces = [by_token] + [along_col(by_token, k) for k in range(1, n)]
    b_pieces = [to_column(by_row, k) for k in range(n)]
    if not split:
        order = (c - jnp.arange(n)) % n
        held = jnp.zeros((n, rows, LANES), BF16).at[order].set(jnp.stack(a_pieces))
        a_pieces = [held.reshape(block * depth, LANES)]
        order = (r - jnp.arange(n)) % n
        held = jnp.zeros((n, depth, own, LANES), BF16)
        held = held.at[order].set(jnp.stack(b_pieces).reshape(n, depth, own, LANES))
        b_pieces = [held.transpose(1, 0, 2, 3).reshape(depth, block, LANES)]
    pieces = len(a_pieces)

    wide = width * depth
    source = jnp.arange(wide)
    perm = (jnp.arange(wide)[None, :] == (source % width * depth + source // width)[:, None]).astype(BF16)
    pairing_wide = pairing_matrix.reshape(width, width * pair)
    up_spec = pl.BlockSpec((chunk, block, pair), lambda g: (g, 0, 0))
    tokens = block * depth
    out_shapes = [
        sds((tokens, LANES), BF16),
        sds((depth, block, LANES), BF16),
        sds((tokens, width), BF16),
        sds((block, wide), BF16),
        sds((steps, block, chunk), F32),
        sds((8, pair), F32),
        sds((width * width, pair), BF16),
        sds((width, tokens), BF16),
    ]
    outs = call(
        functools.partial(weight_kernel, depth, features, n, pieces),
        (steps,),
        [full(p.shape) for p in a_pieces]
        + [full(p.shape) for p in b_pieces]
        + [up_spec]
        + [full(v.shape) for v in (factors, factors_t, perm, pairing_wide)],
        [full(o.shape) for o in out_shapes],
        out_shapes,
        [
            pltpu.VMEM((wide, block), BF16),
            pltpu.VMEM((width, tokens), BF16),
            pltpu.VMEM((width, chunk * depth, pair), BF16),
            pltpu.VMEM((width * width, pair), F32),
        ],
        cost(5e9, 8e6),
    )(*a_pieces, *b_pieces, upstream_adjoint, factors, factors_t, perm, pairing_wide)
    mi, mj, a, b, inv, bias, d_pairing, d_a = outs

    bits = n.bit_length() - 1
    d_pairing = d_pairing.reshape(n, -1, LANES)
    da_all = d_a
    d_a = jnp.stack([lay_out(d_a[:, k * rows : (k + 1) * rows]) for k in range(n)])
    for bit in reversed(range(1, bits)):
        dp_keep, dp_go = halves(split_high(d_pairing), "col", bit, 0)
        da_keep, da_go = halves(split_high(d_a), "col", bit, 0)
        dp_got, da_got = swap_parts([dp_go, da_go], "col", bit, n)
        d_pairing, d_a = add(dp_keep, dp_got), add(da_keep, da_got)

    out_shapes = [sds((width + 16, LANES), BF16), sds((block, wide), BF16)]
    small, d_b = call(
        functools.partial(token_kernel, depth, features),
        (steps,),
        [up_spec]
        + [full(v.shape) for v in (inv, a, pairing_wide, mi, mj, perm, bias)]
        + [full((width, tokens))],
        [full(o.shape) for o in out_shapes],
        out_shapes,
        [pltpu.VMEM((chunk, wide, pair), BF16), pltpu.VMEM((block, wide), F32)],
        cost(5e9, 8e6),
    )(upstream_adjoint, inv, a, pairing_wide, mi, mj, perm, bias, da_all)

    d_b = jnp.stack([lay_out(d_b[k * own : (k + 1) * own]) for k in range(n)])
    dp_keep, dp_go = halves(d_pairing, "col", 0, 0)
    da_keep, da_go = halves(d_a, "col", 0, 0)
    db_keep, db_go = halves(d_b.reshape((n // 2, 2) + d_b.shape[1:]), "col", 0, 1)
    parts = swap_parts([dp_go, da_go, db_go, small], "col", 0, n)
    d_pairing, small = add(dp_keep, parts[0]), add(small, parts[3])
    da_parts = [da_keep, parts[1]]
    d_b = in_order(db_keep, parts[2].reshape(db_keep.shape), "col", 0, 1)
    db_keep, db_go = halves(d_b, "row", 0, 1)
    for bit in range(bits):
        parts = swap_parts([d_pairing, db_go, small], "row", bit, n)
        d_pairing, d_b, small = add(d_pairing, parts[0]), add(db_keep, parts[1]), add(small, parts[2])
        db_keep = db_go = d_b
    d_pairing = d_pairing.reshape(1, -1, LANES)
    small_parts = [small, None]
    for bit in range(1, bits):
        if bit > 1:
            small_parts[0] = add(*small_parts)
        db_keep, db_go = halves(split_high(d_b), "col", bits - bit, 0)
        parts = swap_parts([d_pairing, db_go, small_parts[0]], "col", bits - bit, n)
        got = parts[0].reshape(d_pairing.shape)
        d_pairing = in_order(d_pairing, got, "col", bits - bit, 1)
        d_pairing = d_pairing.reshape((-1,) + d_pairing.shape[2:])
        mine = bit_of("col", bits - bit) == bit_of("row", bits - bit)
        d_b = jnp.where(mine, db_keep, parts[1].reshape(db_keep.shape))
        small_parts[1] = parts[2]
    (got,) = swap_parts([d_pairing], "col", 0, n)
    d_pairing = in_order(d_pairing, got.reshape(d_pairing.shape), "col", 0, 1)
    d_a = [lay_back(part.reshape(-1, LANES), width, rows) for part in da_parts]
    d_b = lay_back(d_b[0], own, wide)

    coupling_update = call(
        functools.partial(update_kernel, depth),
        (steps,),
        [full(v.shape) for v in (inv, a, b, pairing_wide)] + [full((1, pair))],
        up_spec,
        sds((block, block, pair), BF16),
        [pltpu.VMEM((chunk, wide, pair), BF16)],
        cost(5e9, 8e6),
    )(inv, a, b, pairing_wide, offset)

    args = (*d_a, d_b, *small_parts, x, by_row, factors_t, perm)
    out_shapes = [sds((rows, features), F32), sds((features, 2 * width), F32), sds((1, pair), F32)]
    embedding_adjoint, factors_adjoint, offset_slope = call(
        functools.partial(owner_kernel, depth, own, features),
        (),
        [full(v.shape) for v in args],
        [full(o.shape) for o in out_shapes],
        out_shapes,
    )(*args)

    d_pairing = d_pairing.reshape(width, width, pair)
    placed = call(
        place_kernel,
        (),
        [full(d_pairing.shape)],
        full((width, width, pair)),
        sds((width, width, pair), F32),
    )(d_pairing)
    return (
        coupling_update,
        embedding_adjoint.reshape(depth, own, features),
        factors_adjoint,
        placed.reshape(width * width, pair),
        offset_slope.reshape(pair),
    )


def solution(mesh):
    n = mesh.shape["col"]
    placed = (
        P(None, ("groups", "row", "col"), None),
        P(None, ("groups", "row", "col")),
        P("groups"),
        P(),
        P(),
        P(),
        P(("groups", "row"), "col", None),
    )
    return jax.shard_map(
        functools.partial(per_device, n),
        mesh=mesh,
        in_specs=placed,
        out_specs=(
            P(("groups", "row"), "col", None),
            P(None, ("groups", "row", "col"), None),
            P("groups", None),
            P("groups", None),
            P("groups"),
        ),
        check_vma=False,
    )
```

```python
import functools

import jax
import jax.numpy as jnp
from jax import lax
from jax.experimental import pallas as pl
from jax.experimental.pallas import tpu as pltpu
from jax.sharding import PartitionSpec as P

F32 = jnp.float32
BF16 = jnp.bfloat16
LANES = 128
VMEM_LIMIT = 40 * 1024 * 1024
NT = (((1,), (1,)), ((), ()))


def dot(left, right):
    return jnp.dot(left, right, preferred_element_type=F32)


def dot_nt(left, right):
    return lax.dot_general(left, right, NT, preferred_element_type=F32)


def iota(shape, axis):
    return lax.broadcasted_iota(jnp.int32, shape, axis)


def one_hot(mask):
    return jnp.where(mask, 1.0, 0.0).astype(BF16)


def full(shape):
    return pl.BlockSpec(shape, lambda *g: (0,) * len(shape))


def cost(flops, nbytes):
    return pl.CostEstimate(flops=int(flops), bytes_accessed=int(nbytes), transcendentals=0)


def call(kernel, grid, in_specs, out_specs, out_shape, scratch=(), estimate=None):
    return pl.pallas_call(
        kernel,
        grid=grid,
        in_specs=in_specs,
        out_specs=out_specs,
        out_shape=out_shape,
        scratch_shapes=list(scratch),
        compiler_params=pltpu.CompilerParams(vmem_limit_bytes=VMEM_LIMIT),
        cost_estimate=estimate,
    )


def stats(x):
    center = x - jnp.mean(x, axis=-1, keepdims=True)
    scale = lax.rsqrt(jnp.mean(center * center, axis=-1, keepdims=True) + 1e-05)
    return center * scale, scale


def prep_kernel(depth, own, *refs):
    by_token_ref, by_row_ref, w_ref, wt_ref, x_ref, offset_ref = refs[5:11]
    cell_ref, line_ref, factors_ref, sem = refs[11:]
    rows = depth * own
    targets = (x_ref, cell_ref, line_ref, factors_ref, offset_ref)
    copies = [
        pltpu.make_async_copy(src, dst, sem.at[k])
        for k, (src, dst) in enumerate(zip(refs[:5], targets))
    ]
    for copy in copies:
        copy.start()
    p, q = iota((rows, rows), 0), iota((rows, rows), 1)
    swap = one_hot(q == (p % depth) * own + p // depth)
    pick = one_hot(iota((rows, depth), 0) // own == iota((rows, depth), 1))
    here = iota((rows, own), 0) % own == iota((rows, own), 1)
    for copy in copies:
        copy.wait()
    normed, _ = stats(x_ref[...].astype(F32))
    features = normed.shape[1]
    cell = cell_ref[...].astype(F32).astype(BF16)
    line = line_ref[...].astype(F32)
    line_column = jnp.sum(pick.astype(F32) * line, axis=1, keepdims=True)
    cells = dot(pick, cell)
    weight = jnp.sum(jnp.where(here, cells, 0.0), axis=1, keepdims=True) * line_column
    masked = normed.astype(BF16).astype(F32) * weight
    wide = jnp.concatenate([masked, jnp.zeros((rows, LANES - features), F32)], axis=1)
    lane = iota((rows, LANES), 1)
    at = lane == features + iota((rows, LANES), 0) // own
    wide = (wide + jnp.where(at, weight, 0.0)).astype(BF16)
    by_row_ref[...] = wide
    by_token_ref[...] = dot(swap, wide).astype(BF16)
    factors = factors_ref[...]
    width = factors.shape[1]
    w_ref[...] = jnp.concatenate([factors, jnp.zeros((LANES - features, width), BF16)], axis=0)
    same = one_hot(iota((width, width), 0) == iota((width, width), 1))
    turned = lax.dot_general(same, factors, (((1,), (1,)), ((), ())), preferred_element_type=F32)
    pad = jnp.zeros((width, LANES - features), F32)
    wt_ref[...] = jnp.concatenate([turned, pad], axis=1).astype(BF16)


def scaled_pair(up_ref, inv, at):
    parts = [up_ref[i].astype(F32) * inv[:, i : i + 1] for i in (at, at + 1)]
    return jnp.concatenate(parts, axis=1).astype(BF16)


def fill_v(up_ref, inv, bt, v_ref, depth):
    chunk, _, pair = up_ref.shape
    width = v_ref.shape[0]
    for at in range(0, chunk, 2):
        v = dot(bt, scaled_pair(up_ref, inv, at)).astype(BF16)
        for k in range(2):
            part = v[:, k * pair : (k + 1) * pair].reshape(width, depth, pair)
            v_ref[:, (at + k) * depth : (at + k + 1) * depth, :] = part


def fill_t(a_chunk, wc_ref, t_ref, depth):
    chunk, rows, pair = t_ref.shape
    width = rows // depth
    for e in range(0, width, 2):
        t = dot(a_chunk, wc_ref[:, e * pair : (e + 2) * pair]).astype(BF16)
        for k in range(2):
            part = t[:, k * pair : (k + 1) * pair].reshape(chunk, depth, pair)
            t_ref[:, (e + k) * depth : (e + k + 1) * depth, :] = part


def two(ref, at):
    return jnp.concatenate([ref[at], ref[at + 1]], axis=1)


def weight_kernel(depth, features, n, pieces, *refs):
    a_refs, b_refs = refs[:pieces], refs[pieces : 2 * pieces]
    up_ref, w_ref, wt_ref, perm_ref, wc_ref = refs[2 * pieces : 2 * pieces + 5]
    outs = refs[2 * pieces + 5 :]
    mi_ref, mj_ref, a_ref, b_ref, bt_ref, inv_ref, bias_ref, dw_ref, left_ref = outs[:9]
    at_ref, v_ref, acc_ref, wide_ref = outs[9:]
    g, last = pl.program_id(0), pl.num_programs(0) - 1
    chunk, block, pair = up_ref.shape
    width = w_ref.shape[1] // 2
    r, c = lax.axis_index("row"), lax.axis_index("col")

    @pl.when(g == 0)
    def _():
        if pieces == 1:
            mi_ref[...] = a_refs[0][...]
            mj_ref[...] = b_refs[0][...]
        else:
            own = block // pieces
            for k in range(pieces):
                src = lax.rem(c - k + n, n)
                rows = pl.ds(pl.multiple_of(src * own * depth, own * depth), own * depth)
                mi_ref[rows, :] = a_refs[k][...]
                src = lax.rem(r - k + n, n)
                rows = pl.ds(pl.multiple_of(src * own, own), own)
                for s in range(depth):
                    mj_ref[s, rows, :] = b_refs[k][s * own : (s + 1) * own, :]
        w, wt = w_ref[...], wt_ref[...]
        mi = mi_ref[...]
        a_ref[...] = dot(mi, w[:, :width]).astype(BF16)
        same = one_hot(iota((features, LANES), 0) == iota((features, LANES), 1))
        at_ref[...] = dot_nt(jnp.concatenate([wt[:width, :], same], axis=0), mi).astype(BF16)
        b = jnp.zeros((block, width * depth), F32)
        seen = jnp.zeros((block, LANES), F32)
        for s in range(depth):
            mj = mj_ref[s]
            seen = seen + mj.astype(F32)
            part = dot(mj, w[:, width:]).astype(BF16)
            b = b + dot(part, perm_ref[s * width : (s + 1) * width, :])
        b_ref[...] = b.astype(BF16)
        bt_ref[...] = b.T.astype(BF16)
        keep = iota((block, LANES), 1) >= features
        seen_j = jnp.where(keep, seen, 0.0).astype(BF16)
        rows = block * depth
        gather = one_hot(iota((block, rows), 0) == iota((block, rows), 1) // depth)
        seen_i = dot(gather, mi).astype(BF16)
        for k in range(block // chunk):
            count = dot_nt(seen_j, seen_i[k * chunk : (k + 1) * chunk, :])
            inv_ref[k] = 1.0 / (count + 0.001)
        acc_ref[...] = jnp.zeros_like(acc_ref)
        wide_ref[...] = jnp.zeros_like(wide_ref)
        bias_ref[...] = jnp.zeros_like(bias_ref)

    bias_ref[0:1, :] += jnp.sum(
        jnp.sum(up_ref[...].astype(F32), axis=0), axis=0, keepdims=True
    )
    fill_v(up_ref, inv_ref[g], bt_ref[...], v_ref, depth)
    span = chunk * depth
    a_t = at_ref[:, pl.ds(pl.multiple_of(g * span, span), span)]
    for e in range(0, width, 2):
        part = dot(a_t, two(v_ref, e))
        for k in range(2):
            rows = slice((e + k) * width, (e + k + 1) * width)
            acc_ref[rows, :] += part[:width, k * pair : (k + 1) * pair]
        wide_ref[:, e * pair : (e + 2) * pair] += part[width:]

    @pl.when(g == last)
    def _():
        dw_ref[...] = acc_ref[...].astype(BF16)
        left = jnp.zeros((width, features), F32)
        for e in range(0, width, 2):
            lanes = slice(e * pair, (e + 2) * pair)
            left = left + dot_nt(wc_ref[:, lanes], wide_ref[:, lanes].astype(BF16))
        left_ref[...] = left


def left_kernel(depth, up_ref, inv_ref, bt_ref, wc_ref, out_ref, v_ref):
    g = pl.program_id(0)
    chunk, _, pair = up_ref.shape
    width = wc_ref.shape[0]
    span = chunk * depth
    fill_v(up_ref, inv_ref[g], bt_ref[...], v_ref, depth)
    d_a = jnp.zeros((width, span), F32)
    for e in range(0, width, 2):
        d_a = d_a + dot_nt(wc_ref[:, e * pair : (e + 2) * pair], two(v_ref, e))
    out_ref[:, pl.ds(pl.multiple_of(g * span, span), span)] = d_a.astype(BF16)


def token_kernel(depth, features, *refs):
    up_ref, inv_ref, a_ref, wc_ref, mj_ref, perm_ref, bias_ref, left_ref = refs[:8]
    small_ref, out_ref, t_ref, db_ref = refs[8:]
    g, last = pl.program_id(0), pl.num_programs(0) - 1
    chunk = up_ref.shape[0]
    width = wc_ref.shape[0]
    span = chunk * depth
    inv = inv_ref[g]

    @pl.when(g == 0)
    def _():
        db_ref[...] = jnp.zeros_like(db_ref)

    a_chunk = a_ref[pl.ds(pl.multiple_of(g * span, span), span), :]
    fill_t(a_chunk, wc_ref, t_ref, depth)
    d_b = db_ref[...]
    for at in range(0, chunk, 2):
        d_b = d_b + dot_nt(scaled_pair(up_ref, inv, at), two(t_ref, at))
    db_ref[...] = d_b

    @pl.when(g == last)
    def _():
        d_b = db_ref[...].astype(BF16)
        out_ref[...] = d_b
        turned = dot_nt(perm_ref[...], d_b).astype(BF16)
        right = jnp.zeros((width, LANES), F32)
        for s in range(depth):
            right = right + dot(turned[s * width : (s + 1) * width, :], mj_ref[s])
        small = jnp.concatenate([left_ref[...], right[:, :features]], axis=1)
        small_ref[0:width, :] = small.astype(BF16)
        small_ref[width:, :] = jnp.broadcast_to(bias_ref[0:1, :], (16, LANES)).astype(BF16)


def update_kernel(depth, inv_ref, a_ref, b_ref, wc_ref, offset_ref, out_ref, t_ref):
    g = pl.program_id(0)
    chunk, block, pair = out_ref.shape
    span = chunk * depth
    inv = inv_ref[g]
    fill_t(a_ref[pl.ds(pl.multiple_of(g * span, span), span), :], wc_ref, t_ref, depth)
    b = b_ref[...]
    offset = offset_ref[...]
    for at in range(0, chunk, 2):
        part = dot(b, two(t_ref, at))
        for k in range(2):
            value = part[:, k * pair : (k + 1) * pair] * inv[:, at + k : at + k + 1] + offset
            out_ref[at + k] = value.astype(BF16)


def owner_kernel(depth, own, features, *refs):
    da_refs, db_ref, small_refs = refs[:2], refs[2], refs[3:5]
    x_ref, message_ref, wt_ref, perm_ref, out_ref, factors_ref, bias_ref = refs[5:]
    rows = depth * own
    width = wt_ref.shape[0] // 2
    p, q = iota((rows, rows), 0), iota((rows, rows), 1)
    swap = one_hot(q == (p % own) * depth + p // own)
    d_a = dot_nt(swap, da_refs[0][...]) + dot_nt(swap, da_refs[1][...])
    d_b = dot_nt(db_ref[...], perm_ref[...])
    d_b = jnp.concatenate([d_b[:, s * width : (s + 1) * width] for s in range(depth)], axis=0)
    highest = lax.Precision.HIGHEST
    wt = wt_ref[...].astype(F32)
    d_normed = jnp.dot(d_a, wt[:width, :], precision=highest, preferred_element_type=F32)
    d_normed = d_normed + jnp.dot(d_b, wt[width:, :], precision=highest, preferred_element_type=F32)
    message = message_ref[...].astype(F32)
    mask = iota((rows, LANES), 1) >= features
    weight = jnp.sum(jnp.where(mask, message, 0.0), axis=1, keepdims=True)
    d_normed = d_normed[:, :features] * weight
    normed, scale = stats(x_ref[...].astype(F32))
    mean = jnp.mean(d_normed, axis=-1, keepdims=True)
    along = jnp.mean(d_normed * normed, axis=-1, keepdims=True)
    out_ref[...] = scale * (d_normed - mean - normed * along)
    small = small_refs[0][...].astype(F32) + small_refs[1][...].astype(F32)
    turned = small[:width].T
    factors_ref[...] = jnp.concatenate([turned[:features], turned[features:]], axis=1)
    bias_ref[...] = small[width : width + 1]


def place_kernel(in_ref, out_ref):
    for e in range(in_ref.shape[0]):
        out_ref[:, e, :] = in_ref[e].astype(F32)


def lay_out(x):
    rows, lanes = x.shape
    if lanes % LANES:
        return x.reshape(-1, LANES)
    return x.reshape(rows, lanes // LANES, LANES).transpose(1, 0, 2).reshape(-1, LANES)


def lay_back(x, rows, lanes):
    if lanes % LANES:
        return x.reshape(rows, lanes)
    return x.reshape(lanes // LANES, rows, LANES).transpose(1, 0, 2).reshape(rows, lanes)


def bit_of(axis, bit):
    return (lax.axis_index(axis) >> bit) & 1


def swap_parts(parts, axis, bit, n):
    parts = [part.reshape(-1, LANES) for part in parts]
    message = jnp.concatenate(parts, axis=0) if len(parts) > 1 else parts[0]
    message = lax.ppermute(message, axis, [(i, i ^ (1 << bit)) for i in range(n)])
    got, at = [], 0
    for part in parts:
        got.append(message[at : at + part.shape[0]])
        at += part.shape[0]
    return got


def halves(x, axis, bit, at):
    here = bit_of(axis, bit)
    keep = lax.dynamic_index_in_dim(x, here, at, keepdims=False)
    return keep, lax.dynamic_index_in_dim(x, 1 - here, at, keepdims=False)


def split_high(x):
    return x.reshape((2, x.shape[0] // 2) + x.shape[1:])


def in_order(mine, other, axis, bit, at):
    first = bit_of(axis, bit) == 0
    low = jnp.where(first, mine, other)
    return jnp.stack([low, jnp.where(first, other, mine)], axis=at)


def add(mine, other):
    other = other.reshape(mine.shape)
    return lax.optimization_barrier((mine.astype(F32) + other.astype(F32)).astype(BF16))


def per_device(
    n,
    alignment_embedding,
    alignment_cell_exists,
    alignment_lines_exist,
    sitewise_factors,
    pairing_matrix,
    offset_vector,
    upstream_adjoint,
):
    depth, own, features = alignment_embedding.shape
    width = sitewise_factors.shape[1] // 2
    block, pair = upstream_adjoint.shape[0], upstream_adjoint.shape[2]
    rows, chunk = depth * own, 16
    steps = block // chunk
    split = own % 16 == 0
    axes = ("row", "col")
    sds = jax.ShapeDtypeStruct

    def along_col(x, k):
        return lax.ppermute(x, "col", [(i, (i + k) % n) for i in range(n)])

    def along_row(x, k):
        return lax.ppermute(x, "row", [(i, (i + k) % n) for i in range(n)])

    def to_column(x, k):
        pairs = [(i * n + j, (j + k) % n * n + i) for i in range(n) for j in range(n)]
        return lax.ppermute(x, axes, pairs)

    r, c = lax.axis_index("row"), lax.axis_index("col")
    x = alignment_embedding.reshape(rows, features)
    line = alignment_lines_exist.reshape(1, depth)
    offset = offset_vector.reshape(1, pair)
    args = (x, alignment_cell_exists, line, sitewise_factors, offset)
    out_shapes = [
        sds((rows, LANES), BF16),
        sds((rows, LANES), BF16),
        sds((LANES, 2 * width), BF16),
        sds((2 * width, LANES), BF16),
        sds(x.shape, x.dtype),
        sds(offset.shape, F32),
    ]
    by_token, by_row, factors, factors_t, x, offset = call(
        functools.partial(prep_kernel, depth, own),
        (),
        [pl.BlockSpec(memory_space=pltpu.MemorySpace.HBM)] * len(args),
        [full(o.shape) for o in out_shapes],
        out_shapes,
        [pltpu.VMEM(v.shape, v.dtype) for v in args[1:4]] + [pltpu.SemaphoreType.DMA((5,))],
    )(*args)
    a_pieces = [by_token] + [along_col(by_token, k) for k in range(1, n)]
    b_pieces = [to_column(by_row, k) for k in range(n)]
    if not split:
        order = (c - jnp.arange(n)) % n
        held = jnp.zeros((n, rows, LANES), BF16).at[order].set(jnp.stack(a_pieces))
        a_pieces = [held.reshape(block * depth, LANES)]
        order = (r - jnp.arange(n)) % n
        held = jnp.zeros((n, depth, own, LANES), BF16)
        held = held.at[order].set(jnp.stack(b_pieces).reshape(n, depth, own, LANES))
        b_pieces = [held.transpose(1, 0, 2, 3).reshape(depth, block, LANES)]
    pieces = len(a_pieces)

    wide = width * depth
    source = jnp.arange(wide)
    perm = (jnp.arange(wide)[None, :] == (source % width * depth + source // width)[:, None]).astype(BF16)
    pairing_wide = pairing_matrix.reshape(width, width * pair)
    up_spec = pl.BlockSpec((chunk, block, pair), lambda g: (g, 0, 0))
    tokens = block * depth
    out_shapes = [
        sds((tokens, LANES), BF16),
        sds((depth, block, LANES), BF16),
        sds((tokens, width), BF16),
        sds((block, wide), BF16),
        sds((wide, block), BF16),
        sds((steps, block, chunk), F32),
        sds((8, pair), F32),
        sds((width * width, pair), BF16),
        sds((width, features), F32),
    ]
    outs = call(
        functools.partial(weight_kernel, depth, features, n, pieces),
        (steps,),
        [full(p.shape) for p in a_pieces]
        + [full(p.shape) for p in b_pieces]
        + [up_spec]
        + [full(v.shape) for v in (factors, factors_t, perm, pairing_wide)],
        [full(o.shape) for o in out_shapes],
        out_shapes,
        [
            pltpu.VMEM((width + features, tokens), BF16),
            pltpu.VMEM((width, chunk * depth, pair), BF16),
            pltpu.VMEM((width * width, pair), F32),
            pltpu.VMEM((features, width * pair), F32),
        ],
        cost(5e9, 8e6),
    )(*a_pieces, *b_pieces, upstream_adjoint, factors, factors_t, perm, pairing_wide)
    mi, mj, a, b, b_t, inv, bias, d_pairing, left = outs

    bits = n.bit_length() - 1
    d_pairing = d_pairing.reshape(n, -1, LANES)
    for bit in reversed(range(1, bits)):
        keep, go = halves(split_high(d_pairing), "col", bit, 0)
        d_pairing = add(keep, *swap_parts([go], "col", bit, n))

    out_shapes = [sds((width + 16, LANES), BF16), sds((block, wide), BF16)]
    small, d_b = call(
        functools.partial(token_kernel, depth, features),
        (steps,),
        [up_spec]
        + [full(v.shape) for v in (inv, a, pairing_wide, mj, perm, bias, left)],
        [full(o.shape) for o in out_shapes],
        out_shapes,
        [pltpu.VMEM((chunk, wide, pair), BF16), pltpu.VMEM((block, wide), F32)],
        cost(5e9, 8e6),
    )(upstream_adjoint, inv, a, pairing_wide, mj, perm, bias, left)

    d_b = jnp.stack([lay_out(d_b[k * own : (k + 1) * own]) for k in range(n)])
    dp_keep, dp_go = halves(d_pairing, "col", 0, 0)
    db_keep, db_go = halves(d_b.reshape((n // 2, 2) + d_b.shape[1:]), "col", 0, 1)
    parts = swap_parts([dp_go, db_go, small], "col", 0, n)
    d_pairing, small = add(dp_keep, parts[0]), add(small, parts[2])
    d_b = in_order(db_keep, parts[1].reshape(db_keep.shape), "col", 0, 1)
    db_keep, db_go = halves(d_b, "row", 0, 1)
    for bit in range(bits):
        parts = swap_parts([d_pairing, db_go, small], "row", bit, n)
        if bit == 0:
            d_a = call(
                functools.partial(left_kernel, depth),
                (steps,),
                [up_spec] + [full(v.shape) for v in (inv, b_t, pairing_wide)],
                full((width, tokens)),
                sds((width, tokens), BF16),
                [pltpu.VMEM((width, chunk * depth, pair), BF16)],
                cost(6e9, 8e6),
            )(upstream_adjoint, inv, b_t, pairing_wide)
            parts[0], d_a = lax.optimization_barrier((parts[0], d_a))
            d_a = jnp.stack([lay_out(d_a[:, k * rows : (k + 1) * rows]) for k in range(n)])
            d_a = d_a.reshape((n // 2, 2) + d_a.shape[1:])
        if bit == 1:
            da_keep, da_go = halves(d_a, "col", 0, 1)
            d_a = add(da_keep, *swap_parts([da_go], "col", 0, n))
            coupling_update = call(
                functools.partial(update_kernel, depth),
                (steps,),
                [full(v.shape) for v in (inv, a, b, pairing_wide)] + [full((1, pair))],
                up_spec,
                sds((block, block, pair), BF16),
                [pltpu.VMEM((chunk, wide, pair), BF16)],
                cost(6e9, 8e6),
            )(inv, a, b, pairing_wide, offset)
            held = (parts[0], coupling_update, d_a)
            parts[0], coupling_update, d_a = lax.optimization_barrier(held)
        d_pairing, d_b, small = add(d_pairing, parts[0]), add(db_keep, parts[1]), add(small, parts[2])
        db_keep = db_go = d_b
    d_pairing = d_pairing.reshape(1, -1, LANES)
    small_parts, da_parts = [small], [d_a]
    for bit in reversed(range(1, bits)):
        if len(small_parts) > 1:
            small_parts, da_parts = [add(*small_parts)], [add(*da_parts)]
        db_keep, db_go = halves(split_high(d_b), "col", bit, 0)
        da_keep, da_go = halves(split_high(da_parts[0]), "col", bit, 0)
        parts = swap_parts([d_pairing, db_go, da_go, small_parts[0]], "col", bit, n)
        d_pairing = in_order(d_pairing, parts[0].reshape(d_pairing.shape), "col", bit, 1)
        d_pairing = d_pairing.reshape((-1,) + d_pairing.shape[2:])
        mine = bit_of("col", bit) == bit_of("row", bit)
        d_b = jnp.where(mine, db_keep, parts[1].reshape(db_keep.shape))
        da_parts = [da_keep, parts[2].reshape(da_keep.shape)]
        small_parts = [small_parts[0], parts[3]]
    (got,) = swap_parts([d_pairing], "col", 0, n)
    d_pairing = in_order(d_pairing, got.reshape(d_pairing.shape), "col", 0, 1)
    d_a = [lay_back(part.reshape(-1, LANES), width, rows) for part in da_parts]
    d_b = lay_back(d_b[0], own, wide)

    args = (*d_a, d_b, *small_parts, x, by_row, factors_t, perm)
    out_shapes = [sds((rows, features), F32), sds((features, 2 * width), F32), sds((1, pair), F32)]
    embedding_adjoint, factors_adjoint, offset_slope = call(
        functools.partial(owner_kernel, depth, own, features),
        (),
        [full(v.shape) for v in args],
        [full(o.shape) for o in out_shapes],
        out_shapes,
    )(*args)

    d_pairing = d_pairing.reshape(width, width, pair)
    placed = call(
        place_kernel,
        (),
        [full(d_pairing.shape)],
        full((width, width, pair)),
        sds((width, width, pair), F32),
    )(d_pairing)
    return (
        coupling_update,
        embedding_adjoint.reshape(depth, own, features),
        factors_adjoint,
        placed.reshape(width * width, pair),
        offset_slope.reshape(pair),
    )


def solution(mesh):
    n = mesh.shape["col"]
    placed = (
        P(None, ("groups", "row", "col"), None),
        P(None, ("groups", "row", "col")),
        P("groups"),
        P(),
        P(),
        P(),
        P(("groups", "row"), "col", None),
    )
    return jax.shard_map(
        functools.partial(per_device, n),
        mesh=mesh,
        in_specs=placed,
        out_specs=(
            P(("groups", "row"), "col", None),
            P(None, ("groups", "row", "col"), None),
            P("groups", None),
            P("groups", None),
            P("groups"),
        ),
        check_vma=False,
    )
```

```python
import functools

import jax
import jax.numpy as jnp
from jax import lax
from jax.experimental import pallas as pl
from jax.experimental.pallas import tpu as pltpu
from jax.sharding import PartitionSpec as P

F32 = jnp.float32
BF16 = jnp.bfloat16
LANES = 128
VMEM_LIMIT = 40 * 1024 * 1024
NT = (((1,), (1,)), ((), ()))


def dot(left, right):
    return jnp.dot(left, right, preferred_element_type=F32)


def dot_nt(left, right):
    return lax.dot_general(left, right, NT, preferred_element_type=F32)


def iota(shape, axis):
    return lax.broadcasted_iota(jnp.int32, shape, axis)


def one_hot(mask):
    return jnp.where(mask, 1.0, 0.0).astype(BF16)


def full(shape):
    return pl.BlockSpec(shape, lambda *g: (0,) * len(shape))


def cost(flops, nbytes):
    return pl.CostEstimate(flops=int(flops), bytes_accessed=int(nbytes), transcendentals=0)


def call(kernel, grid, in_specs, out_specs, out_shape, scratch=(), estimate=None):
    return pl.pallas_call(
        kernel,
        grid=grid,
        in_specs=in_specs,
        out_specs=out_specs,
        out_shape=out_shape,
        scratch_shapes=list(scratch),
        compiler_params=pltpu.CompilerParams(vmem_limit_bytes=VMEM_LIMIT),
        cost_estimate=estimate,
    )


def stats(x):
    center = x - jnp.mean(x, axis=-1, keepdims=True)
    scale = lax.rsqrt(jnp.mean(center * center, axis=-1, keepdims=True) + 1e-05)
    return center * scale, scale


def prep_kernel(depth, own, x_ref, mask_ref, by_token_ref, by_row_ref):
    rows = depth * own
    normed, _ = stats(x_ref[...].astype(F32))
    features = normed.shape[1]
    pick = one_hot(iota((rows, depth), 0) // own == iota((rows, depth), 1))
    here = iota((rows, own), 0) % own == iota((rows, own), 1)
    weight = dot(pick, mask_ref[...])
    weight = jnp.sum(jnp.where(here, weight, 0.0), axis=1, keepdims=True)
    masked = normed.astype(BF16).astype(F32) * weight
    wide = jnp.concatenate([masked, jnp.zeros((rows, LANES - features), F32)], axis=1)
    lane = iota((rows, LANES), 1)
    at = lane == features + iota((rows, LANES), 0) // own
    wide = (wide + jnp.where(at, weight, 0.0)).astype(BF16)
    by_row_ref[...] = wide
    p, q = iota((rows, rows), 0), iota((rows, rows), 1)
    swap = one_hot(q == (p % depth) * own + p // depth)
    by_token_ref[...] = dot(swap, wide).astype(BF16)


def scaled_pair(up_ref, inv, at):
    parts = [up_ref[i].astype(F32) * inv[:, i : i + 1] for i in (at, at + 1)]
    return jnp.concatenate(parts, axis=1).astype(BF16)


def fill_v(up_ref, inv, bt, v_ref, depth):
    chunk, _, pair = up_ref.shape
    width = v_ref.shape[0]
    for at in range(0, chunk, 2):
        v = dot(bt, scaled_pair(up_ref, inv, at)).astype(BF16)
        for k in range(2):
            part = v[:, k * pair : (k + 1) * pair].reshape(width, depth, pair)
            v_ref[:, (at + k) * depth : (at + k + 1) * depth, :] = part


def fill_t(a_chunk, wc_ref, t_ref, depth):
    chunk, rows, pair = t_ref.shape
    width = rows // depth
    for e in range(0, width, 2):
        t = dot(a_chunk, wc_ref[:, e * pair : (e + 2) * pair]).astype(BF16)
        for k in range(2):
            part = t[:, k * pair : (k + 1) * pair].reshape(chunk, depth, pair)
            t_ref[:, (e + k) * depth : (e + k + 1) * depth, :] = part


def two(ref, at):
    return jnp.concatenate([ref[at], ref[at + 1]], axis=1)


def weight_kernel(depth, features, n, pieces, *refs):
    a_refs, b_refs = refs[:pieces], refs[pieces : 2 * pieces]
    up_ref, w_ref, perm_ref, wc_ref = refs[2 * pieces : 2 * pieces + 4]
    outs = refs[2 * pieces + 4 :]
    mj_ref, a_ref, b_ref, bt_ref, wt_ref, inv_ref, bias_ref, dw_ref, left_ref = outs[:9]
    mi_ref, at_ref, v_ref, acc_ref, wide_ref = outs[9:]
    g, last = pl.program_id(0), pl.num_programs(0) - 1
    chunk, block, pair = up_ref.shape
    width = w_ref.shape[1] // 2
    r, c = lax.axis_index("row"), lax.axis_index("col")

    @pl.when(g == 0)
    def _():
        if pieces == 1:
            mi_ref[...] = a_refs[0][...]
            mj_ref[...] = b_refs[0][...]
        else:
            own = block // pieces
            for k in range(pieces):
                src = lax.rem(c - k + n, n)
                rows = pl.ds(pl.multiple_of(src * own * depth, own * depth), own * depth)
                mi_ref[rows, :] = a_refs[k][...]
                src = lax.rem(r - k + n, n)
                rows = pl.ds(pl.multiple_of(src * own, own), own)
                for s in range(depth):
                    mj_ref[s, rows, :] = b_refs[k][s * own : (s + 1) * own, :]
        pad = jnp.zeros((LANES - features, 2 * width), BF16)
        w = jnp.concatenate([w_ref[...], pad], axis=0)
        same = one_hot(iota((2 * width, 2 * width), 0) == iota((2 * width, 2 * width), 1))
        wt = dot_nt(same, w).astype(BF16)
        wt_ref[...] = wt
        mi = mi_ref[...]
        a_ref[...] = dot(mi, w[:, :width]).astype(BF16)
        same = one_hot(iota((features, LANES), 0) == iota((features, LANES), 1))
        at_ref[...] = dot_nt(jnp.concatenate([wt[:width, :], same], axis=0), mi).astype(BF16)
        b = jnp.zeros((block, width * depth), F32)
        seen = jnp.zeros((block, LANES), F32)
        for s in range(depth):
            mj = mj_ref[s]
            seen = seen + mj.astype(F32)
            part = dot(mj, w[:, width:]).astype(BF16)
            b = b + dot(part, perm_ref[s * width : (s + 1) * width, :])
        b_ref[...] = b.astype(BF16)
        bt_ref[...] = b.T.astype(BF16)
        keep = iota((block, LANES), 1) >= features
        seen_j = jnp.where(keep, seen, 0.0).astype(BF16)
        rows = block * depth
        gather = one_hot(iota((block, rows), 0) == iota((block, rows), 1) // depth)
        seen_i = dot(gather, mi).astype(BF16)
        for k in range(block // chunk):
            count = dot_nt(seen_j, seen_i[k * chunk : (k + 1) * chunk, :])
            inv_ref[k] = 1.0 / (count + 0.001)
        acc_ref[...] = jnp.zeros_like(acc_ref)
        wide_ref[...] = jnp.zeros_like(wide_ref)
        bias_ref[...] = jnp.zeros_like(bias_ref)

    bias_ref[0:1, :] += jnp.sum(
        jnp.sum(up_ref[...].astype(F32), axis=0), axis=0, keepdims=True
    )
    fill_v(up_ref, inv_ref[g], bt_ref[...], v_ref, depth)
    span = chunk * depth
    a_t = at_ref[:, pl.ds(pl.multiple_of(g * span, span), span)]
    for e in range(0, width, 2):
        part = dot(a_t, two(v_ref, e))
        for k in range(2):
            rows = slice((e + k) * width, (e + k + 1) * width)
            acc_ref[rows, :] += part[:width, k * pair : (k + 1) * pair]
        wide_ref[:, e * pair : (e + 2) * pair] += part[width:]

    @pl.when(g == last)
    def _():
        dw_ref[...] = acc_ref[...].astype(BF16)
        left = jnp.zeros((width, features), F32)
        for e in range(0, width, 2):
            lanes = slice(e * pair, (e + 2) * pair)
            left = left + dot_nt(wc_ref[:, lanes], wide_ref[:, lanes].astype(BF16))
        left_ref[...] = left


def left_kernel(depth, up_ref, inv_ref, bt_ref, wc_ref, small_ref, out_ref, pass_ref, v_ref):
    g = pl.program_id(0)
    chunk, _, pair = up_ref.shape
    width = wc_ref.shape[0]
    span = chunk * depth

    @pl.when(g == 0)
    def _():
        pass_ref[...] = small_ref[...]

    fill_v(up_ref, inv_ref[g], bt_ref[...], v_ref, depth)
    d_a = jnp.zeros((span, width), F32)
    for e in range(0, width, 2):
        d_a = d_a + dot_nt(two(v_ref, e), wc_ref[:, e * pair : (e + 2) * pair])
    same = one_hot(iota((width, width), 0) == iota((width, width), 1))
    d_a = dot_nt(same, d_a.astype(BF16)).astype(BF16)
    out_ref[:, pl.ds(pl.multiple_of(g * span, span), span)] = d_a


def token_kernel(depth, features, *refs):
    up_ref, inv_ref, a_ref, wc_ref, mj_ref, perm_ref, bias_ref, left_ref = refs[:8]
    small_ref, out_ref, t_ref, db_ref = refs[8:]
    g, last = pl.program_id(0), pl.num_programs(0) - 1
    chunk = up_ref.shape[0]
    width = wc_ref.shape[0]
    span = chunk * depth
    inv = inv_ref[g]

    @pl.when(g == 0)
    def _():
        db_ref[...] = jnp.zeros_like(db_ref)

    a_chunk = a_ref[pl.ds(pl.multiple_of(g * span, span), span), :]
    fill_t(a_chunk, wc_ref, t_ref, depth)
    d_b = db_ref[...]
    for at in range(0, chunk, 2):
        d_b = d_b + dot_nt(two(t_ref, at), scaled_pair(up_ref, inv, at))
    db_ref[...] = d_b

    @pl.when(g == last)
    def _():
        d_b = db_ref[...].T.astype(BF16)
        out_ref[...] = d_b
        turned = dot_nt(perm_ref[...], d_b).astype(BF16)
        right = jnp.zeros((width, LANES), F32)
        for s in range(depth):
            right = right + dot(turned[s * width : (s + 1) * width, :], mj_ref[s])
        small = jnp.concatenate([left_ref[...], right[:, :features]], axis=1)
        small_ref[0:width, :] = small.astype(BF16)
        small_ref[width:, :] = jnp.broadcast_to(bias_ref[0:1, :], (16, LANES)).astype(BF16)


def update_kernel(depth, count, *refs):
    inv_ref, a_ref, b_ref, wc_ref, offset_ref = refs[:5]
    in_refs, out_ref, pass_refs, t_ref = refs[5 : 5 + count], refs[5 + count], refs[6 + count : -1], refs[-1]
    g = pl.program_id(0)

    @pl.when(g == 0)
    def _():
        for src, dst in zip(in_refs, pass_refs):
            dst[...] = src[...]

    chunk, block, pair = out_ref.shape
    span = chunk * depth
    inv = inv_ref[g]
    fill_t(a_ref[pl.ds(pl.multiple_of(g * span, span), span), :], wc_ref, t_ref, depth)
    b = b_ref[...]
    offset = offset_ref[...]
    for at in range(0, chunk, 2):
        part = dot(b, two(t_ref, at))
        for k in range(2):
            value = part[:, k * pair : (k + 1) * pair] * inv[:, at + k : at + k + 1] + offset
            out_ref[at + k] = value.astype(BF16)


def owner_kernel(depth, own, features, *refs):
    da_refs, db_ref, small_refs = refs[:2], refs[2], refs[3:5]
    x_ref, message_ref, wt_ref, perm_ref, out_ref, factors_ref, bias_ref = refs[5:]
    rows = depth * own
    width = wt_ref.shape[0] // 2
    p, q = iota((rows, rows), 0), iota((rows, rows), 1)
    swap = one_hot(q == (p % own) * depth + p // own)
    d_a = dot_nt(swap, da_refs[0][...]) + dot_nt(swap, da_refs[1][...])
    d_b = dot_nt(db_ref[...], perm_ref[...])
    d_b = jnp.concatenate([d_b[:, s * width : (s + 1) * width] for s in range(depth)], axis=0)
    highest = lax.Precision.HIGHEST
    wt = wt_ref[...].astype(F32)
    d_normed = jnp.dot(d_a, wt[:width, :], precision=highest, preferred_element_type=F32)
    d_normed = d_normed + jnp.dot(d_b, wt[width:, :], precision=highest, preferred_element_type=F32)
    message = message_ref[...].astype(F32)
    mask = iota((rows, LANES), 1) >= features
    weight = jnp.sum(jnp.where(mask, message, 0.0), axis=1, keepdims=True)
    d_normed = d_normed[:, :features] * weight
    normed, scale = stats(x_ref[...].astype(F32))
    mean = jnp.mean(d_normed, axis=-1, keepdims=True)
    along = jnp.mean(d_normed * normed, axis=-1, keepdims=True)
    out_ref[...] = scale * (d_normed - mean - normed * along)
    small = small_refs[0][...].astype(F32) + small_refs[1][...].astype(F32)
    turned = small[:width].T
    factors_ref[...] = jnp.concatenate([turned[:features], turned[features:]], axis=1)
    bias_ref[...] = small[width : width + 1]


def place_kernel(in_ref, out_ref):
    for e in range(in_ref.shape[0]):
        out_ref[:, e, :] = in_ref[e].astype(F32)


def lay_out(x):
    rows, lanes = x.shape
    if lanes % LANES:
        return x.reshape(-1, LANES)
    return x.reshape(rows, lanes // LANES, LANES).transpose(1, 0, 2).reshape(-1, LANES)


def lay_back(x, rows, lanes):
    if lanes % LANES:
        return x.reshape(rows, lanes)
    return x.reshape(lanes // LANES, rows, LANES).transpose(1, 0, 2).reshape(rows, lanes)


def bit_of(axis, bit):
    return (lax.axis_index(axis) >> bit) & 1


def swap_parts(parts, axis, bit, n):
    parts = [part.reshape(-1, LANES) for part in parts]
    message = jnp.concatenate(parts, axis=0) if len(parts) > 1 else parts[0]
    message = lax.ppermute(message, axis, [(i, i ^ (1 << bit)) for i in range(n)])
    got, at = [], 0
    for part in parts:
        got.append(message[at : at + part.shape[0]])
        at += part.shape[0]
    return got


def halves(x, axis, bit, at):
    here = bit_of(axis, bit)
    keep = lax.dynamic_index_in_dim(x, here, at, keepdims=False)
    return keep, lax.dynamic_index_in_dim(x, 1 - here, at, keepdims=False)


def split_high(x):
    return x.reshape((2, x.shape[0] // 2) + x.shape[1:])


def in_order(mine, other, axis, bit, at):
    first = bit_of(axis, bit) == 0
    low = jnp.where(first, mine, other)
    return jnp.stack([low, jnp.where(first, other, mine)], axis=at)


def add(mine, other):
    other = other.reshape(mine.shape)
    return lax.optimization_barrier((mine.astype(F32) + other.astype(F32)).astype(BF16))


def per_device(
    n,
    alignment_embedding,
    alignment_cell_exists,
    alignment_lines_exist,
    sitewise_factors,
    pairing_matrix,
    offset_vector,
    upstream_adjoint,
):
    depth, own, features = alignment_embedding.shape
    width = sitewise_factors.shape[1] // 2
    block, pair = upstream_adjoint.shape[0], upstream_adjoint.shape[2]
    rows, chunk = depth * own, 16
    steps = block // chunk
    split = own % 16 == 0
    axes = ("row", "col")
    sds = jax.ShapeDtypeStruct

    def along_col(x, k):
        return lax.ppermute(x, "col", [(i, (i + k) % n) for i in range(n)])

    def along_row(x, k):
        return lax.ppermute(x, "row", [(i, (i + k) % n) for i in range(n)])

    def to_column(x, k):
        pairs = [(i * n + j, (j + k) % n * n + i) for i in range(n) for j in range(n)]
        return lax.ppermute(x, axes, pairs)

    r, c = lax.axis_index("row"), lax.axis_index("col")
    x = alignment_embedding.reshape(rows, features)
    mask = (alignment_cell_exists * alignment_lines_exist[:, None]).astype(BF16)
    offset = offset_vector.reshape(1, pair)
    by_token, by_row = call(
        functools.partial(prep_kernel, depth, own),
        (),
        [full(x.shape), full(mask.shape)],
        [full((rows, LANES))] * 2,
        [sds((rows, LANES), BF16)] * 2,
    )(x, mask)
    a_pieces = [by_token] + [along_col(by_token, k) for k in range(1, n)]
    b_pieces = [to_column(by_row, k) for k in range(n)]
    if not split:
        order = (c - jnp.arange(n)) % n
        held = jnp.zeros((n, rows, LANES), BF16).at[order].set(jnp.stack(a_pieces))
        a_pieces = [held.reshape(block * depth, LANES)]
        order = (r - jnp.arange(n)) % n
        held = jnp.zeros((n, depth, own, LANES), BF16)
        held = held.at[order].set(jnp.stack(b_pieces).reshape(n, depth, own, LANES))
        b_pieces = [held.transpose(1, 0, 2, 3).reshape(depth, block, LANES)]
    pieces = len(a_pieces)

    wide = width * depth
    source = jnp.arange(wide)
    perm = (jnp.arange(wide)[None, :] == (source % width * depth + source // width)[:, None]).astype(BF16)
    pairing_wide = pairing_matrix.reshape(width, width * pair)
    up_spec = pl.BlockSpec((chunk, block, pair), lambda g: (g, 0, 0))
    tokens = block * depth
    out_shapes = [
        sds((depth, block, LANES), BF16),
        sds((tokens, width), BF16),
        sds((block, wide), BF16),
        sds((wide, block), BF16),
        sds((2 * width, LANES), BF16),
        sds((steps, block, chunk), F32),
        sds((8, pair), F32),
        sds((width * width, pair), BF16),
        sds((width, features), F32),
    ]
    outs = call(
        functools.partial(weight_kernel, depth, features, n, pieces),
        (steps,),
        [full(p.shape) for p in a_pieces]
        + [full(p.shape) for p in b_pieces]
        + [up_spec]
        + [full(v.shape) for v in (sitewise_factors, perm, pairing_wide)],
        [full(o.shape) for o in out_shapes],
        out_shapes,
        [
            pltpu.VMEM((tokens, LANES), BF16),
            pltpu.VMEM((width + features, tokens), BF16),
            pltpu.VMEM((width, chunk * depth, pair), BF16),
            pltpu.VMEM((width * width, pair), F32),
            pltpu.VMEM((features, width * pair), F32),
        ],
        cost(5e9, 8e6),
    )(*a_pieces, *b_pieces, upstream_adjoint, sitewise_factors, perm, pairing_wide)
    mj, a, b, b_t, factors_t, inv, bias, d_pairing, left = outs

    bits = n.bit_length() - 1
    d_pairing = d_pairing.reshape(n, -1, LANES)
    for bit in reversed(range(1, bits)):
        keep, go = halves(split_high(d_pairing), "col", bit, 0)
        d_pairing = add(keep, *swap_parts([go], "col", bit, n))

    out_shapes = [sds((width + 16, LANES), BF16), sds((block, wide), BF16)]
    small, d_b = call(
        functools.partial(token_kernel, depth, features),
        (steps,),
        [up_spec]
        + [full(v.shape) for v in (inv, a, pairing_wide, mj, perm, bias, left)],
        [full(o.shape) for o in out_shapes],
        out_shapes,
        [pltpu.VMEM((chunk, wide, pair), BF16), pltpu.VMEM((wide, block), F32)],
        cost(5e9, 8e6),
    )(upstream_adjoint, inv, a, pairing_wide, mj, perm, bias, left)

    d_b = jnp.stack([lay_out(d_b[k * own : (k + 1) * own]) for k in range(n)])
    dp_keep, dp_go = halves(d_pairing, "col", 0, 0)
    db_keep, db_go = halves(d_b.reshape((n // 2, 2) + d_b.shape[1:]), "col", 0, 1)
    parts = swap_parts([dp_go, db_go, small], "col", 0, n)
    d_pairing, small = add(dp_keep, parts[0]), add(small, parts[2])
    d_b = in_order(db_keep, parts[1].reshape(db_keep.shape), "col", 0, 1)
    db_keep, db_go = halves(d_b, "row", 0, 1)
    for bit in range(bits):
        parts = swap_parts([d_pairing, db_go, small], "row", bit, n)
        if bit == 0:
            out_shapes = [sds((width, tokens), BF16), sds(small.shape, BF16)]
            d_a, small = call(
                functools.partial(left_kernel, depth),
                (steps,),
                [up_spec] + [full(v.shape) for v in (inv, b_t, pairing_wide, small)],
                [full(o.shape) for o in out_shapes],
                out_shapes,
                [pltpu.VMEM((width, chunk * depth, pair), BF16)],
                cost(6e9, 8e6),
            )(upstream_adjoint, inv, b_t, pairing_wide, small)
            d_a = jnp.stack([lay_out(d_a[:, k * rows : (k + 1) * rows]) for k in range(n)])
            da_keep, da_go = halves(d_a.reshape((n // 2, 2) + d_a.shape[1:]), "col", 0, 1)
            d_a = add(da_keep, *swap_parts([da_go], "col", 0, n))
        if bit == 1:
            passed = (small, d_a.reshape(-1, LANES))
            args = (inv, a, b, pairing_wide, offset) + passed
            coupling_update, small, d_a = call(
                functools.partial(update_kernel, depth, len(passed)),
                (steps,),
                [full(v.shape) for v in args],
                [up_spec] + [full(v.shape) for v in passed],
                [sds((block, block, pair), BF16)] + [sds(v.shape, BF16) for v in passed],
                [pltpu.VMEM((chunk, wide, pair), BF16)],
                cost(6e9, 8e6),
            )(*args)
            d_a = d_a.reshape(da_keep.shape)
        d_pairing, d_b, small = add(d_pairing, parts[0]), add(db_keep, parts[1]), add(small, parts[2])
        db_keep = db_go = d_b
    d_pairing = d_pairing.reshape(1, -1, LANES)
    small_parts, da_parts = [small], [d_a]
    for bit in reversed(range(1, bits)):
        if len(small_parts) > 1:
            small_parts, da_parts = [add(*small_parts)], [add(*da_parts)]
        db_keep, db_go = halves(split_high(d_b), "col", bit, 0)
        da_keep, da_go = halves(split_high(da_parts[0]), "col", bit, 0)
        parts = swap_parts([d_pairing, db_go, da_go, small_parts[0]], "col", bit, n)
        d_pairing = in_order(d_pairing, parts[0].reshape(d_pairing.shape), "col", bit, 1)
        d_pairing = d_pairing.reshape((-1,) + d_pairing.shape[2:])
        mine = bit_of("col", bit) == bit_of("row", bit)
        d_b = jnp.where(mine, db_keep, parts[1].reshape(db_keep.shape))
        da_parts = [da_keep, parts[2].reshape(da_keep.shape)]
        small_parts = [small_parts[0], parts[3]]
    (got,) = swap_parts([d_pairing], "col", 0, n)
    d_pairing = in_order(d_pairing, got.reshape(d_pairing.shape), "col", 0, 1)
    d_a = [lay_back(part.reshape(-1, LANES), width, rows) for part in da_parts]
    d_b = lay_back(d_b[0], own, wide)

    args = (*d_a, d_b, *small_parts, x, by_row, factors_t, perm)
    out_shapes = [sds((rows, features), F32), sds((features, 2 * width), F32), sds((1, pair), F32)]
    embedding_adjoint, factors_adjoint, offset_slope = call(
        functools.partial(owner_kernel, depth, own, features),
        (),
        [full(v.shape) for v in args],
        [full(o.shape) for o in out_shapes],
        out_shapes,
    )(*args)

    d_pairing = d_pairing.reshape(width, width, pair)
    placed = call(
        place_kernel,
        (),
        [full(d_pairing.shape)],
        full((width, width, pair)),
        sds((width, width, pair), F32),
    )(d_pairing)
    return (
        coupling_update,
        embedding_adjoint.reshape(depth, own, features),
        factors_adjoint,
        placed.reshape(width * width, pair),
        offset_slope.reshape(pair),
    )


def solution(mesh):
    n = mesh.shape["col"]
    placed = (
        P(None, ("groups", "row", "col"), None),
        P(None, ("groups", "row", "col")),
        P("groups"),
        P(),
        P(),
        P(),
        P(("groups", "row"), "col", None),
    )
    return jax.shard_map(
        functools.partial(per_device, n),
        mesh=mesh,
        in_specs=placed,
        out_specs=(
            P(("groups", "row"), "col", None),
            P(None, ("groups", "row", "col"), None),
            P("groups", None),
            P("groups", None),
            P("groups"),
        ),
        check_vma=False,
    )
```

```python
import functools

import jax
import jax.numpy as jnp
from jax import lax
from jax.experimental import pallas as pl
from jax.experimental.pallas import tpu as pltpu
from jax.sharding import PartitionSpec as P

F32 = jnp.float32
BF16 = jnp.bfloat16
LANES = 128
VMEM_LIMIT = 40 * 1024 * 1024
NT = (((1,), (1,)), ((), ()))


def dot(left, right):
    return jnp.dot(left, right, preferred_element_type=F32)


def dot_nt(left, right):
    return lax.dot_general(left, right, NT, preferred_element_type=F32)


def iota(shape, axis):
    return lax.broadcasted_iota(jnp.int32, shape, axis)


def one_hot(mask):
    return jnp.where(mask, 1.0, 0.0).astype(BF16)


def full(shape):
    return pl.BlockSpec(shape, lambda *g: (0,) * len(shape))


def cost(flops, nbytes):
    return pl.CostEstimate(flops=int(flops), bytes_accessed=int(nbytes), transcendentals=0)


def call(kernel, grid, in_specs, out_specs, out_shape, scratch=(), estimate=None):
    return pl.pallas_call(
        kernel,
        grid=grid,
        in_specs=in_specs,
        out_specs=out_specs,
        out_shape=out_shape,
        scratch_shapes=list(scratch),
        compiler_params=pltpu.CompilerParams(vmem_limit_bytes=VMEM_LIMIT),
        cost_estimate=estimate,
    )


def stats(x):
    center = x - jnp.mean(x, axis=-1, keepdims=True)
    scale = lax.rsqrt(jnp.mean(center * center, axis=-1, keepdims=True) + 1e-05)
    return center * scale, scale


def prep_kernel(depth, own, x_ref, mask_ref, by_token_ref, by_row_ref):
    rows = depth * own
    normed, _ = stats(x_ref[...].astype(F32))
    features = normed.shape[1]
    pick = one_hot(iota((rows, depth), 0) // own == iota((rows, depth), 1))
    here = iota((rows, own), 0) % own == iota((rows, own), 1)
    weight = dot(pick, mask_ref[...])
    weight = jnp.sum(jnp.where(here, weight, 0.0), axis=1, keepdims=True)
    masked = normed.astype(BF16).astype(F32) * weight
    wide = jnp.concatenate([masked, jnp.zeros((rows, LANES - features), F32)], axis=1)
    lane = iota((rows, LANES), 1)
    at = lane == features + iota((rows, LANES), 0) // own
    wide = (wide + jnp.where(at, weight, 0.0)).astype(BF16)
    by_row_ref[...] = wide
    p, q = iota((rows, rows), 0), iota((rows, rows), 1)
    swap = one_hot(q == (p % depth) * own + p // depth)
    by_token_ref[...] = dot(swap, wide).astype(BF16)


def scaled_pair(up_ref, inv, at):
    parts = [up_ref[i].astype(F32) * inv[:, i : i + 1] for i in (at, at + 1)]
    return jnp.concatenate(parts, axis=1).astype(BF16)


def fill_v(up_ref, inv, bt, v_ref, depth):
    chunk, _, pair = up_ref.shape
    width = v_ref.shape[0]
    for at in range(0, chunk, 2):
        v = dot(bt, scaled_pair(up_ref, inv, at)).astype(BF16)
        for k in range(2):
            part = v[:, k * pair : (k + 1) * pair].reshape(width, depth, pair)
            v_ref[:, (at + k) * depth : (at + k + 1) * depth, :] = part


def fill_t(a_chunk, wc_ref, t_ref, depth):
    chunk, rows, pair = t_ref.shape
    width = rows // depth
    for e in range(0, width, 2):
        t = dot(a_chunk, wc_ref[:, e * pair : (e + 2) * pair]).astype(BF16)
        for k in range(2):
            part = t[:, k * pair : (k + 1) * pair].reshape(chunk, depth, pair)
            t_ref[:, (e + k) * depth : (e + k + 1) * depth, :] = part


def two(ref, at):
    return jnp.concatenate([ref[at], ref[at + 1]], axis=1)


def weight_kernel(depth, features, n, pieces, *refs):
    a_refs, b_refs = refs[:pieces], refs[pieces : 2 * pieces]
    up_ref, w_ref, perm_ref, wc_ref = refs[2 * pieces : 2 * pieces + 4]
    outs = refs[2 * pieces + 4 :]
    mj_ref, a_ref, b_ref, bt_ref, wt_ref, inv_ref, bias_ref, dw_ref, left_ref = outs[:9]
    mi_ref, at_ref, v_ref, acc_ref, wide_ref = outs[9:]
    g, last = pl.program_id(0), pl.num_programs(0) - 1
    chunk, block, pair = up_ref.shape
    width = w_ref.shape[1] // 2
    r, c = lax.axis_index("row"), lax.axis_index("col")

    @pl.when(g == 0)
    def _():
        if pieces == 1:
            mi_ref[...] = a_refs[0][...]
            mj_ref[...] = b_refs[0][...]
        else:
            own = block // pieces
            for k in range(pieces):
                src = lax.rem(c - k + n, n)
                rows = pl.ds(pl.multiple_of(src * own * depth, own * depth), own * depth)
                mi_ref[rows, :] = a_refs[k][...]
                src = lax.rem(r - k + n, n)
                rows = pl.ds(pl.multiple_of(src * own, own), own)
                for s in range(depth):
                    mj_ref[s, rows, :] = b_refs[k][s * own : (s + 1) * own, :]
        pad = jnp.zeros((LANES - features, 2 * width), BF16)
        w = jnp.concatenate([w_ref[...], pad], axis=0)
        same = one_hot(iota((2 * width, 2 * width), 0) == iota((2 * width, 2 * width), 1))
        wt = dot_nt(same, w).astype(BF16)
        wt_ref[...] = wt
        mi = mi_ref[...]
        a_ref[...] = dot(mi, w[:, :width]).astype(BF16)
        same = one_hot(iota((features, LANES), 0) == iota((features, LANES), 1))
        at_ref[...] = dot_nt(jnp.concatenate([wt[:width, :], same], axis=0), mi).astype(BF16)
        b = jnp.zeros((block, width * depth), F32)
        seen = jnp.zeros((block, LANES), F32)
        for s in range(depth):
            mj = mj_ref[s]
            seen = seen + mj.astype(F32)
            part = dot(mj, w[:, width:]).astype(BF16)
            b = b + dot(part, perm_ref[s * width : (s + 1) * width, :])
        b_ref[...] = b.astype(BF16)
        bt_ref[...] = b.T.astype(BF16)
        keep = iota((block, LANES), 1) >= features
        seen_j = jnp.where(keep, seen, 0.0).astype(BF16)
        rows = block * depth
        gather = one_hot(iota((block, rows), 0) == iota((block, rows), 1) // depth)
        seen_i = dot(gather, mi).astype(BF16)
        for k in range(block // chunk):
            count = dot_nt(seen_j, seen_i[k * chunk : (k + 1) * chunk, :])
            inv_ref[k] = 1.0 / (count + 0.001)
        acc_ref[...] = jnp.zeros_like(acc_ref)
        wide_ref[...] = jnp.zeros_like(wide_ref)
        bias_ref[...] = jnp.zeros_like(bias_ref)

    bias_ref[0:1, :] += jnp.sum(
        jnp.sum(up_ref[...].astype(F32), axis=0), axis=0, keepdims=True
    )
    fill_v(up_ref, inv_ref[g], bt_ref[...], v_ref, depth)
    span = chunk * depth
    a_t = at_ref[:, pl.ds(pl.multiple_of(g * span, span), span)]
    for e in range(0, width, 2):
        part = dot(a_t, two(v_ref, e))
        for k in range(2):
            rows = slice((e + k) * width, (e + k + 1) * width)
            acc_ref[rows, :] += part[:width, k * pair : (k + 1) * pair]
        wide_ref[:, e * pair : (e + 2) * pair] += part[width:]

    @pl.when(g == last)
    def _():
        dw_ref[...] = acc_ref[...].astype(BF16)
        left = jnp.zeros((width, features), F32)
        for e in range(0, width, 2):
            lanes = slice(e * pair, (e + 2) * pair)
            left = left + dot_nt(wc_ref[:, lanes], wide_ref[:, lanes].astype(BF16))
        left_ref[...] = left


def left_kernel(depth, bit, up_ref, inv_ref, bt_ref, wc_ref, small_ref, keep_ref, go_ref, pass_ref, v_ref, da_ref):
    g, last = pl.program_id(0), pl.num_programs(0) - 1
    chunk, _, pair = up_ref.shape
    width = wc_ref.shape[0]
    span = chunk * depth

    @pl.when(g == 0)
    def _():
        pass_ref[...] = small_ref[...]

    fill_v(up_ref, inv_ref[g], bt_ref[...], v_ref, depth)
    v = jnp.concatenate([v_ref[e] for e in range(width)], axis=1)
    d_a = dot_nt(v, wc_ref[...])
    same = one_hot(iota((width, width), 0) == iota((width, width), 1))
    d_a = dot_nt(same, d_a.astype(BF16)).astype(BF16)
    tiles = span // LANES
    for k in range(tiles):
        da_ref[g * tiles + k] = d_a[:, k * LANES : (k + 1) * LANES]

    @pl.when(g == last)
    def _():
        half = keep_ref.shape[0]
        here = (lax.axis_index("col") >> bit) & 1
        keep_ref[...] = da_ref[pl.ds(here * half, half)]
        go_ref[...] = da_ref[pl.ds((1 - here) * half, half)]


def token_kernel(depth, features, n, *refs):
    up_ref, inv_ref, a_ref, wc_ref, mj_ref, perm_ref, bias_ref, left_ref = refs[:8]
    small_ref, out_ref, t_ref, db_ref = refs[8:]
    g, last = pl.program_id(0), pl.num_programs(0) - 1
    chunk, block = up_ref.shape[:2]
    width = wc_ref.shape[0]
    span = chunk * depth
    inv = inv_ref[g]

    @pl.when(g == 0)
    def _():
        db_ref[...] = jnp.zeros_like(db_ref)

    a_chunk = a_ref[pl.ds(pl.multiple_of(g * span, span), span), :]
    fill_t(a_chunk, wc_ref, t_ref, depth)
    t = jnp.concatenate([t_ref[i] for i in range(chunk)], axis=1)
    scaled = jnp.concatenate([scaled_pair(up_ref, inv, at) for at in range(0, chunk, 2)], axis=1)
    db_ref[...] += dot_nt(t, scaled)

    @pl.when(g == last)
    def _():
        d_b = db_ref[...].T.astype(BF16)
        own = block // n
        for k in range(n):
            part = d_b[k * own : (k + 1) * own, :]
            for q in range(part.shape[1] // LANES):
                out_ref[k, q * own : (q + 1) * own, :] = part[:, q * LANES : (q + 1) * LANES]
        turned = dot_nt(perm_ref[...], d_b).astype(BF16)
        right = jnp.zeros((width, LANES), F32)
        for s in range(depth):
            right = right + dot(turned[s * width : (s + 1) * width, :], mj_ref[s])
        small = jnp.concatenate([left_ref[...], right[:, :features]], axis=1)
        small_ref[0:width, :] = small.astype(BF16)
        small_ref[width:, :] = jnp.broadcast_to(bias_ref[0:1, :], (16, LANES)).astype(BF16)


def update_kernel(depth, inv_ref, a_ref, b_ref, wc_ref, offset_ref, small_ref, out_ref, pass_ref, t_ref):
    g = pl.program_id(0)

    @pl.when(g == 0)
    def _():
        pass_ref[...] = small_ref[...]

    chunk, block, pair = out_ref.shape
    span = chunk * depth
    inv = inv_ref[g]
    fill_t(a_ref[pl.ds(pl.multiple_of(g * span, span), span), :], wc_ref, t_ref, depth)
    b = b_ref[...]
    offset = offset_ref[...]
    for at in range(0, chunk, 2):
        part = dot(b, two(t_ref, at))
        for k in range(2):
            value = part[:, k * pair : (k + 1) * pair] * inv[:, at + k : at + k + 1] + offset
            out_ref[at + k] = value.astype(BF16)


def owner_kernel(depth, own, features, *refs):
    da_refs, db_ref, small_refs = refs[:2], refs[2], refs[3:5]
    x_ref, message_ref, wt_ref, perm_ref, out_ref, factors_ref, bias_ref = refs[5:]
    rows = depth * own
    width = wt_ref.shape[0] // 2
    p, q = iota((rows, rows), 0), iota((rows, rows), 1)
    swap = one_hot(q == (p % own) * depth + p // own)
    d_a = dot_nt(swap, da_refs[0][...]) + dot_nt(swap, da_refs[1][...])
    d_b = dot_nt(db_ref[...], perm_ref[...])
    d_b = jnp.concatenate([d_b[:, s * width : (s + 1) * width] for s in range(depth)], axis=0)
    highest = lax.Precision.HIGHEST
    wt = wt_ref[...].astype(F32)
    d_normed = jnp.dot(d_a, wt[:width, :], precision=highest, preferred_element_type=F32)
    d_normed = d_normed + jnp.dot(d_b, wt[width:, :], precision=highest, preferred_element_type=F32)
    message = message_ref[...].astype(F32)
    mask = iota((rows, LANES), 1) >= features
    weight = jnp.sum(jnp.where(mask, message, 0.0), axis=1, keepdims=True)
    d_normed = d_normed[:, :features] * weight
    normed, scale = stats(x_ref[...].astype(F32))
    mean = jnp.mean(d_normed, axis=-1, keepdims=True)
    along = jnp.mean(d_normed * normed, axis=-1, keepdims=True)
    out_ref[...] = scale * (d_normed - mean - normed * along)
    small = small_refs[0][...].astype(F32) + small_refs[1][...].astype(F32)
    turned = small[:width].T
    factors_ref[...] = jnp.concatenate([turned[:features], turned[features:]], axis=1)
    bias_ref[...] = small[width : width + 1]


def place_kernel(in_ref, out_ref):
    for e in range(in_ref.shape[0]):
        out_ref[:, e, :] = in_ref[e].astype(F32)


def lay_back(x, rows, lanes):
    if lanes % LANES:
        return x.reshape(rows, lanes)
    return x.reshape(lanes // LANES, rows, LANES).transpose(1, 0, 2).reshape(rows, lanes)


def bit_of(axis, bit):
    return (lax.axis_index(axis) >> bit) & 1


def swap_parts(parts, axis, bit, n):
    parts = [part.reshape(-1, LANES) for part in parts]
    message = jnp.concatenate(parts, axis=0) if len(parts) > 1 else parts[0]
    pairs = [(i, i ^ (1 << bit)) for i in range(n)]
    message = lax.ppermute(message, axis, pairs)
    got, at = [], 0
    for part in parts:
        got.append(message[at : at + part.shape[0]])
        at += part.shape[0]
    return got


def halves(x, axis, bit, at):
    here = bit_of(axis, bit)
    keep = lax.dynamic_index_in_dim(x, here, at, keepdims=False)
    return keep, lax.dynamic_index_in_dim(x, 1 - here, at, keepdims=False)


def split_high(x):
    return x.reshape((2, x.shape[0] // 2) + x.shape[1:])


def in_order(mine, other, axis, bit, at):
    first = bit_of(axis, bit) == 0
    low = jnp.where(first, mine, other)
    return jnp.stack([low, jnp.where(first, other, mine)], axis=at)


def add(mine, other):
    other = other.reshape(mine.shape)
    return lax.optimization_barrier((mine.astype(F32) + other.astype(F32)).astype(BF16))


def per_device(
    n,
    alignment_embedding,
    alignment_cell_exists,
    alignment_lines_exist,
    sitewise_factors,
    pairing_matrix,
    offset_vector,
    upstream_adjoint,
):
    depth, own, features = alignment_embedding.shape
    width = sitewise_factors.shape[1] // 2
    block, pair = upstream_adjoint.shape[0], upstream_adjoint.shape[2]
    rows, chunk = depth * own, 16
    steps = block // chunk
    split = own % 16 == 0
    axes = ("row", "col")
    sds = jax.ShapeDtypeStruct

    def along_col(x, k):
        return lax.ppermute(x, "col", [(i, (i + k) % n) for i in range(n)])

    def along_row(x, k):
        return lax.ppermute(x, "row", [(i, (i + k) % n) for i in range(n)])

    def to_column(x, k):
        pairs = [(i * n + j, (j + k) % n * n + i) for i in range(n) for j in range(n)]
        return lax.ppermute(x, axes, pairs)

    r, c = lax.axis_index("row"), lax.axis_index("col")
    x = alignment_embedding.reshape(rows, features)
    mask = (alignment_cell_exists * alignment_lines_exist[:, None]).astype(BF16)
    offset = offset_vector.reshape(1, pair)
    by_token, by_row = call(
        functools.partial(prep_kernel, depth, own),
        (),
        [full(x.shape), full(mask.shape)],
        [full((rows, LANES))] * 2,
        [sds((rows, LANES), BF16)] * 2,
    )(x, mask)
    a_pieces = [by_token] + [along_col(by_token, k) for k in range(1, n)]
    b_pieces = [to_column(by_row, k) for k in range(n)]
    if not split:
        order = (c - jnp.arange(n)) % n
        held = jnp.zeros((n, rows, LANES), BF16).at[order].set(jnp.stack(a_pieces))
        a_pieces = [held.reshape(block * depth, LANES)]
        order = (r - jnp.arange(n)) % n
        held = jnp.zeros((n, depth, own, LANES), BF16)
        held = held.at[order].set(jnp.stack(b_pieces).reshape(n, depth, own, LANES))
        b_pieces = [held.transpose(1, 0, 2, 3).reshape(depth, block, LANES)]
    pieces = len(a_pieces)

    wide = width * depth
    source = jnp.arange(wide)
    perm = (jnp.arange(wide)[None, :] == (source % width * depth + source // width)[:, None]).astype(BF16)
    pairing_wide = pairing_matrix.reshape(width, width * pair)
    up_spec = pl.BlockSpec((chunk, block, pair), lambda g: (g, 0, 0))
    tokens = block * depth
    out_shapes = [
        sds((depth, block, LANES), BF16),
        sds((tokens, width), BF16),
        sds((block, wide), BF16),
        sds((wide, block), BF16),
        sds((2 * width, LANES), BF16),
        sds((steps, block, chunk), F32),
        sds((8, pair), F32),
        sds((width * width, pair), BF16),
        sds((width, features), F32),
    ]
    outs = call(
        functools.partial(weight_kernel, depth, features, n, pieces),
        (steps,),
        [full(p.shape) for p in a_pieces]
        + [full(p.shape) for p in b_pieces]
        + [up_spec]
        + [full(v.shape) for v in (sitewise_factors, perm, pairing_wide)],
        [full(o.shape) for o in out_shapes],
        out_shapes,
        [
            pltpu.VMEM((tokens, LANES), BF16),
            pltpu.VMEM((width + features, tokens), BF16),
            pltpu.VMEM((width, chunk * depth, pair), BF16),
            pltpu.VMEM((width * width, pair), F32),
            pltpu.VMEM((features, width * pair), F32),
        ],
        cost(5e9, 8e6),
    )(*a_pieces, *b_pieces, upstream_adjoint, sitewise_factors, perm, pairing_wide)
    mj, a, b, b_t, factors_t, inv, bias, d_pairing, left = outs

    bits = n.bit_length() - 1
    d_pairing = d_pairing.reshape(n, -1, LANES)
    for bit in reversed(range(1, bits)):
        keep, go = halves(split_high(d_pairing), "col", bit, 0)
        d_pairing = add(keep, *swap_parts([go], "col", bit, n))

    out_shapes = [sds((width + 16, LANES), BF16), sds((n, own * wide // LANES, LANES), BF16)]
    small, d_b = call(
        functools.partial(token_kernel, depth, features, n),
        (steps,),
        [up_spec]
        + [full(v.shape) for v in (inv, a, pairing_wide, mj, perm, bias, left)],
        [full(o.shape) for o in out_shapes],
        out_shapes,
        [pltpu.VMEM((chunk, wide, pair), BF16), pltpu.VMEM((wide, block), F32)],
        cost(8e9, 8e6),
    )(upstream_adjoint, inv, a, pairing_wide, mj, perm, bias, left)

    dp_keep, dp_go = halves(d_pairing, "col", 0, 0)
    db_keep, db_go = halves(d_b.reshape((n // 2, 2) + d_b.shape[1:]), "col", 0, 1)
    parts = swap_parts([dp_go, db_go, small], "col", 0, n)
    d_pairing, small = add(dp_keep, parts[0]), add(small, parts[2])
    d_b = in_order(db_keep, parts[1].reshape(db_keep.shape), "col", 0, 1)
    db_keep, db_go = halves(d_b, "row", 0, 1)
    for bit in range(bits):
        parts = swap_parts([d_pairing, db_go, small], "row", bit, n)
        if bit == 0:
            coupling_update, small = call(
                functools.partial(update_kernel, depth),
                (steps,),
                [full(v.shape) for v in (inv, a, b, pairing_wide, offset, small)],
                [up_spec, full(small.shape)],
                [sds((block, block, pair), BF16), sds(small.shape, BF16)],
                [pltpu.VMEM((chunk, wide, pair), BF16)],
                cost(6e9, 8e6),
            )(inv, a, b, pairing_wide, offset, small)
        if bit == 1:
            half = (tokens // LANES // 2, width, LANES)
            out_shapes = [sds(half, BF16), sds(half, BF16), sds(small.shape, BF16)]
            *d_a, small = call(
                functools.partial(left_kernel, depth, bits - 1),
                (steps,),
                [up_spec] + [full(v.shape) for v in (inv, b_t, pairing_wide, small)],
                [full(o.shape) for o in out_shapes],
                out_shapes,
                [
                    pltpu.VMEM((width, chunk * depth, pair), BF16),
                    pltpu.VMEM((tokens // LANES, width, LANES), BF16),
                ],
                cost(6e9, 8e6),
            )(upstream_adjoint, inv, b_t, pairing_wide, small)
            if rows % LANES:
                shape = (-1, width, LANES // rows, rows)
                d_a = [part.reshape(shape).transpose(0, 2, 1, 3) for part in d_a]
            da_keep, da_go = [part.reshape(n // 2, -1, LANES) for part in d_a]
        d_pairing, d_b, small = add(d_pairing, parts[0]), add(db_keep, parts[1]), add(small, parts[2])
        db_keep = db_go = d_b
    d_pairing = d_pairing.reshape(1, -1, LANES)
    small_parts = [small]
    for bit in reversed(range(1, bits)):
        if bit < bits - 1:
            small_parts = [add(*small_parts)]
            da_keep, da_go = halves(split_high(add(*da_parts)), "col", bit, 0)
        db_keep, db_go = halves(split_high(d_b), "col", bit, 0)
        parts = swap_parts([d_pairing, db_go, da_go, small_parts[0]], "col", bit, n)
        d_pairing = in_order(d_pairing, parts[0].reshape(d_pairing.shape), "col", bit, 1)
        d_pairing = d_pairing.reshape((-1,) + d_pairing.shape[2:])
        mine = bit_of("col", bit) == bit_of("row", bit)
        d_b = jnp.where(mine, db_keep, parts[1].reshape(db_keep.shape))
        da_parts = [da_keep, parts[2].reshape(da_keep.shape)]
        small_parts = [small_parts[0], parts[3]]
    da_keep, da_go = halves(add(*da_parts), "col", 0, 0)
    got, da_got = swap_parts([d_pairing, da_go], "col", 0, n)
    d_pairing = in_order(d_pairing, got.reshape(d_pairing.shape), "col", 0, 1)
    d_a = [lay_back(part.reshape(-1, LANES), width, rows) for part in (da_keep, da_got)]
    d_b = lay_back(d_b[0], own, wide)

    args = (*d_a, d_b, *small_parts, x, by_row, factors_t, perm)
    out_shapes = [sds((rows, features), F32), sds((features, 2 * width), F32), sds((1, pair), F32)]
    embedding_adjoint, factors_adjoint, offset_slope = call(
        functools.partial(owner_kernel, depth, own, features),
        (),
        [full(v.shape) for v in args],
        [full(o.shape) for o in out_shapes],
        out_shapes,
    )(*args)

    d_pairing = d_pairing.reshape(width, width, pair)
    placed = call(
        place_kernel,
        (),
        [full(d_pairing.shape)],
        full((width, width, pair)),
        sds((width, width, pair), F32),
    )(d_pairing)
    return (
        coupling_update,
        embedding_adjoint.reshape(depth, own, features),
        factors_adjoint,
        placed.reshape(width * width, pair),
        offset_slope.reshape(pair),
    )


def solution(mesh):
    n = mesh.shape["col"]
    placed = (
        P(None, ("groups", "row", "col"), None),
        P(None, ("groups", "row", "col")),
        P("groups"),
        P(),
        P(),
        P(),
        P(("groups", "row"), "col", None),
    )
    return jax.shard_map(
        functools.partial(per_device, n),
        mesh=mesh,
        in_specs=placed,
        out_specs=(
            P(("groups", "row"), "col", None),
            P(None, ("groups", "row", "col"), None),
            P("groups", None),
            P("groups", None),
            P("groups"),
        ),
        check_vma=False,
    )
```

```python
import functools

import jax
import jax.numpy as jnp
from jax import lax
from jax.experimental import pallas as pl
from jax.experimental.pallas import tpu as pltpu
from jax.sharding import PartitionSpec as P

F32 = jnp.float32
BF16 = jnp.bfloat16
LANES = 128
VMEM_LIMIT = 32 * 1024 * 1024
NT = (((1,), (1,)), ((), ()))


def dot(left, right):
    return jnp.dot(left, right, preferred_element_type=F32)


def dot_nt(left, right):
    return lax.dot_general(left, right, NT, preferred_element_type=F32)


def iota(shape, axis):
    return lax.broadcasted_iota(jnp.int32, shape, axis)


def one_hot(mask):
    return jnp.where(mask, 1.0, 0.0).astype(BF16)


def full(shape):
    return pl.BlockSpec(shape, lambda *g: (0,) * len(shape))


def cost(flops, nbytes):
    return pl.CostEstimate(flops=int(flops), bytes_accessed=int(nbytes), transcendentals=0)


def call(kernel, grid, in_specs, out_specs, out_shape, scratch=(), estimate=None):
    return pl.pallas_call(
        kernel,
        grid=grid,
        in_specs=in_specs,
        out_specs=out_specs,
        out_shape=out_shape,
        scratch_shapes=list(scratch),
        compiler_params=pltpu.CompilerParams(vmem_limit_bytes=VMEM_LIMIT),
        cost_estimate=estimate,
    )


def stats(x):
    center = x - jnp.mean(x, axis=-1, keepdims=True)
    scale = lax.rsqrt(jnp.mean(center * center, axis=-1, keepdims=True) + 1e-05)
    return center * scale, scale


def prep_kernel(depth, own, x_ref, mask_ref, by_token_ref, by_row_ref):
    rows = depth * own
    normed, _ = stats(x_ref[...].astype(F32))
    features = normed.shape[1]
    pick = one_hot(iota((rows, depth), 0) // own == iota((rows, depth), 1))
    here = iota((rows, own), 0) % own == iota((rows, own), 1)
    weight = dot(pick, mask_ref[...])
    weight = jnp.sum(jnp.where(here, weight, 0.0), axis=1, keepdims=True)
    masked = normed.astype(BF16).astype(F32) * weight
    wide = jnp.concatenate([masked, jnp.zeros((rows, LANES - features), F32)], axis=1)
    lane = iota((rows, LANES), 1)
    at = lane == features + iota((rows, LANES), 0) // own
    wide = (wide + jnp.where(at, weight, 0.0)).astype(BF16)
    by_row_ref[...] = wide
    p, q = iota((rows, rows), 0), iota((rows, rows), 1)
    swap = one_hot(q == (p % depth) * own + p // depth)
    by_token_ref[...] = dot(swap, wide).astype(BF16)


def two(ref, at):
    return jnp.concatenate([ref[at], ref[at + 1]], axis=1)


def fill_v(g_ref, bt, v_ref, depth):
    chunk, _, pair = g_ref.shape
    width = v_ref.shape[0]
    for at in range(0, chunk, 2):
        v = dot(bt, two(g_ref, at)).astype(BF16)
        for k in range(2):
            part = v[:, k * pair : (k + 1) * pair].reshape(width, depth, pair)
            v_ref[:, (at + k) * depth : (at + k + 1) * depth, :] = part


def row_kernel(depth, features, n, pieces, *refs):
    a_refs, (w_ref, wc_ref) = refs[:pieces], refs[pieces : pieces + 2]
    t_ref, at_ref, seen_ref, wt_ref, mi_ref, a_ref = refs[pieces + 2 :]
    g = pl.program_id(0)
    chunk, wide, pair = t_ref.shape
    block = seen_ref.shape[0]
    width = w_ref.shape[1] // 2

    @pl.when(g == 0)
    def _():
        if pieces == 1:
            mi_ref[...] = a_refs[0][...]
        else:
            c = lax.axis_index("col")
            size = a_refs[0].shape[0]
            for k in range(pieces):
                src = lax.rem(c - k + n, n)
                mi_ref[pl.ds(pl.multiple_of(src * size, size), size), :] = a_refs[k][...]
        pad = jnp.zeros((LANES - features, 2 * width), BF16)
        w = jnp.concatenate([w_ref[...], pad], axis=0)
        same = one_hot(iota((2 * width, 2 * width), 0) == iota((2 * width, 2 * width), 1))
        wt = dot_nt(same, w).astype(BF16)
        wt_ref[...] = wt
        mi = mi_ref[...]
        a_ref[...] = dot(mi, w[:, :width]).astype(BF16)
        same = one_hot(iota((features, LANES), 0) == iota((features, LANES), 1))
        at_ref[...] = dot_nt(jnp.concatenate([wt[:width, :], same], axis=0), mi).astype(BF16)
        rows = block * depth
        gather = one_hot(iota((block, rows), 0) == iota((block, rows), 1) // depth)
        seen_ref[...] = dot(gather, mi).astype(BF16)

    span = chunk * depth
    a_chunk = a_ref[pl.ds(pl.multiple_of(g * span, span), span), :]
    for e in range(0, width, 2):
        t = dot(a_chunk, wc_ref[:, e * pair : (e + 2) * pair]).astype(BF16)
        for k in range(2):
            part = t[:, k * pair : (k + 1) * pair].reshape(chunk, depth, pair)
            t_ref[:, (e + k) * depth : (e + k + 1) * depth, :] = part


def weight_kernel(depth, features, n, pieces, *refs):
    b_refs = refs[:pieces]
    up_ref, w_ref, perm_ref, wc_ref, at_ref, seen_ref, offset_ref = refs[pieces : pieces + 7]
    outs = refs[pieces + 7 :]
    g_ref, mj_ref, b_ref, bt_ref, inv_ref, bias_ref, dw_ref, left_ref, pass_ref = outs[:9]
    v_ref, acc_ref, wide_ref = outs[9:]
    g, last = pl.program_id(0), pl.num_programs(0) - 1
    chunk, block, pair = up_ref.shape
    width = w_ref.shape[1] // 2

    @pl.when(g == 0)
    def _():
        if pieces == 1:
            mj_ref[...] = b_refs[0][...]
        else:
            r = lax.axis_index("row")
            own = block // pieces
            for k in range(pieces):
                src = lax.rem(r - k + n, n)
                rows = pl.ds(pl.multiple_of(src * own, own), own)
                for s in range(depth):
                    mj_ref[s, rows, :] = b_refs[k][s * own : (s + 1) * own, :]
        pad = jnp.zeros((LANES - features, width), BF16)
        w = jnp.concatenate([w_ref[:, width:], pad], axis=0)
        b = jnp.zeros((block, width * depth), F32)
        seen = jnp.zeros((block, LANES), F32)
        for s in range(depth):
            mj = mj_ref[s]
            seen = seen + mj.astype(F32)
            part = dot(mj, w).astype(BF16)
            b = b + dot(part, perm_ref[s * width : (s + 1) * width, :])
        b_ref[...] = b.astype(BF16)
        bt_ref[...] = b.T.astype(BF16)
        keep = iota((block, LANES), 1) >= features
        seen = jnp.where(keep, seen, 0.0).astype(BF16)
        for k in range(block // chunk):
            count = dot_nt(seen, seen_ref[k * chunk : (k + 1) * chunk, :])
            inv_ref[k] = 1.0 / (count + 0.001)
        acc_ref[...] = jnp.zeros_like(acc_ref)
        wide_ref[...] = jnp.zeros_like(wide_ref)
        bias_ref[...] = jnp.zeros_like(bias_ref)
        pass_ref[...] = offset_ref[...]

    inv = inv_ref[g]
    bias = jnp.zeros((block, pair), F32)
    for i in range(chunk):
        up = up_ref[i].astype(F32)
        bias = bias + up
        g_ref[i] = (up * inv[:, i : i + 1]).astype(BF16)
    bias_ref[0:1, :] += jnp.sum(bias, axis=0, keepdims=True)
    fill_v(g_ref, bt_ref[...], v_ref, depth)
    span = chunk * depth
    a_t = at_ref[:, pl.ds(pl.multiple_of(g * span, span), span)]
    for e in range(0, width, 2):
        part = dot(a_t, two(v_ref, e))
        for k in range(2):
            rows = slice((e + k) * width, (e + k + 1) * width)
            acc_ref[rows, :] += part[:width, k * pair : (k + 1) * pair]
        wide_ref[:, e * pair : (e + 2) * pair] += part[width:]

    @pl.when(g == last)
    def _():
        dw_ref[...] = acc_ref[...].astype(BF16)
        left = jnp.zeros((width, features), F32)
        for e in range(0, width, 2):
            lanes = slice(e * pair, (e + 2) * pair)
            left = left + dot_nt(wc_ref[:, lanes], wide_ref[:, lanes].astype(BF16))
        left_ref[...] = left


def left_kernel(depth, bit, g_ref, bt_ref, wd_ref, small_ref, keep_ref, go_ref, pass_ref, v_ref, da_ref):
    g, last = pl.program_id(0), pl.num_programs(0) - 1
    chunk, _, pair = g_ref.shape
    width = wd_ref.shape[1]
    span = chunk * depth

    @pl.when(g == 0)
    def _():
        pass_ref[...] = small_ref[...]

    fill_v(g_ref, bt_ref[...], v_ref, depth)
    d_a = []
    each = width // 4
    for e in range(0, width, each):
        v = jnp.concatenate([v_ref[e + k] for k in range(each)], axis=1)
        d_a.append(dot(v, wd_ref[e * pair : (e + each) * pair, :]))
    d_a = (d_a[0] + d_a[1]) + (d_a[2] + d_a[3])
    same = one_hot(iota((width, width), 0) == iota((width, width), 1))
    d_a = dot_nt(same, d_a.astype(BF16)).astype(BF16)
    tiles = span // LANES
    for k in range(tiles):
        da_ref[g * tiles + k] = d_a[:, k * LANES : (k + 1) * LANES]

    @pl.when(g == last)
    def _():
        half = keep_ref.shape[0]
        here = (lax.axis_index("col") >> bit) & 1
        keep_ref[...] = da_ref[pl.ds(here * half, half)]
        go_ref[...] = da_ref[pl.ds((1 - here) * half, half)]


def token_kernel(depth, features, n, g_ref, t_ref, mj_ref, perm_ref, bias_ref, left_ref, small_ref, out_ref, db_ref):
    g, last = pl.program_id(0), pl.num_programs(0) - 1
    chunk, block = g_ref.shape[:2]
    width = left_ref.shape[0]

    @pl.when(g == 0)
    def _():
        db_ref[...] = jnp.zeros_like(db_ref)

    t = jnp.concatenate([t_ref[i] for i in range(chunk)], axis=1)
    scaled = jnp.concatenate([g_ref[i] for i in range(chunk)], axis=1)
    db_ref[...] += dot_nt(t, scaled)

    @pl.when(g == last)
    def _():
        d_b = db_ref[...].T.astype(BF16)
        own = block // n
        for k in range(n):
            part = d_b[k * own : (k + 1) * own, :]
            for q in range(part.shape[1] // LANES):
                out_ref[k, q * own : (q + 1) * own, :] = part[:, q * LANES : (q + 1) * LANES]
        turned = dot_nt(perm_ref[...], d_b).astype(BF16)
        right = jnp.zeros((width, LANES), F32)
        for s in range(depth):
            right = right + dot(turned[s * width : (s + 1) * width, :], mj_ref[s])
        small = jnp.concatenate([left_ref[...], right[:, :features]], axis=1)
        small_ref[0:width, :] = small.astype(BF16)
        small_ref[width:, :] = jnp.broadcast_to(bias_ref[0:1, :], (16, LANES)).astype(BF16)


def update_kernel(inv_ref, b_ref, t_ref, offset_ref, small_ref, out_ref, pass_ref):
    g = pl.program_id(0)

    @pl.when(g == 0)
    def _():
        pass_ref[...] = small_ref[...]

    chunk, block, pair = out_ref.shape
    inv = inv_ref[g]
    b = b_ref[...]
    offset = offset_ref[...]
    for at in range(0, chunk, 2):
        part = dot(b, two(t_ref, at))
        for k in range(2):
            value = part[:, k * pair : (k + 1) * pair] * inv[:, at + k : at + k + 1] + offset
            out_ref[at + k] = value.astype(BF16)


def owner_kernel(depth, own, features, *refs):
    da_refs, db_ref, small_refs = refs[:2], refs[2], refs[3:5]
    x_ref, message_ref, wt_ref, perm_ref, dw_ref = refs[5:10]
    out_ref, factors_ref, bias_ref, placed_ref = refs[10:]
    for e in range(dw_ref.shape[0]):
        placed_ref[:, e, :] = dw_ref[e].astype(F32)
    rows = depth * own
    width = wt_ref.shape[0] // 2
    p, q = iota((rows, rows), 0), iota((rows, rows), 1)
    swap = one_hot(q == (p % own) * depth + p // own)
    d_a = dot_nt(swap, da_refs[0][...]) + dot_nt(swap, da_refs[1][...])
    d_b = dot_nt(db_ref[...], perm_ref[...])
    d_b = jnp.concatenate([d_b[:, s * width : (s + 1) * width] for s in range(depth)], axis=0)
    highest = lax.Precision.HIGHEST
    wt = wt_ref[...].astype(F32)
    d_normed = jnp.dot(d_a, wt[:width, :], precision=highest, preferred_element_type=F32)
    d_normed = d_normed + jnp.dot(d_b, wt[width:, :], precision=highest, preferred_element_type=F32)
    message = message_ref[...].astype(F32)
    mask = iota((rows, LANES), 1) >= features
    weight = jnp.sum(jnp.where(mask, message, 0.0), axis=1, keepdims=True)
    d_normed = d_normed[:, :features] * weight
    normed, scale = stats(x_ref[...].astype(F32))
    mean = jnp.mean(d_normed, axis=-1, keepdims=True)
    along = jnp.mean(d_normed * normed, axis=-1, keepdims=True)
    out_ref[...] = scale * (d_normed - mean - normed * along)
    small = small_refs[0][...].astype(F32) + small_refs[1][...].astype(F32)
    turned = small[:width].T
    factors_ref[...] = jnp.concatenate([turned[:features], turned[features:]], axis=1)
    bias_ref[...] = small[width : width + 1]


def lay_back(x, rows, lanes):
    if lanes % LANES:
        return x.reshape(rows, lanes)
    return x.reshape(lanes // LANES, rows, LANES).transpose(1, 0, 2).reshape(rows, lanes)


def bit_of(axis, bit):
    return (lax.axis_index(axis) >> bit) & 1


def swap_parts(parts, axis, bit, n):
    parts = [part.reshape(-1, LANES) for part in parts]
    message = jnp.concatenate(parts, axis=0) if len(parts) > 1 else parts[0]
    pairs = [(i, i ^ (1 << bit)) for i in range(n)]
    message = lax.ppermute(message, axis, pairs)
    got, at = [], 0
    for part in parts:
        got.append(message[at : at + part.shape[0]])
        at += part.shape[0]
    return got


def halves(x, axis, bit, at):
    here = bit_of(axis, bit)
    keep = lax.dynamic_index_in_dim(x, here, at, keepdims=False)
    return keep, lax.dynamic_index_in_dim(x, 1 - here, at, keepdims=False)


def split_high(x):
    return x.reshape((2, x.shape[0] // 2) + x.shape[1:])


def in_order(mine, other, axis, bit, at):
    first = bit_of(axis, bit) == 0
    low = jnp.where(first, mine, other)
    return jnp.stack([low, jnp.where(first, other, mine)], axis=at)


def add(mine, other):
    other = other.reshape(mine.shape)
    return lax.optimization_barrier((mine.astype(F32) + other.astype(F32)).astype(BF16))


def per_device(
    n,
    alignment_embedding,
    alignment_cell_exists,
    alignment_lines_exist,
    sitewise_factors,
    pairing_matrix,
    offset_vector,
    upstream_adjoint,
):
    depth, own, features = alignment_embedding.shape
    width = sitewise_factors.shape[1] // 2
    block, pair = upstream_adjoint.shape[0], upstream_adjoint.shape[2]
    rows, chunk = depth * own, 16
    steps = block // chunk
    split = own % 16 == 0
    axes = ("row", "col")
    sds = jax.ShapeDtypeStruct

    def along_col(x, k):
        return lax.ppermute(x, "col", [(i, (i + k) % n) for i in range(n)])

    def along_row(x, k):
        return lax.ppermute(x, "row", [(i, (i + k) % n) for i in range(n)])

    def to_column(x, k):
        pairs = [(i * n + j, (j + k) % n * n + i) for i in range(n) for j in range(n)]
        return lax.ppermute(x, axes, pairs)

    r, c = lax.axis_index("row"), lax.axis_index("col")
    x = alignment_embedding.reshape(rows, features)
    mask = (alignment_cell_exists * alignment_lines_exist[:, None]).astype(BF16)
    offset = offset_vector.reshape(1, pair)
    by_token, by_row = call(
        functools.partial(prep_kernel, depth, own),
        (),
        [full(x.shape), full(mask.shape)],
        [full((rows, LANES))] * 2,
        [sds((rows, LANES), BF16)] * 2,
    )(x, mask)
    a_pieces = [by_token] + [along_col(by_token, k) for k in range(1, n)]
    b_pieces = [to_column(by_row, k) for k in range(n)]
    if not split:
        order = (c - jnp.arange(n)) % n
        held = jnp.zeros((n, rows, LANES), BF16).at[order].set(jnp.stack(a_pieces))
        a_pieces = [held.reshape(block * depth, LANES)]
        order = (r - jnp.arange(n)) % n
        held = jnp.zeros((n, depth, own, LANES), BF16)
        held = held.at[order].set(jnp.stack(b_pieces).reshape(n, depth, own, LANES))
        b_pieces = [held.transpose(1, 0, 2, 3).reshape(depth, block, LANES)]
    pieces = len(a_pieces)

    wide = width * depth
    tokens = block * depth
    source = jnp.arange(wide)
    perm = (jnp.arange(wide)[None, :] == (source % width * depth + source // width)[:, None]).astype(BF16)
    pairing_wide = pairing_matrix.reshape(width, width * pair)
    pairing_t = pairing_wide.T
    up_spec = pl.BlockSpec((chunk, block, pair), lambda g: (g, 0, 0))
    t_spec = pl.BlockSpec((chunk, wide, pair), lambda g: (g, 0, 0))
    out_shapes = [
        sds((width + features, tokens), BF16),
        sds((block, LANES), BF16),
        sds((2 * width, LANES), BF16),
    ]
    args = (*a_pieces, sitewise_factors, pairing_wide)
    t, a_t, seen, factors_t = call(
        functools.partial(row_kernel, depth, features, n, pieces),
        (steps,),
        [full(v.shape) for v in args],
        [t_spec] + [full(o.shape) for o in out_shapes],
        [sds((block, wide, pair), BF16)] + out_shapes,
        [pltpu.VMEM((tokens, LANES), BF16), pltpu.VMEM((tokens, width), BF16)],
        cost(3e9, 8e6),
    )(*args)

    out_shapes = [
        sds((depth, block, LANES), BF16),
        sds((block, wide), BF16),
        sds((wide, block), BF16),
        sds((steps, block, chunk), F32),
        sds((8, pair), F32),
        sds((width * width, pair), BF16),
        sds((width, features), F32),
        sds((1, pair), F32),
    ]
    args = (sitewise_factors, perm, pairing_wide, a_t, seen, offset)
    outs = call(
        functools.partial(weight_kernel, depth, features, n, pieces),
        (steps,),
        [full(p.shape) for p in b_pieces] + [up_spec] + [full(v.shape) for v in args],
        [up_spec] + [full(o.shape) for o in out_shapes],
        [sds(upstream_adjoint.shape, BF16)] + out_shapes,
        [
            pltpu.VMEM((width, chunk * depth, pair), BF16),
            pltpu.VMEM((width * width, pair), F32),
            pltpu.VMEM((features, width * pair), F32),
        ],
        cost(5e9, 8e6),
    )(*b_pieces, upstream_adjoint, *args)
    scaled, mj, b, b_t, inv, bias, d_pairing, left, offset = outs

    bits = n.bit_length() - 1
    d_pairing = d_pairing.reshape(n, -1, LANES)
    for bit in reversed(range(1, bits)):
        keep, go = halves(split_high(d_pairing), "col", bit, 0)
        d_pairing = add(keep, *swap_parts([go], "col", bit, n))

    out_shapes = [sds((width + 16, LANES), BF16), sds((n, own * wide // LANES, LANES), BF16)]
    small, d_b = call(
        functools.partial(token_kernel, depth, features, n),
        (steps,),
        [up_spec, t_spec] + [full(v.shape) for v in (mj, perm, bias, left)],
        [full(o.shape) for o in out_shapes],
        out_shapes,
        [pltpu.VMEM((wide, block), F32)],
        cost(6e9, 16e6),
    )(scaled, t, mj, perm, bias, left)

    dp_keep, dp_go = halves(d_pairing, "col", 0, 0)
    db_keep, db_go = halves(d_b.reshape((n // 2, 2) + d_b.shape[1:]), "col", 0, 1)
    parts = swap_parts([dp_go, db_go, small], "col", 0, n)
    d_pairing, small = add(dp_keep, parts[0]), add(small, parts[2])
    d_b = in_order(db_keep, parts[1].reshape(db_keep.shape), "col", 0, 1)
    db_keep, db_go = halves(d_b, "row", 0, 1)
    for bit in range(bits):
        parts = swap_parts([d_pairing, db_go, small], "row", bit, n)
        if bit == 0:
            args = (inv, b, t, offset, small)
            specs = [full(v.shape) for v in args]
            specs[2] = t_spec
            coupling_update, small = call(
                update_kernel,
                (steps,),
                specs,
                [up_spec, full(small.shape)],
                [sds((block, block, pair), BF16), sds(small.shape, BF16)],
                (),
                cost(6e9, 8e6),
            )(*args)
        if bit == 1:
            half = (tokens // LANES // 2, width, LANES)
            out_shapes = [sds(half, BF16), sds(half, BF16), sds(small.shape, BF16)]
            *d_a, small = call(
                functools.partial(left_kernel, depth, bits - 1),
                (steps,),
                [up_spec] + [full(v.shape) for v in (b_t, pairing_t, small)],
                [full(o.shape) for o in out_shapes],
                out_shapes,
                [
                    pltpu.VMEM((width, chunk * depth, pair), BF16),
                    pltpu.VMEM((tokens // LANES, width, LANES), BF16),
                ],
                cost(6e9, 8e6),
            )(scaled, b_t, pairing_t, small)
            if rows % LANES:
                shape = (-1, width, LANES // rows, rows)
                d_a = [part.reshape(shape).transpose(0, 2, 1, 3) for part in d_a]
            da_keep, da_go = [part.reshape(n // 2, -1, LANES) for part in d_a]
        d_pairing, d_b, small = add(d_pairing, parts[0]), add(db_keep, parts[1]), add(small, parts[2])
        db_keep = db_go = d_b
    d_pairing = d_pairing.reshape(1, -1, LANES)
    small_parts = [small]
    for bit in reversed(range(1, bits)):
        if bit < bits - 1:
            small_parts = [add(*small_parts)]
            da_keep, da_go = halves(split_high(add(*da_parts)), "col", bit, 0)
        db_keep, db_go = halves(split_high(d_b), "col", bit, 0)
        parts = swap_parts([d_pairing, db_go, da_go, small_parts[0]], "col", bit, n)
        d_pairing = in_order(d_pairing, parts[0].reshape(d_pairing.shape), "col", bit, 1)
        d_pairing = d_pairing.reshape((-1,) + d_pairing.shape[2:])
        mine = bit_of("col", bit) == bit_of("row", bit)
        d_b = jnp.where(mine, db_keep, parts[1].reshape(db_keep.shape))
        da_parts = [da_keep, parts[2].reshape(da_keep.shape)]
        small_parts = [small_parts[0], parts[3]]
    da_keep, da_go = halves(add(*da_parts), "col", 0, 0)
    got, da_got = swap_parts([d_pairing, da_go], "col", 0, n)
    d_pairing = in_order(d_pairing, got.reshape(d_pairing.shape), "col", 0, 1)
    d_a = [lay_back(part.reshape(-1, LANES), width, rows) for part in (da_keep, da_got)]
    d_b = lay_back(d_b[0], own, wide)

    d_pairing = d_pairing.reshape(width, width, pair)
    args = (*d_a, d_b, *small_parts, x, by_row, factors_t, perm, d_pairing)
    out_shapes = [
        sds((rows, features), F32),
        sds((features, 2 * width), F32),
        sds((1, pair), F32),
        sds((width, width, pair), F32),
    ]
    embedding_adjoint, factors_adjoint, offset_slope, placed = call(
        functools.partial(owner_kernel, depth, own, features),
        (),
        [full(v.shape) for v in args],
        [full(o.shape) for o in out_shapes],
        out_shapes,
    )(*args)
    return (
        coupling_update,
        embedding_adjoint.reshape(depth, own, features),
        factors_adjoint,
        placed.reshape(width * width, pair),
        offset_slope.reshape(pair),
    )


def solution(mesh):
    n = mesh.shape["col"]
    placed = (
        P(None, ("groups", "row", "col"), None),
        P(None, ("groups", "row", "col")),
        P("groups"),
        P(),
        P(),
        P(),
        P(("groups", "row"), "col", None),
    )
    return jax.shard_map(
        functools.partial(per_device, n),
        mesh=mesh,
        in_specs=placed,
        out_specs=(
            P(("groups", "row"), "col", None),
            P(None, ("groups", "row", "col"), None),
            P("groups", None),
            P("groups", None),
            P("groups"),
        ),
        check_vma=False,
    )
```

```python
import functools

import jax
import jax.numpy as jnp
from jax import lax
from jax.experimental import pallas as pl
from jax.experimental.pallas import tpu as pltpu
from jax.sharding import PartitionSpec as P

F32 = jnp.float32
BF16 = jnp.bfloat16
LANES = 128
VMEM_LIMIT = 16 * 1024 * 1024
NT = (((1,), (1,)), ((), ()))


def dot(left, right):
    return jnp.dot(left, right, preferred_element_type=F32)


def dot_nt(left, right):
    return lax.dot_general(left, right, NT, preferred_element_type=F32)


def iota(shape, axis):
    return lax.broadcasted_iota(jnp.int32, shape, axis)


def one_hot(mask):
    return jnp.where(mask, 1.0, 0.0).astype(BF16)


def full(shape):
    return pl.BlockSpec(shape, lambda *g: (0,) * len(shape))


def cost(flops, nbytes):
    return pl.CostEstimate(flops=int(flops), bytes_accessed=int(nbytes), transcendentals=0)


def call(kernel, grid, in_specs, out_specs, out_shape, scratch=(), estimate=None):
    return pl.pallas_call(
        kernel,
        grid=grid,
        in_specs=in_specs,
        out_specs=out_specs,
        out_shape=out_shape,
        scratch_shapes=list(scratch),
        compiler_params=pltpu.CompilerParams(vmem_limit_bytes=VMEM_LIMIT),
        cost_estimate=estimate,
    )


def stats(x):
    center = x - jnp.mean(x, axis=-1, keepdims=True)
    scale = lax.rsqrt(jnp.mean(center * center, axis=-1, keepdims=True) + 1e-05)
    return center * scale, scale


def prep_kernel(depth, own, x_ref, mask_ref, by_token_ref, by_row_ref, mask_out_ref):
    rows = depth * own
    normed, _ = stats(x_ref[...].astype(F32))
    pick = one_hot(iota((rows, depth), 0) // own == iota((rows, depth), 1))
    here = iota((rows, own), 0) % own == iota((rows, own), 1)
    mask = mask_ref[...]
    weight = jnp.sum(jnp.where(here, dot(pick, mask), 0.0), axis=1, keepdims=True)
    masked = normed.astype(BF16).astype(F32) * weight
    half = rows // 2
    by_row_ref[...] = jnp.concatenate([masked[:half], masked[half:]], axis=1).astype(BF16)
    p, q = iota((rows, rows), 0), iota((rows, rows), 1)
    swap = one_hot(q == (p % depth) * own + p // depth)
    turned = dot(swap, masked.astype(BF16))
    by_token_ref[...] = jnp.concatenate([turned[:half], turned[half:]], axis=1).astype(BF16)
    pad = jnp.zeros((LANES - depth, own), BF16)
    same = one_hot(iota((own, own), 0) == iota((own, own), 1))
    mask_out_ref[...] = dot_nt(same, jnp.concatenate([mask, pad], axis=0)).astype(BF16)


def two(ref, at):
    return jnp.concatenate([ref[at], ref[at + 1]], axis=1)


def fill_v(g_ref, bt, v_ref, depth):
    chunk, _, pair = g_ref.shape
    width = v_ref.shape[0]
    for at in range(0, chunk, 2):
        v = dot(bt, two(g_ref, at)).astype(BF16)
        for k in range(2):
            part = v[:, k * pair : (k + 1) * pair].reshape(width, depth, pair)
            v_ref[:, (at + k) * depth : (at + k + 1) * depth, :] = part


def row_kernel(depth, features, mi_ref, w_ref, wide_ref, t_ref, at_ref, wt_ref, wc_ref, a_ref, rows_ref):
    g = pl.program_id(0)
    chunk, wide, pair = t_ref.shape
    width = w_ref.shape[1] // 2

    @pl.when(g == 0)
    def _():
        rows_ref[...] = wide_ref[...].astype(F32)
        for e in range(width):
            part = rows_ref[pl.ds(e, width, stride=width), :]
            wc_ref[:, e * pair : (e + 1) * pair] = part.astype(BF16)
        w = w_ref[...]
        same = one_hot(iota((2 * width, 2 * width), 0) == iota((2 * width, 2 * width), 1))
        wt = dot_nt(same, w).astype(BF16)
        wt_ref[...] = wt
        mi = mi_ref[...]
        a_ref[...] = dot(mi, w[:, :width]).astype(BF16)
        same = one_hot(iota((features, features), 0) == iota((features, features), 1))
        at_ref[...] = dot_nt(jnp.concatenate([wt[:width, :], same], axis=0), mi).astype(BF16)

    span = chunk * depth
    a_chunk = a_ref[pl.ds(pl.multiple_of(g * span, span), span), :]
    for e in range(0, width, 2):
        t = dot(a_chunk, wc_ref[:, e * pair : (e + 2) * pair]).astype(BF16)
        for k in range(2):
            part = t[:, k * pair : (k + 1) * pair].reshape(chunk, depth, pair)
            t_ref[:, (e + k) * depth : (e + k + 1) * depth, :] = part


def weight_kernel(depth, features, *refs):
    up_ref, mj_ref, seen_j_ref, seen_i_ref, w_ref, perm_ref, wc_ref, at_ref, offset_ref = refs[:9]
    g_ref, b_ref, bt_ref, inv_ref, bias_ref, dw_ref, left_ref, pass_ref = refs[9:17]
    v_ref, acc_ref, wide_ref = refs[17:]
    g, last = pl.program_id(0), pl.num_programs(0) - 1
    chunk, block, pair = up_ref.shape
    width = w_ref.shape[1] // 2

    @pl.when(g == 0)
    def _():
        w = w_ref[:, width:]
        b = jnp.zeros((block, width * depth), F32)
        for s in range(depth):
            part = dot(mj_ref[s], w).astype(BF16)
            b = b + dot(part, perm_ref[s * width : (s + 1) * width, :])
        b_ref[...] = b.astype(BF16)
        bt_ref[...] = b.T.astype(BF16)
        for k in range(block // chunk):
            count = dot_nt(seen_j_ref[...], seen_i_ref[k * chunk : (k + 1) * chunk, :])
            inv_ref[k] = 1.0 / (count + 0.001)
        acc_ref[...] = jnp.zeros_like(acc_ref)
        wide_ref[...] = jnp.zeros_like(wide_ref)
        bias_ref[...] = jnp.zeros_like(bias_ref)
        pass_ref[...] = offset_ref[...]

    inv = inv_ref[g]
    bias = jnp.zeros((block, pair), F32)
    for i in range(chunk):
        up = up_ref[i].astype(F32)
        bias = bias + up
        g_ref[i] = (up * inv[:, i : i + 1]).astype(BF16)
    bias_ref[0:1, :] += jnp.sum(bias, axis=0, keepdims=True)
    fill_v(g_ref, bt_ref[...], v_ref, depth)
    span = chunk * depth
    a_t = at_ref[:, pl.ds(pl.multiple_of(g * span, span), span)]
    for e in range(0, width, 2):
        part = dot(a_t, two(v_ref, e))
        for k in range(2):
            rows = slice((e + k) * width, (e + k + 1) * width)
            acc_ref[rows, :] += part[:width, k * pair : (k + 1) * pair]
        wide_ref[:, e * pair : (e + 2) * pair] += part[width:]

    @pl.when(g == last)
    def _():
        dw_ref[...] = acc_ref[...].astype(BF16)
        left = jnp.zeros((width, features), F32)
        for e in range(0, width, 2):
            lanes = slice(e * pair, (e + 2) * pair)
            left = left + dot_nt(wc_ref[:, lanes], wide_ref[:, lanes].astype(BF16))
        left_ref[...] = left


def left_kernel(depth, bit, g_ref, bt_ref, wd_ref, small_ref, keep_ref, go_ref, pass_ref, v_ref, da_ref):
    g, last = pl.program_id(0), pl.num_programs(0) - 1
    chunk, _, pair = g_ref.shape
    width = wd_ref.shape[1]
    span = chunk * depth

    @pl.when(g == 0)
    def _():
        pass_ref[...] = small_ref[...]

    fill_v(g_ref, bt_ref[...], v_ref, depth)
    d_a = []
    each = width // 4
    for e in range(0, width, each):
        v = jnp.concatenate([v_ref[e + k] for k in range(each)], axis=1)
        d_a.append(dot(v, wd_ref[e * pair : (e + each) * pair, :]))
    d_a = (d_a[0] + d_a[1]) + (d_a[2] + d_a[3])
    same = one_hot(iota((width, width), 0) == iota((width, width), 1))
    d_a = dot_nt(same, d_a.astype(BF16)).astype(BF16)
    tiles = span // LANES
    for k in range(tiles):
        da_ref[g * tiles + k] = d_a[:, k * LANES : (k + 1) * LANES]

    @pl.when(g == last)
    def _():
        half = keep_ref.shape[0]
        here = (lax.axis_index("col") >> bit) & 1
        keep_ref[...] = da_ref[pl.ds(here * half, half)]
        go_ref[...] = da_ref[pl.ds((1 - here) * half, half)]


def token_kernel(depth, features, n, g_ref, t_ref, mj_ref, perm_ref, bias_ref, left_ref, small_ref, out_ref, db_ref):
    g, last = pl.program_id(0), pl.num_programs(0) - 1
    chunk, block = g_ref.shape[:2]
    width = left_ref.shape[0]

    @pl.when(g == 0)
    def _():
        db_ref[...] = jnp.zeros_like(db_ref)

    t = jnp.concatenate([t_ref[i] for i in range(chunk)], axis=1)
    scaled = jnp.concatenate([g_ref[i] for i in range(chunk)], axis=1)
    db_ref[...] += dot_nt(t, scaled)

    @pl.when(g == last)
    def _():
        d_b = db_ref[...].T.astype(BF16)
        own = block // n
        for k in range(n):
            part = d_b[k * own : (k + 1) * own, :]
            for q in range(part.shape[1] // LANES):
                out_ref[k, q * own : (q + 1) * own, :] = part[:, q * LANES : (q + 1) * LANES]
        turned = dot_nt(perm_ref[...], d_b).astype(BF16)
        right = jnp.zeros((width, features), F32)
        for s in range(depth):
            right = right + dot(turned[s * width : (s + 1) * width, :], mj_ref[s])
        small = jnp.concatenate([left_ref[...], right], axis=1)
        small_ref[0:width, :] = small.astype(BF16)
        small_ref[width:, :] = jnp.broadcast_to(bias_ref[0:1, :], (16, LANES)).astype(BF16)


def update_kernel(inv_ref, b_ref, t_ref, offset_ref, wc_ref, small_ref, out_ref, wd_ref, pass_ref):
    g = pl.program_id(0)
    chunk, block, pair = out_ref.shape

    @pl.when(g == 0)
    def _():
        pass_ref[...] = small_ref[...]
        same = one_hot(iota((2 * pair, 2 * pair), 0) == iota((2 * pair, 2 * pair), 1))
        for at in range(0, wd_ref.shape[0], 2 * pair):
            wd_ref[at : at + 2 * pair, :] = dot_nt(same, wc_ref[:, at : at + 2 * pair]).astype(BF16)

    inv = inv_ref[g]
    b = b_ref[...]
    offset = offset_ref[...]
    for at in range(0, chunk, 2):
        part = dot(b, two(t_ref, at))
        for k in range(2):
            value = part[:, k * pair : (k + 1) * pair] * inv[:, at + k : at + k + 1] + offset
            out_ref[at + k] = value.astype(BF16)


def owner_kernel(depth, own, features, *refs):
    da_refs, db_ref, small_refs = refs[:2], refs[2], refs[3:5]
    x_ref, mask_ref, wt_ref, perm_ref, dw_ref = refs[5:10]
    out_ref, factors_ref, bias_ref, placed_ref = refs[10:]
    for e in range(dw_ref.shape[0]):
        placed_ref[:, e, :] = dw_ref[e].astype(F32)
    rows = depth * own
    width = wt_ref.shape[0] // 2
    p, q = iota((rows, rows), 0), iota((rows, rows), 1)
    swap = one_hot(q == (p % own) * depth + p // own)
    d_a = dot_nt(swap, da_refs[0][...]) + dot_nt(swap, da_refs[1][...])
    d_b = dot_nt(db_ref[...], perm_ref[...])
    d_b = jnp.concatenate([d_b[:, s * width : (s + 1) * width] for s in range(depth)], axis=0)
    highest = lax.Precision.HIGHEST
    wt = wt_ref[...].astype(F32)
    d_normed = jnp.dot(d_a, wt[:width, :], precision=highest, preferred_element_type=F32)
    d_normed = d_normed + jnp.dot(d_b, wt[width:, :], precision=highest, preferred_element_type=F32)
    pick = one_hot(iota((rows, depth), 0) // own == iota((rows, depth), 1))
    here = iota((rows, own), 0) % own == iota((rows, own), 1)
    weight = jnp.sum(jnp.where(here, dot(pick, mask_ref[...]), 0.0), axis=1, keepdims=True)
    d_normed = d_normed * weight
    normed, scale = stats(x_ref[...].astype(F32))
    mean = jnp.mean(d_normed, axis=-1, keepdims=True)
    along = jnp.mean(d_normed * normed, axis=-1, keepdims=True)
    out_ref[...] = scale * (d_normed - mean - normed * along)
    small = small_refs[0][...].astype(F32) + small_refs[1][...].astype(F32)
    turned = small[:width].T
    factors_ref[...] = jnp.concatenate([turned[:features], turned[features:]], axis=1)
    bias_ref[...] = small[width : width + 1]


def lay_back(x, rows, lanes):
    if lanes % LANES:
        return x.reshape(rows, lanes)
    return x.reshape(lanes // LANES, rows, LANES).transpose(1, 0, 2).reshape(rows, lanes)


def bit_of(axis, bit):
    return (lax.axis_index(axis) >> bit) & 1


def swap_parts(parts, axis, bit, n):
    parts = [part.reshape(-1, LANES) for part in parts]
    message = jnp.concatenate(parts, axis=0) if len(parts) > 1 else parts[0]
    pairs = [(i, i ^ (1 << bit)) for i in range(n)]
    message = lax.ppermute(message, axis, pairs)
    got, at = [], 0
    for part in parts:
        got.append(message[at : at + part.shape[0]])
        at += part.shape[0]
    return got


def halves(x, axis, bit, at):
    here = bit_of(axis, bit)
    keep = lax.dynamic_index_in_dim(x, here, at, keepdims=False)
    return keep, lax.dynamic_index_in_dim(x, 1 - here, at, keepdims=False)


def split_high(x):
    return x.reshape((2, x.shape[0] // 2) + x.shape[1:])


def in_order(mine, other, axis, bit, at):
    first = bit_of(axis, bit) == 0
    low = jnp.where(first, mine, other)
    return jnp.stack([low, jnp.where(first, other, mine)], axis=at)


def add(mine, other):
    other = other.reshape(mine.shape)
    return lax.optimization_barrier((mine.astype(F32) + other.astype(F32)).astype(BF16))


def per_device(
    n,
    alignment_embedding,
    alignment_cell_exists,
    alignment_lines_exist,
    sitewise_factors,
    pairing_matrix,
    offset_vector,
    upstream_adjoint,
):
    depth, own, features = alignment_embedding.shape
    width = sitewise_factors.shape[1] // 2
    block, pair = upstream_adjoint.shape[0], upstream_adjoint.shape[2]
    rows, chunk = depth * own, 16
    steps = block // chunk
    split = own % 16 == 0
    axes = ("row", "col")
    sds = jax.ShapeDtypeStruct

    bits = n.bit_length() - 1
    x = alignment_embedding.reshape(rows, features)
    mask = (alignment_cell_exists * alignment_lines_exist[:, None]).astype(BF16)
    offset = offset_vector.reshape(1, pair)
    out_shapes = [sds((rows // 2, LANES), BF16)] * 2 + [sds((own, LANES), BF16)]
    by_token, by_row, mask_t = call(
        functools.partial(prep_kernel, depth, own),
        (),
        [full(x.shape), full(mask.shape)],
        [full(o.shape) for o in out_shapes],
        out_shapes,
    )(x, mask)
    held = jnp.concatenate([by_row, mask_t], axis=0)[None]
    for bit in reversed(range(bits)):
        (got,) = swap_parts([held], "row", bit, n)
        held = in_order(held, got.reshape(held.shape), "row", bit, 1)
        held = held.reshape((-1,) + held.shape[2:])
    held = held[:, None]
    for bit in reversed(range(bits)):
        keep, go = halves(split_high(held), "col", bit, 0)
        (got,) = swap_parts([go], "col", bit, n)
        held = in_order(keep, got.reshape(keep.shape), "col", bit, 2)
        held = held.reshape((keep.shape[0], -1) + keep.shape[2:])
    seen_j = held[0, :, rows // 2 :].reshape(block, LANES)
    parts = held[0, :, : rows // 2].reshape(n, depth // 2, own, 2, features)
    mj = parts.transpose(3, 1, 0, 2, 4).reshape(depth, block, features)
    held = jnp.concatenate([by_token, mask_t], axis=0)[None]
    for bit in reversed(range(bits)):
        (got,) = swap_parts([held], "col", bit, n)
        held = in_order(held, got.reshape(held.shape), "col", bit, 1)
        held = held.reshape((-1,) + held.shape[2:])
    seen_i = held[:, rows // 2 :].reshape(block, LANES)
    parts = held[:, : rows // 2].reshape(n, rows // 2, 2, features)
    mi = parts.transpose(0, 2, 1, 3).reshape(block * depth, features)

    wide = width * depth
    tokens = block * depth
    source = jnp.arange(wide)
    perm = (jnp.arange(wide)[None, :] == (source % width * depth + source // width)[:, None]).astype(BF16)
    up_spec = pl.BlockSpec((chunk, block, pair), lambda g: (g, 0, 0))
    t_spec = pl.BlockSpec((chunk, wide, pair), lambda g: (g, 0, 0))
    out_shapes = [
        sds((width + features, tokens), BF16),
        sds((2 * width, features), BF16),
        sds((width, width * pair), BF16),
    ]
    args = (mi, sitewise_factors, pairing_matrix)
    t, a_t, factors_t, pairing_wide = call(
        functools.partial(row_kernel, depth, features),
        (steps,),
        [full(v.shape) for v in args],
        [t_spec] + [full(o.shape) for o in out_shapes],
        [sds((block, wide, pair), BF16)] + out_shapes,
        [pltpu.VMEM((tokens, width), BF16), pltpu.VMEM((width * width, pair), F32)],
        cost(4e9, 8e6),
    )(*args)

    out_shapes = [
        sds((block, wide), BF16),
        sds((wide, block), BF16),
        sds((steps, block, chunk), F32),
        sds((8, pair), F32),
        sds((width * width, pair), BF16),
        sds((width, features), F32),
        sds((1, pair), F32),
    ]
    args = (mj, seen_j, seen_i, sitewise_factors, perm, pairing_wide, a_t, offset)
    outs = call(
        functools.partial(weight_kernel, depth, features),
        (steps,),
        [up_spec] + [full(v.shape) for v in args],
        [up_spec] + [full(o.shape) for o in out_shapes],
        [sds(upstream_adjoint.shape, BF16)] + out_shapes,
        [
            pltpu.VMEM((width, chunk * depth, pair), BF16),
            pltpu.VMEM((width * width, pair), F32),
            pltpu.VMEM((features, width * pair), F32),
        ],
        cost(5e9, 8e6),
    )(upstream_adjoint, *args)
    scaled, b, b_t, inv, bias, d_pairing, left, offset = outs

    d_pairing = d_pairing.reshape(n, -1, LANES)
    for bit in reversed(range(1, bits)):
        keep, go = halves(split_high(d_pairing), "col", bit, 0)
        d_pairing = add(keep, *swap_parts([go], "col", bit, n))

    out_shapes = [sds((width + 16, LANES), BF16), sds((n, own * wide // LANES, LANES), BF16)]
    small, d_b = call(
        functools.partial(token_kernel, depth, features, n),
        (steps,),
        [up_spec, t_spec] + [full(v.shape) for v in (mj, perm, bias, left)],
        [full(o.shape) for o in out_shapes],
        out_shapes,
        [pltpu.VMEM((wide, block), F32)],
        cost(6e9, 16e6),
    )(scaled, t, mj, perm, bias, left)

    dp_keep, dp_go = halves(d_pairing, "col", 0, 0)
    db_keep, db_go = halves(d_b.reshape((n // 2, 2) + d_b.shape[1:]), "col", 0, 1)
    parts = swap_parts([dp_go, db_go, small], "col", 0, n)
    d_pairing, small = add(dp_keep, parts[0]), add(small, parts[2])
    d_b = in_order(db_keep, parts[1].reshape(db_keep.shape), "col", 0, 1)
    db_keep, db_go = halves(d_b, "row", 0, 1)
    for bit in range(bits):
        parts = swap_parts([d_pairing, db_go, small], "row", bit, n)
        if bit == 0:
            args = (inv, b, t, offset, pairing_wide, small)
            specs = [full(v.shape) for v in args]
            specs[2] = t_spec
            coupling_update, pairing_t, small = call(
                update_kernel,
                (steps,),
                specs,
                [up_spec, full((width * pair, width)), full(small.shape)],
                [
                    sds((block, block, pair), BF16),
                    sds((width * pair, width), BF16),
                    sds(small.shape, BF16),
                ],
                (),
                cost(6e9, 8e6),
            )(*args)
        if bit == 1:
            half = (tokens // LANES // 2, width, LANES)
            out_shapes = [sds(half, BF16), sds(half, BF16), sds(small.shape, BF16)]
            *d_a, small = call(
                functools.partial(left_kernel, depth, bits - 1),
                (steps,),
                [up_spec] + [full(v.shape) for v in (b_t, pairing_t, small)],
                [full(o.shape) for o in out_shapes],
                out_shapes,
                [
                    pltpu.VMEM((width, chunk * depth, pair), BF16),
                    pltpu.VMEM((tokens // LANES, width, LANES), BF16),
                ],
                cost(6e9, 8e6),
            )(scaled, b_t, pairing_t, small)
            if rows % LANES:
                shape = (-1, width, LANES // rows, rows)
                d_a = [part.reshape(shape).transpose(0, 2, 1, 3) for part in d_a]
            da_keep, da_go = [part.reshape(n // 2, -1, LANES) for part in d_a]
        d_pairing, d_b, small = add(d_pairing, parts[0]), add(db_keep, parts[1]), add(small, parts[2])
        db_keep = db_go = d_b
    d_pairing = d_pairing.reshape(1, -1, LANES)
    small_parts = [small]
    for bit in reversed(range(1, bits)):
        if bit < bits - 1:
            small_parts = [add(*small_parts)]
            da_keep, da_go = halves(split_high(add(*da_parts)), "col", bit, 0)
        db_keep, db_go = halves(split_high(d_b), "col", bit, 0)
        parts = swap_parts([d_pairing, db_go, da_go, small_parts[0]], "col", bit, n)
        d_pairing = in_order(d_pairing, parts[0].reshape(d_pairing.shape), "col", bit, 1)
        d_pairing = d_pairing.reshape((-1,) + d_pairing.shape[2:])
        mine = bit_of("col", bit) == bit_of("row", bit)
        d_b = jnp.where(mine, db_keep, parts[1].reshape(db_keep.shape))
        da_parts = [da_keep, parts[2].reshape(da_keep.shape)]
        small_parts = [small_parts[0], parts[3]]
    da_keep, da_go = halves(add(*da_parts), "col", 0, 0)
    got, da_got = swap_parts([d_pairing, da_go], "col", 0, n)
    d_pairing = in_order(d_pairing, got.reshape(d_pairing.shape), "col", 0, 1)
    d_a = [lay_back(part.reshape(-1, LANES), width, rows) for part in (da_keep, da_got)]
    d_b = lay_back(d_b[0], own, wide)

    d_pairing = d_pairing.reshape(width, width, pair)
    args = (*d_a, d_b, *small_parts, x, mask, factors_t, perm, d_pairing)
    out_shapes = [
        sds((rows, features), F32),
        sds((features, 2 * width), F32),
        sds((1, pair), F32),
        sds((width, width, pair), F32),
    ]
    embedding_adjoint, factors_adjoint, offset_slope, placed = call(
        functools.partial(owner_kernel, depth, own, features),
        (),
        [full(v.shape) for v in args],
        [full(o.shape) for o in out_shapes],
        out_shapes,
    )(*args)
    return (
        coupling_update,
        embedding_adjoint.reshape(depth, own, features),
        factors_adjoint,
        placed.reshape(width * width, pair),
        offset_slope.reshape(pair),
    )


def solution(mesh):
    n = mesh.shape["col"]
    placed = (
        P(None, ("groups", "row", "col"), None),
        P(None, ("groups", "row", "col")),
        P("groups"),
        P(),
        P(),
        P(),
        P(("groups", "row"), "col", None),
    )
    return jax.shard_map(
        functools.partial(per_device, n),
        mesh=mesh,
        in_specs=placed,
        out_specs=(
            P(("groups", "row"), "col", None),
            P(None, ("groups", "row", "col"), None),
            P("groups", None),
            P("groups", None),
            P("groups"),
        ),
        check_vma=False,
    )
```

```python
import functools

import jax
import jax.numpy as jnp
from jax import lax
from jax.experimental import pallas as pl
from jax.experimental.pallas import tpu as pltpu
from jax.sharding import PartitionSpec as P

F32 = jnp.float32
BF16 = jnp.bfloat16
LANES = 128
VMEM_LIMIT = 57 * 1024 * 1024
NT = (((1,), (1,)), ((), ()))


def dot(left, right):
    return jnp.dot(left, right, preferred_element_type=F32)


def dot_nt(left, right):
    return lax.dot_general(left, right, NT, preferred_element_type=F32)


def iota(shape, axis):
    return lax.broadcasted_iota(jnp.int32, shape, axis)


def one_hot(mask):
    return jnp.where(mask, 1.0, 0.0).astype(BF16)


def full(shape):
    return pl.BlockSpec(shape, lambda *g: (0,) * len(shape))


def cost(flops, nbytes):
    return pl.CostEstimate(flops=int(flops), bytes_accessed=int(nbytes), transcendentals=0)


def call(kernel, grid, in_specs, out_specs, out_shape, scratch=(), estimate=None):
    return pl.pallas_call(
        kernel,
        grid=grid,
        in_specs=in_specs,
        out_specs=out_specs,
        out_shape=out_shape,
        scratch_shapes=list(scratch),
        compiler_params=pltpu.CompilerParams(vmem_limit_bytes=VMEM_LIMIT),
        cost_estimate=estimate,
    )


def stats(x):
    center = x - jnp.mean(x, axis=-1, keepdims=True)
    scale = lax.rsqrt(jnp.mean(center * center, axis=-1, keepdims=True) + 1e-05)
    return center * scale, scale


def prep_kernel(depth, own, x_ref, cell_ref, line_ref, by_token_ref, by_row_ref, mask_out_ref, mask_ref):
    rows = depth * own
    same = iota((depth, depth), 0) == iota((depth, depth), 1)
    line = jnp.sum(jnp.where(same, line_ref[...].astype(F32), 0.0), axis=1, keepdims=True)
    mask_ref[...] = (cell_ref[...].astype(F32) * line).astype(BF16)
    normed, _ = stats(x_ref[...].astype(F32))
    pick = one_hot(iota((rows, depth), 0) // own == iota((rows, depth), 1))
    here = iota((rows, own), 0) % own == iota((rows, own), 1)
    mask = mask_ref[...]
    weight = jnp.sum(jnp.where(here, dot(pick, mask), 0.0), axis=1, keepdims=True)
    masked = normed.astype(BF16).astype(F32) * weight
    half = rows // 2
    by_row_ref[...] = jnp.concatenate([masked[:half], masked[half:]], axis=1).astype(BF16)
    p, q = iota((rows, rows), 0), iota((rows, rows), 1)
    swap = one_hot(q == (p % depth) * own + p // depth)
    turned = dot(swap, masked.astype(BF16))
    by_token_ref[...] = jnp.concatenate([turned[:half], turned[half:]], axis=1).astype(BF16)
    pad = jnp.zeros((LANES - depth, own), BF16)
    same = one_hot(iota((own, own), 0) == iota((own, own), 1))
    mask_out_ref[...] = dot_nt(same, jnp.concatenate([mask, pad], axis=0)).astype(BF16)


def two(ref, at):
    return jnp.concatenate([ref[at], ref[at + 1]], axis=1)


def fill_v(g_ref, bt, v_ref, depth):
    chunk, _, pair = g_ref.shape
    width = v_ref.shape[0]
    for at in range(0, chunk, 2):
        v = dot(bt, two(g_ref, at)).astype(BF16)
        for k in range(2):
            part = v[:, k * pair : (k + 1) * pair].reshape(width, depth, pair)
            v_ref[:, (at + k) * depth : (at + k + 1) * depth, :] = part


def row_kernel(depth, features, mi_ref, w_ref, wide_ref, t_ref, at_ref, wt_ref, wc_ref, a_ref, rows_ref):
    g = pl.program_id(0)
    chunk, wide, pair = t_ref.shape
    width = w_ref.shape[1] // 2

    @pl.when(g == 0)
    def _():
        rows_ref[...] = wide_ref[...].astype(F32)
        for e in range(width):
            part = rows_ref[pl.ds(e, width, stride=width), :]
            wc_ref[:, e * pair : (e + 1) * pair] = part.astype(BF16)
        w = w_ref[...]
        same = one_hot(iota((2 * width, 2 * width), 0) == iota((2 * width, 2 * width), 1))
        wt = dot_nt(same, w).astype(BF16)
        wt_ref[...] = wt
        mi = mi_ref[...]
        a_ref[...] = dot(mi, w[:, :width]).astype(BF16)
        same = one_hot(iota((features, features), 0) == iota((features, features), 1))
        at_ref[...] = dot_nt(jnp.concatenate([wt[:width, :], same], axis=0), mi).astype(BF16)

    span = chunk * depth
    a_chunk = a_ref[pl.ds(pl.multiple_of(g * span, span), span), :]
    for e in range(0, width, 2):
        t = dot(a_chunk, wc_ref[:, e * pair : (e + 2) * pair]).astype(BF16)
        for k in range(2):
            part = t[:, k * pair : (k + 1) * pair].reshape(chunk, depth, pair)
            t_ref[:, (e + k) * depth : (e + k + 1) * depth, :] = part


def weight_kernel(depth, features, *refs):
    up_ref, mj_ref, seen_j_ref, seen_i_ref, w_ref, perm_ref, wc_ref, at_ref, offset_ref = refs[:9]
    g_ref, b_ref, bt_ref, inv_ref, bias_ref, dw_ref, left_ref, pass_ref = refs[9:17]
    v_ref, acc_ref, wide_ref = refs[17:]
    g, last = pl.program_id(0), pl.num_programs(0) - 1
    chunk, block, pair = up_ref.shape
    width = w_ref.shape[1] // 2

    @pl.when(g == 0)
    def _():
        w = w_ref[:, width:]
        b = jnp.zeros((block, width * depth), F32)
        for s in range(depth):
            part = dot(mj_ref[s], w).astype(BF16)
            b = b + dot(part, perm_ref[s * width : (s + 1) * width, :])
        b_ref[...] = b.astype(BF16)
        bt_ref[...] = b.T.astype(BF16)
        for k in range(block // chunk):
            count = dot_nt(seen_j_ref[...], seen_i_ref[k * chunk : (k + 1) * chunk, :])
            inv_ref[k] = 1.0 / (count + 0.001)
        acc_ref[...] = jnp.zeros_like(acc_ref)
        wide_ref[...] = jnp.zeros_like(wide_ref)
        bias_ref[...] = jnp.zeros_like(bias_ref)
        pass_ref[...] = offset_ref[...]

    inv = inv_ref[g]
    bias = jnp.zeros((block, pair), F32)
    for i in range(chunk):
        up = up_ref[i].astype(F32)
        bias = bias + up
        g_ref[i] = (up * inv[:, i : i + 1]).astype(BF16)
    bias_ref[0:1, :] += jnp.sum(bias, axis=0, keepdims=True)
    fill_v(g_ref, bt_ref[...], v_ref, depth)
    span = chunk * depth
    a_t = at_ref[:, pl.ds(pl.multiple_of(g * span, span), span)]
    for e in range(0, width, 2):
        part = dot(a_t, two(v_ref, e))
        for k in range(2):
            rows = slice((e + k) * width, (e + k + 1) * width)
            acc_ref[rows, :] += part[:width, k * pair : (k + 1) * pair]
        wide_ref[:, e * pair : (e + 2) * pair] += part[width:]

    @pl.when(g == last)
    def _():
        dw_ref[...] = acc_ref[...].astype(BF16)
        left = jnp.zeros((width, features), F32)
        for e in range(0, width, 2):
            lanes = slice(e * pair, (e + 2) * pair)
            left = left + dot_nt(wc_ref[:, lanes], wide_ref[:, lanes].astype(BF16))
        left_ref[...] = left


def left_kernel(depth, bit, g_ref, bt_ref, wd_ref, small_ref, keep_ref, go_ref, pass_ref, v_ref, da_ref):
    g, last = pl.program_id(0), pl.num_programs(0) - 1
    chunk, _, pair = g_ref.shape
    width = wd_ref.shape[1]
    span = chunk * depth

    @pl.when(g == 0)
    def _():
        pass_ref[...] = small_ref[...]

    fill_v(g_ref, bt_ref[...], v_ref, depth)
    d_a = []
    each = width // 4
    for e in range(0, width, each):
        v = jnp.concatenate([v_ref[e + k] for k in range(each)], axis=1)
        d_a.append(dot(v, wd_ref[e * pair : (e + each) * pair, :]))
    d_a = (d_a[0] + d_a[1]) + (d_a[2] + d_a[3])
    same = one_hot(iota((width, width), 0) == iota((width, width), 1))
    d_a = dot_nt(same, d_a.astype(BF16)).astype(BF16)
    tiles = span // LANES
    for k in range(tiles):
        da_ref[g * tiles + k] = d_a[:, k * LANES : (k + 1) * LANES]

    @pl.when(g == last)
    def _():
        half = keep_ref.shape[0]
        here = (lax.axis_index("col") >> bit) & 1
        keep_ref[...] = da_ref[pl.ds(here * half, half)]
        go_ref[...] = da_ref[pl.ds((1 - here) * half, half)]


def token_kernel(depth, features, n, g_ref, t_ref, mj_ref, perm_ref, bias_ref, left_ref, small_ref, out_ref, db_ref):
    g, last = pl.program_id(0), pl.num_programs(0) - 1
    chunk, block = g_ref.shape[:2]
    width = left_ref.shape[0]

    @pl.when(g == 0)
    def _():
        db_ref[...] = jnp.zeros_like(db_ref)

    t = jnp.concatenate([t_ref[i] for i in range(chunk)], axis=1)
    scaled = jnp.concatenate([g_ref[i] for i in range(chunk)], axis=1)
    db_ref[...] += dot_nt(t, scaled)

    @pl.when(g == last)
    def _():
        d_b = db_ref[...].T.astype(BF16)
        own = block // n
        for k in range(n):
            part = d_b[k * own : (k + 1) * own, :]
            for q in range(part.shape[1] // LANES):
                out_ref[k, q * own : (q + 1) * own, :] = part[:, q * LANES : (q + 1) * LANES]
        turned = dot_nt(perm_ref[...], d_b).astype(BF16)
        right = jnp.zeros((width, features), F32)
        for s in range(depth):
            right = right + dot(turned[s * width : (s + 1) * width, :], mj_ref[s])
        small = jnp.concatenate([left_ref[...], right], axis=1)
        small_ref[0:width, :] = small.astype(BF16)
        small_ref[width:, :] = jnp.broadcast_to(bias_ref[0:1, :], (16, LANES)).astype(BF16)


def update_kernel(inv_ref, b_ref, t_ref, offset_ref, wc_ref, small_ref, out_ref, wd_ref, pass_ref):
    g = pl.program_id(0)
    chunk, block, pair = out_ref.shape

    @pl.when(g == 0)
    def _():
        pass_ref[...] = small_ref[...]
        same = one_hot(iota((2 * pair, 2 * pair), 0) == iota((2 * pair, 2 * pair), 1))
        for at in range(0, wd_ref.shape[0], 2 * pair):
            wd_ref[at : at + 2 * pair, :] = dot_nt(same, wc_ref[:, at : at + 2 * pair]).astype(BF16)

    inv = inv_ref[g]
    b = b_ref[...]
    offset = offset_ref[...]
    for at in range(0, chunk, 2):
        part = dot(b, two(t_ref, at))
        for k in range(2):
            value = part[:, k * pair : (k + 1) * pair] * inv[:, at + k : at + k + 1] + offset
            out_ref[at + k] = value.astype(BF16)


def owner_kernel(depth, own, features, *refs):
    da_refs, db_ref, small_refs = refs[:2], refs[2], refs[3:5]
    x_ref, mask_ref, wt_ref, perm_ref, dw_ref = refs[5:10]
    out_ref, factors_ref, bias_ref, placed_ref = refs[10:]
    for e in range(dw_ref.shape[0]):
        placed_ref[:, e, :] = dw_ref[e].astype(F32)
    rows = depth * own
    width = wt_ref.shape[0] // 2
    p, q = iota((rows, rows), 0), iota((rows, rows), 1)
    swap = one_hot(q == (p % own) * depth + p // own)
    d_a = dot_nt(swap, da_refs[0][...]) + dot_nt(swap, da_refs[1][...])
    d_b = dot_nt(db_ref[...], perm_ref[...])
    d_b = jnp.concatenate([d_b[:, s * width : (s + 1) * width] for s in range(depth)], axis=0)
    highest = lax.Precision.HIGHEST
    wt = wt_ref[...].astype(F32)
    d_normed = jnp.dot(d_a, wt[:width, :], precision=highest, preferred_element_type=F32)
    d_normed = d_normed + jnp.dot(d_b, wt[width:, :], precision=highest, preferred_element_type=F32)
    pick = one_hot(iota((rows, depth), 0) // own == iota((rows, depth), 1))
    here = iota((rows, own), 0) % own == iota((rows, own), 1)
    weight = jnp.sum(jnp.where(here, dot(pick, mask_ref[...]), 0.0), axis=1, keepdims=True)
    d_normed = d_normed * weight
    normed, scale = stats(x_ref[...].astype(F32))
    mean = jnp.mean(d_normed, axis=-1, keepdims=True)
    along = jnp.mean(d_normed * normed, axis=-1, keepdims=True)
    out_ref[...] = scale * (d_normed - mean - normed * along)
    small = small_refs[0][...].astype(F32) + small_refs[1][...].astype(F32)
    turned = small[:width].T
    factors_ref[...] = jnp.concatenate([turned[:features], turned[features:]], axis=1)
    bias_ref[...] = small[width : width + 1]


def lay_back(x, rows, lanes):
    if lanes % LANES:
        return x.reshape(rows, lanes)
    return x.reshape(lanes // LANES, rows, LANES).transpose(1, 0, 2).reshape(rows, lanes)


def bit_of(axis, bit):
    return (lax.axis_index(axis) >> bit) & 1


def swap_parts(parts, axis, bit, n):
    parts = [part.reshape(-1, LANES) for part in parts]
    message = jnp.concatenate(parts, axis=0) if len(parts) > 1 else parts[0]
    pairs = [(i, i ^ (1 << bit)) for i in range(n)]
    message = lax.ppermute(message, axis, pairs)
    got, at = [], 0
    for part in parts:
        got.append(message[at : at + part.shape[0]])
        at += part.shape[0]
    return got


def halves(x, axis, bit, at):
    here = bit_of(axis, bit)
    keep = lax.dynamic_index_in_dim(x, here, at, keepdims=False)
    return keep, lax.dynamic_index_in_dim(x, 1 - here, at, keepdims=False)


def split_high(x):
    return x.reshape((2, x.shape[0] // 2) + x.shape[1:])


def in_order(mine, other, axis, bit, at):
    first = bit_of(axis, bit) == 0
    low = jnp.where(first, mine, other)
    return jnp.stack([low, jnp.where(first, other, mine)], axis=at)


def unswap(x, axis):
    n = x.shape[0]
    for bit in range(n.bit_length() - 1):
        y = x.reshape((n >> (bit + 1), 2, 1 << bit) + x.shape[1:])
        x = jnp.where(bit_of(axis, bit) == 0, y, y[:, ::-1]).reshape(x.shape)
    return x


def add(mine, other):
    other = other.reshape(mine.shape)
    return lax.optimization_barrier((mine.astype(F32) + other.astype(F32)).astype(BF16))


def per_device(
    n,
    alignment_embedding,
    alignment_cell_exists,
    alignment_lines_exist,
    sitewise_factors,
    pairing_matrix,
    offset_vector,
    upstream_adjoint,
):
    depth, own, features = alignment_embedding.shape
    width = sitewise_factors.shape[1] // 2
    block, pair = upstream_adjoint.shape[0], upstream_adjoint.shape[2]
    rows, chunk = depth * own, 16
    steps = block // chunk
    split = own % 16 == 0
    axes = ("row", "col")
    sds = jax.ShapeDtypeStruct

    bits = n.bit_length() - 1
    x = alignment_embedding.reshape(rows, features)
    offset = offset_vector.reshape(1, pair)
    args = (x, alignment_cell_exists, alignment_lines_exist.reshape(1, depth))
    out_shapes = [sds((rows // 2, LANES), BF16)] * 2 + [sds((own, LANES), BF16), sds((depth, own), BF16)]
    by_token, by_row, mask_t, mask = call(
        functools.partial(prep_kernel, depth, own),
        (1,),
        [full(v.shape) for v in args],
        [full(o.shape) for o in out_shapes],
        out_shapes,
    )(*args)
    message = jnp.concatenate([by_token, mask_t], axis=0)
    held = [message]
    for k in range(1, n):
        held.append(lax.ppermute(message, "col", [(j, j ^ k) for j in range(n)]))
    held = unswap(jnp.stack(held), "col")
    seen_i = held[:, rows // 2 :].reshape(block, LANES)
    parts = held[:, : rows // 2].reshape(n, rows // 2, 2, features)
    mi = parts.transpose(0, 2, 1, 3).reshape(block * depth, features)
    message = jnp.concatenate([by_row, mask_t], axis=0)
    held = []
    for k in range(n):
        pairs = [(i * n + j, (j ^ k) * n + i) for i in range(n) for j in range(n)]
        held.append(lax.ppermute(message, axes, pairs))
    held = unswap(jnp.stack(held), "row")
    seen_j = held[:, rows // 2 :].reshape(block, LANES)
    parts = held[:, : rows // 2].reshape(n, depth // 2, own, 2, features)
    mj = parts.transpose(3, 1, 0, 2, 4).reshape(depth, block, features)

    wide = width * depth
    tokens = block * depth
    source = jnp.arange(wide)
    perm = (jnp.arange(wide)[None, :] == (source % width * depth + source // width)[:, None]).astype(BF16)
    up_spec = pl.BlockSpec((chunk, block, pair), lambda g: (g, 0, 0))
    t_spec = pl.BlockSpec((chunk, wide, pair), lambda g: (g, 0, 0))
    out_shapes = [
        sds((width + features, tokens), BF16),
        sds((2 * width, features), BF16),
        sds((width, width * pair), BF16),
    ]
    args = (mi, sitewise_factors, pairing_matrix)
    t, a_t, factors_t, pairing_wide = call(
        functools.partial(row_kernel, depth, features),
        (steps,),
        [full(v.shape) for v in args],
        [t_spec] + [full(o.shape) for o in out_shapes],
        [sds((block, wide, pair), BF16)] + out_shapes,
        [pltpu.VMEM((tokens, width), BF16), pltpu.VMEM((width * width, pair), F32)],
        cost(4e9, 8e6),
    )(*args)

    out_shapes = [
        sds((block, wide), BF16),
        sds((wide, block), BF16),
        sds((steps, block, chunk), F32),
        sds((8, pair), F32),
        sds((width * width, pair), BF16),
        sds((width, features), F32),
        sds((1, pair), F32),
    ]
    args = (mj, seen_j, seen_i, sitewise_factors, perm, pairing_wide, a_t, offset)
    outs = call(
        functools.partial(weight_kernel, depth, features),
        (steps,),
        [up_spec] + [full(v.shape) for v in args],
        [up_spec] + [full(o.shape) for o in out_shapes],
        [sds(upstream_adjoint.shape, BF16)] + out_shapes,
        [
            pltpu.VMEM((width, chunk * depth, pair), BF16),
            pltpu.VMEM((width * width, pair), F32),
            pltpu.VMEM((features, width * pair), F32),
        ],
        cost(5e9, 8e6),
    )(upstream_adjoint, *args)
    scaled, b, b_t, inv, bias, d_pairing, left, offset = outs

    d_pairing = d_pairing.reshape(n, -1, LANES)
    for bit in reversed(range(1, bits)):
        keep, go = halves(split_high(d_pairing), "col", bit, 0)
        d_pairing = add(keep, *swap_parts([go], "col", bit, n))

    out_shapes = [sds((width + 16, LANES), BF16), sds((n, own * wide // LANES, LANES), BF16)]
    small, d_b = call(
        functools.partial(token_kernel, depth, features, n),
        (steps,),
        [up_spec, t_spec] + [full(v.shape) for v in (mj, perm, bias, left)],
        [full(o.shape) for o in out_shapes],
        out_shapes,
        [pltpu.VMEM((wide, block), F32)],
        cost(6e9, 16e6),
    )(scaled, t, mj, perm, bias, left)

    dp_keep, dp_go = halves(d_pairing, "col", 0, 0)
    db_keep, db_go = halves(d_b.reshape((n // 2, 2) + d_b.shape[1:]), "col", 0, 1)
    parts = swap_parts([dp_go, db_go, small], "col", 0, n)
    d_pairing, small = add(dp_keep, parts[0]), add(small, parts[2])
    d_b = in_order(db_keep, parts[1].reshape(db_keep.shape), "col", 0, 1)
    db_keep, db_go = halves(d_b, "row", 0, 1)
    for bit in range(bits):
        parts = swap_parts([d_pairing, db_go, small], "row", bit, n)
        if bit == 0:
            args = (inv, b, t, offset, pairing_wide, small)
            specs = [full(v.shape) for v in args]
            specs[2] = t_spec
            coupling_update, pairing_t, small = call(
                update_kernel,
                (steps,),
                specs,
                [up_spec, full((width * pair, width)), full(small.shape)],
                [
                    sds((block, block, pair), BF16),
                    sds((width * pair, width), BF16),
                    sds(small.shape, BF16),
                ],
                (),
                cost(6e9, 8e6),
            )(*args)
        if bit == 1:
            half = (tokens // LANES // 2, width, LANES)
            out_shapes = [sds(half, BF16), sds(half, BF16), sds(small.shape, BF16)]
            *d_a, small = call(
                functools.partial(left_kernel, depth, bits - 1),
                (steps,),
                [up_spec] + [full(v.shape) for v in (b_t, pairing_t, small)],
                [full(o.shape) for o in out_shapes],
                out_shapes,
                [
                    pltpu.VMEM((width, chunk * depth, pair), BF16),
                    pltpu.VMEM((tokens // LANES, width, LANES), BF16),
                ],
                cost(6e9, 8e6),
            )(scaled, b_t, pairing_t, small)
            if rows % LANES:
                shape = (-1, width, LANES // rows, rows)
                d_a = [part.reshape(shape).transpose(0, 2, 1, 3) for part in d_a]
            da_keep, da_go = [part.reshape(n // 2, -1, LANES) for part in d_a]
        d_pairing, d_b, small = add(d_pairing, parts[0]), add(db_keep, parts[1]), add(small, parts[2])
        db_keep = db_go = d_b
    d_pairing = d_pairing.reshape(1, -1, LANES)
    small_parts = [small]
    for bit in reversed(range(1, bits)):
        if bit < bits - 1:
            small_parts = [add(*small_parts)]
            da_keep, da_go = halves(split_high(add(*da_parts)), "col", bit, 0)
        db_keep, db_go = halves(split_high(d_b), "col", bit, 0)
        parts = swap_parts([d_pairing, db_go, da_go, small_parts[0]], "col", bit, n)
        d_pairing = in_order(d_pairing, parts[0].reshape(d_pairing.shape), "col", bit, 1)
        d_pairing = d_pairing.reshape((-1,) + d_pairing.shape[2:])
        mine = bit_of("col", bit) == bit_of("row", bit)
        d_b = jnp.where(mine, db_keep, parts[1].reshape(db_keep.shape))
        da_parts = [da_keep, parts[2].reshape(da_keep.shape)]
        small_parts = [small_parts[0], parts[3]]
    da_keep, da_go = halves(add(*da_parts), "col", 0, 0)
    got, da_got = swap_parts([d_pairing, da_go], "col", 0, n)
    d_pairing = in_order(d_pairing, got.reshape(d_pairing.shape), "col", 0, 1)
    d_a = [lay_back(part.reshape(-1, LANES), width, rows) for part in (da_keep, da_got)]
    d_b = lay_back(d_b[0], own, wide)

    d_pairing = d_pairing.reshape(width, width, pair)
    args = (*d_a, d_b, *small_parts, x, mask, factors_t, perm, d_pairing)
    out_shapes = [
        sds((rows, features), F32),
        sds((features, 2 * width), F32),
        sds((1, pair), F32),
        sds((width, width, pair), F32),
    ]
    embedding_adjoint, factors_adjoint, offset_slope, placed = call(
        functools.partial(owner_kernel, depth, own, features),
        (),
        [full(v.shape) for v in args],
        [full(o.shape) for o in out_shapes],
        out_shapes,
    )(*args)
    return (
        coupling_update,
        embedding_adjoint.reshape(depth, own, features),
        factors_adjoint,
        placed.reshape(width * width, pair),
        offset_slope.reshape(pair),
    )


def solution(mesh):
    n = mesh.shape["col"]
    placed = (
        P(None, ("groups", "row", "col"), None),
        P(None, ("groups", "row", "col")),
        P("groups"),
        P(),
        P(),
        P(),
        P(("groups", "row"), "col", None),
    )
    return jax.shard_map(
        functools.partial(per_device, n),
        mesh=mesh,
        in_specs=placed,
        out_specs=(
            P(("groups", "row"), "col", None),
            P(None, ("groups", "row", "col"), None),
            P("groups", None),
            P("groups", None),
            P("groups"),
        ),
        check_vma=False,
    )
```

```python
import functools

import jax
import jax.numpy as jnp
from jax import lax
from jax.experimental import pallas as pl
from jax.experimental.pallas import tpu as pltpu
from jax.sharding import PartitionSpec as P

F32 = jnp.float32
BF16 = jnp.bfloat16
LANES = 128
VMEM_LIMIT = 24 * 1024 * 1024
NT = (((1,), (1,)), ((), ()))


def dot(left, right):
    return jnp.dot(left, right, preferred_element_type=F32)


def dot_nt(left, right):
    return lax.dot_general(left, right, NT, preferred_element_type=F32)


def iota(shape, axis):
    return lax.broadcasted_iota(jnp.int32, shape, axis)


def one_hot(mask):
    return jnp.where(mask, 1.0, 0.0).astype(BF16)


def full(shape):
    return pl.BlockSpec(shape, lambda *g: (0,) * len(shape))


def cost(flops, nbytes):
    return pl.CostEstimate(flops=int(flops), bytes_accessed=int(nbytes), transcendentals=0)


def call(kernel, grid, in_specs, out_specs, out_shape, scratch=(), estimate=None):
    return pl.pallas_call(
        kernel,
        grid=grid,
        in_specs=in_specs,
        out_specs=out_specs,
        out_shape=out_shape,
        scratch_shapes=list(scratch),
        compiler_params=pltpu.CompilerParams(vmem_limit_bytes=VMEM_LIMIT),
        cost_estimate=estimate,
    )


def stats(x):
    center = x - jnp.mean(x, axis=-1, keepdims=True)
    scale = lax.rsqrt(jnp.mean(center * center, axis=-1, keepdims=True) + 1e-05)
    return center * scale, scale


def prep_kernel(depth, own, features, x_ref, by_token_ref, by_row_ref):
    rows = depth * own
    half = rows // 2
    x = x_ref[...].astype(F32)
    weight = x[:, features : features + 1]
    normed, _ = stats(x[:, :features])
    masked = normed.astype(BF16).astype(F32) * weight
    by_row_ref[:half, :] = jnp.concatenate([masked[:half], masked[half:]], axis=1).astype(BF16)
    p, q = iota((rows, rows), 0), iota((rows, rows), 1)
    swap = one_hot(q == (p % depth) * own + p // depth)
    turned = dot(swap, masked.astype(BF16))
    by_token_ref[:half, :] = jnp.concatenate([turned[:half], turned[half:]], axis=1).astype(BF16)
    here = one_hot(iota((own, rows), 0) == iota((own, rows), 1) % own)
    at = iota((rows, LANES), 1) == iota((rows, LANES), 0) // own
    mask = dot(here, jnp.where(at, weight, 0.0).astype(BF16)).astype(BF16)
    by_row_ref[half:, :] = mask
    by_token_ref[half:, :] = mask


def two(ref, at):
    return jnp.concatenate([ref[at], ref[at + 1]], axis=1)


def fill_v(g_ref, bt, v_ref, depth):
    chunk, _, pair = g_ref.shape
    width = v_ref.shape[0]
    for at in range(0, chunk, 2):
        v = dot(bt, two(g_ref, at)).astype(BF16)
        for k in range(2):
            part = v[:, k * pair : (k + 1) * pair].reshape(width, depth, pair)
            v_ref[:, (at + k) * depth : (at + k + 1) * depth, :] = part


def fill_t(a_chunk, wc_ref, t_ref, depth):
    chunk, wide, pair = t_ref.shape
    width = wide // depth
    for e in range(0, width, 2):
        t = dot(a_chunk, wc_ref[:, e * pair : (e + 2) * pair]).astype(BF16)
        for k in range(2):
            part = t[:, k * pair : (k + 1) * pair].reshape(chunk, depth, pair)
            t_ref[:, (e + k) * depth : (e + k + 1) * depth, :] = part


def row_kernel(mi_ref, w_ref, wide_ref, a_ref, at_ref, wt_ref, wc_ref, rows_ref):
    features, width = w_ref.shape[0], w_ref.shape[1] // 2
    pair = wide_ref.shape[1]
    rows_ref[...] = wide_ref[...].astype(F32)
    for e in range(width):
        part = rows_ref[pl.ds(e, width, stride=width), :]
        wc_ref[:, e * pair : (e + 1) * pair] = part.astype(BF16)
    w = w_ref[...]
    same = one_hot(iota((2 * width, 2 * width), 0) == iota((2 * width, 2 * width), 1))
    wt = dot_nt(same, w).astype(BF16)
    wt_ref[...] = wt
    mi = mi_ref[...]
    a_ref[...] = dot(mi, w[:, :width]).astype(BF16)
    same = one_hot(iota((features, features), 0) == iota((features, features), 1))
    at_ref[...] = dot_nt(jnp.concatenate([wt[:width, :], same], axis=0), mi).astype(BF16)


def weight_kernel(depth, features, *refs):
    up_ref, mj_ref, seen_j_ref, seen_i_ref, w_ref, perm_ref, wc_ref, at_ref, offset_ref = refs[:9]
    g_ref, b_ref, bt_ref, inv_ref, bias_ref, dw_ref, left_ref, pass_ref = refs[9:17]
    v_ref, acc_ref, wide_ref = refs[17:]
    g, last = pl.program_id(0), pl.num_programs(0) - 1
    chunk, block, pair = up_ref.shape
    width = w_ref.shape[1] // 2

    @pl.when(g == 0)
    def _():
        w = w_ref[:, width:]
        b = jnp.zeros((block, width * depth), F32)
        for s in range(depth):
            part = dot(mj_ref[s], w).astype(BF16)
            b = b + dot(part, perm_ref[s * width : (s + 1) * width, :])
        b_ref[...] = b.astype(BF16)
        bt_ref[...] = b.T.astype(BF16)
        for k in range(block // chunk):
            count = dot_nt(seen_j_ref[...], seen_i_ref[k * chunk : (k + 1) * chunk, :])
            inv_ref[k] = 1.0 / (count + 0.001)
        acc_ref[...] = jnp.zeros_like(acc_ref)
        wide_ref[...] = jnp.zeros_like(wide_ref)
        bias_ref[...] = jnp.zeros_like(bias_ref)
        pass_ref[...] = offset_ref[...]

    inv = inv_ref[g]
    bias = jnp.zeros((block, pair), F32)
    for i in range(chunk):
        up = up_ref[i].astype(F32)
        bias = bias + up
        g_ref[i] = (up * inv[:, i : i + 1]).astype(BF16)
    bias_ref[0:1, :] += jnp.sum(bias, axis=0, keepdims=True)
    fill_v(g_ref, bt_ref[...], v_ref, depth)
    span = chunk * depth
    a_t = at_ref[:, pl.ds(pl.multiple_of(g * span, span), span)]
    for e in range(0, width, 2):
        part = dot(a_t, two(v_ref, e))
        for k in range(2):
            rows = slice((e + k) * width, (e + k + 1) * width)
            acc_ref[rows, :] += part[:width, k * pair : (k + 1) * pair]
        wide_ref[:, e * pair : (e + 2) * pair] += part[width:]

    @pl.when(g == last)
    def _():
        dw_ref[...] = acc_ref[...].astype(BF16)
        left = jnp.zeros((width, features), F32)
        for e in range(0, width, 2):
            lanes = slice(e * pair, (e + 2) * pair)
            left = left + dot_nt(wc_ref[:, lanes], wide_ref[:, lanes].astype(BF16))
        left_ref[...] = left


def left_kernel(depth, bit, g_ref, bt_ref, wd_ref, small_ref, keep_ref, go_ref, pass_ref, v_ref, da_ref):
    g, last = pl.program_id(0), pl.num_programs(0) - 1
    chunk, _, pair = g_ref.shape
    width = wd_ref.shape[1]
    span = chunk * depth

    @pl.when(g == 0)
    def _():
        pass_ref[...] = small_ref[...]

    fill_v(g_ref, bt_ref[...], v_ref, depth)
    d_a = []
    each = width // 4
    for e in range(0, width, each):
        v = jnp.concatenate([v_ref[e + k] for k in range(each)], axis=1)
        d_a.append(dot(v, wd_ref[e * pair : (e + each) * pair, :]))
    d_a = (d_a[0] + d_a[1]) + (d_a[2] + d_a[3])
    same = one_hot(iota((width, width), 0) == iota((width, width), 1))
    d_a = dot_nt(same, d_a.astype(BF16)).astype(BF16)
    tiles = span // LANES
    for k in range(tiles):
        da_ref[g * tiles + k] = d_a[:, k * LANES : (k + 1) * LANES]

    @pl.when(g == last)
    def _():
        half = keep_ref.shape[0]
        here = (lax.axis_index("col") >> bit) & 1
        keep_ref[...] = da_ref[pl.ds(here * half, half)]
        go_ref[...] = da_ref[pl.ds((1 - here) * half, half)]


def token_kernel(depth, features, n, *refs):
    g_ref, a_ref, wc_ref, mj_ref, perm_ref, bias_ref, left_ref = refs[:7]
    small_ref, out_ref, t_ref, db_ref = refs[7:]
    g, last = pl.program_id(0), pl.num_programs(0) - 1
    chunk, block = g_ref.shape[:2]
    width = left_ref.shape[0]

    @pl.when(g == 0)
    def _():
        db_ref[...] = jnp.zeros_like(db_ref)

    span = chunk * depth
    fill_t(a_ref[pl.ds(pl.multiple_of(g * span, span), span), :], wc_ref, t_ref, depth)
    t = jnp.concatenate([t_ref[i] for i in range(chunk)], axis=1)
    scaled = jnp.concatenate([g_ref[i] for i in range(chunk)], axis=1)
    db_ref[...] += dot_nt(t, scaled)

    @pl.when(g == last)
    def _():
        d_b = db_ref[...].T.astype(BF16)
        own = block // n
        for k in range(n):
            part = d_b[k * own : (k + 1) * own, :]
            for q in range(part.shape[1] // LANES):
                out_ref[k, q * own : (q + 1) * own, :] = part[:, q * LANES : (q + 1) * LANES]
        turned = dot_nt(perm_ref[...], d_b).astype(BF16)
        right = jnp.zeros((width, features), F32)
        for s in range(depth):
            right = right + dot(turned[s * width : (s + 1) * width, :], mj_ref[s])
        small = jnp.concatenate([left_ref[...], right], axis=1)
        small_ref[0:width, :] = small.astype(BF16)
        small_ref[width:, :] = jnp.broadcast_to(bias_ref[0:1, :], (16, LANES)).astype(BF16)


def update_kernel(depth, *refs):
    inv_ref, a_ref, b_ref, offset_ref, wc_ref, small_ref, out_ref, wd_ref, pass_ref, t_ref = refs
    g = pl.program_id(0)
    chunk, block, pair = out_ref.shape

    @pl.when(g == 0)
    def _():
        pass_ref[...] = small_ref[...]
        same = one_hot(iota((2 * pair, 2 * pair), 0) == iota((2 * pair, 2 * pair), 1))
        for at in range(0, wd_ref.shape[0], 2 * pair):
            wd_ref[at : at + 2 * pair, :] = dot_nt(same, wc_ref[:, at : at + 2 * pair]).astype(BF16)

    span = chunk * depth
    fill_t(a_ref[pl.ds(pl.multiple_of(g * span, span), span), :], wc_ref, t_ref, depth)
    inv = inv_ref[g]
    b = b_ref[...]
    offset = offset_ref[...]
    for at in range(0, chunk, 2):
        part = dot(b, two(t_ref, at))
        for k in range(2):
            value = part[:, k * pair : (k + 1) * pair] * inv[:, at + k : at + k + 1] + offset
            out_ref[at + k] = value.astype(BF16)


def owner_kernel(depth, own, features, *refs):
    da_refs, db_ref, small_refs = refs[:2], refs[2], refs[3:5]
    x_ref, wt_ref, perm_ref, dw_ref = refs[5:9]
    out_ref, factors_ref, bias_ref, placed_ref = refs[9:]
    for e in range(dw_ref.shape[0]):
        placed_ref[:, e, :] = dw_ref[e].astype(F32)
    rows = depth * own
    width = wt_ref.shape[0] // 2
    p, q = iota((rows, rows), 0), iota((rows, rows), 1)
    swap = one_hot(q == (p % own) * depth + p // own)
    d_a = dot_nt(swap, da_refs[0][...]) + dot_nt(swap, da_refs[1][...])
    d_b = dot_nt(db_ref[...], perm_ref[...])
    d_b = jnp.concatenate([d_b[:, s * width : (s + 1) * width] for s in range(depth)], axis=0)
    highest = lax.Precision.HIGHEST
    wt = wt_ref[...].astype(F32)
    d_normed = jnp.dot(d_a, wt[:width, :], precision=highest, preferred_element_type=F32)
    d_normed = d_normed + jnp.dot(d_b, wt[width:, :], precision=highest, preferred_element_type=F32)
    x = x_ref[...].astype(F32)
    d_normed = d_normed * x[:, features : features + 1]
    normed, scale = stats(x[:, :features])
    mean = jnp.mean(d_normed, axis=-1, keepdims=True)
    along = jnp.mean(d_normed * normed, axis=-1, keepdims=True)
    out_ref[...] = scale * (d_normed - mean - normed * along)
    small = small_refs[0][...].astype(F32) + small_refs[1][...].astype(F32)
    turned = small[:width].T
    factors_ref[...] = jnp.concatenate([turned[:features], turned[features:]], axis=1)
    bias_ref[...] = small[width : width + 1]


def lay_back(x, rows, lanes):
    if lanes % LANES:
        return x.reshape(rows, lanes)
    return x.reshape(lanes // LANES, rows, LANES).transpose(1, 0, 2).reshape(rows, lanes)


def bit_of(axis, bit):
    return (lax.axis_index(axis) >> bit) & 1


def swap_parts(parts, axis, bit, n):
    parts = [part.reshape(-1, LANES) for part in parts]
    message = jnp.concatenate(parts, axis=0) if len(parts) > 1 else parts[0]
    pairs = [(i, i ^ (1 << bit)) for i in range(n)]
    message = lax.ppermute(message, axis, pairs)
    got, at = [], 0
    for part in parts:
        got.append(message[at : at + part.shape[0]])
        at += part.shape[0]
    return got


def halves(x, axis, bit, at):
    here = bit_of(axis, bit)
    keep = lax.dynamic_index_in_dim(x, here, at, keepdims=False)
    return keep, lax.dynamic_index_in_dim(x, 1 - here, at, keepdims=False)


def split_high(x):
    return x.reshape((2, x.shape[0] // 2) + x.shape[1:])


def in_order(mine, other, axis, bit, at):
    first = bit_of(axis, bit) == 0
    low = jnp.where(first, mine, other)
    return jnp.stack([low, jnp.where(first, other, mine)], axis=at)


def unswap(x, axis):
    n = x.shape[0]
    for bit in range(n.bit_length() - 1):
        y = x.reshape((n >> (bit + 1), 2, 1 << bit) + x.shape[1:])
        x = jnp.where(bit_of(axis, bit) == 0, y, y[:, ::-1]).reshape(x.shape)
    return x


def add(mine, other):
    other = other.reshape(mine.shape)
    return lax.optimization_barrier((mine.astype(F32) + other.astype(F32)).astype(BF16))


def per_device(
    n,
    alignment_embedding,
    alignment_cell_exists,
    alignment_lines_exist,
    sitewise_factors,
    pairing_matrix,
    offset_vector,
    upstream_adjoint,
):
    depth, own, features = alignment_embedding.shape
    width = sitewise_factors.shape[1] // 2
    block, pair = upstream_adjoint.shape[0], upstream_adjoint.shape[2]
    rows, chunk = depth * own, 16
    steps = block // chunk
    split = own % 16 == 0
    axes = ("row", "col")
    sds = jax.ShapeDtypeStruct

    bits = n.bit_length() - 1
    mask = (alignment_cell_exists * alignment_lines_exist[:, None]).astype(BF16)
    mask = jnp.broadcast_to(mask[:, :, None], (depth, own, LANES - features))
    x = jnp.concatenate([alignment_embedding, mask], axis=2).reshape(rows, LANES)
    offset = offset_vector.reshape(1, pair)
    out_shapes = [sds((rows // 2 + own, LANES), BF16)] * 2
    by_token, by_row = call(
        functools.partial(prep_kernel, depth, own, features),
        (),
        [full(x.shape)],
        [full(o.shape) for o in out_shapes],
        out_shapes,
    )(x)
    message = by_token
    held = [message]
    for k in range(1, n):
        held.append(lax.ppermute(message, "col", [(j, j ^ k) for j in range(n)]))
    held = unswap(jnp.stack(held), "col")
    seen_i = held[:, rows // 2 :].reshape(block, LANES)
    parts = held[:, : rows // 2].reshape(n, rows // 2, 2, features)
    mi = parts.transpose(0, 2, 1, 3).reshape(block * depth, features)
    message = by_row
    held = []
    for k in range(n):
        pairs = [(i * n + j, (j ^ k) * n + i) for i in range(n) for j in range(n)]
        held.append(lax.ppermute(message, axes, pairs))
    held = unswap(jnp.stack(held), "row")
    seen_j = held[:, rows // 2 :].reshape(block, LANES)
    parts = held[:, : rows // 2].reshape(n, depth // 2, own, 2, features)
    mj = parts.transpose(3, 1, 0, 2, 4).reshape(depth, block, features)

    wide = width * depth
    tokens = block * depth
    source = jnp.arange(wide)
    perm = (jnp.arange(wide)[None, :] == (source % width * depth + source // width)[:, None]).astype(BF16)
    up_spec = pl.BlockSpec((chunk, block, pair), lambda g: (g, 0, 0))
    args = (mi, sitewise_factors, pairing_matrix)
    out_shapes = [
        sds((tokens, width), BF16),
        sds((width + features, tokens), BF16),
        sds((2 * width, features), BF16),
        sds((width, width * pair), BF16),
    ]
    a, a_t, factors_t, pairing_wide = call(
        row_kernel,
        (),
        [full(v.shape) for v in args],
        [full(o.shape) for o in out_shapes],
        out_shapes,
        [pltpu.VMEM((width * width, pair), F32)],
    )(*args)

    out_shapes = [
        sds((block, wide), BF16),
        sds((wide, block), BF16),
        sds((steps, block, chunk), F32),
        sds((8, pair), F32),
        sds((width * width, pair), BF16),
        sds((width, features), F32),
        sds((1, pair), F32),
    ]
    args = (mj, seen_j, seen_i, sitewise_factors, perm, pairing_wide, a_t, offset)
    outs = call(
        functools.partial(weight_kernel, depth, features),
        (steps,),
        [up_spec] + [full(v.shape) for v in args],
        [up_spec] + [full(o.shape) for o in out_shapes],
        [sds(upstream_adjoint.shape, BF16)] + out_shapes,
        [
            pltpu.VMEM((width, chunk * depth, pair), BF16),
            pltpu.VMEM((width * width, pair), F32),
            pltpu.VMEM((features, width * pair), F32),
        ],
        cost(5e9, 8e6),
    )(upstream_adjoint, *args)
    scaled, b, b_t, inv, bias, d_pairing, left, offset = outs

    d_pairing = d_pairing.reshape(n, -1, LANES)
    for bit in reversed(range(1, bits)):
        keep, go = halves(split_high(d_pairing), "col", bit, 0)
        d_pairing = add(keep, *swap_parts([go], "col", bit, n))

    out_shapes = [sds((width + 16, LANES), BF16), sds((n, own * wide // LANES, LANES), BF16)]
    small, d_b = call(
        functools.partial(token_kernel, depth, features, n),
        (steps,),
        [up_spec] + [full(v.shape) for v in (a, pairing_wide, mj, perm, bias, left)],
        [full(o.shape) for o in out_shapes],
        out_shapes,
        [pltpu.VMEM((chunk, wide, pair), BF16), pltpu.VMEM((wide, block), F32)],
        cost(8e9, 8e6),
    )(scaled, a, pairing_wide, mj, perm, bias, left)

    dp_keep, dp_go = halves(d_pairing, "col", 0, 0)
    db_keep, db_go = halves(d_b.reshape((n // 2, 2) + d_b.shape[1:]), "col", 0, 1)
    parts = swap_parts([dp_go, db_go, small], "col", 0, n)
    d_pairing, small = add(dp_keep, parts[0]), add(small, parts[2])
    d_b = in_order(db_keep, parts[1].reshape(db_keep.shape), "col", 0, 1)
    db_keep, db_go = halves(d_b, "row", 0, 1)
    for bit in range(bits):
        parts = swap_parts([d_pairing, db_go, small], "row", bit, n)
        if bit == 0:
            args = (inv, a, b, offset, pairing_wide, small)
            coupling_update, pairing_t, small = call(
                functools.partial(update_kernel, depth),
                (steps,),
                [full(v.shape) for v in args],
                [up_spec, full((width * pair, width)), full(small.shape)],
                [
                    sds((block, block, pair), BF16),
                    sds((width * pair, width), BF16),
                    sds(small.shape, BF16),
                ],
                [pltpu.VMEM((chunk, wide, pair), BF16)],
                cost(6e9, 8e6),
            )(*args)
        if bit == 1:
            half = (tokens // LANES // 2, width, LANES)
            out_shapes = [sds(half, BF16), sds(half, BF16), sds(small.shape, BF16)]
            *d_a, small = call(
                functools.partial(left_kernel, depth, bits - 1),
                (steps,),
                [up_spec] + [full(v.shape) for v in (b_t, pairing_t, small)],
                [full(o.shape) for o in out_shapes],
                out_shapes,
                [
                    pltpu.VMEM((width, chunk * depth, pair), BF16),
                    pltpu.VMEM((tokens // LANES, width, LANES), BF16),
                ],
                cost(6e9, 8e6),
            )(scaled, b_t, pairing_t, small)
            if rows % LANES:
                shape = (-1, width, LANES // rows, rows)
                d_a = [part.reshape(shape).transpose(0, 2, 1, 3) for part in d_a]
            da_keep, da_go = [part.reshape(n // 2, -1, LANES) for part in d_a]
        d_pairing, d_b, small = add(d_pairing, parts[0]), add(db_keep, parts[1]), add(small, parts[2])
        db_keep = db_go = d_b
    d_pairing = d_pairing.reshape(1, -1, LANES)
    small_parts = [small]
    for bit in reversed(range(1, bits)):
        if bit < bits - 1:
            small_parts = [add(*small_parts)]
            da_keep, da_go = halves(split_high(add(*da_parts)), "col", bit, 0)
        db_keep, db_go = halves(split_high(d_b), "col", bit, 0)
        parts = swap_parts([d_pairing, db_go, da_go, small_parts[0]], "col", bit, n)
        d_pairing = in_order(d_pairing, parts[0].reshape(d_pairing.shape), "col", bit, 1)
        d_pairing = d_pairing.reshape((-1,) + d_pairing.shape[2:])
        mine = bit_of("col", bit) == bit_of("row", bit)
        d_b = jnp.where(mine, db_keep, parts[1].reshape(db_keep.shape))
        da_parts = [da_keep, parts[2].reshape(da_keep.shape)]
        small_parts = [small_parts[0], parts[3]]
    da_keep, da_go = halves(add(*da_parts), "col", 0, 0)
    got, da_got = swap_parts([d_pairing, da_go], "col", 0, n)
    d_pairing = in_order(d_pairing, got.reshape(d_pairing.shape), "col", 0, 1)
    d_a = [lay_back(part.reshape(-1, LANES), width, rows) for part in (da_keep, da_got)]
    d_b = lay_back(d_b[0], own, wide)

    d_pairing = d_pairing.reshape(width, width, pair)
    args = (*d_a, d_b, *small_parts, x, factors_t, perm, d_pairing)
    out_shapes = [
        sds((rows, features), F32),
        sds((features, 2 * width), F32),
        sds((1, pair), F32),
        sds((width, width, pair), F32),
    ]
    embedding_adjoint, factors_adjoint, offset_slope, placed = call(
        functools.partial(owner_kernel, depth, own, features),
        (),
        [full(v.shape) for v in args],
        [full(o.shape) for o in out_shapes],
        out_shapes,
    )(*args)
    return (
        coupling_update,
        embedding_adjoint.reshape(depth, own, features),
        factors_adjoint,
        placed.reshape(width * width, pair),
        offset_slope.reshape(pair),
    )


def solution(mesh):
    n = mesh.shape["col"]
    placed = (
        P(None, ("groups", "row", "col"), None),
        P(None, ("groups", "row", "col")),
        P("groups"),
        P(),
        P(),
        P(),
        P(("groups", "row"), "col", None),
    )
    return jax.shard_map(
        functools.partial(per_device, n),
        mesh=mesh,
        in_specs=placed,
        out_specs=(
            P(("groups", "row"), "col", None),
            P(None, ("groups", "row", "col"), None),
            P("groups", None),
            P("groups", None),
            P("groups"),
        ),
        check_vma=False,
    )
```

```python
import functools

import jax
import jax.numpy as jnp
from jax import lax
from jax.experimental import pallas as pl
from jax.experimental.pallas import tpu as pltpu
from jax.sharding import PartitionSpec as P

F32 = jnp.float32
BF16 = jnp.bfloat16
LANES = 128
VMEM_LIMIT = 24 * 1024 * 1024
NT = (((1,), (1,)), ((), ()))


def dot(left, right):
    return jnp.dot(left, right, preferred_element_type=F32)


def dot_nt(left, right):
    return lax.dot_general(left, right, NT, preferred_element_type=F32)


def iota(shape, axis):
    return lax.broadcasted_iota(jnp.int32, shape, axis)


def one_hot(mask):
    return jnp.where(mask, 1.0, 0.0).astype(BF16)


def full(shape):
    return pl.BlockSpec(shape, lambda *g: (0,) * len(shape))


def cost(flops, nbytes):
    return pl.CostEstimate(flops=int(flops), bytes_accessed=int(nbytes), transcendentals=0)


def call(kernel, grid, in_specs, out_specs, out_shape, scratch=(), estimate=None):
    return pl.pallas_call(
        kernel,
        grid=grid,
        in_specs=in_specs,
        out_specs=out_specs,
        out_shape=out_shape,
        scratch_shapes=list(scratch),
        compiler_params=pltpu.CompilerParams(vmem_limit_bytes=VMEM_LIMIT),
        cost_estimate=estimate,
    )


def stats(x):
    center = x - jnp.mean(x, axis=-1, keepdims=True)
    scale = lax.rsqrt(jnp.mean(center * center, axis=-1, keepdims=True) + 1e-05)
    return center * scale, scale


def prep_kernel(depth, own, features, x_ref, by_token_ref, by_row_ref):
    rows = depth * own
    half = rows // 2
    x = x_ref[...].astype(F32)
    weight = x[:, features : features + 1]
    normed, _ = stats(x[:, :features])
    masked = normed.astype(BF16).astype(F32) * weight
    by_row_ref[:half, :] = jnp.concatenate([masked[:half], masked[half:]], axis=1).astype(BF16)
    p, q = iota((rows, rows), 0), iota((rows, rows), 1)
    swap = one_hot(q == (p % depth) * own + p // depth)
    turned = dot(swap, masked.astype(BF16))
    by_token_ref[:half, :] = jnp.concatenate([turned[:half], turned[half:]], axis=1).astype(BF16)
    here = one_hot(iota((own, rows), 0) == iota((own, rows), 1) % own)
    at = iota((rows, LANES), 1) == iota((rows, LANES), 0) // own
    mask = dot(here, jnp.where(at, weight, 0.0).astype(BF16)).astype(BF16)
    by_row_ref[half:, :] = mask
    by_token_ref[half:, :] = mask


def two(ref, at):
    return jnp.concatenate([ref[at], ref[at + 1]], axis=1)


def fill_v(g_ref, bt, v_ref, depth):
    chunk, _, pair = g_ref.shape
    width = v_ref.shape[0]
    for at in range(0, chunk, 2):
        v = dot(bt, two(g_ref, at)).astype(BF16)
        for k in range(2):
            part = v[:, k * pair : (k + 1) * pair].reshape(width, depth, pair)
            v_ref[:, (at + k) * depth : (at + k + 1) * depth, :] = part


def fill_t(a_chunk, wc_ref, t_ref, depth):
    chunk, wide, pair = t_ref.shape
    width = wide // depth
    for e in range(0, width, 2):
        t = dot(a_chunk, wc_ref[:, e * pair : (e + 2) * pair]).astype(BF16)
        for k in range(2):
            part = t[:, k * pair : (k + 1) * pair].reshape(chunk, depth, pair)
            t_ref[:, (e + k) * depth : (e + k + 1) * depth, :] = part


def factor_kernel(w_ref, wide_ref, offset_ref, wt_ref, wc_ref, pass_ref, rows_ref):
    width = w_ref.shape[1] // 2
    pair = wide_ref.shape[1]
    pass_ref[...] = offset_ref[...]
    rows_ref[...] = wide_ref[...].astype(F32)
    for e in range(width):
        part = rows_ref[pl.ds(e, width, stride=width), :]
        wc_ref[:, e * pair : (e + 1) * pair] = part.astype(BF16)
    same = one_hot(iota((2 * width, 2 * width), 0) == iota((2 * width, 2 * width), 1))
    wt_ref[...] = dot_nt(same, w_ref[...]).astype(BF16)


def weight_kernel(depth, features, *refs):
    up_ref, mi_ref, mj_ref, seen_i_ref, seen_j_ref, wt_ref, perm_ref, wc_ref = refs[:8]
    g_ref, a_ref, b_ref, bt_ref, inv_ref, bias_ref, dw_ref, left_ref = refs[8:16]
    at_ref, v_ref, acc_ref, wide_ref = refs[16:]
    g, last = pl.program_id(0), pl.num_programs(0) - 1
    chunk, block, pair = up_ref.shape
    part_size = inv_ref.shape[2]
    width = wt_ref.shape[0] // 2

    @pl.when(g == 0)
    def _():
        wt = wt_ref[...]
        mi = mi_ref[...]
        a_ref[...] = dot_nt(mi, wt[:width, :]).astype(BF16)
        same = one_hot(iota((features, features), 0) == iota((features, features), 1))
        at_ref[...] = dot_nt(jnp.concatenate([wt[:width, :], same], axis=0), mi).astype(BF16)
        b = jnp.zeros((block, width * depth), F32)
        for s in range(depth):
            part = dot_nt(mj_ref[s], wt[width:, :]).astype(BF16)
            b = b + dot(part, perm_ref[s * width : (s + 1) * width, :])
        b_ref[...] = b.astype(BF16)
        bt_ref[...] = b.T.astype(BF16)
        for k in range(block // part_size):
            rows = slice(k * part_size, (k + 1) * part_size)
            count = dot_nt(seen_j_ref[...], seen_i_ref[rows, :])
            inv_ref[k] = 1.0 / (count + 0.001)
        acc_ref[...] = jnp.zeros_like(acc_ref)
        wide_ref[...] = jnp.zeros_like(wide_ref)
        bias_ref[...] = jnp.zeros_like(bias_ref)

    bias = jnp.zeros((block, pair), F32)
    for k in range(chunk // part_size):
        inv = inv_ref[g * (chunk // part_size) + k]
        for i in range(part_size):
            up = up_ref[k * part_size + i].astype(F32)
            bias = bias + up
            g_ref[k * part_size + i] = (up * inv[:, i : i + 1]).astype(BF16)
    bias_ref[0:1, :] += jnp.sum(bias, axis=0, keepdims=True)
    fill_v(g_ref, bt_ref[...], v_ref, depth)
    span = chunk * depth
    a_t = at_ref[:, pl.ds(pl.multiple_of(g * span, span), span)]
    for e in range(0, width, 2):
        part = dot(a_t, two(v_ref, e))
        for k in range(2):
            rows = slice((e + k) * width, (e + k + 1) * width)
            acc_ref[rows, :] += part[:width, k * pair : (k + 1) * pair]
        wide_ref[:, e * pair : (e + 2) * pair] += part[width:]

    @pl.when(g == last)
    def _():
        dw_ref[...] = acc_ref[...].astype(BF16)
        left = jnp.zeros((width, features), F32)
        for e in range(0, width, 2):
            lanes = slice(e * pair, (e + 2) * pair)
            left = left + dot_nt(wc_ref[:, lanes], wide_ref[:, lanes].astype(BF16))
        left_ref[...] = left


def left_kernel(depth, bit, *refs):
    g_ref, bt_ref, wc_ref, small_ref, keep_ref, go_ref, pass_ref, v_ref, wd_ref, da_ref = refs
    g, last = pl.program_id(0), pl.num_programs(0) - 1
    chunk, _, pair = g_ref.shape
    width = wc_ref.shape[0]
    span = chunk * depth

    @pl.when(g == 0)
    def _():
        pass_ref[...] = small_ref[...]
        same = one_hot(iota((2 * pair, 2 * pair), 0) == iota((2 * pair, 2 * pair), 1))
        for at in range(0, wd_ref.shape[0], 2 * pair):
            wd_ref[at : at + 2 * pair, :] = dot_nt(same, wc_ref[:, at : at + 2 * pair]).astype(BF16)

    fill_v(g_ref, bt_ref[...], v_ref, depth)
    d_a = []
    each = width // 4
    for e in range(0, width, each):
        v = jnp.concatenate([v_ref[e + k] for k in range(each)], axis=1)
        d_a.append(dot(v, wd_ref[e * pair : (e + each) * pair, :]))
    d_a = (d_a[0] + d_a[1]) + (d_a[2] + d_a[3])
    same = one_hot(iota((width, width), 0) == iota((width, width), 1))
    d_a = dot_nt(same, d_a.astype(BF16)).astype(BF16)
    tiles = span // LANES
    for k in range(tiles):
        da_ref[g * tiles + k] = d_a[:, k * LANES : (k + 1) * LANES]

    @pl.when(g == last)
    def _():
        half = keep_ref.shape[0]
        here = (lax.axis_index("col") >> bit) & 1
        keep_ref[...] = da_ref[pl.ds(here * half, half)]
        go_ref[...] = da_ref[pl.ds((1 - here) * half, half)]


def token_kernel(depth, features, n, *refs):
    g_ref, a_ref, wc_ref, mj_ref, perm_ref, bias_ref, left_ref = refs[:7]
    small_ref, out_ref, t_ref, db_ref = refs[-4:]
    g, last = pl.program_id(0), pl.num_programs(0) - 1
    chunk, block = g_ref.shape[:2]
    width = left_ref.shape[0]

    @pl.when(g == 0)
    def _():
        db_ref[...] = jnp.zeros_like(db_ref)

    span = chunk * depth
    fill_t(a_ref[pl.ds(pl.multiple_of(g * span, span), span), :], wc_ref, t_ref, depth)
    t = jnp.concatenate([t_ref[i] for i in range(chunk)], axis=1)
    scaled = jnp.concatenate([g_ref[i] for i in range(chunk)], axis=1)
    db_ref[...] += dot_nt(t, scaled)

    @pl.when(g == last)
    def _():
        d_b = db_ref[...].T.astype(BF16)
        own = block // n
        for k in range(n):
            part = d_b[k * own : (k + 1) * own, :]
            for q in range(part.shape[1] // LANES):
                out_ref[k, q * own : (q + 1) * own, :] = part[:, q * LANES : (q + 1) * LANES]
        turned = dot_nt(perm_ref[...], d_b).astype(BF16)
        right = jnp.zeros((width, features), F32)
        for s in range(depth):
            right = right + dot(turned[s * width : (s + 1) * width, :], mj_ref[s])
        small = jnp.concatenate([left_ref[...], right], axis=1)
        small_ref[0:width, :] = small.astype(BF16)
        small_ref[width:, :] = jnp.broadcast_to(bias_ref[0:1, :], (16, LANES)).astype(BF16)


def update_kernel(depth, *refs):
    inv_ref, a_ref, b_ref, offset_ref, wc_ref, small_ref, out_ref, pass_ref, t_ref = refs
    g = pl.program_id(0)
    chunk, block, pair = out_ref.shape

    @pl.when(g == 0)
    def _():
        pass_ref[...] = small_ref[...]

    span = chunk * depth
    fill_t(a_ref[pl.ds(pl.multiple_of(g * span, span), span), :], wc_ref, t_ref, depth)
    inv = inv_ref[g]
    b = b_ref[...]
    offset = offset_ref[...]
    for at in range(0, chunk, 2):
        part = dot(b, two(t_ref, at))
        for k in range(2):
            value = part[:, k * pair : (k + 1) * pair] * inv[:, at + k : at + k + 1] + offset
            out_ref[at + k] = value.astype(BF16)


def owner_kernel(depth, own, features, *refs):
    da_refs, db_ref, small_refs = refs[:2], refs[2], refs[3:5]
    x_ref, wt_ref, perm_ref, dw_ref = refs[5:9]
    out_ref, factors_ref, bias_ref, placed_ref = refs[9:]
    for e in range(dw_ref.shape[0]):
        placed_ref[:, e, :] = dw_ref[e].astype(F32)
    rows = depth * own
    width = wt_ref.shape[0] // 2
    p, q = iota((rows, rows), 0), iota((rows, rows), 1)
    swap = one_hot(q == (p % own) * depth + p // own)
    d_a = dot_nt(swap, da_refs[0][...]) + dot_nt(swap, da_refs[1][...])
    d_b = dot_nt(db_ref[...], perm_ref[...])
    d_b = jnp.concatenate([d_b[:, s * width : (s + 1) * width] for s in range(depth)], axis=0)
    highest = lax.Precision.HIGHEST
    wt = wt_ref[...].astype(F32)
    d_normed = jnp.dot(d_a, wt[:width, :], precision=highest, preferred_element_type=F32)
    d_normed = d_normed + jnp.dot(d_b, wt[width:, :], precision=highest, preferred_element_type=F32)
    x = x_ref[...].astype(F32)
    d_normed = d_normed * x[:, features : features + 1]
    normed, scale = stats(x[:, :features])
    mean = jnp.mean(d_normed, axis=-1, keepdims=True)
    along = jnp.mean(d_normed * normed, axis=-1, keepdims=True)
    out_ref[...] = scale * (d_normed - mean - normed * along)
    small = small_refs[0][...].astype(F32) + small_refs[1][...].astype(F32)
    turned = small[:width].T
    factors_ref[...] = jnp.concatenate([turned[:features], turned[features:]], axis=1)
    bias_ref[...] = small[width : width + 1]


def lay_back(x, rows, lanes):
    if lanes % LANES:
        return x.reshape(rows, lanes)
    return x.reshape(lanes // LANES, rows, LANES).transpose(1, 0, 2).reshape(rows, lanes)


def bit_of(axis, bit):
    return (lax.axis_index(axis) >> bit) & 1


def swap_parts(parts, axis, bit, n):
    parts = [part.reshape(-1, LANES) for part in parts]
    message = jnp.concatenate(parts, axis=0) if len(parts) > 1 else parts[0]
    pairs = [(i, i ^ (1 << bit)) for i in range(n)]
    message = lax.ppermute(message, axis, pairs)
    got, at = [], 0
    for part in parts:
        got.append(message[at : at + part.shape[0]])
        at += part.shape[0]
    return got


def halves(x, axis, bit, at):
    here = bit_of(axis, bit)
    keep = lax.dynamic_index_in_dim(x, here, at, keepdims=False)
    return keep, lax.dynamic_index_in_dim(x, 1 - here, at, keepdims=False)


def split_high(x):
    return x.reshape((2, x.shape[0] // 2) + x.shape[1:])


def in_order(mine, other, axis, bit, at):
    first = bit_of(axis, bit) == 0
    low = jnp.where(first, mine, other)
    return jnp.stack([low, jnp.where(first, other, mine)], axis=at)


def unswap(x, axis):
    n = x.shape[0]
    for bit in range(n.bit_length() - 1):
        y = x.reshape((n >> (bit + 1), 2, 1 << bit) + x.shape[1:])
        x = jnp.where(bit_of(axis, bit) == 0, y, y[:, ::-1]).reshape(x.shape)
    return x


def add(mine, other):
    other = other.reshape(mine.shape)
    return lax.optimization_barrier((mine.astype(F32) + other.astype(F32)).astype(BF16))


def per_device(
    n,
    alignment_embedding,
    alignment_cell_exists,
    alignment_lines_exist,
    sitewise_factors,
    pairing_matrix,
    offset_vector,
    upstream_adjoint,
):
    depth, own, features = alignment_embedding.shape
    width = sitewise_factors.shape[1] // 2
    block, pair = upstream_adjoint.shape[0], upstream_adjoint.shape[2]
    rows, chunk = depth * own, 16
    steps = block // chunk
    split = own % 16 == 0
    axes = ("row", "col")
    sds = jax.ShapeDtypeStruct

    bits = n.bit_length() - 1
    mask = (alignment_cell_exists * alignment_lines_exist[:, None]).astype(BF16)
    mask = jnp.broadcast_to(mask[:, :, None], (depth, own, LANES - features))
    x = jnp.concatenate([alignment_embedding, mask], axis=2).reshape(rows, LANES)
    offset = offset_vector.reshape(1, pair)
    out_shapes = [sds((rows // 2 + own, LANES), BF16)] * 2
    by_token, by_row = call(
        functools.partial(prep_kernel, depth, own, features),
        (),
        [full(x.shape)],
        [full(o.shape) for o in out_shapes],
        out_shapes,
    )(x)
    message = by_token
    held = [message]
    for k in range(1, n):
        held.append(lax.ppermute(message, "col", [(j, j ^ k) for j in range(n)]))
    held = unswap(jnp.stack(held), "col")
    seen_i = held[:, rows // 2 :].reshape(block, LANES)
    parts = held[:, : rows // 2].reshape(n, rows // 2, 2, features)
    mi = parts.transpose(0, 2, 1, 3).reshape(block * depth, features)
    message = by_row
    held = []
    for k in range(n):
        pairs = [(i * n + j, (j ^ k) * n + i) for i in range(n) for j in range(n)]
        held.append(lax.ppermute(message, axes, pairs))
    held = unswap(jnp.stack(held), "row")
    seen_j = held[:, rows // 2 :].reshape(block, LANES)
    parts = held[:, : rows // 2].reshape(n, depth // 2, own, 2, features)
    mj = parts.transpose(3, 1, 0, 2, 4).reshape(depth, block, features)

    wide = width * depth
    tokens = block * depth
    source = jnp.arange(wide)
    perm = (jnp.arange(wide)[None, :] == (source % width * depth + source // width)[:, None]).astype(BF16)
    up_spec = pl.BlockSpec((chunk, block, pair), lambda g: (g, 0, 0))
    args = (sitewise_factors, pairing_matrix, offset)
    out_shapes = [
        sds((2 * width, features), BF16),
        sds((width, width * pair), BF16),
        sds((1, pair), F32),
    ]
    factors_t, pairing_wide, offset = call(
        factor_kernel,
        (),
        [full(v.shape) for v in args],
        [full(o.shape) for o in out_shapes],
        out_shapes,
        [pltpu.VMEM((width * width, pair), F32)],
    )(*args)

    out_shapes = [
        sds((tokens, width), BF16),
        sds((block, wide), BF16),
        sds((wide, block), BF16),
        sds((steps, block, chunk), F32),
        sds((8, pair), F32),
        sds((width * width, pair), BF16),
        sds((width, features), F32),
    ]
    args = (mi, mj, seen_i, seen_j, factors_t, perm, pairing_wide)
    large = 2 * chunk
    large_spec = pl.BlockSpec((large, block, pair), lambda g: (g, 0, 0))
    outs = call(
        functools.partial(weight_kernel, depth, features),
        (block // large,),
        [large_spec] + [full(v.shape) for v in args],
        [large_spec] + [full(o.shape) for o in out_shapes],
        [sds(upstream_adjoint.shape, BF16)] + out_shapes,
        [
            pltpu.VMEM((width + features, tokens), BF16),
            pltpu.VMEM((width, large * depth, pair), BF16),
            pltpu.VMEM((width * width, pair), F32),
            pltpu.VMEM((features, width * pair), F32),
        ],
        cost(5e9, 8e6),
    )(upstream_adjoint, *args)
    scaled, a, b, b_t, inv, bias, d_pairing, left = outs

    d_pairing = d_pairing.reshape(n, -1, LANES)
    for bit in reversed(range(1, bits)):
        keep, go = halves(split_high(d_pairing), "col", bit, 0)
        d_pairing = add(keep, *swap_parts([go], "col", bit, n))

    out_shapes = [sds((width + 16, LANES), BF16), sds((n, own * wide // LANES, LANES), BF16)]
    small, d_b = call(
        functools.partial(token_kernel, depth, features, n),
        (steps,),
        [up_spec]
        + [full(v.shape) for v in (a, pairing_wide, mj, perm, bias, left)]
        + [pl.BlockSpec(memory_space=pl.ANY)] * 4,
        [full(o.shape) for o in out_shapes],
        out_shapes,
        [pltpu.VMEM((chunk, wide, pair), BF16), pltpu.VMEM((wide, block), F32)],
        cost(8e9, 8e6),
    )(scaled, a, pairing_wide, mj, perm, bias, left, b, b_t, inv, offset)

    dp_keep, dp_go = halves(d_pairing, "col", 0, 0)
    db_keep, db_go = halves(d_b.reshape((n // 2, 2) + d_b.shape[1:]), "col", 0, 1)
    parts = swap_parts([dp_go, db_go, small], "col", 0, n)
    d_pairing, small = add(dp_keep, parts[0]), add(small, parts[2])
    d_b = in_order(db_keep, parts[1].reshape(db_keep.shape), "col", 0, 1)
    db_keep, db_go = halves(d_b, "row", 0, 1)
    for bit in range(bits):
        parts = swap_parts([d_pairing, db_go, small], "row", bit, n)
        if bit == 0:
            args = (inv, a, b, offset, pairing_wide, small)
            coupling_update, small = call(
                functools.partial(update_kernel, depth),
                (steps,),
                [full(v.shape) for v in args],
                [up_spec, full(small.shape)],
                [sds((block, block, pair), BF16), sds(small.shape, BF16)],
                [pltpu.VMEM((chunk, wide, pair), BF16)],
                cost(6e9, 8e6),
            )(*args)
        if bit == 1:
            half = (tokens // LANES // 2, width, LANES)
            out_shapes = [sds(half, BF16), sds(half, BF16), sds(small.shape, BF16)]
            *d_a, small = call(
                functools.partial(left_kernel, depth, bits - 1),
                (steps,),
                [up_spec] + [full(v.shape) for v in (b_t, pairing_wide, small)],
                [full(o.shape) for o in out_shapes],
                out_shapes,
                [
                    pltpu.VMEM((width, chunk * depth, pair), BF16),
                    pltpu.VMEM((width * pair, width), BF16),
                    pltpu.VMEM((tokens // LANES, width, LANES), BF16),
                ],
                cost(6e9, 8e6),
            )(scaled, b_t, pairing_wide, small)
            if rows % LANES:
                shape = (-1, width, LANES // rows, rows)
                d_a = [part.reshape(shape).transpose(0, 2, 1, 3) for part in d_a]
            da_keep, da_go = [part.reshape(n // 2, -1, LANES) for part in d_a]
        d_pairing, d_b, small = add(d_pairing, parts[0]), add(db_keep, parts[1]), add(small, parts[2])
        db_keep = db_go = d_b
    d_pairing = d_pairing.reshape(1, -1, LANES)
    small_parts = [small]
    for bit in reversed(range(1, bits)):
        if bit < bits - 1:
            small_parts = [add(*small_parts)]
            da_keep, da_go = halves(split_high(add(*da_parts)), "col", bit, 0)
        db_keep, db_go = halves(split_high(d_b), "col", bit, 0)
        parts = swap_parts([d_pairing, db_go, da_go, small_parts[0]], "col", bit, n)
        d_pairing = in_order(d_pairing, parts[0].reshape(d_pairing.shape), "col", bit, 1)
        d_pairing = d_pairing.reshape((-1,) + d_pairing.shape[2:])
        mine = bit_of("col", bit) == bit_of("row", bit)
        d_b = jnp.where(mine, db_keep, parts[1].reshape(db_keep.shape))
        da_parts = [da_keep, parts[2].reshape(da_keep.shape)]
        small_parts = [small_parts[0], parts[3]]
    da_keep, da_go = halves(add(*da_parts), "col", 0, 0)
    got, da_got = swap_parts([d_pairing, da_go], "col", 0, n)
    d_pairing = in_order(d_pairing, got.reshape(d_pairing.shape), "col", 0, 1)
    d_a = [lay_back(part.reshape(-1, LANES), width, rows) for part in (da_keep, da_got)]
    d_b = lay_back(d_b[0], own, wide)

    d_pairing = d_pairing.reshape(width, width, pair)
    args = (*d_a, d_b, *small_parts, x, factors_t, perm, d_pairing)
    out_shapes = [
        sds((rows, features), F32),
        sds((features, 2 * width), F32),
        sds((1, pair), F32),
        sds((width, width, pair), F32),
    ]
    embedding_adjoint, factors_adjoint, offset_slope, placed = call(
        functools.partial(owner_kernel, depth, own, features),
        (),
        [full(v.shape) for v in args],
        [full(o.shape) for o in out_shapes],
        out_shapes,
    )(*args)
    return (
        coupling_update,
        embedding_adjoint.reshape(depth, own, features),
        factors_adjoint,
        placed.reshape(width * width, pair),
        offset_slope.reshape(pair),
    )


def solution(mesh):
    n = mesh.shape["col"]
    placed = (
        P(None, ("groups", "row", "col"), None),
        P(None, ("groups", "row", "col")),
        P("groups"),
        P(),
        P(),
        P(),
        P(("groups", "row"), "col", None),
    )
    return jax.shard_map(
        functools.partial(per_device, n),
        mesh=mesh,
        in_specs=placed,
        out_specs=(
            P(("groups", "row"), "col", None),
            P(None, ("groups", "row", "col"), None),
            P("groups", None),
            P("groups", None),
            P("groups"),
        ),
        check_vma=False,
    )
```

```python
import functools

import jax
import jax.numpy as jnp
from jax import lax
from jax.experimental import pallas as pl
from jax.experimental.pallas import tpu as pltpu
from jax.sharding import PartitionSpec as P

F32 = jnp.float32
BF16 = jnp.bfloat16
LANES = 128
VMEM_LIMIT = 24 * 1024 * 1024
NT = (((1,), (1,)), ((), ()))


def dot(left, right):
    return jnp.dot(left, right, preferred_element_type=F32)


def dot_nt(left, right):
    return lax.dot_general(left, right, NT, preferred_element_type=F32)


def iota(shape, axis):
    return lax.broadcasted_iota(jnp.int32, shape, axis)


def one_hot(mask):
    return jnp.where(mask, 1.0, 0.0).astype(BF16)


def full(shape):
    return pl.BlockSpec(shape, lambda *g: (0,) * len(shape))


def cost(flops, nbytes):
    return pl.CostEstimate(flops=int(flops), bytes_accessed=int(nbytes), transcendentals=0)


def call(kernel, grid, in_specs, out_specs, out_shape, scratch=(), estimate=None):
    return pl.pallas_call(
        kernel,
        grid=grid,
        in_specs=in_specs,
        out_specs=out_specs,
        out_shape=out_shape,
        scratch_shapes=list(scratch),
        compiler_params=pltpu.CompilerParams(vmem_limit_bytes=VMEM_LIMIT),
        cost_estimate=estimate,
    )


def stats(x):
    center = x - jnp.mean(x, axis=-1, keepdims=True)
    scale = lax.rsqrt(jnp.mean(center * center, axis=-1, keepdims=True) + 1e-05)
    return center * scale, scale


def prep_kernel(depth, own, features, x_ref, by_token_ref, by_row_ref):
    rows = depth * own
    half = rows // 2
    x = x_ref[...].astype(F32)
    weight = x[:, features : features + 1]
    normed, _ = stats(x[:, :features])
    masked = normed.astype(BF16).astype(F32) * weight
    by_row_ref[:half, :] = jnp.concatenate([masked[:half], masked[half:]], axis=1).astype(BF16)
    p, q = iota((rows, rows), 0), iota((rows, rows), 1)
    swap = one_hot(q == (p % depth) * own + p // depth)
    turned = dot(swap, masked.astype(BF16))
    by_token_ref[:half, :] = jnp.concatenate([turned[:half], turned[half:]], axis=1).astype(BF16)
    here = one_hot(iota((own, rows), 0) == iota((own, rows), 1) % own)
    at = iota((rows, LANES), 1) == iota((rows, LANES), 0) // own
    mask = dot(here, jnp.where(at, weight, 0.0).astype(BF16)).astype(BF16)
    by_row_ref[half:, :] = mask
    by_token_ref[half:, :] = mask


def two(ref, at):
    return jnp.concatenate([ref[at], ref[at + 1]], axis=1)


def fill_v(g_ref, bt, v_ref, depth):
    chunk, _, pair = g_ref.shape
    width = v_ref.shape[0]
    for at in range(0, chunk, 2):
        v = dot(bt, two(g_ref, at)).astype(BF16)
        for k in range(2):
            part = v[:, k * pair : (k + 1) * pair].reshape(width, depth, pair)
            v_ref[:, (at + k) * depth : (at + k + 1) * depth, :] = part


def fill_t(a_chunk, wc_ref, t_ref, depth):
    chunk, wide, pair = t_ref.shape
    width = wide // depth
    for e in range(0, width, 2):
        t = dot(a_chunk, wc_ref[:, e * pair : (e + 2) * pair]).astype(BF16)
        for k in range(2):
            part = t[:, k * pair : (k + 1) * pair].reshape(chunk, depth, pair)
            t_ref[:, (e + k) * depth : (e + k + 1) * depth, :] = part


def held_b(held_ref, block, width, depth):
    at = block * depth
    tiles = width * depth // LANES
    return jnp.concatenate([held_ref[at + k * block : at + (k + 1) * block, :] for k in range(tiles)], axis=1)


def factor_kernel(own, pieces, w_ref, wide_ref, offset_ref, up_ref, *refs):
    wt_ref, wc_ref, pass_ref, bias_ref, a_ref, at_ref, seen_ref, rows_ref, mi_ref = refs[pieces:]
    features, width = w_ref.shape[0], w_ref.shape[1] // 2
    pair = wide_ref.shape[1]
    if own % 16 == 0:
        half = refs[0].shape[1] - own
        for k in range(pieces):
            for core in range(2):
                at = ((lax.axis_index("col") >> 1) ^ k) * 2 + core
                for q in range(2):
                    rows = pl.ds(pl.multiple_of((at * 2 + q) * half, half), half)
                    mi_ref[rows, :] = refs[k][core, :half, q * features : (q + 1) * features]
                rows = pl.ds(pl.multiple_of(at * own, own), own)
                seen_ref[rows, :] = refs[k][core, half:, :]
    else:
        mi_ref[...] = refs[0][...]
        seen_ref[...] = refs[1][...]
    pass_ref[...] = offset_ref[...]
    rows_ref[...] = wide_ref[...].astype(F32)
    for e in range(width):
        part = rows_ref[pl.ds(e, width, stride=width), :]
        wc_ref[:, e * pair : (e + 1) * pair] = part.astype(BF16)
    same = one_hot(iota((2 * width, 2 * width), 0) == iota((2 * width, 2 * width), 1))
    wt = dot_nt(same, w_ref[...]).astype(BF16)
    wt_ref[...] = wt
    mi = mi_ref[...]
    a_ref[...] = dot_nt(mi, wt[:width, :]).astype(BF16)
    same = one_hot(iota((features, features), 0) == iota((features, features), 1))
    at_ref[...] = dot_nt(jnp.concatenate([wt[:width, :], same], axis=0), mi).astype(BF16)
    bias = [jnp.zeros(up_ref.shape[1:], F32)] * 2
    for i in range(up_ref.shape[0]):
        bias[i % 2] = bias[i % 2] + up_ref[i].astype(F32)
    bias = jnp.sum(bias[0] + bias[1], axis=0, keepdims=True)
    bias_ref[...] = jnp.broadcast_to(bias, bias_ref.shape)


def weight_kernel(depth, features, own, pieces, part_size, *refs):
    up_ref, a_ref, at_ref, seen_i_ref, wt_ref, perm_ref, wc_ref = refs[:7]
    j_refs, refs = refs[7 : 7 + pieces], refs[7 + pieces :]
    g_ref, held_ref, dw_ref, left_ref, mj_ref, seen_j_ref, bt_ref, inv_ref, v_ref, acc_ref, wide_ref = refs
    g, last = pl.program_id(0), pl.num_programs(0) - 1
    chunk, block, pair = up_ref.shape
    width = wt_ref.shape[0] // 2

    @pl.when(g == 0)
    def _():
        if own % 16 == 0:
            half = depth // 2
            for k in range(pieces):
                for core in range(2):
                    at = ((lax.axis_index("row") >> 1) ^ k) * 2 + core
                    rows = pl.ds(pl.multiple_of(at * own, own), own)
                    seen_j_ref[rows, :] = j_refs[k][core, :own, :]
                    for s in range(depth):
                        lanes = slice(s // half * features, (s // half + 1) * features)
                        start = own + s % half * own
                        mj_ref[s, rows, :] = j_refs[k][core, start : start + own, lanes]
        else:
            mj_ref[...] = j_refs[0][...]
            seen_j_ref[...] = j_refs[1][...]
        wt = wt_ref[...]
        b = jnp.zeros((block, width * depth), F32)
        for s in range(depth):
            part = dot_nt(mj_ref[s], wt[width:, :]).astype(BF16)
            b = b + dot(part, perm_ref[s * width : (s + 1) * width, :])
        bt_ref[...] = b.T.astype(BF16)
        at = block * depth
        held_ref[:at, :width] = a_ref[...]
        for k in range(width * depth // LANES):
            held_ref[at : at + block, :] = b[:, k * LANES : (k + 1) * LANES].astype(BF16)
            at += block
        for k in range(block // part_size):
            rows = slice(k * part_size, (k + 1) * part_size)
            count = dot_nt(seen_j_ref[...], seen_i_ref[rows, :])
            inv_ref[k] = 1.0 / (count + 0.001)
            held_ref[at : at + block, :part_size] = count.astype(BF16)
            at += block
        acc_ref[...] = jnp.zeros_like(acc_ref)
        wide_ref[...] = jnp.zeros_like(wide_ref)

    for k in range(chunk // part_size):
        inv = inv_ref[g * (chunk // part_size) + k]
        for i in range(part_size):
            up = up_ref[k * part_size + i].astype(F32)
            g_ref[k * part_size + i] = (up * inv[:, i : i + 1]).astype(BF16)
    fill_v(g_ref, bt_ref[...], v_ref, depth)
    span = chunk * depth
    a_t = at_ref[:, pl.ds(pl.multiple_of(g * span, span), span)]
    for e in range(0, width, 2):
        part = dot(a_t, two(v_ref, e))
        for k in range(2):
            rows = slice((e + k) * width, (e + k + 1) * width)
            acc_ref[rows, :] += part[:width, k * pair : (k + 1) * pair]
        wide_ref[:, e * pair : (e + 2) * pair] += part[width:]

    @pl.when(g == last)
    def _():
        dw_ref[...] = acc_ref[...].astype(BF16)
        left = jnp.zeros((width, features), F32)
        for e in range(0, width, 2):
            lanes = slice(e * pair, (e + 2) * pair)
            left = left + dot_nt(wc_ref[:, lanes], wide_ref[:, lanes].astype(BF16))
        left_ref[...] = left


def left_kernel(depth, bit, *refs):
    g_ref, held_ref, wc_ref, small_ref, keep_ref, go_ref, pass_ref, v_ref, wd_ref, da_ref, bt_ref = refs
    g, last = pl.program_id(0), pl.num_programs(0) - 1
    chunk, block, pair = g_ref.shape
    width = wc_ref.shape[0]
    span = chunk * depth

    @pl.when(g == 0)
    def _():
        pass_ref[...] = small_ref[...]
        bt_ref[...] = held_b(held_ref, block, width, depth).astype(F32).T.astype(BF16)
        same = one_hot(iota((2 * pair, 2 * pair), 0) == iota((2 * pair, 2 * pair), 1))
        for at in range(0, wd_ref.shape[0], 2 * pair):
            wd_ref[at : at + 2 * pair, :] = dot_nt(same, wc_ref[:, at : at + 2 * pair]).astype(BF16)

    fill_v(g_ref, bt_ref[...], v_ref, depth)
    d_a = []
    each = width // 4
    for e in range(0, width, each):
        v = jnp.concatenate([v_ref[e + k] for k in range(each)], axis=1)
        d_a.append(dot(v, wd_ref[e * pair : (e + each) * pair, :]))
    d_a = (d_a[0] + d_a[1]) + (d_a[2] + d_a[3])
    same = one_hot(iota((width, width), 0) == iota((width, width), 1))
    d_a = dot_nt(same, d_a.astype(BF16)).astype(BF16)
    tiles = span // LANES
    for k in range(tiles):
        da_ref[g * tiles + k] = d_a[:, k * LANES : (k + 1) * LANES]

    @pl.when(g == last)
    def _():
        half = keep_ref.shape[0]
        here = (lax.axis_index("col") >> bit) & 1
        keep_ref[...] = da_ref[pl.ds(here * half, half)]
        go_ref[...] = da_ref[pl.ds((1 - here) * half, half)]


def token_kernel(depth, features, n, *refs):
    g_ref, held_ref, wc_ref, mj_ref, perm_ref, bias_ref, left_ref = refs[:7]
    small_ref, out_ref, t_ref, db_ref = refs[7:]
    g, last = pl.program_id(0), pl.num_programs(0) - 1
    chunk, block = g_ref.shape[:2]
    width = left_ref.shape[0]

    @pl.when(g == 0)
    def _():
        db_ref[...] = jnp.zeros_like(db_ref)

    span = chunk * depth
    fill_t(held_ref[pl.ds(pl.multiple_of(g * span, span), span), :width], wc_ref, t_ref, depth)
    t = jnp.concatenate([t_ref[i] for i in range(chunk)], axis=1)
    scaled = jnp.concatenate([g_ref[i] for i in range(chunk)], axis=1)
    db_ref[...] += dot_nt(t, scaled)

    @pl.when(g == last)
    def _():
        d_b = db_ref[...].T.astype(BF16)
        own = block // n
        for k in range(n):
            part = d_b[k * own : (k + 1) * own, :]
            for q in range(part.shape[1] // LANES):
                out_ref[k, q * own : (q + 1) * own, :] = part[:, q * LANES : (q + 1) * LANES]
        turned = dot_nt(perm_ref[...], d_b).astype(BF16)
        right = jnp.zeros((width, features), F32)
        for s in range(depth):
            right = right + dot(turned[s * width : (s + 1) * width, :], mj_ref[s])
        small = jnp.concatenate([left_ref[...], right], axis=1)
        small_ref[0:width, :] = small.astype(BF16)
        small_ref[width:, :] = jnp.broadcast_to(bias_ref[0:1, :], (16, LANES)).astype(BF16)


def update_kernel(depth, *refs):
    held_ref, offset_ref, wc_ref, small_ref, out_ref, pass_ref, t_ref = refs
    g = pl.program_id(0)
    chunk, block, pair = out_ref.shape
    width = wc_ref.shape[0]

    @pl.when(g == 0)
    def _():
        pass_ref[...] = small_ref[...]

    span = chunk * depth
    fill_t(held_ref[pl.ds(pl.multiple_of(g * span, span), span), :width], wc_ref, t_ref, depth)
    rows = held_ref.shape[0] - (pl.num_programs(0) - g) * block
    count = held_ref[pl.ds(pl.multiple_of(rows, block), block), :chunk]
    inv = 1.0 / (count.astype(F32) + 0.001)
    b = held_b(held_ref, block, width, depth)
    offset = offset_ref[...]
    for at in range(0, chunk, 2):
        part = dot(b, two(t_ref, at))
        for k in range(2):
            value = part[:, k * pair : (k + 1) * pair] * inv[:, at + k : at + k + 1] + offset
            out_ref[at + k] = value.astype(BF16)


def owner_kernel(depth, own, features, *refs):
    da_refs, db_ref, small_refs = refs[:2], refs[2], refs[3:5]
    x_ref, wt_ref, perm_ref, dw_ref = refs[5:9]
    out_ref, factors_ref, bias_ref, placed_ref = refs[9:]
    for e in range(dw_ref.shape[0]):
        placed_ref[:, e, :] = dw_ref[e].astype(F32)
    rows = depth * own
    width = wt_ref.shape[0] // 2
    p, q = iota((rows, rows), 0), iota((rows, rows), 1)
    swap = one_hot(q == (p % own) * depth + p // own)
    d_a = dot_nt(swap, da_refs[0][...]) + dot_nt(swap, da_refs[1][...])
    d_b = dot_nt(db_ref[...], perm_ref[...])
    d_b = jnp.concatenate([d_b[:, s * width : (s + 1) * width] for s in range(depth)], axis=0)
    highest = lax.Precision.HIGHEST
    wt = wt_ref[...].astype(F32)
    d_normed = jnp.dot(d_a, wt[:width, :], precision=highest, preferred_element_type=F32)
    d_normed = d_normed + jnp.dot(d_b, wt[width:, :], precision=highest, preferred_element_type=F32)
    x = x_ref[...].astype(F32)
    d_normed = d_normed * x[:, features : features + 1]
    normed, scale = stats(x[:, :features])
    mean = jnp.mean(d_normed, axis=-1, keepdims=True)
    along = jnp.mean(d_normed * normed, axis=-1, keepdims=True)
    out_ref[...] = scale * (d_normed - mean - normed * along)
    small = small_refs[0][...].astype(F32) + small_refs[1][...].astype(F32)
    turned = small[:width].T
    factors_ref[...] = jnp.concatenate([turned[:features], turned[features:]], axis=1)
    bias_ref[...] = small[width : width + 1]


def lay_back(x, rows, lanes):
    if lanes % LANES:
        return x.reshape(rows, lanes)
    return x.reshape(lanes // LANES, rows, LANES).transpose(1, 0, 2).reshape(rows, lanes)


def bit_of(axis, bit):
    return (lax.axis_index(axis) >> bit) & 1


def swap_parts(parts, axis, bit, n):
    parts = [part.reshape(-1, LANES) for part in parts]
    message = jnp.concatenate(parts, axis=0) if len(parts) > 1 else parts[0]
    pairs = [(i, i ^ (1 << bit)) for i in range(n)]
    message = lax.ppermute(message, axis, pairs)
    got, at = [], 0
    for part in parts:
        got.append(message[at : at + part.shape[0]])
        at += part.shape[0]
    return got


def halves(x, axis, bit, at):
    here = bit_of(axis, bit)
    keep = lax.dynamic_index_in_dim(x, here, at, keepdims=False)
    return keep, lax.dynamic_index_in_dim(x, 1 - here, at, keepdims=False)


def split_high(x):
    return x.reshape((2, x.shape[0] // 2) + x.shape[1:])


def in_order(mine, other, axis, bit, at):
    first = bit_of(axis, bit) == 0
    low = jnp.where(first, mine, other)
    return jnp.stack([low, jnp.where(first, other, mine)], axis=at)


def unswap(x, axis):
    n = x.shape[0]
    for bit in range(n.bit_length() - 1):
        y = x.reshape((n >> (bit + 1), 2, 1 << bit) + x.shape[1:])
        x = jnp.where(bit_of(axis, bit + 1) == 0, y, y[:, ::-1]).reshape(x.shape)
    return x


def add(mine, other):
    other = other.reshape(mine.shape)
    return lax.optimization_barrier((mine.astype(F32) + other.astype(F32)).astype(BF16))


def per_device(
    n,
    alignment_embedding,
    alignment_cell_exists,
    alignment_lines_exist,
    sitewise_factors,
    pairing_matrix,
    offset_vector,
    upstream_adjoint,
):
    depth, own, features = alignment_embedding.shape
    width = sitewise_factors.shape[1] // 2
    block, pair = upstream_adjoint.shape[0], upstream_adjoint.shape[2]
    rows, chunk = depth * own, 16
    steps = block // chunk
    split = own % 16 == 0
    axes = ("row", "col")
    sds = jax.ShapeDtypeStruct

    bits = n.bit_length() - 1
    mask = (alignment_cell_exists * alignment_lines_exist[:, None]).astype(BF16)
    mask = jnp.broadcast_to(mask[:, :, None], (depth, own, LANES - features))
    x = jnp.concatenate([alignment_embedding, mask], axis=2).reshape(rows, LANES)
    offset = offset_vector.reshape(1, pair)
    out_shapes = [sds((rows // 2 + own, LANES), BF16)] * 2
    by_token, by_row = call(
        functools.partial(prep_kernel, depth, own, features),
        (),
        [full(x.shape)],
        [full(o.shape) for o in out_shapes],
        out_shapes,
    )(x)
    message = jnp.concatenate([by_token, by_row[: rows // 2]], axis=0)
    both = in_order(message, *swap_parts([message], "col", 0, n), "col", 0, 0)
    message = both[:, : rows // 2 + own]
    held = [message]
    for k in range(2, n, 2):
        held.append(lax.ppermute(message, "col", [(j, j ^ k) for j in range(n)]))
    a_pieces = held
    if own % 16:
        held = unswap(jnp.stack(held), "col").reshape((n,) + message.shape[1:])
        parts = held[:, : rows // 2].reshape(n, rows // 2, 2, features)
        mi = parts.transpose(0, 2, 1, 3).reshape(block * depth, features)
        a_pieces = [mi, held[:, rows // 2 :].reshape(block, LANES)]
    message = both[:, rows // 2 :]
    held = []
    for k in range(0, n, 2):
        pairs = [(i * n + j, (j ^ k) * n + i) for i in range(n) for j in range(n)]
        held.append(lax.ppermute(message, axes, pairs))
    j_pieces = held
    if own % 16:
        held = unswap(jnp.stack(held), "row").reshape((n,) + message.shape[1:])
        parts = held[:, own:].reshape(n, depth // 2, own, 2, features)
        mj = parts.transpose(3, 1, 0, 2, 4).reshape(depth, block, features)
        j_pieces = [mj, held[:, :own].reshape(block, LANES)]

    wide = width * depth
    tokens = block * depth
    source = jnp.arange(wide)
    perm = (jnp.arange(wide)[None, :] == (source % width * depth + source // width)[:, None]).astype(BF16)
    up_spec = pl.BlockSpec((chunk, block, pair), lambda g: (g, 0, 0))
    args = (sitewise_factors, pairing_matrix, offset, upstream_adjoint, *a_pieces)
    out_shapes = [
        sds((2 * width, features), BF16),
        sds((width, width * pair), BF16),
        sds((1, pair), F32),
        sds((8, pair), F32),
        sds((tokens, width), BF16),
        sds((width + features, tokens), BF16),
        sds((block, LANES), BF16),
    ]
    factors_t, pairing_wide, offset, bias, a, a_t, seen = call(
        functools.partial(factor_kernel, own, len(a_pieces)),
        (),
        [full(v.shape) for v in args],
        [full(o.shape) for o in out_shapes],
        out_shapes,
        [pltpu.VMEM((width * width, pair), F32), pltpu.VMEM((tokens, features), BF16)],
        cost(3e9, 4e6),
    )(*args)

    out_shapes = [
        sds((tokens + block * wide // LANES + block * steps, LANES), BF16),
        sds((width * width, pair), BF16),
        sds((width, features), F32),
        sds((depth, block, features), BF16),
    ]
    args = (a, a_t, seen, factors_t, perm, pairing_wide, *j_pieces)
    large = 2 * chunk
    large_spec = pl.BlockSpec((large, block, pair), lambda g: (g, 0, 0))
    scaled, held, d_pairing, left, mj = call(
        functools.partial(weight_kernel, depth, features, own, len(j_pieces), chunk),
        (block // large,),
        [large_spec] + [full(v.shape) for v in args],
        [large_spec] + [full(o.shape) for o in out_shapes],
        [sds(upstream_adjoint.shape, BF16)] + out_shapes,
        [
            pltpu.VMEM((block, LANES), BF16),
            pltpu.VMEM((wide, block), BF16),
            pltpu.VMEM((steps, block, chunk), F32),
            pltpu.VMEM((width, large * depth, pair), BF16),
            pltpu.VMEM((width * width, pair), F32),
            pltpu.VMEM((features, width * pair), F32),
        ],
        cost(5e9, 8e6),
    )(upstream_adjoint, *args)

    d_pairing = d_pairing.reshape(n, -1, LANES)
    for bit in reversed(range(1, bits)):
        keep, go = halves(split_high(d_pairing), "col", bit, 0)
        d_pairing = add(keep, *swap_parts([go], "col", bit, n))

    out_shapes = [sds((width + 16, LANES), BF16), sds((n, own * wide // LANES, LANES), BF16)]
    small, d_b = call(
        functools.partial(token_kernel, depth, features, n),
        (steps,),
        [up_spec]
        + [full(v.shape) for v in (held, pairing_wide, mj, perm, bias, left)],
        [full(o.shape) for o in out_shapes],
        out_shapes,
        [pltpu.VMEM((chunk, wide, pair), BF16), pltpu.VMEM((wide, block), F32)],
        cost(8e9, 8e6),
    )(scaled, held, pairing_wide, mj, perm, bias, left)

    dp_keep, dp_go = halves(d_pairing, "col", 0, 0)
    db_keep, db_go = halves(d_b.reshape((n // 2, 2) + d_b.shape[1:]), "col", 0, 1)
    parts = swap_parts([dp_go, db_go, small], "col", 0, n)
    d_pairing, small = add(dp_keep, parts[0]), add(small, parts[2])
    d_b = in_order(db_keep, parts[1].reshape(db_keep.shape), "col", 0, 1)
    db_keep, db_go = halves(d_b, "row", 0, 1)
    for bit in range(bits):
        parts = swap_parts([d_pairing, db_go, small], "row", bit, n)
        if bit == 0:
            args = (held, offset, pairing_wide, small)
            coupling_update, small = call(
                functools.partial(update_kernel, depth),
                (steps,),
                [full(v.shape) for v in args],
                [up_spec, full(small.shape)],
                [sds((block, block, pair), BF16), sds(small.shape, BF16)],
                [pltpu.VMEM((chunk, wide, pair), BF16)],
                cost(6e9, 8e6),
            )(*args)
        if bit == 1:
            half = (tokens // LANES // 2, width, LANES)
            out_shapes = [sds(half, BF16), sds(half, BF16), sds(small.shape, BF16)]
            *d_a, small = call(
                functools.partial(left_kernel, depth, bits - 1),
                (steps,),
                [up_spec] + [full(v.shape) for v in (held, pairing_wide, small)],
                [full(o.shape) for o in out_shapes],
                out_shapes,
                [
                    pltpu.VMEM((width, chunk * depth, pair), BF16),
                    pltpu.VMEM((width * pair, width), BF16),
                    pltpu.VMEM((tokens // LANES, width, LANES), BF16),
                    pltpu.VMEM((wide, block), BF16),
                ],
                cost(6e9, 8e6),
            )(scaled, held, pairing_wide, small)
            if rows % LANES:
                shape = (-1, width, LANES // rows, rows)
                d_a = [part.reshape(shape).transpose(0, 2, 1, 3) for part in d_a]
            da_keep, da_go = [part.reshape(n // 2, -1, LANES) for part in d_a]
        d_pairing, d_b, small = add(d_pairing, parts[0]), add(db_keep, parts[1]), add(small, parts[2])
        db_keep = db_go = d_b
    d_pairing = d_pairing.reshape(1, -1, LANES)
    small_parts = [small]
    for bit in reversed(range(1, bits)):
        if bit < bits - 1:
            small_parts = [add(*small_parts)]
            da_keep, da_go = halves(split_high(add(*da_parts)), "col", bit, 0)
        db_keep, db_go = halves(split_high(d_b), "col", bit, 0)
        parts = swap_parts([d_pairing, db_go, da_go, small_parts[0]], "col", bit, n)
        d_pairing = in_order(d_pairing, parts[0].reshape(d_pairing.shape), "col", bit, 1)
        d_pairing = d_pairing.reshape((-1,) + d_pairing.shape[2:])
        mine = bit_of("col", bit) == bit_of("row", bit)
        d_b = jnp.where(mine, db_keep, parts[1].reshape(db_keep.shape))
        da_parts = [da_keep, parts[2].reshape(da_keep.shape)]
        small_parts = [small_parts[0], parts[3]]
    da_keep, da_go = halves(add(*da_parts), "col", 0, 0)
    got, da_got = swap_parts([d_pairing, da_go], "col", 0, n)
    d_pairing = in_order(d_pairing, got.reshape(d_pairing.shape), "col", 0, 1)
    d_a = [lay_back(part.reshape(-1, LANES), width, rows) for part in (da_keep, da_got)]
    d_b = lay_back(d_b[0], own, wide)

    d_pairing = d_pairing.reshape(width, width, pair)
    args = (*d_a, d_b, *small_parts, x, factors_t, perm, d_pairing)
    out_shapes = [
        sds((rows, features), F32),
        sds((features, 2 * width), F32),
        sds((1, pair), F32),
        sds((width, width, pair), F32),
    ]
    embedding_adjoint, factors_adjoint, offset_slope, placed = call(
        functools.partial(owner_kernel, depth, own, features),
        (),
        [full(v.shape) for v in args],
        [full(o.shape) for o in out_shapes],
        out_shapes,
    )(*args)
    return (
        coupling_update,
        embedding_adjoint.reshape(depth, own, features),
        factors_adjoint,
        placed.reshape(width * width, pair),
        offset_slope.reshape(pair),
    )


def solution(mesh):
    n = mesh.shape["col"]
    placed = (
        P(None, ("groups", "row", "col"), None),
        P(None, ("groups", "row", "col")),
        P("groups"),
        P(),
        P(),
        P(),
        P(("groups", "row"), "col", None),
    )
    return jax.shard_map(
        functools.partial(per_device, n),
        mesh=mesh,
        in_specs=placed,
        out_specs=(
            P(("groups", "row"), "col", None),
            P(None, ("groups", "row", "col"), None),
            P("groups", None),
            P("groups", None),
            P("groups"),
        ),
        check_vma=False,
    )
```

```python
import functools

import jax
import jax.numpy as jnp
from jax import lax
from jax.experimental import pallas as pl
from jax.experimental.pallas import tpu as pltpu
from jax.sharding import PartitionSpec as P

F32 = jnp.float32
BF16 = jnp.bfloat16
LANES = 128
VMEM_LIMIT = 24 * 1024 * 1024
NT = (((1,), (1,)), ((), ()))


def dot(left, right):
    return jnp.dot(left, right, preferred_element_type=F32)


def dot_nt(left, right):
    return lax.dot_general(left, right, NT, preferred_element_type=F32)


def iota(shape, axis):
    return lax.broadcasted_iota(jnp.int32, shape, axis)


def one_hot(mask):
    return jnp.where(mask, 1.0, 0.0).astype(BF16)


def full(shape):
    return pl.BlockSpec(shape, lambda *g: (0,) * len(shape))


def cost(flops, nbytes):
    return pl.CostEstimate(flops=int(flops), bytes_accessed=int(nbytes), transcendentals=0)


def call(kernel, grid, in_specs, out_specs, out_shape, scratch=(), estimate=None):
    return pl.pallas_call(
        kernel,
        grid=grid,
        in_specs=in_specs,
        out_specs=out_specs,
        out_shape=out_shape,
        scratch_shapes=list(scratch),
        compiler_params=pltpu.CompilerParams(vmem_limit_bytes=VMEM_LIMIT),
        cost_estimate=estimate,
    )


def stats(x):
    center = x - jnp.mean(x, axis=-1, keepdims=True)
    scale = lax.rsqrt(jnp.mean(center * center, axis=-1, keepdims=True) + 1e-05)
    return center * scale, scale


def prep_kernel(depth, own, features, x_ref, by_token_ref, by_row_ref):
    rows = depth * own
    half = rows // 2
    x = x_ref[...].astype(F32)
    weight = x[:, features : features + 1]
    normed, _ = stats(x[:, :features])
    masked = normed.astype(BF16).astype(F32) * weight
    by_row_ref[:half, :] = jnp.concatenate([masked[:half], masked[half:]], axis=1).astype(BF16)
    p, q = iota((rows, rows), 0), iota((rows, rows), 1)
    swap = one_hot(q == (p % depth) * own + p // depth)
    turned = dot(swap, masked.astype(BF16))
    by_token_ref[:half, :] = jnp.concatenate([turned[:half], turned[half:]], axis=1).astype(BF16)
    here = one_hot(iota((own, rows), 0) == iota((own, rows), 1) % own)
    at = iota((rows, LANES), 1) == iota((rows, LANES), 0) // own
    mask = dot(here, jnp.where(at, weight, 0.0).astype(BF16)).astype(BF16)
    by_row_ref[half:, :] = mask
    by_token_ref[half:, :] = mask


def two(ref, at):
    return jnp.concatenate([ref[at], ref[at + 1]], axis=1)


def fill_v(g_ref, bt, v_ref, depth):
    chunk, _, pair = g_ref.shape
    width = v_ref.shape[0]
    for at in range(0, chunk, 2):
        v = dot(bt, two(g_ref, at)).astype(BF16)
        for k in range(2):
            part = v[:, k * pair : (k + 1) * pair].reshape(width, depth, pair)
            v_ref[:, (at + k) * depth : (at + k + 1) * depth, :] = part


def fill_t(a_chunk, wc_ref, t_ref, depth):
    chunk, wide, pair = t_ref.shape
    width = wide // depth
    for e in range(0, width, 2):
        t = dot(a_chunk, wc_ref[:, e * pair : (e + 2) * pair]).astype(BF16)
        for k in range(2):
            part = t[:, k * pair : (k + 1) * pair].reshape(chunk, depth, pair)
            t_ref[:, (e + k) * depth : (e + k + 1) * depth, :] = part


def held_b(held_ref, block, width, depth):
    at = block * depth
    tiles = width * depth // LANES
    return jnp.concatenate([held_ref[at + k * block : at + (k + 1) * block, :] for k in range(tiles)], axis=1)


def factor_kernel(own, depth, pieces, *refs):
    g = pl.program_id(0)

    @pl.when(g == 0)
    def _():
        factors(own, pieces, *refs[: 4 + pieces], *refs[5 + pieces :])

    t_ref, _, wc_ref, _, _, a_ref = refs[4 + pieces : 10 + pieces]
    span = t_ref.shape[0] * depth
    fill_t(a_ref[pl.ds(pl.multiple_of(g * span, span), span), :], wc_ref, t_ref, depth)


def factors(own, pieces, w_ref, wide_ref, offset_ref, up_ref, *refs):
    wt_ref, wc_ref, pass_ref, bias_ref, a_ref, at_ref, seen_ref, rows_ref, mi_ref = refs[pieces:]
    features, width = w_ref.shape[0], w_ref.shape[1] // 2
    pair = wide_ref.shape[1]
    if own % 16 == 0:
        half = refs[0].shape[1] - own
        for k in range(pieces):
            for core in range(2):
                at = ((lax.axis_index("col") >> 1) ^ k) * 2 + core
                for q in range(2):
                    rows = pl.ds(pl.multiple_of((at * 2 + q) * half, half), half)
                    mi_ref[rows, :] = refs[k][core, :half, q * features : (q + 1) * features]
                rows = pl.ds(pl.multiple_of(at * own, own), own)
                seen_ref[rows, :] = refs[k][core, half:, :]
    else:
        mi_ref[...] = refs[0][...]
        seen_ref[...] = refs[1][...]
    pass_ref[...] = offset_ref[...]
    rows_ref[...] = wide_ref[...].astype(F32)
    for e in range(width):
        part = rows_ref[pl.ds(e, width, stride=width), :]
        wc_ref[:, e * pair : (e + 1) * pair] = part.astype(BF16)
    same = one_hot(iota((2 * width, 2 * width), 0) == iota((2 * width, 2 * width), 1))
    wt = dot_nt(same, w_ref[...]).astype(BF16)
    wt_ref[...] = wt
    mi = mi_ref[...]
    a_ref[...] = dot_nt(mi, wt[:width, :]).astype(BF16)
    same = one_hot(iota((features, features), 0) == iota((features, features), 1))
    at_ref[...] = dot_nt(jnp.concatenate([wt[:width, :], same], axis=0), mi).astype(BF16)
    bias = [jnp.zeros(up_ref.shape[1:], F32)] * 2
    for i in range(up_ref.shape[0]):
        bias[i % 2] = bias[i % 2] + up_ref[i].astype(F32)
    bias = jnp.sum(bias[0] + bias[1], axis=0, keepdims=True)
    bias_ref[...] = jnp.broadcast_to(bias, bias_ref.shape)


def weight_kernel(depth, features, own, pieces, part_size, *refs):
    up_ref, _, a_ref, at_ref, seen_i_ref, wt_ref, perm_ref, wc_ref = refs[:8]
    j_refs, refs = refs[8 : 8 + pieces], refs[8 + pieces :]
    g_ref, held_ref, dw_ref, left_ref, mj_ref, seen_j_ref, bt_ref, inv_ref, v_ref, acc_ref, wide_ref = refs
    g, last = pl.program_id(0), pl.num_programs(0) - 1
    chunk, block, pair = up_ref.shape
    width = wt_ref.shape[0] // 2

    @pl.when(g == 0)
    def _():
        if own % 16 == 0:
            half = depth // 2
            for k in range(pieces):
                for core in range(2):
                    at = ((lax.axis_index("row") >> 1) ^ k) * 2 + core
                    rows = pl.ds(pl.multiple_of(at * own, own), own)
                    seen_j_ref[rows, :] = j_refs[k][core, :own, :]
                    for s in range(depth):
                        lanes = slice(s // half * features, (s // half + 1) * features)
                        start = own + s % half * own
                        mj_ref[s, rows, :] = j_refs[k][core, start : start + own, lanes]
        else:
            mj_ref[...] = j_refs[0][...]
            seen_j_ref[...] = j_refs[1][...]
        wt = wt_ref[...]
        b = jnp.zeros((block, width * depth), F32)
        for s in range(depth):
            part = dot_nt(mj_ref[s], wt[width:, :]).astype(BF16)
            b = b + dot(part, perm_ref[s * width : (s + 1) * width, :])
        bt_ref[...] = b.T.astype(BF16)
        at = block * depth
        held_ref[:at, :width] = a_ref[...]
        for k in range(width * depth // LANES):
            held_ref[at : at + block, :] = b[:, k * LANES : (k + 1) * LANES].astype(BF16)
            at += block
        for k in range(block // part_size):
            rows = slice(k * part_size, (k + 1) * part_size)
            count = dot_nt(seen_j_ref[...], seen_i_ref[rows, :])
            inv_ref[k] = 1.0 / (count + 0.001)
            held_ref[at : at + block, :part_size] = count.astype(BF16)
            at += block
        acc_ref[...] = jnp.zeros_like(acc_ref)
        wide_ref[...] = jnp.zeros_like(wide_ref)

    for k in range(chunk // part_size):
        inv = inv_ref[g * (chunk // part_size) + k]
        for i in range(part_size):
            up = up_ref[k * part_size + i].astype(F32)
            g_ref[k * part_size + i] = (up * inv[:, i : i + 1]).astype(BF16)
    fill_v(g_ref, bt_ref[...], v_ref, depth)
    span = chunk * depth
    a_t = at_ref[:, pl.ds(pl.multiple_of(g * span, span), span)]
    for e in range(0, width, 2):
        part = dot(a_t, two(v_ref, e))
        for k in range(2):
            rows = slice((e + k) * width, (e + k + 1) * width)
            acc_ref[rows, :] += part[:width, k * pair : (k + 1) * pair]
        wide_ref[:, e * pair : (e + 2) * pair] += part[width:]

    @pl.when(g == last)
    def _():
        dw_ref[...] = acc_ref[...].astype(BF16)
        left = jnp.zeros((width, features), F32)
        for e in range(0, width, 2):
            lanes = slice(e * pair, (e + 2) * pair)
            left = left + dot_nt(wc_ref[:, lanes], wide_ref[:, lanes].astype(BF16))
        left_ref[...] = left


def left_kernel(depth, bit, *refs):
    g_ref, held_ref, wc_ref, small_ref, keep_ref, go_ref, pass_ref, v_ref, wd_ref, da_ref, bt_ref = refs
    g, last = pl.program_id(0), pl.num_programs(0) - 1
    chunk, block, pair = g_ref.shape
    width = wc_ref.shape[0]
    span = chunk * depth

    @pl.when(g == 0)
    def _():
        pass_ref[...] = small_ref[...]
        bt_ref[...] = held_b(held_ref, block, width, depth).astype(F32).T.astype(BF16)
        same = one_hot(iota((2 * pair, 2 * pair), 0) == iota((2 * pair, 2 * pair), 1))
        for at in range(0, wd_ref.shape[0], 2 * pair):
            wd_ref[at : at + 2 * pair, :] = dot_nt(same, wc_ref[:, at : at + 2 * pair]).astype(BF16)

    fill_v(g_ref, bt_ref[...], v_ref, depth)
    d_a = []
    each = width // 4
    for e in range(0, width, each):
        v = jnp.concatenate([v_ref[e + k] for k in range(each)], axis=1)
        d_a.append(dot(v, wd_ref[e * pair : (e + each) * pair, :]))
    d_a = (d_a[0] + d_a[1]) + (d_a[2] + d_a[3])
    same = one_hot(iota((width, width), 0) == iota((width, width), 1))
    d_a = dot_nt(same, d_a.astype(BF16)).astype(BF16)
    tiles = span // LANES
    for k in range(tiles):
        da_ref[g * tiles + k] = d_a[:, k * LANES : (k + 1) * LANES]

    @pl.when(g == last)
    def _():
        half = keep_ref.shape[0]
        here = (lax.axis_index("col") >> bit) & 1
        keep_ref[...] = da_ref[pl.ds(here * half, half)]
        go_ref[...] = da_ref[pl.ds((1 - here) * half, half)]


def token_kernel(depth, features, n, *refs):
    g_ref, t_ref, _, mj_ref, perm_ref, bias_ref, left_ref, small_ref, out_ref, db_ref = refs
    g, last = pl.program_id(0), pl.num_programs(0) - 1
    chunk, block = g_ref.shape[:2]
    width = left_ref.shape[0]

    @pl.when(g == 0)
    def _():
        db_ref[...] = jnp.zeros_like(db_ref)

    t = jnp.concatenate([t_ref[i] for i in range(chunk)], axis=1)
    scaled = jnp.concatenate([g_ref[i] for i in range(chunk)], axis=1)
    db_ref[...] += dot_nt(t, scaled)

    @pl.when(g == last)
    def _():
        d_b = db_ref[...].T.astype(BF16)
        own = block // n
        for k in range(n):
            part = d_b[k * own : (k + 1) * own, :]
            for q in range(part.shape[1] // LANES):
                out_ref[k, q * own : (q + 1) * own, :] = part[:, q * LANES : (q + 1) * LANES]
        turned = dot_nt(perm_ref[...], d_b).astype(BF16)
        right = jnp.zeros((width, features), F32)
        for s in range(depth):
            right = right + dot(turned[s * width : (s + 1) * width, :], mj_ref[s])
        small = jnp.concatenate([left_ref[...], right], axis=1)
        small_ref[0:width, :] = small.astype(BF16)
        small_ref[width:, :] = jnp.broadcast_to(bias_ref[0:1, :], (16, LANES)).astype(BF16)


def update_kernel(depth, *refs):
    held_ref, offset_ref, wc_ref, small_ref, out_ref, pass_ref, t_ref = refs
    g = pl.program_id(0)
    chunk, block, pair = out_ref.shape
    width = wc_ref.shape[0]

    @pl.when(g == 0)
    def _():
        pass_ref[...] = small_ref[...]

    span = chunk * depth
    fill_t(held_ref[pl.ds(pl.multiple_of(g * span, span), span), :width], wc_ref, t_ref, depth)
    rows = held_ref.shape[0] - (pl.num_programs(0) - g) * block
    count = held_ref[pl.ds(pl.multiple_of(rows, block), block), :chunk]
    inv = 1.0 / (count.astype(F32) + 0.001)
    b = held_b(held_ref, block, width, depth)
    offset = offset_ref[...]
    for at in range(0, chunk, 2):
        part = dot(b, two(t_ref, at))
        for k in range(2):
            value = part[:, k * pair : (k + 1) * pair] * inv[:, at + k : at + k + 1] + offset
            out_ref[at + k] = value.astype(BF16)


def owner_kernel(depth, own, features, *refs):
    da_refs, db_ref, small_refs = refs[:2], refs[2], refs[3:5]
    x_ref, wt_ref, perm_ref, dw_ref = refs[5:9]
    out_ref, factors_ref, bias_ref, placed_ref = refs[9:]
    for e in range(dw_ref.shape[0]):
        placed_ref[:, e, :] = dw_ref[e].astype(F32)
    rows = depth * own
    width = wt_ref.shape[0] // 2
    p, q = iota((rows, rows), 0), iota((rows, rows), 1)
    swap = one_hot(q == (p % own) * depth + p // own)
    d_a = dot_nt(swap, da_refs[0][...]) + dot_nt(swap, da_refs[1][...])
    d_b = dot_nt(db_ref[...], perm_ref[...])
    d_b = jnp.concatenate([d_b[:, s * width : (s + 1) * width] for s in range(depth)], axis=0)
    highest = lax.Precision.HIGHEST
    wt = wt_ref[...].astype(F32)
    d_normed = jnp.dot(d_a, wt[:width, :], precision=highest, preferred_element_type=F32)
    d_normed = d_normed + jnp.dot(d_b, wt[width:, :], precision=highest, preferred_element_type=F32)
    x = x_ref[...].astype(F32)
    d_normed = d_normed * x[:, features : features + 1]
    normed, scale = stats(x[:, :features])
    mean = jnp.mean(d_normed, axis=-1, keepdims=True)
    along = jnp.mean(d_normed * normed, axis=-1, keepdims=True)
    out_ref[...] = scale * (d_normed - mean - normed * along)
    small = small_refs[0][...].astype(F32) + small_refs[1][...].astype(F32)
    turned = small[:width].T
    factors_ref[...] = jnp.concatenate([turned[:features], turned[features:]], axis=1)
    bias_ref[...] = small[width : width + 1]


def lay_back(x, rows, lanes):
    if lanes % LANES:
        return x.reshape(rows, lanes)
    return x.reshape(lanes // LANES, rows, LANES).transpose(1, 0, 2).reshape(rows, lanes)


def bit_of(axis, bit):
    return (lax.axis_index(axis) >> bit) & 1


def swap_parts(parts, axis, bit, n):
    parts = [part.reshape(-1, LANES) for part in parts]
    message = jnp.concatenate(parts, axis=0) if len(parts) > 1 else parts[0]
    pairs = [(i, i ^ (1 << bit)) for i in range(n)]
    message = lax.ppermute(message, axis, pairs)
    got, at = [], 0
    for part in parts:
        got.append(message[at : at + part.shape[0]])
        at += part.shape[0]
    return got


def halves(x, axis, bit, at):
    here = bit_of(axis, bit)
    keep = lax.dynamic_index_in_dim(x, here, at, keepdims=False)
    return keep, lax.dynamic_index_in_dim(x, 1 - here, at, keepdims=False)


def split_high(x):
    return x.reshape((2, x.shape[0] // 2) + x.shape[1:])


def in_order(mine, other, axis, bit, at):
    first = bit_of(axis, bit) == 0
    low = jnp.where(first, mine, other)
    return jnp.stack([low, jnp.where(first, other, mine)], axis=at)


def unswap(x, axis):
    n = x.shape[0]
    for bit in range(n.bit_length() - 1):
        y = x.reshape((n >> (bit + 1), 2, 1 << bit) + x.shape[1:])
        x = jnp.where(bit_of(axis, bit + 1) == 0, y, y[:, ::-1]).reshape(x.shape)
    return x


def add(mine, other):
    other = other.reshape(mine.shape)
    return lax.optimization_barrier((mine.astype(F32) + other.astype(F32)).astype(BF16))


def per_device(
    n,
    alignment_embedding,
    alignment_cell_exists,
    alignment_lines_exist,
    sitewise_factors,
    pairing_matrix,
    offset_vector,
    upstream_adjoint,
):
    depth, own, features = alignment_embedding.shape
    width = sitewise_factors.shape[1] // 2
    block, pair = upstream_adjoint.shape[0], upstream_adjoint.shape[2]
    rows, chunk = depth * own, 16
    steps = block // chunk
    split = own % 16 == 0
    axes = ("row", "col")
    sds = jax.ShapeDtypeStruct

    bits = n.bit_length() - 1
    mask = (alignment_cell_exists * alignment_lines_exist[:, None]).astype(BF16)
    mask = jnp.broadcast_to(mask[:, :, None], (depth, own, LANES - features))
    x = jnp.concatenate([alignment_embedding, mask], axis=2).reshape(rows, LANES)
    offset = offset_vector.reshape(1, pair)
    out_shapes = [sds((rows // 2 + own, LANES), BF16)] * 2
    by_token, by_row = call(
        functools.partial(prep_kernel, depth, own, features),
        (),
        [full(x.shape)],
        [full(o.shape) for o in out_shapes],
        out_shapes,
    )(x)
    message = jnp.concatenate([by_token, by_row[: rows // 2]], axis=0)
    both = in_order(message, *swap_parts([message], "col", 0, n), "col", 0, 0)
    message = both[:, : rows // 2 + own]
    held = [message]
    for k in range(2, n, 2):
        held.append(lax.ppermute(message, "col", [(j, j ^ k) for j in range(n)]))
    a_pieces = held
    if own % 16:
        held = unswap(jnp.stack(held), "col").reshape((n,) + message.shape[1:])
        parts = held[:, : rows // 2].reshape(n, rows // 2, 2, features)
        mi = parts.transpose(0, 2, 1, 3).reshape(block * depth, features)
        a_pieces = [mi, held[:, rows // 2 :].reshape(block, LANES)]
    message = both[:, rows // 2 :]
    held = []
    for k in range(0, n, 2):
        pairs = [(i * n + j, (j ^ k) * n + i) for i in range(n) for j in range(n)]
        held.append(lax.ppermute(message, axes, pairs))
    j_pieces = held
    if own % 16:
        held = unswap(jnp.stack(held), "row").reshape((n,) + message.shape[1:])
        parts = held[:, own:].reshape(n, depth // 2, own, 2, features)
        mj = parts.transpose(3, 1, 0, 2, 4).reshape(depth, block, features)
        j_pieces = [mj, held[:, :own].reshape(block, LANES)]

    wide = width * depth
    tokens = block * depth
    source = jnp.arange(wide)
    perm = (jnp.arange(wide)[None, :] == (source % width * depth + source // width)[:, None]).astype(BF16)
    up_spec = pl.BlockSpec((chunk, block, pair), lambda g: (g, 0, 0))
    args = (sitewise_factors, pairing_matrix, offset, upstream_adjoint, *a_pieces)
    out_shapes = [
        sds((2 * width, features), BF16),
        sds((width, width * pair), BF16),
        sds((1, pair), F32),
        sds((8, pair), F32),
        sds((tokens, width), BF16),
        sds((width + features, tokens), BF16),
        sds((block, LANES), BF16),
    ]
    t_spec = pl.BlockSpec((chunk, wide, pair), lambda g: (g, 0, 0))
    t, factors_t, pairing_wide, offset, bias, a, a_t, seen = call(
        functools.partial(factor_kernel, own, depth, len(a_pieces)),
        (steps,),
        [full(v.shape) for v in args],
        [t_spec] + [full(o.shape) for o in out_shapes],
        [sds((block, wide, pair), BF16)] + out_shapes,
        [pltpu.VMEM((width * width, pair), F32), pltpu.VMEM((tokens, features), BF16)],
        cost(3e9, 4e6),
    )(*args)

    out_shapes = [
        sds((tokens + block * wide // LANES + block * steps, LANES), BF16),
        sds((width * width, pair), BF16),
        sds((width, features), F32),
        sds((depth, block, features), BF16),
    ]
    args = (a, a_t, seen, factors_t, perm, pairing_wide, *j_pieces)
    large = 2 * chunk
    large_spec = pl.BlockSpec((large, block, pair), lambda g: (g, 0, 0))
    scaled, held, d_pairing, left, mj = call(
        functools.partial(weight_kernel, depth, features, own, len(j_pieces), chunk),
        (block // large,),
        [large_spec, pl.BlockSpec(memory_space=pl.ANY)] + [full(v.shape) for v in args],
        [large_spec] + [full(o.shape) for o in out_shapes],
        [sds(upstream_adjoint.shape, BF16)] + out_shapes,
        [
            pltpu.VMEM((block, LANES), BF16),
            pltpu.VMEM((wide, block), BF16),
            pltpu.VMEM((steps, block, chunk), F32),
            pltpu.VMEM((width, large * depth, pair), BF16),
            pltpu.VMEM((width * width, pair), F32),
            pltpu.VMEM((features, width * pair), F32),
        ],
        cost(5e9, 8e6),
    )(upstream_adjoint, t, *args)

    d_pairing = d_pairing.reshape(n, -1, LANES)
    for bit in reversed(range(1, bits)):
        keep, go = halves(split_high(d_pairing), "col", bit, 0)
        d_pairing = add(keep, *swap_parts([go], "col", bit, n))

    out_shapes = [sds((width + 16, LANES), BF16), sds((n, own * wide // LANES, LANES), BF16)]
    small, d_b = call(
        functools.partial(token_kernel, depth, features, n),
        (steps,),
        [up_spec, t_spec] + [full(v.shape) for v in (held, mj, perm, bias, left)],
        [full(o.shape) for o in out_shapes],
        out_shapes,
        [pltpu.VMEM((wide, block), F32)],
        cost(8e9, 8e6),
    )(scaled, t, held, mj, perm, bias, left)

    dp_keep, dp_go = halves(d_pairing, "col", 0, 0)
    db_keep, db_go = halves(d_b.reshape((n // 2, 2) + d_b.shape[1:]), "col", 0, 1)
    parts = swap_parts([dp_go, db_go, small], "col", 0, n)
    d_pairing, small = add(dp_keep, parts[0]), add(small, parts[2])
    d_b = in_order(db_keep, parts[1].reshape(db_keep.shape), "col", 0, 1)
    db_keep, db_go = halves(d_b, "row", 0, 1)
    for bit in range(bits):
        parts = swap_parts([d_pairing, db_go, small], "row", bit, n)
        if bit == 0:
            args = (held, offset, pairing_wide, small)
            coupling_update, small = call(
                functools.partial(update_kernel, depth),
                (steps,),
                [full(v.shape) for v in args],
                [up_spec, full(small.shape)],
                [sds((block, block, pair), BF16), sds(small.shape, BF16)],
                [pltpu.VMEM((chunk, wide, pair), BF16)],
                cost(6e9, 8e6),
            )(*args)
        if bit == 1:
            half = (tokens // LANES // 2, width, LANES)
            out_shapes = [sds(half, BF16), sds(half, BF16), sds(small.shape, BF16)]
            *d_a, small = call(
                functools.partial(left_kernel, depth, bits - 1),
                (block // large,),
                [large_spec] + [full(v.shape) for v in (held, pairing_wide, small)],
                [full(o.shape) for o in out_shapes],
                out_shapes,
                [
                    pltpu.VMEM((width, large * depth, pair), BF16),
                    pltpu.VMEM((width * pair, width), BF16),
                    pltpu.VMEM((tokens // LANES, width, LANES), BF16),
                    pltpu.VMEM((wide, block), BF16),
                ],
                cost(6e9, 8e6),
            )(scaled, held, pairing_wide, small)
            if rows % LANES:
                shape = (-1, width, LANES // rows, rows)
                d_a = [part.reshape(shape).transpose(0, 2, 1, 3) for part in d_a]
            da_keep, da_go = [part.reshape(n // 2, -1, LANES) for part in d_a]
        d_pairing, d_b, small = add(d_pairing, parts[0]), add(db_keep, parts[1]), add(small, parts[2])
        db_keep = db_go = d_b
    d_pairing = d_pairing.reshape(1, -1, LANES)
    small_parts = [small]
    for bit in reversed(range(1, bits)):
        if bit < bits - 1:
            small_parts = [add(*small_parts)]
            da_keep, da_go = halves(split_high(add(*da_parts)), "col", bit, 0)
        db_keep, db_go = halves(split_high(d_b), "col", bit, 0)
        parts = swap_parts([d_pairing, db_go, da_go, small_parts[0]], "col", bit, n)
        d_pairing = in_order(d_pairing, parts[0].reshape(d_pairing.shape), "col", bit, 1)
        d_pairing = d_pairing.reshape((-1,) + d_pairing.shape[2:])
        mine = bit_of("col", bit) == bit_of("row", bit)
        d_b = jnp.where(mine, db_keep, parts[1].reshape(db_keep.shape))
        da_parts = [da_keep, parts[2].reshape(da_keep.shape)]
        small_parts = [small_parts[0], parts[3]]
    da_keep, da_go = halves(add(*da_parts), "col", 0, 0)
    got, da_got = swap_parts([d_pairing, da_go], "col", 0, n)
    d_pairing = in_order(d_pairing, got.reshape(d_pairing.shape), "col", 0, 1)
    d_a = [lay_back(part.reshape(-1, LANES), width, rows) for part in (da_keep, da_got)]
    d_b = lay_back(d_b[0], own, wide)

    d_pairing = d_pairing.reshape(width, width, pair)
    args = (*d_a, d_b, *small_parts, x, factors_t, perm, d_pairing)
    out_shapes = [
        sds((rows, features), F32),
        sds((features, 2 * width), F32),
        sds((1, pair), F32),
        sds((width, width, pair), F32),
    ]
    embedding_adjoint, factors_adjoint, offset_slope, placed = call(
        functools.partial(owner_kernel, depth, own, features),
        (),
        [full(v.shape) for v in args],
        [full(o.shape) for o in out_shapes],
        out_shapes,
    )(*args)
    return (
        coupling_update,
        embedding_adjoint.reshape(depth, own, features),
        factors_adjoint,
        placed.reshape(width * width, pair),
        offset_slope.reshape(pair),
    )


def solution(mesh):
    n = mesh.shape["col"]
    placed = (
        P(None, ("groups", "row", "col"), None),
        P(None, ("groups", "row", "col")),
        P("groups"),
        P(),
        P(),
        P(),
        P(("groups", "row"), "col", None),
    )
    return jax.shard_map(
        functools.partial(per_device, n),
        mesh=mesh,
        in_specs=placed,
        out_specs=(
            P(("groups", "row"), "col", None),
            P(None, ("groups", "row", "col"), None),
            P("groups", None),
            P("groups", None),
            P("groups"),
        ),
        check_vma=False,
    )
```

```python
import functools

import jax
import jax.numpy as jnp
from jax import lax
from jax.experimental import pallas as pl
from jax.experimental.pallas import tpu as pltpu
from jax.sharding import PartitionSpec as P

F32 = jnp.float32
BF16 = jnp.bfloat16
LANES = 128
VMEM_LIMIT = 24 * 1024 * 1024
NT = (((1,), (1,)), ((), ()))


def dot(left, right):
    return jnp.dot(left, right, preferred_element_type=F32)


def dot_nt(left, right):
    return lax.dot_general(left, right, NT, preferred_element_type=F32)


def iota(shape, axis):
    return lax.broadcasted_iota(jnp.int32, shape, axis)


def one_hot(mask):
    return jnp.where(mask, 1.0, 0.0).astype(BF16)


def full(shape):
    return pl.BlockSpec(shape, lambda *g: (0,) * len(shape))


def cost(flops, nbytes):
    return pl.CostEstimate(flops=int(flops), bytes_accessed=int(nbytes), transcendentals=0)


def call(kernel, grid, in_specs, out_specs, out_shape, scratch=(), estimate=None):
    return pl.pallas_call(
        kernel,
        grid=grid,
        in_specs=in_specs,
        out_specs=out_specs,
        out_shape=out_shape,
        scratch_shapes=list(scratch),
        compiler_params=pltpu.CompilerParams(vmem_limit_bytes=VMEM_LIMIT),
        cost_estimate=estimate,
    )


def stats(x):
    center = x - jnp.mean(x, axis=-1, keepdims=True)
    scale = lax.rsqrt(jnp.mean(center * center, axis=-1, keepdims=True) + 1e-05)
    return center * scale, scale


def prep_kernel(depth, own, features, x_ref, by_token_ref, by_row_ref):
    rows = depth * own
    half = rows // 2
    x = x_ref[...].astype(F32)
    weight = x[:, features : features + 1]
    normed, _ = stats(x[:, :features])
    masked = normed.astype(BF16).astype(F32) * weight
    by_row_ref[:half, :] = jnp.concatenate([masked[:half], masked[half:]], axis=1).astype(BF16)
    p, q = iota((rows, rows), 0), iota((rows, rows), 1)
    swap = one_hot(q == (p % depth) * own + p // depth)
    turned = dot(swap, masked.astype(BF16))
    by_token_ref[:half, :] = jnp.concatenate([turned[:half], turned[half:]], axis=1).astype(BF16)
    here = one_hot(iota((own, rows), 0) == iota((own, rows), 1) % own)
    at = iota((rows, LANES), 1) == iota((rows, LANES), 0) // own
    mask = dot(here, jnp.where(at, weight, 0.0).astype(BF16)).astype(BF16)
    by_row_ref[half:, :] = mask
    by_token_ref[half:, :] = mask


def fill_v(g_ref, bt, v_ref, depth):
    width = bt.shape[0] // depth
    pair = v_ref.shape[1] // width
    for at in range(0, v_ref.shape[0] // depth, 2):
        v = dot(bt, g_ref[:, at * pair : (at + 2) * pair]).astype(BF16)
        for k in range(2):
            rows = slice((at + k) * depth, (at + k + 1) * depth)
            for e in range(width):
                part = v[e * depth : (e + 1) * depth, k * pair : (k + 1) * pair]
                v_ref[rows, e * pair : (e + 1) * pair] = part


def fill_t(a_chunk, wc_ref, t_ref, depth):
    width = wc_ref.shape[0]
    pair = wc_ref.shape[1] // width
    for e in range(0, width, 2):
        t = dot(a_chunk, wc_ref[:, e * pair : (e + 2) * pair]).astype(BF16)
        for k in range(2):
            rows = slice((e + k) * depth, (e + k + 1) * depth)
            for i in range(a_chunk.shape[0] // depth):
                part = t[i * depth : (i + 1) * depth, k * pair : (k + 1) * pair]
                t_ref[rows, i * pair : (i + 1) * pair] = part


def held_b(held_ref, block, width, depth):
    at = block * depth
    tiles = width * depth // LANES
    return jnp.concatenate([held_ref[at + k * block : at + (k + 1) * block, :] for k in range(tiles)], axis=1)


def factor_kernel(own, pieces, w_ref, wide_ref, offset_ref, up_ref, *refs):
    wt_ref, wc_ref, pass_ref, bias_ref, a_ref, at_ref, seen_ref, rows_ref, mi_ref = refs[pieces:]
    features, width = w_ref.shape[0], w_ref.shape[1] // 2
    pair = wide_ref.shape[1]
    if own % 16 == 0:
        half = refs[0].shape[1] - own
        for k in range(pieces):
            for core in range(2):
                at = ((lax.axis_index("col") >> 1) ^ k) * 2 + core
                for q in range(2):
                    rows = pl.ds(pl.multiple_of((at * 2 + q) * half, half), half)
                    mi_ref[rows, :] = refs[k][core, :half, q * features : (q + 1) * features]
                rows = pl.ds(pl.multiple_of(at * own, own), own)
                seen_ref[rows, :] = refs[k][core, half:, :]
    else:
        mi_ref[...] = refs[0][...]
        seen_ref[...] = refs[1][...]
    pass_ref[...] = offset_ref[...]
    rows_ref[...] = wide_ref[...].astype(F32)
    for e in range(width):
        part = rows_ref[pl.ds(e, width, stride=width), :]
        wc_ref[:, e * pair : (e + 1) * pair] = part.astype(BF16)
    same = one_hot(iota((2 * width, 2 * width), 0) == iota((2 * width, 2 * width), 1))
    wt = dot_nt(same, w_ref[...]).astype(BF16)
    wt_ref[...] = wt
    mi = mi_ref[...]
    a_ref[...] = dot_nt(mi, wt[:width, :]).astype(BF16)
    same = one_hot(iota((features, features), 0) == iota((features, features), 1))
    at_ref[...] = dot_nt(jnp.concatenate([wt[:width, :], same], axis=0), mi).astype(BF16)
    bias = [jnp.zeros(up_ref.shape[1:], F32)] * 2
    for i in range(up_ref.shape[0]):
        bias[i % 2] = bias[i % 2] + up_ref[i].astype(F32)
    bias = jnp.sum(bias[0] + bias[1], axis=0, keepdims=True)
    bias_ref[...] = jnp.broadcast_to(bias, bias_ref.shape)


def weight_kernel(depth, features, own, pieces, part_size, *refs):
    up_ref, a_ref, at_ref, seen_i_ref, wt_ref, perm_ref, wc_ref = refs[:7]
    j_refs, refs = refs[7 : 7 + pieces], refs[7 + pieces :]
    g_ref, held_ref, dw_ref, left_ref, mj_ref, seen_j_ref, bt_ref, inv_ref, v_ref, acc_ref, wide_ref = refs
    g, last = pl.program_id(0), pl.num_programs(0) - 1
    chunk, block, pair = up_ref.shape
    width = wt_ref.shape[0] // 2

    @pl.when(g == 0)
    def _():
        if own % 16 == 0:
            half = depth // 2
            for k in range(pieces):
                for core in range(2):
                    at = ((lax.axis_index("row") >> 1) ^ k) * 2 + core
                    rows = pl.ds(pl.multiple_of(at * own, own), own)
                    seen_j_ref[rows, :] = j_refs[k][core, :own, :]
                    for s in range(depth):
                        lanes = slice(s // half * features, (s // half + 1) * features)
                        start = own + s % half * own
                        mj_ref[s, rows, :] = j_refs[k][core, start : start + own, lanes]
        else:
            mj_ref[...] = j_refs[0][...]
            seen_j_ref[...] = j_refs[1][...]
        wt = wt_ref[...]
        b = jnp.zeros((block, width * depth), F32)
        for s in range(depth):
            part = dot_nt(mj_ref[s], wt[width:, :]).astype(BF16)
            b = b + dot(part, perm_ref[s * width : (s + 1) * width, :])
        bt_ref[...] = b.T.astype(BF16)
        at = block * depth
        held_ref[:at, :width] = a_ref[...]
        for k in range(width * depth // LANES):
            held_ref[at : at + block, :] = b[:, k * LANES : (k + 1) * LANES].astype(BF16)
            at += block
        for k in range(block // part_size):
            rows = slice(k * part_size, (k + 1) * part_size)
            count = dot_nt(seen_j_ref[...], seen_i_ref[rows, :])
            inv_ref[k] = 1.0 / (count + 0.001)
            held_ref[at : at + block, :part_size] = count.astype(BF16)
            at += block
        acc_ref[...] = jnp.zeros_like(acc_ref)
        wide_ref[...] = jnp.zeros_like(wide_ref)

    for k in range(chunk // part_size):
        inv = inv_ref[g * (chunk // part_size) + k]
        for i in range(part_size):
            up = up_ref[k * part_size + i].astype(F32)
            at = (k * part_size + i) * pair
            g_ref[:, at : at + pair] = (up * inv[:, i : i + 1]).astype(BF16)
    fill_v(g_ref, bt_ref[...], v_ref, depth)
    span = chunk * depth
    a_t = at_ref[:, pl.ds(pl.multiple_of(g * span, span), span)]
    for e in range(0, width, 2):
        part = dot(a_t, v_ref[:, e * pair : (e + 2) * pair])
        for k in range(2):
            rows = slice((e + k) * width, (e + k + 1) * width)
            acc_ref[rows, :] += part[:width, k * pair : (k + 1) * pair]
        wide_ref[:, e * pair : (e + 2) * pair] += part[width:]

    @pl.when(g == last)
    def _():
        dw_ref[...] = acc_ref[...].astype(BF16)
        left = jnp.zeros((width, features), F32)
        for e in range(0, width, 2):
            lanes = slice(e * pair, (e + 2) * pair)
            left = left + dot_nt(wc_ref[:, lanes], wide_ref[:, lanes].astype(BF16))
        left_ref[...] = left


def left_kernel(depth, bit, *refs):
    g_ref, held_ref, wc_ref, small_ref, keep_ref, go_ref, pass_ref, v_ref, wd_ref, da_ref, bt_ref = refs
    g, last = pl.program_id(0), pl.num_programs(0) - 1
    block, width = g_ref.shape[0], wc_ref.shape[0]
    pair = wc_ref.shape[1] // width
    span = v_ref.shape[0]

    @pl.when(g == 0)
    def _():
        pass_ref[...] = small_ref[...]
        bt_ref[...] = held_b(held_ref, block, width, depth).astype(F32).T.astype(BF16)
        same = one_hot(iota((2 * pair, 2 * pair), 0) == iota((2 * pair, 2 * pair), 1))
        for at in range(0, wd_ref.shape[0], 2 * pair):
            wd_ref[at : at + 2 * pair, :] = dot_nt(same, wc_ref[:, at : at + 2 * pair]).astype(BF16)

    fill_v(g_ref, bt_ref[...], v_ref, depth)
    d_a = jnp.zeros((span, width), F32)
    each = v_ref.shape[1] // 4
    for at in range(0, 4 * each, each):
        d_a = d_a + dot(v_ref[:, at : at + each], wd_ref[at : at + each, :])
    same = one_hot(iota((width, width), 0) == iota((width, width), 1))
    d_a = dot_nt(same, d_a.astype(BF16)).astype(BF16)
    tiles = span // LANES
    for k in range(tiles):
        da_ref[g * tiles + k] = d_a[:, k * LANES : (k + 1) * LANES]

    @pl.when(g == last)
    def _():
        half = keep_ref.shape[0]
        here = (lax.axis_index("col") >> bit) & 1
        keep_ref[...] = da_ref[pl.ds(here * half, half)]
        go_ref[...] = da_ref[pl.ds((1 - here) * half, half)]


def token_kernel(depth, features, n, *refs):
    g_ref, held_ref, wc_ref, mj_ref, perm_ref, bias_ref, left_ref = refs[:7]
    small_ref, out_ref, t_ref, db_ref = refs[7:]
    g, last = pl.program_id(0), pl.num_programs(0) - 1
    block, width = g_ref.shape[0], left_ref.shape[0]
    chunk = t_ref.shape[1] // (wc_ref.shape[1] // width)

    @pl.when(g == 0)
    def _():
        db_ref[...] = jnp.zeros_like(db_ref)

    span = chunk * depth
    fill_t(held_ref[pl.ds(pl.multiple_of(g * span, span), span), :width], wc_ref, t_ref, depth)
    db_ref[...] += dot_nt(t_ref[...], g_ref[...])

    @pl.when(g == last)
    def _():
        d_b = db_ref[...].T.astype(BF16)
        own = block // n
        for k in range(n):
            part = d_b[k * own : (k + 1) * own, :]
            for q in range(part.shape[1] // LANES):
                out_ref[k, q * own : (q + 1) * own, :] = part[:, q * LANES : (q + 1) * LANES]
        turned = dot_nt(perm_ref[...], d_b).astype(BF16)
        right = jnp.zeros((width, features), F32)
        for s in range(depth):
            right = right + dot(turned[s * width : (s + 1) * width, :], mj_ref[s])
        small = jnp.concatenate([left_ref[...], right], axis=1)
        small_ref[0:width, :] = small.astype(BF16)
        small_ref[width:, :] = jnp.broadcast_to(bias_ref[0:1, :], (16, LANES)).astype(BF16)


def update_kernel(depth, *refs):
    held_ref, offset_ref, wc_ref, small_ref, out_ref, pass_ref, t_ref = refs
    g = pl.program_id(0)
    chunk, block, pair = out_ref.shape
    width = wc_ref.shape[0]

    @pl.when(g == 0)
    def _():
        pass_ref[...] = small_ref[...]

    span = chunk * depth
    fill_t(held_ref[pl.ds(pl.multiple_of(g * span, span), span), :width], wc_ref, t_ref, depth)
    rows = held_ref.shape[0] - (pl.num_programs(0) - g) * block
    count = held_ref[pl.ds(pl.multiple_of(rows, block), block), :chunk]
    inv = 1.0 / (count.astype(F32) + 0.001)
    b = held_b(held_ref, block, width, depth)
    offset = offset_ref[...]
    for at in range(0, chunk, 2):
        part = dot(b, t_ref[:, at * pair : (at + 2) * pair])
        for k in range(2):
            value = part[:, k * pair : (k + 1) * pair] * inv[:, at + k : at + k + 1] + offset
            out_ref[at + k] = value.astype(BF16)


def owner_kernel(depth, own, features, *refs):
    da_refs, db_ref, small_refs = refs[:2], refs[2], refs[3:5]
    x_ref, wt_ref, perm_ref, dw_ref = refs[5:9]
    out_ref, factors_ref, bias_ref, placed_ref = refs[9:]
    for e in range(dw_ref.shape[0]):
        placed_ref[:, e, :] = dw_ref[e].astype(F32)
    rows = depth * own
    width = wt_ref.shape[0] // 2
    p, q = iota((rows, rows), 0), iota((rows, rows), 1)
    swap = one_hot(q == (p % own) * depth + p // own)
    d_a = dot_nt(swap, da_refs[0][...]) + dot_nt(swap, da_refs[1][...])
    d_b = dot_nt(db_ref[...], perm_ref[...])
    d_b = jnp.concatenate([d_b[:, s * width : (s + 1) * width] for s in range(depth)], axis=0)
    highest = lax.Precision.HIGHEST
    wt = wt_ref[...].astype(F32)
    d_normed = jnp.dot(d_a, wt[:width, :], precision=highest, preferred_element_type=F32)
    d_normed = d_normed + jnp.dot(d_b, wt[width:, :], precision=highest, preferred_element_type=F32)
    x = x_ref[...].astype(F32)
    d_normed = d_normed * x[:, features : features + 1]
    normed, scale = stats(x[:, :features])
    mean = jnp.mean(d_normed, axis=-1, keepdims=True)
    along = jnp.mean(d_normed * normed, axis=-1, keepdims=True)
    out_ref[...] = scale * (d_normed - mean - normed * along)
    small = small_refs[0][...].astype(F32) + small_refs[1][...].astype(F32)
    turned = small[:width].T
    factors_ref[...] = jnp.concatenate([turned[:features], turned[features:]], axis=1)
    bias_ref[...] = small[width : width + 1]


def lay_back(x, rows, lanes):
    if lanes % LANES:
        return x.reshape(rows, lanes)
    return x.reshape(lanes // LANES, rows, LANES).transpose(1, 0, 2).reshape(rows, lanes)


def bit_of(axis, bit):
    return (lax.axis_index(axis) >> bit) & 1


def swap_parts(parts, axis, bit, n):
    parts = [part.reshape(-1, LANES) for part in parts]
    message = jnp.concatenate(parts, axis=0) if len(parts) > 1 else parts[0]
    pairs = [(i, i ^ (1 << bit)) for i in range(n)]
    message = lax.ppermute(message, axis, pairs)
    got, at = [], 0
    for part in parts:
        got.append(message[at : at + part.shape[0]])
        at += part.shape[0]
    return got


def halves(x, axis, bit, at):
    here = bit_of(axis, bit)
    keep = lax.dynamic_index_in_dim(x, here, at, keepdims=False)
    return keep, lax.dynamic_index_in_dim(x, 1 - here, at, keepdims=False)


def split_high(x):
    return x.reshape((2, x.shape[0] // 2) + x.shape[1:])


def in_order(mine, other, axis, bit, at):
    first = bit_of(axis, bit) == 0
    low = jnp.where(first, mine, other)
    return jnp.stack([low, jnp.where(first, other, mine)], axis=at)


def unswap(x, axis):
    n = x.shape[0]
    for bit in range(n.bit_length() - 1):
        y = x.reshape((n >> (bit + 1), 2, 1 << bit) + x.shape[1:])
        x = jnp.where(bit_of(axis, bit + 1) == 0, y, y[:, ::-1]).reshape(x.shape)
    return x


def add(mine, other):
    other = other.reshape(mine.shape)
    return lax.optimization_barrier((mine.astype(F32) + other.astype(F32)).astype(BF16))


def per_device(
    n,
    alignment_embedding,
    alignment_cell_exists,
    alignment_lines_exist,
    sitewise_factors,
    pairing_matrix,
    offset_vector,
    upstream_adjoint,
):
    depth, own, features = alignment_embedding.shape
    width = sitewise_factors.shape[1] // 2
    block, pair = upstream_adjoint.shape[0], upstream_adjoint.shape[2]
    rows, chunk = depth * own, 16
    steps = block // chunk
    split = own % 16 == 0
    axes = ("row", "col")
    sds = jax.ShapeDtypeStruct

    bits = n.bit_length() - 1
    mask = (alignment_cell_exists * alignment_lines_exist[:, None]).astype(BF16)
    mask = jnp.broadcast_to(mask[:, :, None], (depth, own, LANES - features))
    x = jnp.concatenate([alignment_embedding, mask], axis=2).reshape(rows, LANES)
    offset = offset_vector.reshape(1, pair)
    out_shapes = [sds((rows // 2 + own, LANES), BF16)] * 2
    by_token, by_row = call(
        functools.partial(prep_kernel, depth, own, features),
        (),
        [full(x.shape)],
        [full(o.shape) for o in out_shapes],
        out_shapes,
    )(x)
    message = jnp.concatenate([by_token, by_row[: rows // 2]], axis=0)
    both = in_order(message, *swap_parts([message], "col", 0, n), "col", 0, 0)
    message = both[:, : rows // 2 + own]
    held = [message]
    for k in range(2, n, 2):
        held.append(lax.ppermute(message, "col", [(j, j ^ k) for j in range(n)]))
    a_pieces = held
    if own % 16:
        held = unswap(jnp.stack(held), "col").reshape((n,) + message.shape[1:])
        parts = held[:, : rows // 2].reshape(n, rows // 2, 2, features)
        mi = parts.transpose(0, 2, 1, 3).reshape(block * depth, features)
        a_pieces = [mi, held[:, rows // 2 :].reshape(block, LANES)]
    message = both[:, rows // 2 :]
    held = []
    for k in range(0, n, 2):
        pairs = [(i * n + j, (j ^ k) * n + i) for i in range(n) for j in range(n)]
        held.append(lax.ppermute(message, axes, pairs))
    j_pieces = held
    if own % 16:
        held = unswap(jnp.stack(held), "row").reshape((n,) + message.shape[1:])
        parts = held[:, own:].reshape(n, depth // 2, own, 2, features)
        mj = parts.transpose(3, 1, 0, 2, 4).reshape(depth, block, features)
        j_pieces = [mj, held[:, :own].reshape(block, LANES)]

    wide = width * depth
    tokens = block * depth
    source = jnp.arange(wide)
    perm = (jnp.arange(wide)[None, :] == (source % width * depth + source // width)[:, None]).astype(BF16)
    up_spec = pl.BlockSpec((chunk, block, pair), lambda g: (g, 0, 0))
    args = (sitewise_factors, pairing_matrix, offset, upstream_adjoint, *a_pieces)
    out_shapes = [
        sds((2 * width, features), BF16),
        sds((width, width * pair), BF16),
        sds((1, pair), F32),
        sds((8, pair), F32),
        sds((tokens, width), BF16),
        sds((width + features, tokens), BF16),
        sds((block, LANES), BF16),
    ]
    factors_t, pairing_wide, offset, bias, a, a_t, seen = call(
        functools.partial(factor_kernel, own, len(a_pieces)),
        (),
        [full(v.shape) for v in args],
        [full(o.shape) for o in out_shapes],
        out_shapes,
        [pltpu.VMEM((width * width, pair), F32), pltpu.VMEM((tokens, features), BF16)],
    )(*args)

    out_shapes = [
        sds((tokens + block * wide // LANES + block * steps, LANES), BF16),
        sds((width * width, pair), BF16),
        sds((width, features), F32),
        sds((depth, block, features), BF16),
    ]
    args = (a, a_t, seen, factors_t, perm, pairing_wide, *j_pieces)
    large = 2 * chunk
    g_spec = pl.BlockSpec((block, chunk * pair), lambda g: (0, g))
    large_spec = pl.BlockSpec((large, block, pair), lambda g: (g, 0, 0))
    scaled, held, d_pairing, left, mj = call(
        functools.partial(weight_kernel, depth, features, own, len(j_pieces), chunk),
        (block // large,),
        [large_spec] + [full(v.shape) for v in args],
        [pl.BlockSpec((block, large * pair), lambda g: (0, g))] + [full(o.shape) for o in out_shapes],
        [sds((block, block * pair), BF16)] + out_shapes,
        [
            pltpu.VMEM((block, LANES), BF16),
            pltpu.VMEM((wide, block), BF16),
            pltpu.VMEM((steps, block, chunk), F32),
            pltpu.VMEM((large * depth, width * pair), BF16),
            pltpu.VMEM((width * width, pair), F32),
            pltpu.VMEM((features, width * pair), F32),
        ],
        cost(5e9, 8e6),
    )(upstream_adjoint, *args)

    d_pairing = d_pairing.reshape(n, -1, LANES)
    for bit in reversed(range(1, bits)):
        keep, go = halves(split_high(d_pairing), "col", bit, 0)
        d_pairing = add(keep, *swap_parts([go], "col", bit, n))

    out_shapes = [sds((width + 16, LANES), BF16), sds((n, own * wide // LANES, LANES), BF16)]
    small, d_b = call(
        functools.partial(token_kernel, depth, features, n),
        (steps,),
        [g_spec] + [full(v.shape) for v in (held, pairing_wide, mj, perm, bias, left)],
        [full(o.shape) for o in out_shapes],
        out_shapes,
        [pltpu.VMEM((wide, chunk * pair), BF16), pltpu.VMEM((wide, block), F32)],
        cost(8e9, 8e6),
    )(scaled, held, pairing_wide, mj, perm, bias, left)

    dp_keep, dp_go = halves(d_pairing, "col", 0, 0)
    db_keep, db_go = halves(d_b.reshape((n // 2, 2) + d_b.shape[1:]), "col", 0, 1)
    parts = swap_parts([dp_go, db_go, small], "col", 0, n)
    d_pairing, small = add(dp_keep, parts[0]), add(small, parts[2])
    d_b = in_order(db_keep, parts[1].reshape(db_keep.shape), "col", 0, 1)
    db_keep, db_go = halves(d_b, "row", 0, 1)
    for bit in range(bits):
        parts = swap_parts([d_pairing, db_go, small], "row", bit, n)
        if bit == 0:
            args = (held, offset, pairing_wide, small)
            coupling_update, small = call(
                functools.partial(update_kernel, depth),
                (steps,),
                [full(v.shape) for v in args],
                [up_spec, full(small.shape)],
                [sds((block, block, pair), BF16), sds(small.shape, BF16)],
                [pltpu.VMEM((wide, chunk * pair), BF16)],
                cost(6e9, 8e6),
            )(*args)
        if bit == 1:
            half = (tokens // LANES // 2, width, LANES)
            out_shapes = [sds(half, BF16), sds(half, BF16), sds(small.shape, BF16)]
            *d_a, small = call(
                functools.partial(left_kernel, depth, bits - 1),
                (steps,),
                [g_spec] + [full(v.shape) for v in (held, pairing_wide, small)],
                [full(o.shape) for o in out_shapes],
                out_shapes,
                [
                    pltpu.VMEM((chunk * depth, width * pair), BF16),
                    pltpu.VMEM((width * pair, width), BF16),
                    pltpu.VMEM((tokens // LANES, width, LANES), BF16),
                    pltpu.VMEM((wide, block), BF16),
                ],
                cost(6e9, 8e6),
            )(scaled, held, pairing_wide, small)
            if rows % LANES:
                shape = (-1, width, LANES // rows, rows)
                d_a = [part.reshape(shape).transpose(0, 2, 1, 3) for part in d_a]
            da_keep, da_go = [part.reshape(n // 2, -1, LANES) for part in d_a]
        d_pairing, d_b, small = add(d_pairing, parts[0]), add(db_keep, parts[1]), add(small, parts[2])
        db_keep = db_go = d_b
    d_pairing = d_pairing.reshape(1, -1, LANES)
    small_parts = [small]
    for bit in reversed(range(1, bits)):
        if bit < bits - 1:
            small_parts = [add(*small_parts)]
            da_keep, da_go = halves(split_high(add(*da_parts)), "col", bit, 0)
        db_keep, db_go = halves(split_high(d_b), "col", bit, 0)
        parts = swap_parts([d_pairing, db_go, da_go, small_parts[0]], "col", bit, n)
        d_pairing = in_order(d_pairing, parts[0].reshape(d_pairing.shape), "col", bit, 1)
        d_pairing = d_pairing.reshape((-1,) + d_pairing.shape[2:])
        mine = bit_of("col", bit) == bit_of("row", bit)
        d_b = jnp.where(mine, db_keep, parts[1].reshape(db_keep.shape))
        da_parts = [da_keep, parts[2].reshape(da_keep.shape)]
        small_parts = [small_parts[0], parts[3]]
    da_keep, da_go = halves(add(*da_parts), "col", 0, 0)
    got, da_got = swap_parts([d_pairing, da_go], "col", 0, n)
    d_pairing = in_order(d_pairing, got.reshape(d_pairing.shape), "col", 0, 1)
    d_a = [lay_back(part.reshape(-1, LANES), width, rows) for part in (da_keep, da_got)]
    d_b = lay_back(d_b[0], own, wide)

    d_pairing = d_pairing.reshape(width, width, pair)
    args = (*d_a, d_b, *small_parts, x, factors_t, perm, d_pairing)
    out_shapes = [
        sds((rows, features), F32),
        sds((features, 2 * width), F32),
        sds((1, pair), F32),
        sds((width, width, pair), F32),
    ]
    embedding_adjoint, factors_adjoint, offset_slope, placed = call(
        functools.partial(owner_kernel, depth, own, features),
        (),
        [full(v.shape) for v in args],
        [full(o.shape) for o in out_shapes],
        out_shapes,
    )(*args)
    return (
        coupling_update,
        embedding_adjoint.reshape(depth, own, features),
        factors_adjoint,
        placed.reshape(width * width, pair),
        offset_slope.reshape(pair),
    )


def solution(mesh):
    n = mesh.shape["col"]
    placed = (
        P(None, ("groups", "row", "col"), None),
        P(None, ("groups", "row", "col")),
        P("groups"),
        P(),
        P(),
        P(),
        P(("groups", "row"), "col", None),
    )
    return jax.shard_map(
        functools.partial(per_device, n),
        mesh=mesh,
        in_specs=placed,
        out_specs=(
            P(("groups", "row"), "col", None),
            P(None, ("groups", "row", "col"), None),
            P("groups", None),
            P("groups", None),
            P("groups"),
        ),
        check_vma=False,
    )
```

```python
import functools

import jax
import jax.numpy as jnp
from jax import lax
from jax.experimental import pallas as pl
from jax.experimental.pallas import tpu as pltpu
from jax.sharding import PartitionSpec as P

F32 = jnp.float32
BF16 = jnp.bfloat16
LANES = 128
VMEM_LIMIT = 24 * 1024 * 1024
NT = (((1,), (1,)), ((), ()))


def dot(left, right):
    return jnp.dot(left, right, preferred_element_type=F32)


def dot_nt(left, right):
    return lax.dot_general(left, right, NT, preferred_element_type=F32)


def iota(shape, axis):
    return lax.broadcasted_iota(jnp.int32, shape, axis)


def one_hot(mask):
    return jnp.where(mask, 1.0, 0.0).astype(BF16)


def full(shape):
    return pl.BlockSpec(shape, lambda *g: (0,) * len(shape))


def cost(flops, nbytes):
    return pl.CostEstimate(flops=int(flops), bytes_accessed=int(nbytes), transcendentals=0)


def call(kernel, grid, in_specs, out_specs, out_shape, scratch=(), estimate=None):
    return pl.pallas_call(
        kernel,
        grid=grid,
        in_specs=in_specs,
        out_specs=out_specs,
        out_shape=out_shape,
        scratch_shapes=list(scratch),
        compiler_params=pltpu.CompilerParams(vmem_limit_bytes=VMEM_LIMIT),
        cost_estimate=estimate,
    )


def stats(x):
    center = x - jnp.mean(x, axis=-1, keepdims=True)
    scale = lax.rsqrt(jnp.mean(center * center, axis=-1, keepdims=True) + 1e-05)
    return center * scale, scale


def prep_kernel(depth, own, features, x_ref, by_token_ref, by_row_ref):
    rows = depth * own
    half = rows // 2
    x = x_ref[...].astype(F32)
    weight = x[:, features : features + 1]
    normed, _ = stats(x[:, :features])
    masked = normed.astype(BF16).astype(F32) * weight
    by_row_ref[:half, :] = jnp.concatenate([masked[:half], masked[half:]], axis=1).astype(BF16)
    p, q = iota((rows, rows), 0), iota((rows, rows), 1)
    swap = one_hot(q == (p % depth) * own + p // depth)
    turned = dot(swap, masked.astype(BF16))
    by_token_ref[:half, :] = jnp.concatenate([turned[:half], turned[half:]], axis=1).astype(BF16)
    here = one_hot(iota((own, rows), 0) == iota((own, rows), 1) % own)
    at = iota((rows, LANES), 1) == iota((rows, LANES), 0) // own
    mask = dot(here, jnp.where(at, weight, 0.0).astype(BF16)).astype(BF16)
    by_row_ref[half:, :] = mask
    by_token_ref[half:, :] = mask


def fill_v(g_ref, bt, v_ref, depth):
    width = bt.shape[0] // depth
    pair = v_ref.shape[1] // width
    for at in range(0, v_ref.shape[0] // depth, 2):
        v = dot(bt, g_ref[:, at * pair : (at + 2) * pair]).astype(BF16)
        for k in range(2):
            rows = slice((at + k) * depth, (at + k + 1) * depth)
            for e in range(width):
                part = v[e * depth : (e + 1) * depth, k * pair : (k + 1) * pair]
                v_ref[rows, e * pair : (e + 1) * pair] = part


def fill_t(a_chunk, wc_ref, t_ref, depth):
    width = wc_ref.shape[0]
    pair = wc_ref.shape[1] // width
    for e in range(0, width, 2):
        t = dot(a_chunk, wc_ref[:, e * pair : (e + 2) * pair]).astype(BF16)
        for k in range(2):
            rows = slice((e + k) * depth, (e + k + 1) * depth)
            for i in range(a_chunk.shape[0] // depth):
                part = t[i * depth : (i + 1) * depth, k * pair : (k + 1) * pair]
                t_ref[rows, i * pair : (i + 1) * pair] = part


def held_b(held_ref, block, width, depth):
    at = block * depth
    tiles = width * depth // LANES
    return jnp.concatenate([held_ref[at + k * block : at + (k + 1) * block, :] for k in range(tiles)], axis=1)


def factor_kernel(w_ref, wide_ref, offset_ref, up_ref, wt_ref, wc_ref, pass_ref, bias_ref, rows_ref):
    width = w_ref.shape[1] // 2
    pair = wide_ref.shape[1]
    pass_ref[...] = offset_ref[...]
    rows_ref[...] = wide_ref[...].astype(F32)
    for e in range(width):
        part = rows_ref[pl.ds(e, width, stride=width), :]
        wc_ref[:, e * pair : (e + 1) * pair] = part.astype(BF16)
    same = one_hot(iota((2 * width, 2 * width), 0) == iota((2 * width, 2 * width), 1))
    wt_ref[...] = dot_nt(same, w_ref[...]).astype(BF16)
    bias = [jnp.zeros(up_ref.shape[1:], F32)] * 2
    for i in range(up_ref.shape[0]):
        bias[i % 2] = bias[i % 2] + up_ref[i].astype(F32)
    bias = jnp.sum(bias[0] + bias[1], axis=0, keepdims=True)
    bias_ref[...] = jnp.broadcast_to(bias, bias_ref.shape)


def unpack(depth, own, features, a_refs, j_refs, mi_ref, mj_ref, seen_i_ref, seen_j_ref):
    half = depth * own // 2
    for k, ref in enumerate(a_refs):
        for core in range(2):
            at = ((lax.axis_index("col") >> 1) ^ k) * 2 + core
            for q in range(2):
                rows = pl.ds(pl.multiple_of((at * 2 + q) * half, half), half)
                mi_ref[rows, :] = ref[core, :half, q * features : (q + 1) * features]
            rows = pl.ds(pl.multiple_of(at * own, own), own)
            seen_i_ref[rows, :] = ref[core, half:, :]
    half = depth // 2
    for k, ref in enumerate(j_refs):
        for core in range(2):
            at = ((lax.axis_index("row") >> 1) ^ k) * 2 + core
            rows = pl.ds(pl.multiple_of(at * own, own), own)
            seen_j_ref[rows, :] = ref[core, :own, :]
            for s in range(depth):
                lanes = slice(s // half * features, (s // half + 1) * features)
                start = own + s % half * own
                mj_ref[s, rows, :] = ref[core, start : start + own, lanes]


def weight_kernel(depth, features, own, pieces, chunk, *refs):
    up_ref, wt_ref, perm_ref, wc_ref = refs[:4]
    a_refs, j_refs, refs = refs[4 : 4 + pieces], refs[4 + pieces : 4 + 2 * pieces], refs[4 + 2 * pieces :]
    g_ref, held_ref, dw_ref, left_ref, mj_ref = refs[:5]
    mi_ref, seen_i_ref, seen_j_ref, bt_ref, inv_ref, v_ref = refs[5:]
    block, pair = up_ref.shape[1:]
    width = wt_ref.shape[0] // 2
    if own % 16 == 0:
        unpack(depth, own, features, a_refs, j_refs, mi_ref, mj_ref, seen_i_ref, seen_j_ref)
    else:
        mi_ref[...], seen_i_ref[...] = a_refs[0][...], a_refs[1][...]
        mj_ref[...], seen_j_ref[...] = j_refs[0][...], j_refs[1][...]
    wt = wt_ref[...]
    mi = mi_ref[...]
    held_ref[: block * depth, :width] = dot_nt(mi, wt[:width, :]).astype(BF16)
    same = one_hot(iota((features, features), 0) == iota((features, features), 1))
    a_t = dot_nt(jnp.concatenate([wt[:width, :], same], axis=0), mi).astype(BF16)
    b = jnp.zeros((block, width * depth), F32)
    for s in range(depth):
        part = dot_nt(mj_ref[s], wt[width:, :]).astype(BF16)
        b = b + dot(part, perm_ref[s * width : (s + 1) * width, :])
    bt_ref[...] = b.T.astype(BF16)
    at = block * depth
    for k in range(width * depth // LANES):
        held_ref[at : at + block, :] = b[:, k * LANES : (k + 1) * LANES].astype(BF16)
        at += block
    for k in range(block // chunk):
        count = dot_nt(seen_j_ref[...], seen_i_ref[k * chunk : (k + 1) * chunk, :])
        inv_ref[k] = 1.0 / (count + 0.001)
        held_ref[at : at + block, :chunk] = count.astype(BF16)
        at += block

    def fill(k, carry):
        inv = inv_ref[k]
        b_t = bt_ref[...]
        for i in range(0, chunk, 2):
            parts = [up_ref[k * chunk + i + q].astype(F32) * inv[:, i + q : i + q + 1] for q in range(2)]
            scaled = jnp.concatenate(parts, axis=1).astype(BF16)
            g_ref[:, pl.ds(pl.multiple_of((k * chunk + i) * pair, 2 * pair), 2 * pair)] = scaled
            v = dot(b_t, scaled).astype(BF16)
            for q in range(2):
                rows = pl.ds(pl.multiple_of((k * chunk + i + q) * depth, depth), depth)
                for e in range(width):
                    part = v[e * depth : (e + 1) * depth, q * pair : (q + 1) * pair]
                    v_ref[rows, e * pair : (e + 1) * pair] = part
        return carry

    lax.fori_loop(0, block // chunk, fill, 0)
    left = jnp.zeros((width, features), F32)
    for e in range(0, width, 2):
        lanes = slice(e * pair, (e + 2) * pair)
        part = dot(a_t, v_ref[:, lanes]).astype(BF16)
        for k in range(2):
            dw_ref[(e + k) * width : (e + k + 1) * width, :] = part[:width, k * pair : (k + 1) * pair]
        left = left + dot_nt(wc_ref[:, lanes], part[width:])
    left_ref[...] = left


def left_kernel(depth, bit, *refs):
    g_ref, held_ref, wc_ref, small_ref, keep_ref, go_ref, pass_ref, v_ref, wd_ref, da_ref, bt_ref = refs
    g, last = pl.program_id(0), pl.num_programs(0) - 1
    block, width = g_ref.shape[0], wc_ref.shape[0]
    pair = wc_ref.shape[1] // width
    span = v_ref.shape[0]

    @pl.when(g == 0)
    def _():
        pass_ref[...] = small_ref[...]
        bt_ref[...] = held_b(held_ref, block, width, depth).astype(F32).T.astype(BF16)
        same = one_hot(iota((2 * pair, 2 * pair), 0) == iota((2 * pair, 2 * pair), 1))
        for at in range(0, wd_ref.shape[0], 2 * pair):
            wd_ref[at : at + 2 * pair, :] = dot_nt(same, wc_ref[:, at : at + 2 * pair]).astype(BF16)

    fill_v(g_ref, bt_ref[...], v_ref, depth)
    d_a = jnp.zeros((span, width), F32)
    each = v_ref.shape[1] // 4
    for at in range(0, 4 * each, each):
        d_a = d_a + dot(v_ref[:, at : at + each], wd_ref[at : at + each, :])
    same = one_hot(iota((width, width), 0) == iota((width, width), 1))
    d_a = dot_nt(same, d_a.astype(BF16)).astype(BF16)
    tiles = span // LANES
    for k in range(tiles):
        da_ref[g * tiles + k] = d_a[:, k * LANES : (k + 1) * LANES]

    @pl.when(g == last)
    def _():
        half = keep_ref.shape[0]
        here = (lax.axis_index("col") >> bit) & 1
        keep_ref[...] = da_ref[pl.ds(here * half, half)]
        go_ref[...] = da_ref[pl.ds((1 - here) * half, half)]


def token_kernel(depth, features, n, *refs):
    g_ref, held_ref, wc_ref, mj_ref, perm_ref, bias_ref, left_ref = refs[:7]
    small_ref, out_ref, t_ref, db_ref = refs[7:]
    g, last = pl.program_id(0), pl.num_programs(0) - 1
    block, width = g_ref.shape[0], left_ref.shape[0]
    chunk = t_ref.shape[1] // (wc_ref.shape[1] // width)

    @pl.when(g == 0)
    def _():
        db_ref[...] = jnp.zeros_like(db_ref)

    span = chunk * depth
    fill_t(held_ref[pl.ds(pl.multiple_of(g * span, span), span), :width], wc_ref, t_ref, depth)
    db_ref[...] += dot_nt(t_ref[...], g_ref[...])

    @pl.when(g == last)
    def _():
        d_b = db_ref[...].T.astype(BF16)
        own = block // n
        for k in range(n):
            part = d_b[k * own : (k + 1) * own, :]
            for q in range(part.shape[1] // LANES):
                out_ref[k, q * own : (q + 1) * own, :] = part[:, q * LANES : (q + 1) * LANES]
        turned = dot_nt(perm_ref[...], d_b).astype(BF16)
        right = jnp.zeros((width, features), F32)
        for s in range(depth):
            right = right + dot(turned[s * width : (s + 1) * width, :], mj_ref[s])
        small = jnp.concatenate([left_ref[...], right], axis=1)
        small_ref[0:width, :] = small.astype(BF16)
        small_ref[width:, :] = jnp.broadcast_to(bias_ref[0:1, :], (16, LANES)).astype(BF16)


def update_kernel(depth, *refs):
    held_ref, offset_ref, wc_ref, small_ref, out_ref, pass_ref, t_ref = refs
    g = pl.program_id(0)
    chunk, block, pair = out_ref.shape
    width = wc_ref.shape[0]

    @pl.when(g == 0)
    def _():
        pass_ref[...] = small_ref[...]

    span = chunk * depth
    fill_t(held_ref[pl.ds(pl.multiple_of(g * span, span), span), :width], wc_ref, t_ref, depth)
    rows = held_ref.shape[0] - (pl.num_programs(0) - g) * block
    count = held_ref[pl.ds(pl.multiple_of(rows, block), block), :chunk]
    inv = 1.0 / (count.astype(F32) + 0.001)
    b = held_b(held_ref, block, width, depth)
    offset = offset_ref[...]
    for at in range(0, chunk, 2):
        part = dot(b, t_ref[:, at * pair : (at + 2) * pair])
        for k in range(2):
            value = part[:, k * pair : (k + 1) * pair] * inv[:, at + k : at + k + 1] + offset
            out_ref[at + k] = value.astype(BF16)


def owner_kernel(depth, own, features, *refs):
    da_refs, db_ref, small_refs = refs[:2], refs[2], refs[3:5]
    x_ref, wt_ref, perm_ref, dw_ref = refs[5:9]
    out_ref, factors_ref, bias_ref, placed_ref = refs[9:]
    for e in range(dw_ref.shape[0]):
        placed_ref[:, e, :] = dw_ref[e].astype(F32)
    rows = depth * own
    width = wt_ref.shape[0] // 2
    p, q = iota((rows, rows), 0), iota((rows, rows), 1)
    swap = one_hot(q == (p % own) * depth + p // own)
    d_a = dot_nt(swap, da_refs[0][...]) + dot_nt(swap, da_refs[1][...])
    d_b = dot_nt(db_ref[...], perm_ref[...])
    d_b = jnp.concatenate([d_b[:, s * width : (s + 1) * width] for s in range(depth)], axis=0)
    highest = lax.Precision.HIGHEST
    wt = wt_ref[...].astype(F32)
    d_normed = jnp.dot(d_a, wt[:width, :], precision=highest, preferred_element_type=F32)
    d_normed = d_normed + jnp.dot(d_b, wt[width:, :], precision=highest, preferred_element_type=F32)
    x = x_ref[...].astype(F32)
    d_normed = d_normed * x[:, features : features + 1]
    normed, scale = stats(x[:, :features])
    mean = jnp.mean(d_normed, axis=-1, keepdims=True)
    along = jnp.mean(d_normed * normed, axis=-1, keepdims=True)
    out_ref[...] = scale * (d_normed - mean - normed * along)
    small = small_refs[0][...].astype(F32) + small_refs[1][...].astype(F32)
    turned = small[:width].T
    factors_ref[...] = jnp.concatenate([turned[:features], turned[features:]], axis=1)
    bias_ref[...] = small[width : width + 1]


def lay_back(x, rows, lanes):
    if lanes % LANES:
        return x.reshape(rows, lanes)
    return x.reshape(lanes // LANES, rows, LANES).transpose(1, 0, 2).reshape(rows, lanes)


def bit_of(axis, bit):
    return (lax.axis_index(axis) >> bit) & 1


def swap_parts(parts, axis, bit, n):
    parts = [part.reshape(-1, LANES) for part in parts]
    message = jnp.concatenate(parts, axis=0) if len(parts) > 1 else parts[0]
    pairs = [(i, i ^ (1 << bit)) for i in range(n)]
    message = lax.ppermute(message, axis, pairs)
    got, at = [], 0
    for part in parts:
        got.append(message[at : at + part.shape[0]])
        at += part.shape[0]
    return got


def halves(x, axis, bit, at):
    here = bit_of(axis, bit)
    keep = lax.dynamic_index_in_dim(x, here, at, keepdims=False)
    return keep, lax.dynamic_index_in_dim(x, 1 - here, at, keepdims=False)


def split_high(x):
    return x.reshape((2, x.shape[0] // 2) + x.shape[1:])


def in_order(mine, other, axis, bit, at):
    first = bit_of(axis, bit) == 0
    low = jnp.where(first, mine, other)
    return jnp.stack([low, jnp.where(first, other, mine)], axis=at)


def unswap(x, axis):
    n = x.shape[0]
    for bit in range(n.bit_length() - 1):
        y = x.reshape((n >> (bit + 1), 2, 1 << bit) + x.shape[1:])
        x = jnp.where(bit_of(axis, bit + 1) == 0, y, y[:, ::-1]).reshape(x.shape)
    return x


def add(mine, other):
    other = other.reshape(mine.shape)
    return lax.optimization_barrier((mine.astype(F32) + other.astype(F32)).astype(BF16))


def per_device(
    n,
    alignment_embedding,
    alignment_cell_exists,
    alignment_lines_exist,
    sitewise_factors,
    pairing_matrix,
    offset_vector,
    upstream_adjoint,
):
    depth, own, features = alignment_embedding.shape
    width = sitewise_factors.shape[1] // 2
    block, pair = upstream_adjoint.shape[0], upstream_adjoint.shape[2]
    rows, chunk = depth * own, 16
    steps = block // chunk
    split = own % 16 == 0
    axes = ("row", "col")
    sds = jax.ShapeDtypeStruct

    bits = n.bit_length() - 1
    mask = (alignment_cell_exists * alignment_lines_exist[:, None]).astype(BF16)
    mask = jnp.broadcast_to(mask[:, :, None], (depth, own, LANES - features))
    x = jnp.concatenate([alignment_embedding, mask], axis=2).reshape(rows, LANES)
    offset = offset_vector.reshape(1, pair)
    out_shapes = [sds((rows // 2 + own, LANES), BF16)] * 2
    by_token, by_row = call(
        functools.partial(prep_kernel, depth, own, features),
        (),
        [full(x.shape)],
        [full(o.shape) for o in out_shapes],
        out_shapes,
    )(x)
    message = jnp.concatenate([by_token, by_row[: rows // 2]], axis=0)
    both = in_order(message, *swap_parts([message], "col", 0, n), "col", 0, 0)
    message = both[:, : rows // 2 + own]
    held = [message]
    for k in range(2, n, 2):
        held.append(lax.ppermute(message, "col", [(j, j ^ k) for j in range(n)]))
    a_pieces = held
    if own % 16:
        held = unswap(jnp.stack(held), "col").reshape((n,) + message.shape[1:])
        parts = held[:, : rows // 2].reshape(n, rows // 2, 2, features)
        mi = parts.transpose(0, 2, 1, 3).reshape(block * depth, features)
        a_pieces = [mi, held[:, rows // 2 :].reshape(block, LANES)]
    message = both[:, rows // 2 :]
    held = []
    for k in range(0, n, 2):
        pairs = [(i * n + j, (j ^ k) * n + i) for i in range(n) for j in range(n)]
        held.append(lax.ppermute(message, axes, pairs))
    j_pieces = held
    if own % 16:
        held = unswap(jnp.stack(held), "row").reshape((n,) + message.shape[1:])
        parts = held[:, own:].reshape(n, depth // 2, own, 2, features)
        mj = parts.transpose(3, 1, 0, 2, 4).reshape(depth, block, features)
        j_pieces = [mj, held[:, :own].reshape(block, LANES)]

    wide = width * depth
    tokens = block * depth
    source = jnp.arange(wide)
    perm = (jnp.arange(wide)[None, :] == (source % width * depth + source // width)[:, None]).astype(BF16)
    up_spec = pl.BlockSpec((chunk, block, pair), lambda g: (g, 0, 0))
    args = (sitewise_factors, pairing_matrix, offset, upstream_adjoint)
    out_shapes = [
        sds((2 * width, features), BF16),
        sds((width, width * pair), BF16),
        sds((1, pair), F32),
        sds((8, pair), F32),
    ]
    factors_t, pairing_wide, offset, bias = call(
        factor_kernel,
        (),
        [full(v.shape) for v in args],
        [full(o.shape) for o in out_shapes],
        out_shapes,
        [pltpu.VMEM((width * width, pair), F32)],
    )(*args)

    out_shapes = [
        sds((block, block * pair), BF16),
        sds((tokens + block * wide // LANES + block * steps, LANES), BF16),
        sds((width * width, pair), BF16),
        sds((width, features), F32),
        sds((depth, block, features), BF16),
    ]
    args = (upstream_adjoint, factors_t, perm, pairing_wide, *a_pieces, *j_pieces)
    scaled, held, d_pairing, left, mj = call(
        functools.partial(weight_kernel, depth, features, own, len(a_pieces), chunk),
        (),
        [full(v.shape) for v in args],
        [full(o.shape) for o in out_shapes],
        out_shapes,
        [
            pltpu.VMEM((tokens, features), BF16),
            pltpu.VMEM((block, LANES), BF16),
            pltpu.VMEM((block, LANES), BF16),
            pltpu.VMEM((wide, block), BF16),
            pltpu.VMEM((steps, block, chunk), F32),
            pltpu.VMEM((tokens, width * pair), BF16),
        ],
        cost(5e9, 8e6),
    )(*args)
    large = 2 * chunk
    g_spec = pl.BlockSpec((block, chunk * pair), lambda g: (0, g))

    d_pairing = d_pairing.reshape(n, -1, LANES)
    for bit in reversed(range(1, bits)):
        keep, go = halves(split_high(d_pairing), "col", bit, 0)
        d_pairing = add(keep, *swap_parts([go], "col", bit, n))

    out_shapes = [sds((width + 16, LANES), BF16), sds((n, own * wide // LANES, LANES), BF16)]
    small, d_b = call(
        functools.partial(token_kernel, depth, features, n),
        (block // large,),
        [pl.BlockSpec((block, large * pair), lambda g: (0, g))] + [full(v.shape) for v in (held, pairing_wide, mj, perm, bias, left)],
        [full(o.shape) for o in out_shapes],
        out_shapes,
        [pltpu.VMEM((wide, large * pair), BF16), pltpu.VMEM((wide, block), F32)],
        cost(8e9, 8e6),
    )(scaled, held, pairing_wide, mj, perm, bias, left)

    dp_keep, dp_go = halves(d_pairing, "col", 0, 0)
    db_keep, db_go = halves(d_b.reshape((n // 2, 2) + d_b.shape[1:]), "col", 0, 1)
    parts = swap_parts([dp_go, db_go, small], "col", 0, n)
    d_pairing, small = add(dp_keep, parts[0]), add(small, parts[2])
    d_b = in_order(db_keep, parts[1].reshape(db_keep.shape), "col", 0, 1)
    db_keep, db_go = halves(d_b, "row", 0, 1)
    for bit in range(bits):
        parts = swap_parts([d_pairing, db_go, small], "row", bit, n)
        if bit == 0:
            args = (held, offset, pairing_wide, small)
            coupling_update, small = call(
                functools.partial(update_kernel, depth),
                (steps,),
                [full(v.shape) for v in args],
                [up_spec, full(small.shape)],
                [sds((block, block, pair), BF16), sds(small.shape, BF16)],
                [pltpu.VMEM((wide, chunk * pair), BF16)],
                cost(6e9, 8e6),
            )(*args)
        if bit == 1:
            half = (tokens // LANES // 2, width, LANES)
            out_shapes = [sds(half, BF16), sds(half, BF16), sds(small.shape, BF16)]
            *d_a, small = call(
                functools.partial(left_kernel, depth, bits - 1),
                (steps,),
                [g_spec] + [full(v.shape) for v in (held, pairing_wide, small)],
                [full(o.shape) for o in out_shapes],
                out_shapes,
                [
                    pltpu.VMEM((chunk * depth, width * pair), BF16),
                    pltpu.VMEM((width * pair, width), BF16),
                    pltpu.VMEM((tokens // LANES, width, LANES), BF16),
                    pltpu.VMEM((wide, block), BF16),
                ],
                cost(6e9, 8e6),
            )(scaled, held, pairing_wide, small)
            if rows % LANES:
                shape = (-1, width, LANES // rows, rows)
                d_a = [part.reshape(shape).transpose(0, 2, 1, 3) for part in d_a]
            da_keep, da_go = [part.reshape(n // 2, -1, LANES) for part in d_a]
        d_pairing, d_b, small = add(d_pairing, parts[0]), add(db_keep, parts[1]), add(small, parts[2])
        db_keep = db_go = d_b
    d_pairing = d_pairing.reshape(1, -1, LANES)
    small_parts = [small]
    for bit in reversed(range(1, bits)):
        if bit < bits - 1:
            small_parts = [add(*small_parts)]
            da_keep, da_go = halves(split_high(add(*da_parts)), "col", bit, 0)
        db_keep, db_go = halves(split_high(d_b), "col", bit, 0)
        parts = swap_parts([d_pairing, db_go, da_go, small_parts[0]], "col", bit, n)
        d_pairing = in_order(d_pairing, parts[0].reshape(d_pairing.shape), "col", bit, 1)
        d_pairing = d_pairing.reshape((-1,) + d_pairing.shape[2:])
        mine = bit_of("col", bit) == bit_of("row", bit)
        d_b = jnp.where(mine, db_keep, parts[1].reshape(db_keep.shape))
        da_parts = [da_keep, parts[2].reshape(da_keep.shape)]
        small_parts = [small_parts[0], parts[3]]
    da_keep, da_go = halves(add(*da_parts), "col", 0, 0)
    got, da_got = swap_parts([d_pairing, da_go], "col", 0, n)
    d_pairing = in_order(d_pairing, got.reshape(d_pairing.shape), "col", 0, 1)
    d_a = [lay_back(part.reshape(-1, LANES), width, rows) for part in (da_keep, da_got)]
    d_b = lay_back(d_b[0], own, wide)

    d_pairing = d_pairing.reshape(width, width, pair)
    args = (*d_a, d_b, *small_parts, x, factors_t, perm, d_pairing)
    out_shapes = [
        sds((rows, features), F32),
        sds((features, 2 * width), F32),
        sds((1, pair), F32),
        sds((width, width, pair), F32),
    ]
    embedding_adjoint, factors_adjoint, offset_slope, placed = call(
        functools.partial(owner_kernel, depth, own, features),
        (),
        [full(v.shape) for v in args],
        [full(o.shape) for o in out_shapes],
        out_shapes,
    )(*args)
    return (
        coupling_update,
        embedding_adjoint.reshape(depth, own, features),
        factors_adjoint,
        placed.reshape(width * width, pair),
        offset_slope.reshape(pair),
    )


def solution(mesh):
    n = mesh.shape["col"]
    placed = (
        P(None, ("groups", "row", "col"), None),
        P(None, ("groups", "row", "col")),
        P("groups"),
        P(),
        P(),
        P(),
        P(("groups", "row"), "col", None),
    )
    return jax.shard_map(
        functools.partial(per_device, n),
        mesh=mesh,
        in_specs=placed,
        out_specs=(
            P(("groups", "row"), "col", None),
            P(None, ("groups", "row", "col"), None),
            P("groups", None),
            P("groups", None),
            P("groups"),
        ),
        check_vma=False,
    )
```

```python
import functools

import jax
import jax.numpy as jnp
from jax import lax
from jax.experimental import pallas as pl
from jax.experimental.pallas import tpu as pltpu
from jax.sharding import PartitionSpec as P

F32 = jnp.float32
BF16 = jnp.bfloat16
LANES = 128
VMEM_LIMIT = 24 * 1024 * 1024
NT = (((1,), (1,)), ((), ()))


def dot(left, right):
    return jnp.dot(left, right, preferred_element_type=F32)


def dot_nt(left, right):
    return lax.dot_general(left, right, NT, preferred_element_type=F32)


def iota(shape, axis):
    return lax.broadcasted_iota(jnp.int32, shape, axis)


def one_hot(mask):
    return jnp.where(mask, 1.0, 0.0).astype(BF16)


def full(shape):
    return pl.BlockSpec(shape, lambda *g: (0,) * len(shape))


def cost(flops, nbytes):
    return pl.CostEstimate(flops=int(flops), bytes_accessed=int(nbytes), transcendentals=0)


def call(kernel, grid, in_specs, out_specs, out_shape, scratch=(), estimate=None):
    return pl.pallas_call(
        kernel,
        grid=grid,
        in_specs=in_specs,
        out_specs=out_specs,
        out_shape=out_shape,
        scratch_shapes=list(scratch),
        compiler_params=pltpu.CompilerParams(vmem_limit_bytes=VMEM_LIMIT),
        cost_estimate=estimate,
    )


def stats(x):
    center = x - jnp.mean(x, axis=-1, keepdims=True)
    scale = lax.rsqrt(jnp.mean(center * center, axis=-1, keepdims=True) + 1e-05)
    return center * scale, scale


def prep_kernel(depth, own, features, x_ref, by_token_ref, by_row_ref):
    rows = depth * own
    half = rows // 2
    x = x_ref[...].astype(F32)
    weight = x[:, features : features + 1]
    normed, _ = stats(x[:, :features])
    masked = normed.astype(BF16).astype(F32) * weight
    by_row_ref[:half, :] = jnp.concatenate([masked[:half], masked[half:]], axis=1).astype(BF16)
    p, q = iota((rows, rows), 0), iota((rows, rows), 1)
    swap = one_hot(q == (p % depth) * own + p // depth)
    turned = dot(swap, masked.astype(BF16))
    by_token_ref[:half, :] = jnp.concatenate([turned[:half], turned[half:]], axis=1).astype(BF16)
    here = one_hot(iota((own, rows), 0) == iota((own, rows), 1) % own)
    at = iota((rows, LANES), 1) == iota((rows, LANES), 0) // own
    mask = dot(here, jnp.where(at, weight, 0.0).astype(BF16)).astype(BF16)
    by_row_ref[half:, :] = mask
    by_token_ref[half:, :] = mask


def fill_v(g_ref, bt, v_ref, depth):
    width = bt.shape[0] // depth
    pair = v_ref.shape[1] // width
    for at in range(0, v_ref.shape[0] // depth, 2):
        v = dot(bt, g_ref[:, at * pair : (at + 2) * pair]).astype(BF16)
        for k in range(2):
            rows = slice((at + k) * depth, (at + k + 1) * depth)
            for e in range(width):
                part = v[e * depth : (e + 1) * depth, k * pair : (k + 1) * pair]
                v_ref[rows, e * pair : (e + 1) * pair] = part


def fill_t(a_chunk, wc_ref, t_ref, depth):
    width = wc_ref.shape[0]
    pair = wc_ref.shape[1] // width
    for e in range(0, width, 2):
        t = dot(a_chunk, wc_ref[:, e * pair : (e + 2) * pair]).astype(BF16)
        for k in range(2):
            rows = slice((e + k) * depth, (e + k + 1) * depth)
            for i in range(a_chunk.shape[0] // depth):
                part = t[i * depth : (i + 1) * depth, k * pair : (k + 1) * pair]
                t_ref[rows, i * pair : (i + 1) * pair] = part


def held_b(held_ref, block, width, depth):
    at = block * depth
    tiles = width * depth // LANES
    return jnp.concatenate([held_ref[at + k * block : at + (k + 1) * block, :] for k in range(tiles)], axis=1)


def factor_kernel(w_ref, wide_ref, offset_ref, up_ref, wt_ref, wc_ref, pass_ref, bias_ref, rows_ref):
    width = w_ref.shape[1] // 2
    pair = wide_ref.shape[1]
    pass_ref[...] = offset_ref[...]
    rows_ref[...] = wide_ref[...].astype(F32)
    for e in range(width):
        part = rows_ref[pl.ds(e, width, stride=width), :]
        wc_ref[:, e * pair : (e + 1) * pair] = part.astype(BF16)
    same = one_hot(iota((2 * width, 2 * width), 0) == iota((2 * width, 2 * width), 1))
    wt_ref[...] = dot_nt(same, w_ref[...]).astype(BF16)
    bias = [jnp.zeros(up_ref.shape[1:], F32)] * 2
    for i in range(up_ref.shape[0]):
        bias[i % 2] = bias[i % 2] + up_ref[i].astype(F32)
    bias = jnp.sum(bias[0] + bias[1], axis=0, keepdims=True)
    bias_ref[...] = jnp.broadcast_to(bias, bias_ref.shape)


def unpack(depth, own, features, a_refs, j_refs, mi_ref, mj_ref, seen_i_ref, seen_j_ref):
    half = depth * own // 2
    for k, ref in enumerate(a_refs):
        for core in range(2):
            at = ((lax.axis_index("col") >> 1) ^ k) * 2 + core
            for q in range(2):
                rows = pl.ds(pl.multiple_of((at * 2 + q) * half, half), half)
                mi_ref[rows, :] = ref[core, :half, q * features : (q + 1) * features]
            rows = pl.ds(pl.multiple_of(at * own, own), own)
            seen_i_ref[rows, :] = ref[core, half:, :]
    half = depth // 2
    for k, ref in enumerate(j_refs):
        for core in range(2):
            at = ((lax.axis_index("row") & (len(j_refs) - 1)) ^ k) * 2 + core
            rows = pl.ds(pl.multiple_of(at * own, own), own)
            seen_j_ref[rows, :] = ref[core, :own, :]
            for s in range(depth):
                lanes = slice(s // half * features, (s // half + 1) * features)
                start = own + s % half * own
                mj_ref[s, rows, :] = ref[core, start : start + own, lanes]


def weight_kernel(depth, features, own, pieces, part_size, *refs):
    up_ref, wt_ref, perm_ref, wc_ref = refs[:4]
    a_refs, j_refs, refs = refs[4 : 4 + pieces], refs[4 + pieces : 4 + 2 * pieces], refs[4 + 2 * pieces :]
    g_ref, held_ref, dw_ref, left_ref, mj_ref = refs[:5]
    mi_ref, seen_i_ref, seen_j_ref, at_ref, bt_ref, inv_ref, v_ref, acc_ref, wide_ref = refs[5:]
    g, last = pl.program_id(0), pl.num_programs(0) - 1
    chunk, block, pair = up_ref.shape
    width = wt_ref.shape[0] // 2

    @pl.when(g == 0)
    def _():
        if own % 16 == 0:
            unpack(depth, own, features, a_refs, j_refs, mi_ref, mj_ref, seen_i_ref, seen_j_ref)
        else:
            mi_ref[...], seen_i_ref[...] = a_refs[0][...], a_refs[1][...]
            mj_ref[...], seen_j_ref[...] = j_refs[0][...], j_refs[1][...]
        wt = wt_ref[...]
        mi = mi_ref[...]
        held_ref[: block * depth, :width] = dot_nt(mi, wt[:width, :]).astype(BF16)
        same = one_hot(iota((features, features), 0) == iota((features, features), 1))
        at_ref[...] = dot_nt(jnp.concatenate([wt[:width, :], same], axis=0), mi).astype(BF16)
        b = jnp.zeros((block, width * depth), F32)
        for s in range(depth):
            part = dot_nt(mj_ref[s], wt[width:, :]).astype(BF16)
            b = b + dot(part, perm_ref[s * width : (s + 1) * width, :])
        bt_ref[...] = b.T.astype(BF16)
        at = block * depth
        for k in range(width * depth // LANES):
            held_ref[at : at + block, :] = b[:, k * LANES : (k + 1) * LANES].astype(BF16)
            at += block
        for k in range(block // part_size):
            rows = slice(k * part_size, (k + 1) * part_size)
            count = dot_nt(seen_j_ref[...], seen_i_ref[rows, :])
            inv_ref[k] = 1.0 / (count + 0.001)
            held_ref[at : at + block, :part_size] = count.astype(BF16)
            at += block
        acc_ref[...] = jnp.zeros_like(acc_ref)
        wide_ref[...] = jnp.zeros_like(wide_ref)

    for k in range(chunk // part_size):
        inv = inv_ref[g * (chunk // part_size) + k]
        for i in range(part_size):
            up = up_ref[k * part_size + i].astype(F32)
            at = (k * part_size + i) * pair
            g_ref[:, at : at + pair] = (up * inv[:, i : i + 1]).astype(BF16)
    fill_v(g_ref, bt_ref[...], v_ref, depth)
    span = chunk * depth
    a_t = at_ref[:, pl.ds(pl.multiple_of(g * span, span), span)]
    for e in range(0, width, 2):
        part = dot(a_t, v_ref[:, e * pair : (e + 2) * pair])
        for k in range(2):
            rows = slice((e + k) * width, (e + k + 1) * width)
            acc_ref[rows, :] += part[:width, k * pair : (k + 1) * pair]
        wide_ref[:, e * pair : (e + 2) * pair] += part[width:]

    @pl.when(g == last)
    def _():
        dw_ref[...] = acc_ref[...].astype(BF16)
        left = jnp.zeros((width, features), F32)
        for e in range(0, width, 2):
            lanes = slice(e * pair, (e + 2) * pair)
            left = left + dot_nt(wc_ref[:, lanes], wide_ref[:, lanes].astype(BF16))
        left_ref[...] = left


def left_kernel(depth, bit, *refs):
    g_ref, held_ref, wc_ref, small_ref, keep_ref, go_ref, pass_ref, v_ref, wd_ref, da_ref, bt_ref = refs
    g, last = pl.program_id(0), pl.num_programs(0) - 1
    block, width = g_ref.shape[0], wc_ref.shape[0]
    pair = wc_ref.shape[1] // width
    span = v_ref.shape[0]

    @pl.when(g == 0)
    def _():
        pass_ref[...] = small_ref[...]
        bt_ref[...] = held_b(held_ref, block, width, depth).astype(F32).T.astype(BF16)
        same = one_hot(iota((2 * pair, 2 * pair), 0) == iota((2 * pair, 2 * pair), 1))
        for at in range(0, wd_ref.shape[0], 2 * pair):
            wd_ref[at : at + 2 * pair, :] = dot_nt(same, wc_ref[:, at : at + 2 * pair]).astype(BF16)

    fill_v(g_ref, bt_ref[...], v_ref, depth)
    d_a = jnp.zeros((span, width), F32)
    each = v_ref.shape[1] // 4
    for at in range(0, 4 * each, each):
        d_a = d_a + dot(v_ref[:, at : at + each], wd_ref[at : at + each, :])
    same = one_hot(iota((width, width), 0) == iota((width, width), 1))
    d_a = dot_nt(same, d_a.astype(BF16)).astype(BF16)
    tiles = span // LANES
    for k in range(tiles):
        da_ref[g * tiles + k] = d_a[:, k * LANES : (k + 1) * LANES]

    @pl.when(g == last)
    def _():
        half = keep_ref.shape[0]
        here = (lax.axis_index("col") >> bit) & 1
        keep_ref[...] = da_ref[pl.ds(here * half, half)]
        go_ref[...] = da_ref[pl.ds((1 - here) * half, half)]


def token_kernel(depth, features, n, *refs):
    g_ref, held_ref, wc_ref, mj_ref, perm_ref, bias_ref, left_ref = refs[:7]
    small_ref, out_ref, t_ref, db_ref = refs[7:]
    g, last = pl.program_id(0), pl.num_programs(0) - 1
    block, width = g_ref.shape[0], left_ref.shape[0]
    chunk = t_ref.shape[1] // (wc_ref.shape[1] // width)

    @pl.when(g == 0)
    def _():
        db_ref[...] = jnp.zeros_like(db_ref)

    span = chunk * depth
    fill_t(held_ref[pl.ds(pl.multiple_of(g * span, span), span), :width], wc_ref, t_ref, depth)
    db_ref[...] += dot_nt(t_ref[...], g_ref[...])

    @pl.when(g == last)
    def _():
        d_b = db_ref[...].T.astype(BF16)
        own = block // n
        for k in range(n):
            part = d_b[k * own : (k + 1) * own, :]
            for q in range(part.shape[1] // LANES):
                out_ref[k, q * own : (q + 1) * own, :] = part[:, q * LANES : (q + 1) * LANES]
        turned = dot_nt(perm_ref[...], d_b).astype(BF16)
        right = jnp.zeros((width, features), F32)
        for s in range(depth):
            right = right + dot(turned[s * width : (s + 1) * width, :], mj_ref[s])
        small = jnp.concatenate([left_ref[...], right], axis=1)
        small_ref[0:width, :] = small.astype(BF16)
        small_ref[width:, :] = jnp.broadcast_to(bias_ref[0:1, :], (16, LANES)).astype(BF16)


def update_kernel(depth, *refs):
    held_ref, offset_ref, wc_ref, small_ref, out_ref, pass_ref, t_ref = refs
    g = pl.program_id(0)
    chunk, block, pair = out_ref.shape
    width = wc_ref.shape[0]

    @pl.when(g == 0)
    def _():
        pass_ref[...] = small_ref[...]

    span = chunk * depth
    fill_t(held_ref[pl.ds(pl.multiple_of(g * span, span), span), :width], wc_ref, t_ref, depth)
    rows = held_ref.shape[0] - (pl.num_programs(0) - g) * block
    count = held_ref[pl.ds(pl.multiple_of(rows, block), block), :chunk]
    inv = 1.0 / (count.astype(F32) + 0.001)
    b = held_b(held_ref, block, width, depth)
    offset = offset_ref[...]
    for at in range(0, chunk, 2):
        part = dot(b, t_ref[:, at * pair : (at + 2) * pair])
        for k in range(2):
            value = part[:, k * pair : (k + 1) * pair] * inv[:, at + k : at + k + 1] + offset
            out_ref[at + k] = value.astype(BF16)


def owner_kernel(depth, own, features, *refs):
    da_refs, db_ref, small_refs = refs[:2], refs[2], refs[3:5]
    x_ref, wt_ref, perm_ref, dw_ref = refs[5:9]
    out_ref, factors_ref, bias_ref, placed_ref = refs[9:]
    for e in range(dw_ref.shape[0]):
        placed_ref[:, e, :] = dw_ref[e].astype(F32)
    rows = depth * own
    width = wt_ref.shape[0] // 2
    p, q = iota((rows, rows), 0), iota((rows, rows), 1)
    swap = one_hot(q == (p % own) * depth + p // own)
    d_a = dot_nt(swap, da_refs[0][...]) + dot_nt(swap, da_refs[1][...])
    d_b = dot_nt(db_ref[...], perm_ref[...])
    d_b = jnp.concatenate([d_b[:, s * width : (s + 1) * width] for s in range(depth)], axis=0)
    highest = lax.Precision.HIGHEST
    wt = wt_ref[...].astype(F32)
    d_normed = jnp.dot(d_a, wt[:width, :], precision=highest, preferred_element_type=F32)
    d_normed = d_normed + jnp.dot(d_b, wt[width:, :], precision=highest, preferred_element_type=F32)
    x = x_ref[...].astype(F32)
    d_normed = d_normed * x[:, features : features + 1]
    normed, scale = stats(x[:, :features])
    mean = jnp.mean(d_normed, axis=-1, keepdims=True)
    along = jnp.mean(d_normed * normed, axis=-1, keepdims=True)
    out_ref[...] = scale * (d_normed - mean - normed * along)
    small = small_refs[0][...].astype(F32) + small_refs[1][...].astype(F32)
    turned = small[:width].T
    factors_ref[...] = jnp.concatenate([turned[:features], turned[features:]], axis=1)
    bias_ref[...] = small[width : width + 1]


def lay_back(x, rows, lanes):
    if lanes % LANES:
        return x.reshape(rows, lanes)
    return x.reshape(lanes // LANES, rows, LANES).transpose(1, 0, 2).reshape(rows, lanes)


def bit_of(axis, bit):
    return (lax.axis_index(axis) >> bit) & 1


def swap_parts(parts, axis, bit, n):
    parts = [part.reshape(-1, LANES) for part in parts]
    message = jnp.concatenate(parts, axis=0) if len(parts) > 1 else parts[0]
    pairs = [(i, i ^ (1 << bit)) for i in range(n)]
    message = lax.ppermute(message, axis, pairs)
    got, at = [], 0
    for part in parts:
        got.append(message[at : at + part.shape[0]])
        at += part.shape[0]
    return got


def halves(x, axis, bit, at):
    here = bit_of(axis, bit)
    keep = lax.dynamic_index_in_dim(x, here, at, keepdims=False)
    return keep, lax.dynamic_index_in_dim(x, 1 - here, at, keepdims=False)


def split_high(x):
    return x.reshape((2, x.shape[0] // 2) + x.shape[1:])


def in_order(mine, other, axis, bit, at):
    first = bit_of(axis, bit) == 0
    low = jnp.where(first, mine, other)
    return jnp.stack([low, jnp.where(first, other, mine)], axis=at)


def unswap(x, axis, first):
    n = x.shape[0]
    for bit in range(n.bit_length() - 1):
        y = x.reshape((n >> (bit + 1), 2, 1 << bit) + x.shape[1:])
        x = jnp.where(bit_of(axis, bit + first) == 0, y, y[:, ::-1]).reshape(x.shape)
    return x


def add(mine, other):
    other = other.reshape(mine.shape)
    return lax.optimization_barrier((mine.astype(F32) + other.astype(F32)).astype(BF16))


def per_device(
    n,
    alignment_embedding,
    alignment_cell_exists,
    alignment_lines_exist,
    sitewise_factors,
    pairing_matrix,
    offset_vector,
    upstream_adjoint,
):
    depth, own, features = alignment_embedding.shape
    width = sitewise_factors.shape[1] // 2
    block, pair = upstream_adjoint.shape[0], upstream_adjoint.shape[2]
    rows, chunk = depth * own, 16
    steps = block // chunk
    split = own % 16 == 0
    axes = ("row", "col")
    sds = jax.ShapeDtypeStruct

    bits = n.bit_length() - 1
    mask = (alignment_cell_exists * alignment_lines_exist[:, None]).astype(BF16)
    mask = jnp.broadcast_to(mask[:, :, None], (depth, own, LANES - features))
    x = jnp.concatenate([alignment_embedding, mask], axis=2).reshape(rows, LANES)
    offset = offset_vector.reshape(1, pair)
    out_shapes = [sds((rows // 2 + own, LANES), BF16)] * 2
    by_token, by_row = call(
        functools.partial(prep_kernel, depth, own, features),
        (),
        [full(x.shape)],
        [full(o.shape) for o in out_shapes],
        out_shapes,
    )(x)
    message = jnp.concatenate([by_token, by_row[: rows // 2]], axis=0)
    both = in_order(message, *swap_parts([message], "col", 0, n), "col", 0, 0)
    message = both[:, : rows // 2 + own]
    held = [message]
    for k in range(2, n, 2):
        held.append(lax.ppermute(message, "col", [(j, j ^ k) for j in range(n)]))
    a_pieces = held
    if own % 16:
        held = unswap(jnp.stack(held), "col", 1).reshape((n,) + message.shape[1:])
        parts = held[:, : rows // 2].reshape(n, rows // 2, 2, features)
        mi = parts.transpose(0, 2, 1, 3).reshape(block * depth, features)
        a_pieces = [mi, held[:, rows // 2 :].reshape(block, LANES)]
    message = both[:, rows // 2 :]
    held = []
    half = n // 2
    for k in range(half):
        target = [((j >> 1) | (j & 1) * half) ^ half ^ k for j in range(n)]
        pairs = [(i * n + j, target[j] * n + i) for i in range(n) for j in range(n)]
        held.append(lax.ppermute(message, axes, pairs))
    j_pieces = held
    if own % 16:
        held = unswap(jnp.stack(held), "row", 0).reshape((n,) + message.shape[1:])
        parts = held[:, own:].reshape(n, depth // 2, own, 2, features)
        mj = parts.transpose(3, 1, 0, 2, 4).reshape(depth, block, features)
        j_pieces = [mj, held[:, :own].reshape(block, LANES)]

    wide = width * depth
    tokens = block * depth
    source = jnp.arange(wide)
    perm = (jnp.arange(wide)[None, :] == (source % width * depth + source // width)[:, None]).astype(BF16)
    up_spec = pl.BlockSpec((chunk, block, pair), lambda g: (g, 0, 0))
    args = (sitewise_factors, pairing_matrix, offset, upstream_adjoint)
    out_shapes = [
        sds((2 * width, features), BF16),
        sds((width, width * pair), BF16),
        sds((1, pair), F32),
        sds((8, pair), F32),
    ]
    factors_t, pairing_wide, offset, bias = call(
        factor_kernel,
        (),
        [full(v.shape) for v in args],
        [full(o.shape) for o in out_shapes],
        out_shapes,
        [pltpu.VMEM((width * width, pair), F32)],
    )(*args)

    out_shapes = [
        sds((block, block * pair), BF16),
        sds((tokens + block * wide // LANES + block * steps, LANES), BF16),
        sds((width * width, pair), BF16),
        sds((width, features), F32),
        sds((depth, block, features), BF16),
    ]
    args = (upstream_adjoint, factors_t, perm, pairing_wide, *a_pieces, *j_pieces)
    large = 2 * chunk
    g_spec = pl.BlockSpec((block, chunk * pair), lambda g: (0, g))
    large_spec = pl.BlockSpec((block, large * pair), lambda g: (0, g))
    scaled, held, d_pairing, left, mj = call(
        functools.partial(weight_kernel, depth, features, own, len(a_pieces), chunk),
        (block // large,),
        [pl.BlockSpec((large, block, pair), lambda g: (g, 0, 0))] + [full(v.shape) for v in args[1:]],
        [large_spec] + [full(o.shape) for o in out_shapes[1:]],
        out_shapes,
        [
            pltpu.VMEM((tokens, features), BF16),
            pltpu.VMEM((block, LANES), BF16),
            pltpu.VMEM((block, LANES), BF16),
            pltpu.VMEM((width + features, tokens), BF16),
            pltpu.VMEM((wide, block), BF16),
            pltpu.VMEM((steps, block, chunk), F32),
            pltpu.VMEM((large * depth, width * pair), BF16),
            pltpu.VMEM((width * width, pair), F32),
            pltpu.VMEM((features, width * pair), F32),
        ],
        cost(5e9, 8e6),
    )(*args)

    d_pairing = d_pairing.reshape(n, -1, LANES)
    for bit in reversed(range(1, bits)):
        keep, go = halves(split_high(d_pairing), "col", bit, 0)
        d_pairing = add(keep, *swap_parts([go], "col", bit, n))

    out_shapes = [sds((width + 16, LANES), BF16), sds((n, own * wide // LANES, LANES), BF16)]
    small, d_b = call(
        functools.partial(token_kernel, depth, features, n),
        (block // large,),
        [large_spec] + [full(v.shape) for v in (held, pairing_wide, mj, perm, bias, left)],
        [full(o.shape) for o in out_shapes],
        out_shapes,
        [pltpu.VMEM((wide, large * pair), BF16), pltpu.VMEM((wide, block), F32)],
        cost(8e9, 8e6),
    )(scaled, held, pairing_wide, mj, perm, bias, left)

    dp_keep, dp_go = halves(d_pairing, "col", 0, 0)
    db_keep, db_go = halves(d_b.reshape((n // 2, 2) + d_b.shape[1:]), "col", 0, 1)
    parts = swap_parts([dp_go, db_go, small], "col", 0, n)
    d_pairing, small = add(dp_keep, parts[0]), add(small, parts[2])
    d_b = in_order(db_keep, parts[1].reshape(db_keep.shape), "col", 0, 1)
    db_keep, db_go = halves(d_b, "row", 0, 1)
    for bit in range(bits):
        parts = swap_parts([d_pairing, db_go, small], "row", bit, n)
        if bit == 0:
            args = (held, offset, pairing_wide, small)
            coupling_update, small = call(
                functools.partial(update_kernel, depth),
                (steps,),
                [full(v.shape) for v in args],
                [up_spec, full(small.shape)],
                [sds((block, block, pair), BF16), sds(small.shape, BF16)],
                [pltpu.VMEM((wide, chunk * pair), BF16)],
                cost(6e9, 8e6),
            )(*args)
        if bit == 1:
            half = (tokens // LANES // 2, width, LANES)
            out_shapes = [sds(half, BF16), sds(half, BF16), sds(small.shape, BF16)]
            *d_a, small = call(
                functools.partial(left_kernel, depth, bits - 1),
                (steps,),
                [g_spec] + [full(v.shape) for v in (held, pairing_wide, small)],
                [full(o.shape) for o in out_shapes],
                out_shapes,
                [
                    pltpu.VMEM((chunk * depth, width * pair), BF16),
                    pltpu.VMEM((width * pair, width), BF16),
                    pltpu.VMEM((tokens // LANES, width, LANES), BF16),
                    pltpu.VMEM((wide, block), BF16),
                ],
                cost(6e9, 8e6),
            )(scaled, held, pairing_wide, small)
            if rows % LANES:
                shape = (-1, width, LANES // rows, rows)
                d_a = [part.reshape(shape).transpose(0, 2, 1, 3) for part in d_a]
            da_keep, da_go = [part.reshape(n // 2, -1, LANES) for part in d_a]
        d_pairing, d_b, small = add(d_pairing, parts[0]), add(db_keep, parts[1]), add(small, parts[2])
        db_keep = db_go = d_b
    d_pairing = d_pairing.reshape(1, -1, LANES)
    small_parts = [small]
    for bit in reversed(range(1, bits)):
        if bit < bits - 1:
            small_parts = [add(*small_parts)]
            da_keep, da_go = halves(split_high(add(*da_parts)), "col", bit, 0)
        db_keep, db_go = halves(split_high(d_b), "col", bit, 0)
        parts = swap_parts([d_pairing, db_go, da_go, small_parts[0]], "col", bit, n)
        d_pairing = in_order(d_pairing, parts[0].reshape(d_pairing.shape), "col", bit, 1)
        d_pairing = d_pairing.reshape((-1,) + d_pairing.shape[2:])
        mine = bit_of("col", bit) == bit_of("row", bit)
        d_b = jnp.where(mine, db_keep, parts[1].reshape(db_keep.shape))
        da_parts = [da_keep, parts[2].reshape(da_keep.shape)]
        small_parts = [small_parts[0], parts[3]]
    da_keep, da_go = halves(add(*da_parts), "col", 0, 0)
    got, da_got = swap_parts([d_pairing, da_go], "col", 0, n)
    d_pairing = in_order(d_pairing, got.reshape(d_pairing.shape), "col", 0, 1)
    d_a = [lay_back(part.reshape(-1, LANES), width, rows) for part in (da_keep, da_got)]
    d_b = lay_back(d_b[0], own, wide)

    d_pairing = d_pairing.reshape(width, width, pair)
    args = (*d_a, d_b, *small_parts, x, factors_t, perm, d_pairing)
    out_shapes = [
        sds((rows, features), F32),
        sds((features, 2 * width), F32),
        sds((1, pair), F32),
        sds((width, width, pair), F32),
    ]
    embedding_adjoint, factors_adjoint, offset_slope, placed = call(
        functools.partial(owner_kernel, depth, own, features),
        (),
        [full(v.shape) for v in args],
        [full(o.shape) for o in out_shapes],
        out_shapes,
    )(*args)
    return (
        coupling_update,
        embedding_adjoint.reshape(depth, own, features),
        factors_adjoint,
        placed.reshape(width * width, pair),
        offset_slope.reshape(pair),
    )


def solution(mesh):
    n = mesh.shape["col"]
    placed = (
        P(None, ("groups", "row", "col"), None),
        P(None, ("groups", "row", "col")),
        P("groups"),
        P(),
        P(),
        P(),
        P(("groups", "row"), "col", None),
    )
    return jax.shard_map(
        functools.partial(per_device, n),
        mesh=mesh,
        in_specs=placed,
        out_specs=(
            P(("groups", "row"), "col", None),
            P(None, ("groups", "row", "col"), None),
            P("groups", None),
            P("groups", None),
            P("groups"),
        ),
        check_vma=False,
    )
```

```python
import functools

import jax
import jax.numpy as jnp
from jax import lax
from jax.experimental import pallas as pl
from jax.experimental.pallas import tpu as pltpu
from jax.sharding import PartitionSpec as P

F32 = jnp.float32
BF16 = jnp.bfloat16
LANES = 128
VMEM_LIMIT = 16 * 1024 * 1024
NT = (((1,), (1,)), ((), ()))


def dot(left, right):
    return jnp.dot(left, right, preferred_element_type=F32)


def dot_nt(left, right):
    return lax.dot_general(left, right, NT, preferred_element_type=F32)


def iota(shape, axis):
    return lax.broadcasted_iota(jnp.int32, shape, axis)


def one_hot(mask):
    return jnp.where(mask, 1.0, 0.0).astype(BF16)


def full(shape):
    return pl.BlockSpec(shape, lambda *g: (0,) * len(shape))


def cost(flops, nbytes):
    return pl.CostEstimate(flops=int(flops), bytes_accessed=int(nbytes), transcendentals=0)


def call(kernel, grid, in_specs, out_specs, out_shape, scratch=(), estimate=None):
    return pl.pallas_call(
        kernel,
        grid=grid,
        in_specs=in_specs,
        out_specs=out_specs,
        out_shape=out_shape,
        scratch_shapes=list(scratch),
        compiler_params=pltpu.CompilerParams(vmem_limit_bytes=VMEM_LIMIT),
        cost_estimate=estimate,
    )


def stats(x):
    center = x - jnp.mean(x, axis=-1, keepdims=True)
    scale = lax.rsqrt(jnp.mean(center * center, axis=-1, keepdims=True) + 1e-05)
    return center * scale, scale


def prep_kernel(depth, own, features, x_ref, by_token_ref, by_row_ref):
    rows = depth * own
    half = rows // 2
    x = x_ref[...].astype(F32)
    weight = x[:, features : features + 1]
    normed, _ = stats(x[:, :features])
    masked = normed.astype(BF16).astype(F32) * weight
    by_row_ref[:half, :] = jnp.concatenate([masked[:half], masked[half:]], axis=1).astype(BF16)
    p, q = iota((rows, rows), 0), iota((rows, rows), 1)
    swap = one_hot(q == (p % depth) * own + p // depth)
    turned = dot(swap, masked.astype(BF16))
    by_token_ref[:half, :] = jnp.concatenate([turned[:half], turned[half:]], axis=1).astype(BF16)
    here = one_hot(iota((own, rows), 0) == iota((own, rows), 1) % own)
    at = iota((rows, LANES), 1) == iota((rows, LANES), 0) // own
    mask = dot(here, jnp.where(at, weight, 0.0).astype(BF16)).astype(BF16)
    by_row_ref[half:, :] = mask
    by_token_ref[half:, :] = mask


def fill_v(g_ref, bt, v_ref, depth):
    width = bt.shape[0] // depth
    pair = v_ref.shape[1] // width
    for at in range(0, v_ref.shape[0] // depth, 2):
        v = dot(bt, g_ref[:, at * pair : (at + 2) * pair]).astype(BF16)
        for k in range(2):
            rows = slice((at + k) * depth, (at + k + 1) * depth)
            for e in range(width):
                part = v[e * depth : (e + 1) * depth, k * pair : (k + 1) * pair]
                v_ref[rows, e * pair : (e + 1) * pair] = part


def fill_t(a_chunk, wc_ref, t_ref, depth):
    width = wc_ref.shape[0]
    pair = wc_ref.shape[1] // width
    for e in range(0, width, 2):
        t = dot(a_chunk, wc_ref[:, e * pair : (e + 2) * pair]).astype(BF16)
        for k in range(2):
            rows = slice((e + k) * depth, (e + k + 1) * depth)
            for i in range(a_chunk.shape[0] // depth):
                part = t[i * depth : (i + 1) * depth, k * pair : (k + 1) * pair]
                t_ref[rows, i * pair : (i + 1) * pair] = part


def held_b(held_ref, block, width, depth):
    at = block * depth
    tiles = width * depth // LANES
    return jnp.concatenate([held_ref[at + k * block : at + (k + 1) * block, :] for k in range(tiles)], axis=1)


def factor_kernel(own, depth, features, pieces, *refs):
    w_ref, wide_ref, offset_ref = refs[:3]
    a_refs, refs = refs[3 : 3 + pieces], refs[3 + pieces :]
    t_ref, wt_ref, wc_ref, pass_ref, a_ref, at_ref, seen_ref, rows_ref, mi_ref = refs
    g = pl.program_id(0)
    width = w_ref.shape[1] // 2
    pair = wide_ref.shape[1]

    @pl.when(g == 0)
    def _():
        pass_ref[...] = offset_ref[...]
        rows_ref[...] = wide_ref[...].astype(F32)
        for e in range(width):
            part = rows_ref[pl.ds(e, width, stride=width), :]
            wc_ref[:, e * pair : (e + 1) * pair] = part.astype(BF16)
        if own % 16 == 0:
            unpack(depth, own, features, a_refs, (), mi_ref, None, seen_ref, None)
        else:
            mi_ref[...], seen_ref[...] = a_refs[0][...], a_refs[1][...]
        same = one_hot(iota((2 * width, 2 * width), 0) == iota((2 * width, 2 * width), 1))
        wt = dot_nt(same, w_ref[...]).astype(BF16)
        wt_ref[...] = wt
        mi = mi_ref[...]
        a_ref[...] = dot_nt(mi, wt[:width, :]).astype(BF16)
        same = one_hot(iota((features, features), 0) == iota((features, features), 1))
        at_ref[...] = dot_nt(jnp.concatenate([wt[:width, :], same], axis=0), mi).astype(BF16)

    span = t_ref.shape[1] // pair * depth
    fill_t(a_ref[pl.ds(pl.multiple_of(g * span, span), span), :], wc_ref, t_ref, depth)


def unpack(depth, own, features, a_refs, j_refs, mi_ref, mj_ref, seen_i_ref, seen_j_ref):
    half = depth * own // 2
    for k, ref in enumerate(a_refs):
        for core in range(2):
            at = ((lax.axis_index("col") >> 1) ^ k) * 2 + core
            for q in range(2):
                rows = pl.ds(pl.multiple_of((at * 2 + q) * half, half), half)
                mi_ref[rows, :] = ref[core, :half, q * features : (q + 1) * features]
            rows = pl.ds(pl.multiple_of(at * own, own), own)
            seen_i_ref[rows, :] = ref[core, half:, :]
    half = depth // 2
    for k, ref in enumerate(j_refs):
        for core in range(2):
            at = ((lax.axis_index("row") & (len(j_refs) - 1)) ^ k) * 2 + core
            rows = pl.ds(pl.multiple_of(at * own, own), own)
            seen_j_ref[rows, :] = ref[core, :own, :]
            for s in range(depth):
                lanes = slice(s // half * features, (s // half + 1) * features)
                start = own + s % half * own
                mj_ref[s, rows, :] = ref[core, start : start + own, lanes]


def weight_kernel(depth, features, own, pieces, part_size, *refs):
    up_ref, _, wt_ref, perm_ref, wc_ref, a_ref, at_ref, seen_i_ref = refs[:8]
    j_refs, refs = refs[8 : 8 + pieces], refs[8 + pieces :]
    g_ref, held_ref, dw_ref, left_ref, mj_ref, bias_ref = refs[:6]
    seen_j_ref, bt_ref, inv_ref, v_ref, acc_ref, wide_ref = refs[6:]
    g, last = pl.program_id(0), pl.num_programs(0) - 1
    chunk, block, pair = up_ref.shape
    width = wt_ref.shape[0] // 2

    @pl.when(g == 0)
    def _():
        if own % 16 == 0:
            unpack(depth, own, features, (), j_refs, None, mj_ref, None, seen_j_ref)
        else:
            mj_ref[...], seen_j_ref[...] = j_refs[0][...], j_refs[1][...]
        wt = wt_ref[...]
        held_ref[: block * depth, :width] = a_ref[...]
        bias_ref[...] = jnp.zeros_like(bias_ref)
        b = jnp.zeros((block, width * depth), F32)
        for s in range(depth):
            part = dot_nt(mj_ref[s], wt[width:, :]).astype(BF16)
            b = b + dot(part, perm_ref[s * width : (s + 1) * width, :])
        bt_ref[...] = b.T.astype(BF16)
        at = block * depth
        for k in range(width * depth // LANES):
            held_ref[at : at + block, :] = b[:, k * LANES : (k + 1) * LANES].astype(BF16)
            at += block
        for k in range(block // part_size):
            rows = slice(k * part_size, (k + 1) * part_size)
            count = dot_nt(seen_j_ref[...], seen_i_ref[rows, :])
            inv_ref[k] = 1.0 / (count + 0.001)
            held_ref[at : at + block, :part_size] = count.astype(BF16)
            at += block
        acc_ref[...] = jnp.zeros_like(acc_ref)
        wide_ref[...] = jnp.zeros_like(wide_ref)

    bias = jnp.zeros((block, pair), F32)
    for k in range(chunk // part_size):
        inv = inv_ref[g * (chunk // part_size) + k]
        for i in range(part_size):
            up = up_ref[k * part_size + i].astype(F32)
            bias = bias + up
            at = (k * part_size + i) * pair
            g_ref[:, at : at + pair] = (up * inv[:, i : i + 1]).astype(BF16)
    bias_ref[0:1, :] += jnp.sum(bias, axis=0, keepdims=True)
    fill_v(g_ref, bt_ref[...], v_ref, depth)
    span = chunk * depth
    a_t = at_ref[:, pl.ds(pl.multiple_of(g * span, span), span)]
    for e in range(0, width, 2):
        part = dot(a_t, v_ref[:, e * pair : (e + 2) * pair])
        for k in range(2):
            rows = slice((e + k) * width, (e + k + 1) * width)
            acc_ref[rows, :] += part[:width, k * pair : (k + 1) * pair]
        wide_ref[:, e * pair : (e + 2) * pair] += part[width:]

    @pl.when(g == last)
    def _():
        dw_ref[...] = acc_ref[...].astype(BF16)
        left = jnp.zeros((width, features), F32)
        for e in range(0, width, 2):
            lanes = slice(e * pair, (e + 2) * pair)
            left = left + dot_nt(wc_ref[:, lanes], wide_ref[:, lanes].astype(BF16))
        left_ref[...] = left


def left_kernel(depth, bit, *refs):
    g_ref, held_ref, wc_ref, small_ref, keep_ref, go_ref, pass_ref, v_ref, wd_ref, da_ref, bt_ref = refs
    g, last = pl.program_id(0), pl.num_programs(0) - 1
    block, width = g_ref.shape[0], wc_ref.shape[0]
    pair = wc_ref.shape[1] // width
    span = v_ref.shape[0]

    @pl.when(g == 0)
    def _():
        pass_ref[...] = small_ref[...]
        bt_ref[...] = held_b(held_ref, block, width, depth).astype(F32).T.astype(BF16)
        same = one_hot(iota((2 * pair, 2 * pair), 0) == iota((2 * pair, 2 * pair), 1))
        for at in range(0, wd_ref.shape[0], 2 * pair):
            wd_ref[at : at + 2 * pair, :] = dot_nt(same, wc_ref[:, at : at + 2 * pair]).astype(BF16)

    fill_v(g_ref, bt_ref[...], v_ref, depth)
    d_a = jnp.zeros((span, width), F32)
    each = v_ref.shape[1] // 4
    for at in range(0, 4 * each, each):
        d_a = d_a + dot(v_ref[:, at : at + each], wd_ref[at : at + each, :])
    same = one_hot(iota((width, width), 0) == iota((width, width), 1))
    d_a = dot_nt(same, d_a.astype(BF16)).astype(BF16)
    tiles = span // LANES
    for k in range(tiles):
        da_ref[g * tiles + k] = d_a[:, k * LANES : (k + 1) * LANES]

    @pl.when(g == last)
    def _():
        half = keep_ref.shape[0]
        here = (lax.axis_index("col") >> bit) & 1
        keep_ref[...] = da_ref[pl.ds(here * half, half)]
        go_ref[...] = da_ref[pl.ds((1 - here) * half, half)]


def token_kernel(depth, features, n, *refs):
    g_ref, t_ref, _, mj_ref, perm_ref, bias_ref, left_ref, small_ref, out_ref, db_ref = refs
    g, last = pl.program_id(0), pl.num_programs(0) - 1
    block, width = g_ref.shape[0], left_ref.shape[0]

    @pl.when(g == 0)
    def _():
        db_ref[...] = jnp.zeros_like(db_ref)

    db_ref[...] += dot_nt(t_ref[...], g_ref[...])

    @pl.when(g == last)
    def _():
        d_b = db_ref[...].T.astype(BF16)
        own = block // n
        for k in range(n):
            part = d_b[k * own : (k + 1) * own, :]
            for q in range(part.shape[1] // LANES):
                out_ref[k, q * own : (q + 1) * own, :] = part[:, q * LANES : (q + 1) * LANES]
        turned = dot_nt(perm_ref[...], d_b).astype(BF16)
        right = jnp.zeros((width, features), F32)
        for s in range(depth):
            right = right + dot(turned[s * width : (s + 1) * width, :], mj_ref[s])
        small = jnp.concatenate([left_ref[...], right], axis=1)
        small_ref[0:width, :] = small.astype(BF16)
        small_ref[width:, :] = jnp.broadcast_to(bias_ref[0:1, :], (16, LANES)).astype(BF16)


def update_kernel(depth, *refs):
    held_ref, offset_ref, wc_ref, small_ref, out_ref, pass_ref, t_ref = refs
    g = pl.program_id(0)
    chunk, block, pair = out_ref.shape
    width = wc_ref.shape[0]

    @pl.when(g == 0)
    def _():
        pass_ref[...] = small_ref[...]

    span = chunk * depth
    fill_t(held_ref[pl.ds(pl.multiple_of(g * span, span), span), :width], wc_ref, t_ref, depth)
    rows = held_ref.shape[0] - (pl.num_programs(0) - g) * block
    count = held_ref[pl.ds(pl.multiple_of(rows, block), block), :chunk]
    inv = 1.0 / (count.astype(F32) + 0.001)
    b = held_b(held_ref, block, width, depth)
    offset = offset_ref[...]
    for at in range(0, chunk, 2):
        part = dot(b, t_ref[:, at * pair : (at + 2) * pair])
        for k in range(2):
            value = part[:, k * pair : (k + 1) * pair] * inv[:, at + k : at + k + 1] + offset
            out_ref[at + k] = value.astype(BF16)


def owner_kernel(depth, own, features, *refs):
    da_refs, db_ref, small_refs = refs[:2], refs[2], refs[3:5]
    x_ref, wt_ref, perm_ref, dw_ref = refs[5:9]
    out_ref, factors_ref, bias_ref, placed_ref = refs[9:]
    for e in range(dw_ref.shape[0]):
        placed_ref[:, e, :] = dw_ref[e].astype(F32)
    rows = depth * own
    width = wt_ref.shape[0] // 2
    p, q = iota((rows, rows), 0), iota((rows, rows), 1)
    swap = one_hot(q == (p % own) * depth + p // own)
    d_a = dot_nt(swap, da_refs[0][...]) + dot_nt(swap, da_refs[1][...])
    d_b = dot_nt(db_ref[...], perm_ref[...])
    d_b = jnp.concatenate([d_b[:, s * width : (s + 1) * width] for s in range(depth)], axis=0)
    highest = lax.Precision.HIGHEST
    wt = wt_ref[...].astype(F32)
    d_normed = jnp.dot(d_a, wt[:width, :], precision=highest, preferred_element_type=F32)
    d_normed = d_normed + jnp.dot(d_b, wt[width:, :], precision=highest, preferred_element_type=F32)
    x = x_ref[...].astype(F32)
    d_normed = d_normed * x[:, features : features + 1]
    normed, scale = stats(x[:, :features])
    mean = jnp.mean(d_normed, axis=-1, keepdims=True)
    along = jnp.mean(d_normed * normed, axis=-1, keepdims=True)
    out_ref[...] = scale * (d_normed - mean - normed * along)
    small = small_refs[0][...].astype(F32) + small_refs[1][...].astype(F32)
    turned = small[:width].T
    factors_ref[...] = jnp.concatenate([turned[:features], turned[features:]], axis=1)
    bias_ref[...] = small[width : width + 1]


def lay_back(x, rows, lanes):
    if lanes % LANES:
        return x.reshape(rows, lanes)
    return x.reshape(lanes // LANES, rows, LANES).transpose(1, 0, 2).reshape(rows, lanes)


def bit_of(axis, bit):
    return (lax.axis_index(axis) >> bit) & 1


def swap_parts(parts, axis, bit, n):
    parts = [part.reshape(-1, LANES) for part in parts]
    message = jnp.concatenate(parts, axis=0) if len(parts) > 1 else parts[0]
    pairs = [(i, i ^ (1 << bit)) for i in range(n)]
    message = lax.ppermute(message, axis, pairs)
    got, at = [], 0
    for part in parts:
        got.append(message[at : at + part.shape[0]])
        at += part.shape[0]
    return got


def halves(x, axis, bit, at):
    here = bit_of(axis, bit)
    keep = lax.dynamic_index_in_dim(x, here, at, keepdims=False)
    return keep, lax.dynamic_index_in_dim(x, 1 - here, at, keepdims=False)


def split_high(x):
    return x.reshape((2, x.shape[0] // 2) + x.shape[1:])


def in_order(mine, other, axis, bit, at):
    first = bit_of(axis, bit) == 0
    low = jnp.where(first, mine, other)
    return jnp.stack([low, jnp.where(first, other, mine)], axis=at)


def unswap(x, axis, first):
    n = x.shape[0]
    for bit in range(n.bit_length() - 1):
        y = x.reshape((n >> (bit + 1), 2, 1 << bit) + x.shape[1:])
        x = jnp.where(bit_of(axis, bit + first) == 0, y, y[:, ::-1]).reshape(x.shape)
    return x


def add(mine, other):
    other = other.reshape(mine.shape)
    return lax.optimization_barrier((mine.astype(F32) + other.astype(F32)).astype(BF16))


def per_device(
    n,
    alignment_embedding,
    alignment_cell_exists,
    alignment_lines_exist,
    sitewise_factors,
    pairing_matrix,
    offset_vector,
    upstream_adjoint,
):
    depth, own, features = alignment_embedding.shape
    width = sitewise_factors.shape[1] // 2
    block, pair = upstream_adjoint.shape[0], upstream_adjoint.shape[2]
    rows, chunk = depth * own, 16
    steps = block // chunk
    split = own % 16 == 0
    axes = ("row", "col")
    sds = jax.ShapeDtypeStruct

    bits = n.bit_length() - 1
    mask = (alignment_cell_exists * alignment_lines_exist[:, None]).astype(BF16)
    mask = jnp.broadcast_to(mask[:, :, None], (depth, own, LANES - features))
    x = jnp.concatenate([alignment_embedding, mask], axis=2).reshape(rows, LANES)
    offset = offset_vector.reshape(1, pair)
    out_shapes = [sds((rows // 2 + own, LANES), BF16)] * 2
    by_token, by_row = call(
        functools.partial(prep_kernel, depth, own, features),
        (),
        [full(x.shape)],
        [full(o.shape) for o in out_shapes],
        out_shapes,
    )(x)
    message = jnp.concatenate([by_token, by_row[: rows // 2]], axis=0)
    both = in_order(message, *swap_parts([message], "col", 0, n), "col", 0, 0)
    message = both[:, : rows // 2 + own]
    held = [message]
    for k in range(2, n, 2):
        held.append(lax.ppermute(message, "col", [(j, j ^ k) for j in range(n)]))
    a_pieces = held
    if own % 16:
        held = unswap(jnp.stack(held), "col", 1).reshape((n,) + message.shape[1:])
        parts = held[:, : rows // 2].reshape(n, rows // 2, 2, features)
        mi = parts.transpose(0, 2, 1, 3).reshape(block * depth, features)
        a_pieces = [mi, held[:, rows // 2 :].reshape(block, LANES)]
    message = both[:, rows // 2 :]
    held = []
    half = n // 2
    for k in range(half):
        target = [((j >> 1) | (j & 1) * half) ^ half ^ k for j in range(n)]
        pairs = [(i * n + j, target[j] * n + i) for i in range(n) for j in range(n)]
        held.append(lax.ppermute(message, axes, pairs))
    j_pieces = held
    if own % 16:
        held = unswap(jnp.stack(held), "row", 0).reshape((n,) + message.shape[1:])
        parts = held[:, own:].reshape(n, depth // 2, own, 2, features)
        mj = parts.transpose(3, 1, 0, 2, 4).reshape(depth, block, features)
        j_pieces = [mj, held[:, :own].reshape(block, LANES)]

    wide = width * depth
    tokens = block * depth
    source = jnp.arange(wide)
    perm = (jnp.arange(wide)[None, :] == (source % width * depth + source // width)[:, None]).astype(BF16)
    up_spec = pl.BlockSpec((chunk, block, pair), lambda g: (g, 0, 0))
    args = (sitewise_factors, pairing_matrix, offset, *a_pieces)
    out_shapes = [
        sds((wide, block * pair), BF16),
        sds((2 * width, features), BF16),
        sds((width, width * pair), BF16),
        sds((1, pair), F32),
        sds((tokens, width), BF16),
        sds((width + features, tokens), BF16),
        sds((block, LANES), BF16),
    ]
    t, factors_t, pairing_wide, offset, a, a_t, seen = call(
        functools.partial(factor_kernel, own, depth, features, len(a_pieces)),
        (steps,),
        [full(v.shape) for v in args],
        [pl.BlockSpec((wide, chunk * pair), lambda g: (0, g))] + [full(o.shape) for o in out_shapes[1:]],
        out_shapes,
        [pltpu.VMEM((width * width, pair), F32), pltpu.VMEM((tokens, features), BF16)],
        cost(3e9, 8e6),
    )(*args)

    out_shapes = [
        sds((block, block * pair), BF16),
        sds((tokens + block * wide // LANES + block * steps, LANES), BF16),
        sds((width * width, pair), BF16),
        sds((width, features), F32),
        sds((depth, block, features), BF16),
        sds((8, pair), F32),
    ]
    args = (upstream_adjoint, t, factors_t, perm, pairing_wide, a, a_t, seen, *j_pieces)
    large = 2 * chunk
    g_spec = pl.BlockSpec((block, chunk * pair), lambda g: (0, g))
    large_spec = pl.BlockSpec((block, large * pair), lambda g: (0, g))
    scaled, held, d_pairing, left, mj, bias = call(
        functools.partial(weight_kernel, depth, features, own, len(j_pieces), chunk),
        (block // large,),
        [pl.BlockSpec((large, block, pair), lambda g: (g, 0, 0)), pl.BlockSpec(memory_space=pl.ANY)]
        + [full(v.shape) for v in args[2:]],
        [large_spec] + [full(o.shape) for o in out_shapes[1:]],
        out_shapes,
        [
            pltpu.VMEM((block, LANES), BF16),
            pltpu.VMEM((wide, block), BF16),
            pltpu.VMEM((steps, block, chunk), F32),
            pltpu.VMEM((large * depth, width * pair), BF16),
            pltpu.VMEM((width * width, pair), F32),
            pltpu.VMEM((features, width * pair), F32),
        ],
        cost(5e9, 8e6),
    )(*args)

    d_pairing = d_pairing.reshape(n, -1, LANES)
    for bit in reversed(range(1, bits)):
        keep, go = halves(split_high(d_pairing), "col", bit, 0)
        d_pairing = add(keep, *swap_parts([go], "col", bit, n))

    out_shapes = [sds((width + 16, LANES), BF16), sds((n, own * wide // LANES, LANES), BF16)]
    small, d_b = call(
        functools.partial(token_kernel, depth, features, n),
        (block // large,),
        [large_spec, pl.BlockSpec((wide, large * pair), lambda g: (0, g))]
        + [full(v.shape) for v in (held, mj, perm, bias, left)],
        [full(o.shape) for o in out_shapes],
        out_shapes,
        [pltpu.VMEM((wide, block), F32)],
        cost(8e9, 8e6),
    )(scaled, t, held, mj, perm, bias, left)

    dp_keep, dp_go = halves(d_pairing, "col", 0, 0)
    db_keep, db_go = halves(d_b.reshape((n // 2, 2) + d_b.shape[1:]), "col", 0, 1)
    parts = swap_parts([dp_go, db_go, small], "col", 0, n)
    d_pairing, small = add(dp_keep, parts[0]), add(small, parts[2])
    d_b = in_order(db_keep, parts[1].reshape(db_keep.shape), "col", 0, 1)
    db_keep, db_go = halves(d_b, "row", 0, 1)
    for bit in range(bits):
        parts = swap_parts([d_pairing, db_go, small], "row", bit, n)
        if bit == 0:
            args = (held, offset, pairing_wide, small)
            coupling_update, small = call(
                functools.partial(update_kernel, depth),
                (steps,),
                [full(v.shape) for v in args],
                [up_spec, full(small.shape)],
                [sds((block, block, pair), BF16), sds(small.shape, BF16)],
                [pltpu.VMEM((wide, chunk * pair), BF16)],
                cost(6e9, 8e6),
            )(*args)
        if bit == 1:
            half = (tokens // LANES // 2, width, LANES)
            out_shapes = [sds(half, BF16), sds(half, BF16), sds(small.shape, BF16)]
            *d_a, small = call(
                functools.partial(left_kernel, depth, bits - 1),
                (steps,),
                [g_spec] + [full(v.shape) for v in (held, pairing_wide, small)],
                [full(o.shape) for o in out_shapes],
                out_shapes,
                [
                    pltpu.VMEM((chunk * depth, width * pair), BF16),
                    pltpu.VMEM((width * pair, width), BF16),
                    pltpu.VMEM((tokens // LANES, width, LANES), BF16),
                    pltpu.VMEM((wide, block), BF16),
                ],
                cost(6e9, 8e6),
            )(scaled, held, pairing_wide, small)
            if rows % LANES:
                shape = (-1, width, LANES // rows, rows)
                d_a = [part.reshape(shape).transpose(0, 2, 1, 3) for part in d_a]
            da_keep, da_go = [part.reshape(n // 2, -1, LANES) for part in d_a]
        d_pairing, d_b, small = add(d_pairing, parts[0]), add(db_keep, parts[1]), add(small, parts[2])
        db_keep = db_go = d_b
    d_pairing = d_pairing.reshape(1, -1, LANES)
    small_parts = [small]
    for bit in reversed(range(1, bits)):
        if bit < bits - 1:
            small_parts = [add(*small_parts)]
            da_keep, da_go = halves(split_high(add(*da_parts)), "col", bit, 0)
        db_keep, db_go = halves(split_high(d_b), "col", bit, 0)
        parts = swap_parts([d_pairing, db_go, da_go, small_parts[0]], "col", bit, n)
        d_pairing = in_order(d_pairing, parts[0].reshape(d_pairing.shape), "col", bit, 1)
        d_pairing = d_pairing.reshape((-1,) + d_pairing.shape[2:])
        mine = bit_of("col", bit) == bit_of("row", bit)
        d_b = jnp.where(mine, db_keep, parts[1].reshape(db_keep.shape))
        da_parts = [da_keep, parts[2].reshape(da_keep.shape)]
        small_parts = [small_parts[0], parts[3]]
    da_keep, da_go = halves(add(*da_parts), "col", 0, 0)
    got, da_got = swap_parts([d_pairing, da_go], "col", 0, n)
    d_pairing = in_order(d_pairing, got.reshape(d_pairing.shape), "col", 0, 1)
    d_a = [lay_back(part.reshape(-1, LANES), width, rows) for part in (da_keep, da_got)]
    d_b = lay_back(d_b[0], own, wide)

    d_pairing = d_pairing.reshape(width, width, pair)
    args = (*d_a, d_b, *small_parts, x, factors_t, perm, d_pairing)
    out_shapes = [
        sds((rows, features), F32),
        sds((features, 2 * width), F32),
        sds((1, pair), F32),
        sds((width, width, pair), F32),
    ]
    embedding_adjoint, factors_adjoint, offset_slope, placed = call(
        functools.partial(owner_kernel, depth, own, features),
        (),
        [full(v.shape) for v in args],
        [full(o.shape) for o in out_shapes],
        out_shapes,
    )(*args)
    return (
        coupling_update,
        embedding_adjoint.reshape(depth, own, features),
        factors_adjoint,
        placed.reshape(width * width, pair),
        offset_slope.reshape(pair),
    )


def solution(mesh):
    n = mesh.shape["col"]
    placed = (
        P(None, ("groups", "row", "col"), None),
        P(None, ("groups", "row", "col")),
        P("groups"),
        P(),
        P(),
        P(),
        P(("groups", "row"), "col", None),
    )
    return jax.shard_map(
        functools.partial(per_device, n),
        mesh=mesh,
        in_specs=placed,
        out_specs=(
            P(("groups", "row"), "col", None),
            P(None, ("groups", "row", "col"), None),
            P("groups", None),
            P("groups", None),
            P("groups"),
        ),
        check_vma=False,
    )
```
